32 devices in a mesh: groups: 2 (over y), expert: 16 (over z, x, core).
Axes of the slice: x: 2, y: 2, z: 4, core: 2. Of those that a mesh axis runs over, the one named last changes fastest.
Arguments:
- hidden_of_route: bfloat16 [4096, 8, 1024], P(('groups', 'expert')), parts along dimension 0, may hold values from -6 to 6
- expert_of_route: int32 [4096, 8], P(('groups', 'expert')), parts along dimension 0, may hold values from 0 to 15, all different within a row; in each aligned block of 128 rows (0 to 127, 128 to 255, ...) at most 128 rows name the same one
- gate_of_route: bfloat16 [4096, 8], P(('groups', 'expert')), parts along dimension 0, may hold values from 0.019897461 to 0.25
- capacity: int32 [32], P('groups'), parts along dimension 0, may hold values from 512 to 2048
- output_gradient: bfloat16 [4096, 2048], P(('groups', 'expert')), parts along dimension 0, may hold values from -0.796875 to 0.796875
- curvature: float32 [4096], P(('groups', 'expert')), parts along dimension 0, may hold values from 0.01 to 0.1
- adapter_down: float32 [16, 1024, 16], P('expert'), may hold values from -0.1875 to 0.1875
- adapter_up: float32 [16, 16, 2048], P('expert'), may hold values from -1.5 to 1.5
- down_direction: float32 [32, 1024, 16], P(('groups', 'expert')), parts along dimension 0, may hold values from -0.1875 to 0.1875
- up_direction: float32 [32, 16, 2048], P(('groups', 'expert')), parts along dimension 0, may hold values from -1.5 to 1.5
Outputs:
- down_gradient: float32 [32, 1024, 16], P(('groups', 'expert')), parts along dimension 0
- up_gradient: float32 [32, 16, 2048], P(('groups', 'expert')), parts along dimension 0
- curvature_down: float32 [32, 1024, 16], P(('groups', 'expert')), parts along dimension 0
- curvature_up: float32 [32, 16, 2048], P(('groups', 'expert')), parts along dimension 0
The draws below stay inside these ranges and needn't reach their ends.
There are 2 independent parts, one for each index of `groups`. The reference program is written for one: setup_inputs(seed, part) draws one part's arguments, and reference() takes and returns one part's arrays. A program takes and returns all parts, laid end to end along the dimension named above; an argument that names none is the same for every part. Nothing has to cross between parts.
Inputs may be any that keep to these rules, and one draw needn't show every extreme that they name: `expert_of_route`: each token names 8 different experts; the tokens of one block of 128 name one expert at most 128 times, a bound that some block reaches.
All inputs are finite; a program needn't handle non-finite values.
Results may differ from the reference program's by a relative error of at most 0.0017.
Values may be sent and summed in bfloat16 or wider, within the bound.
No kernel may reach another device: no remote copies, remote signals or barrier semaphores. Data moves between devices by JAX's collectives and lax.ppermute only.
A program may use at most 128 MiB of HBM per device.

```python
import math
import jax
import jax.numpy as jnp
import numpy as np
from jax import lax

OUTPUT_FEATURES = 2048
EXPERT_HIDDEN = 1024
ADAPTER_RANK = 16
TOP = 8
EXP_DEV = 1
TOK_DEV = 128
EXPERT_TOTAL = 16
TOKENS = 2048
MOST = 128
N_EXPERT = 16


def plant(drawn, key, smallest, largest):
    place = [jax.random.randint(jax.random.fold_in(key, axis), (), 0, length) for axis, length in enumerate(drawn.shape)]
    main_axis = drawn.shape.index(max(drawn.shape))
    neighbour = place[:main_axis] + [(place[main_axis] + 1) % drawn.shape[main_axis]] + place[main_axis + 1:]
    return drawn.at[tuple(place)].set(smallest).at[tuple(neighbour)].set(largest)


def shard_levels(own_key, shape, split, low, largest):
    def one(position, shards_of):
        draws = jax.random.uniform(jax.random.fold_in(jax.random.fold_in(own_key, 6), position), (shards_of,), jnp.float32, low / len(split), largest / len(split))
        return jnp.repeat(jnp.exp(draws), shape[position] // shards_of).reshape((-1,) + (1,) * (len(shape) - position - 1))

    gain = one(*split[0])
    for cut in split[1:]:
        gain = gain * one(*cut)
    return gain


def routed_block(stream_key, own, number, rows, amount, top, limit, slope):
    sequence = jax.random.permutation(stream_key, amount)
    heavy_load, common = shares(amount, rows * top, limit, slope, True), shares(amount, rows * top, limit, slope, False)
    places = jnp.arange(amount)

    def named(lengths, offset_by):
        used = int((lengths > 0).sum())
        fixed = max(1, used // 4)
        shifted = fixed + (places - fixed + offset_by * (used - fixed)) % max(1, amount - fixed)
        return jnp.zeros((amount,), jnp.int32).at[sequence[jnp.where(places < fixed, places, shifted)]].set(jnp.asarray(lengths, jnp.int32))

    lengths = jnp.where(number % 4 == 0, named(heavy_load, number // 4), named(common, number - number // 4 - 1))
    mixed = jax.random.permutation(jax.random.fold_in(own, 3), amount)
    donor, sink = mixed[0:amount // 2 * 2:2], mixed[1:amount // 2 * 2:2]
    margin = jnp.minimum(lengths[donor] - 1, limit - lengths[sink]) // 2
    margin = jnp.where((donor == sequence[0]) | (sink == sequence[0]) | (lengths[sink] == 0), 0, jnp.maximum(margin, 0))
    shifted = jax.random.randint(jax.random.fold_in(own, 4), (amount // 2,), 0, 1 << 20) % (margin + 1)
    lengths = lengths.at[donor].add(-shifted).at[sink].add(shifted)
    members = jnp.searchsorted(jnp.cumsum(lengths), jnp.arange(rows * top), side="right").astype(jnp.int32)
    grid = members.reshape(top, rows).T
    grid = grid[jax.random.permutation(jax.random.fold_in(own, 1), rows)]
    offset_by = jax.random.randint(jax.random.fold_in(own, 2), (rows, 1), 0, top)
    return jnp.take_along_axis(grid, (jnp.arange(top)[None, :] + offset_by) % top, axis=1)


def shares(amount, total, limit, skew, full):
    weights = [(1 << 20) // math.isqrt(standing ** skew) + 1 for standing in range(1, amount + 1)]
    largest = limit if full else min(limit, max(-(-total // amount), total * weights[0] // sum(weights)))
    least = 1 if total - largest >= amount - 1 else 0
    given, surplus = [largest] + [least] * (amount - 1), total - largest - least * (amount - 1)
    while surplus > 0:
        candidates = [i for i in range(1, amount) if given[i] < largest] or [i for i in range(1, amount) if given[i] < limit]
        mass, left = sum([weights[i] for i in candidates]), surplus
        for i in candidates:
            addition = min(limit - given[i], max(1, left * weights[i] // mass), surplus)
            given[i] = given[i] + addition
            surplus = surplus - addition
    return np.array(given)


def bell_draw(stream_key, shape, width, most, shards=(), kind=jnp.bfloat16):
    entries = jax.random.normal(stream_key, shape, jnp.float32) * width
    if len(shards) > 0:
        entries = shard_levels(stream_key, shape, shards, -0.22, 0.18) * entries
    return jnp.clip(entries, min=-most, max=most).astype(kind)


def setup_inputs(seed: int = 0, part: int = 0) -> dict:
    keys = jax.random.split(jax.random.key(seed), 11)
    own_keys = jax.random.split(jax.random.fold_in(keys[10], part), 11)
    hidden_of_route = bell_draw(own_keys[0], (TOKENS, TOP, EXPERT_HIDDEN), 1.0, 6.0, ((0, 16),))
    expert_of_route_keys = jax.random.split(jax.random.fold_in(own_keys[1], 1), TOKENS // TOK_DEV)
    expert_of_route_turns = jax.random.permutation(jax.random.fold_in(own_keys[1], 3), TOKENS // TOK_DEV)
    expert_of_route = jax.vmap(lambda own, number: routed_block(jax.random.fold_in(own_keys[1], 2), own, number, TOK_DEV, EXPERT_TOTAL, TOP, MOST, 2))(expert_of_route_keys, expert_of_route_turns).reshape((TOKENS, TOP))
    gate_of_route = jnp.clip(0.019897461 + 0.23010254 * jax.random.uniform(own_keys[2], (TOKENS, TOP), jnp.float32) ** shard_levels(own_keys[2], (TOKENS, TOP), ((0, 16),), -0.2, 0.2), 0.019897461, 0.25).astype(jnp.bfloat16)
    capacity = plant(jax.random.randint(own_keys[3], (EXPERT_TOTAL,), TOK_DEV * TOP // (2 * EXP_DEV), 2 * TOK_DEV * TOP // EXP_DEV + 1), jax.random.fold_in(own_keys[3], 1), TOK_DEV * TOP // (2 * EXP_DEV), (2 * TOK_DEV * TOP // EXP_DEV + 1) - 1).astype(jnp.int32)
    output_gradient = bell_draw(own_keys[4], (TOKENS, OUTPUT_FEATURES), 0.1, 0.796875, ((0, 16),))
    curvature = jnp.clip(jnp.exp(math.log(0.1) - 2.3025851 * jax.random.uniform(own_keys[5], (TOKENS,), jnp.float32) ** shard_levels(own_keys[5], (TOKENS,), ((0, 16),), -0.2, 0.2)), 0.01, 0.1)
    adapter_down = bell_draw(keys[6], (EXPERT_TOTAL, EXPERT_HIDDEN, ADAPTER_RANK), EXPERT_HIDDEN ** -0.5, 0.1875, ((0, 16),), jnp.float32)
    adapter_up = bell_draw(keys[7], (EXPERT_TOTAL, ADAPTER_RANK, OUTPUT_FEATURES), ADAPTER_RANK ** -0.5, 1.5, ((0, 16),), jnp.float32)
    down_direction = bell_draw(own_keys[8], (EXPERT_TOTAL, EXPERT_HIDDEN, ADAPTER_RANK), EXPERT_HIDDEN ** -0.5, 0.1875, ((0, 16),), jnp.float32)
    up_direction = bell_draw(own_keys[9], (EXPERT_TOTAL, ADAPTER_RANK, OUTPUT_FEATURES), ADAPTER_RANK ** -0.5, 1.5, ((0, 16),), jnp.float32)
    return {"hidden_of_route": hidden_of_route, "expert_of_route": expert_of_route, "gate_of_route": gate_of_route, "capacity": capacity, "output_gradient": output_gradient, "curvature": curvature, "adapter_down": adapter_down, "adapter_up": adapter_up, "down_direction": down_direction, "up_direction": up_direction}


adapter_scale = 2.0


def reference(hidden_of_route, expert_of_route, gate_of_route, capacity, output_gradient, curvature, adapter_down, adapter_up, down_direction, up_direction):
    finest_precision = lax.Precision.HIGHEST
    routes_per_block = TOK_DEV * TOP
    routes = expert_of_route.reshape(N_EXPERT, routes_per_block)
    onehot = (routes[:, :, None] == jnp.arange(EXPERT_TOTAL, dtype=jnp.int32)[None, None, :]).astype(jnp.int32)
    earlier = jnp.cumsum(onehot, axis=1) - onehot
    local_rank = jnp.sum(earlier * onehot, axis=2).astype(jnp.int32)
    counts = jnp.sum(onehot, axis=1)
    prior_count = (jnp.cumsum(counts, axis=0) - counts).astype(jnp.int32)
    global_rank = local_rank + jnp.take_along_axis(prior_count, routes, axis=1)
    retained_mask = (global_rank < capacity[routes]).astype(jnp.float32)
    weight_of_route = adapter_scale * gate_of_route.reshape(N_EXPERT, routes_per_block).astype(jnp.float32) * retained_mask
    slot_index = jnp.arange(N_EXPERT, dtype=jnp.int32)[:, None] * MOST + local_rank
    route_ids = jnp.arange(TOKENS * TOP, dtype=jnp.int32).reshape(N_EXPERT, routes_per_block)
    route_per_slot = jnp.zeros((EXPERT_TOTAL, N_EXPERT * MOST), jnp.int32).at[routes, slot_index].set(route_ids)
    weight_per_slot = jnp.zeros((EXPERT_TOTAL, N_EXPERT * MOST), jnp.float32).at[routes, slot_index].set(weight_of_route)
    hidden_flat = hidden_of_route.reshape(TOKENS * TOP, EXPERT_HIDDEN)
    down_stacked = jnp.concatenate([adapter_down, down_direction], axis=2)
    up_stacked = jnp.concatenate([adapter_up, up_direction], axis=1)

    def forward(total, inputs_now):
        row_ids, weights, factor_a, factor_b = inputs_now
        row_data = hidden_flat[row_ids].astype(jnp.float32)
        reduced_hidden = jnp.dot(row_data, factor_a, precision=finest_precision)
        exchanged_rows = jnp.concatenate([reduced_hidden[:, ADAPTER_RANK:], reduced_hidden[:, :ADAPTER_RANK]], axis=1)
        tangent = (weights[:, None] * jnp.dot(exchanged_rows, factor_b, precision=finest_precision)).astype(jnp.bfloat16)
        tangent = lax.optimization_barrier(tangent)
        total = total.at[row_ids // TOP].add(tangent.astype(jnp.float32))
        return total, reduced_hidden

    out_tangent, reduced_hidden_full = lax.scan(forward, jnp.zeros((TOKENS, OUTPUT_FEATURES), jnp.float32), (route_per_slot, weight_per_slot, down_stacked, up_stacked))
    resid_tangent = lax.optimization_barrier((curvature[:, None] * out_tangent).astype(jnp.bfloat16))

    def reverse_pass(inputs_now):
        row_ids, weights, reduced_hidden, factor_b, direction_b = inputs_now
        token_ids = row_ids // TOP
        row_data = hidden_flat[row_ids].astype(jnp.float32)
        residual = output_gradient[token_ids].astype(jnp.float32)
        tangent = resid_tangent[token_ids].astype(jnp.float32)
        residual_reduced = jnp.dot(residual, jnp.concatenate([factor_b, direction_b], axis=0).T, precision=finest_precision)
        reduced_tangent = jnp.dot(tangent, factor_b.T, precision=finest_precision)
        weight_column = weights[:, None]
        left_terms = jnp.concatenate([weight_column * residual_reduced[:, :ADAPTER_RANK], weight_column * (reduced_tangent + residual_reduced[:, ADAPTER_RANK:])], axis=1)
        down_terms = jnp.dot(row_data.T, left_terms, precision=finest_precision)
        raised_update = weight_column * reduced_hidden[:, :ADAPTER_RANK]
        raised_tangent_update = weight_column * reduced_hidden[:, ADAPTER_RANK:]
        up_terms = jnp.dot(jnp.concatenate([raised_update, raised_tangent_update], axis=1).T, residual, precision=finest_precision)
        curvature_piece = up_terms[ADAPTER_RANK:] + jnp.dot(raised_update.T, tangent, precision=finest_precision)
        return down_terms[:, :ADAPTER_RANK], up_terms[:ADAPTER_RANK], down_terms[:, ADAPTER_RANK:], curvature_piece

    down_gradient, up_gradient, curvature_down, curvature_up = lax.map(reverse_pass, (route_per_slot, weight_per_slot, reduced_hidden_full, adapter_up, up_direction))
    return (down_gradient, up_gradient, curvature_down, curvature_up)
```

```python
import functools

import jax
import jax.numpy as jnp
from jax import lax
from jax.experimental import pallas as pl
from jax.experimental.pallas import tpu as pltpu
from jax.sharding import PartitionSpec as P

adapter_scale = 2.0
f32 = jnp.float32
bf16 = jnp.bfloat16
kernel_vmem = 56 * 2**20


def halves(value):
    high = value.astype(bf16)
    return high, (value - high.astype(f32)).astype(bf16)


def dot(a, b, a_dim, b_dim):
    return lax.dot_general(a, b, (((a_dim,), (b_dim,)), ((), ())), preferred_element_type=f32)


def dot_exact_left(a, b, a_dim, b_dim):
    return dot(a, b[0], a_dim, b_dim) + dot(a, b[1], a_dim, b_dim)


def dot_pairs(a, b, a_dim, b_dim):
    return dot(a[0], b[0], a_dim, b_dim) + (dot(a[1], b[0], a_dim, b_dim) + dot(a[0], b[1], a_dim, b_dim))


def token_kernel(
    hidden_width,
    hidden_ref,
    expert_ref,
    gate_ref,
    prior_ref,
    capacity_ref,
    gradient_ref,
    curvature_ref,
    factor_ref,
    out_ref,
    left_ref,
):
    experts, _, rank, _ = factor_ref.shape
    tokens, top = expert_ref.shape
    wide = experts * rank
    model_width = gradient_ref.shape[1]
    column_expert = lax.broadcasted_iota(jnp.int32, (tokens, wide), 1) // rank

    named = [expert_ref[:, k : k + 1] == column_expert for k in range(top)]
    gate = jnp.zeros((tokens, wide), f32)
    member = jnp.zeros((tokens, wide), f32)
    for k in range(top):
        gate = jnp.where(named[k], gate_ref[:, k : k + 1], gate)
        member = jnp.where(named[k], 1.0, member)
    below = (
        lax.broadcasted_iota(jnp.int32, (tokens, tokens), 0)
        > lax.broadcasted_iota(jnp.int32, (tokens, tokens), 1)
    )
    local_rank = dot(jnp.where(below, 1.0, 0.0).astype(bf16), member.astype(bf16), 1, 0)
    retained = local_rank + prior_ref[...] < capacity_ref[...]
    weight = jnp.where(retained, adapter_scale * gate, 0.0)

    def factor(kind, start, width):
        block = factor_ref[:, kind, :, start : start + width]
        return halves(block.reshape(wide, width))

    def reduced(kind):
        full = dot_exact_left(hidden_ref[...], factor(kind, 0, hidden_width), 1, 1)
        total = jnp.zeros((tokens, wide), f32)
        for k in range(top):
            total = jnp.where(named[k], full[k * tokens : (k + 1) * tokens], total)
        return halves(weight * total)

    weighted_du = reduced(0)
    weighted_u = reduced(1)

    adapter_up = factor(0, hidden_width, model_width)
    up_direction = factor(1, hidden_width, model_width)
    out_tangent = dot_pairs(weighted_du, adapter_up, 1, 0) + dot_pairs(weighted_u, up_direction, 1, 0)
    resid = halves(curvature_ref[...] * out_tangent)

    gradient = gradient_ref[...]
    up_shape = (experts, rank, model_width)
    up_gradient = dot(weighted_u[0], gradient, 0, 0) + dot(weighted_u[1], gradient, 0, 0)
    out_ref[:, 1, :, hidden_width:] = up_gradient.reshape(up_shape)
    up_curvature = (
        dot(weighted_du[0], gradient, 0, 0)
        + dot(weighted_du[1], gradient, 0, 0)
        + dot_pairs(weighted_u, resid, 0, 0)
    )
    out_ref[:, 0, :, hidden_width:] = up_curvature.reshape(up_shape)

    to_gradient = weight * dot_exact_left(gradient, adapter_up, 1, 1)
    to_curvature = weight * (
        dot_pairs(resid, adapter_up, 1, 1) + dot_exact_left(gradient, up_direction, 1, 1)
    )
    down_shape = (experts, rank, hidden_width)
    for kind, terms in ((1, to_gradient), (0, to_curvature)):
        for part, half in enumerate(halves(terms)):
            for k in range(top):
                left_ref[part, k * tokens : (k + 1) * tokens] = jnp.where(
                    named[k], half, jnp.zeros_like(half)
                )
        down = dot(left_ref[0], hidden_ref[...], 0, 0) + dot(left_ref[1], hidden_ref[...], 0, 0)
        out_ref[:, kind, :, :hidden_width] = down.reshape(down_shape)


def gathered_plan(
    hidden_of_route,
    expert_of_route,
    gate_of_route,
    capacity,
    output_gradient,
    curvature,
    adapter_down,
    adapter_up,
    down_direction,
    up_direction,
):
    group_size = lax.axis_size("expert")
    tokens, top = expert_of_route.shape
    hidden_width = hidden_of_route.shape[2]
    resident, _, rank = adapter_down.shape
    model_width = output_gradient.shape[1]
    experts = resident * group_size
    wide = experts * rank

    names = jnp.arange(experts, dtype=jnp.int32)
    counts = jnp.sum((expert_of_route[:, :, None] == names).astype(jnp.int32), axis=(0, 1))
    all_counts = lax.all_gather(counts, "expert")
    earlier = jnp.arange(group_size)[:, None] < lax.axis_index("expert")
    prior = jnp.sum(jnp.where(earlier, all_counts, 0), axis=0)

    def by_column(per_expert):
        return jnp.repeat(per_expert.astype(f32), rank)[None, :]

    own = jnp.stack(
        [
            jnp.concatenate([down_direction.transpose(0, 2, 1), adapter_up], axis=2),
            jnp.concatenate([adapter_down.transpose(0, 2, 1), up_direction], axis=2),
        ],
        axis=1,
    )
    factors = lax.all_gather(own, "expert", axis=0, tiled=True)
    hidden_by_position = hidden_of_route.transpose(1, 0, 2).reshape(top * tokens, hidden_width)
    partial_sums = pl.pallas_call(
        functools.partial(token_kernel, hidden_width),
        out_shape=jax.ShapeDtypeStruct((experts, 2, rank, hidden_width + model_width), f32),
        scratch_shapes=[pltpu.VMEM((2, top * tokens, wide), bf16)],
        compiler_params=pltpu.CompilerParams(vmem_limit_bytes=kernel_vmem),
    )(
        hidden_by_position,
        expert_of_route,
        gate_of_route.astype(f32),
        by_column(prior),
        by_column(capacity),
        output_gradient,
        curvature[:, None],
        factors,
    )
    summed = lax.psum_scatter(partial_sums, "expert", scatter_dimension=0, tiled=True)
    down = summed[..., :hidden_width].transpose(0, 1, 3, 2)
    up = summed[..., hidden_width:]
    return down[:, 1], up[:, 1], down[:, 0], up[:, 0]


def carried_in(value, axis, join, neutral):
    count, mine = (lax.axis_size(axis), lax.axis_index(axis))
    pieces = lax.all_gather(value, axis)
    so_far = jnp.full_like(value, 0) + jnp.asarray(neutral, value.dtype)

    def lap(position, so_far):
        longer = join(so_far, pieces[position])
        return jnp.where(position < mine, longer, so_far)

    return lax.fori_loop(0, count - 1, lap, so_far)


def add_counts(earlier, later):
    return earlier + later


def routed_plan(
    hidden_of_route,
    expert_of_route,
    gate_of_route,
    capacity,
    output_gradient,
    curvature,
    adapter_down,
    adapter_up,
    down_direction,
    up_direction,
):
    finest_precision = lax.Precision.HIGHEST
    group_size = lax.axis_size("expert")
    tok_rows, top_count = expert_of_route.shape
    hidden_width = hidden_of_route.shape[2]
    resident_experts = adapter_down.shape[0]
    adapter_rank = adapter_down.shape[2]
    model_width = output_gradient.shape[1]
    experts = resident_experts * group_size
    slot_most = 2 * tok_rows * top_count // experts
    routes = expert_of_route.reshape(-1)
    onehot = (routes[:, None] == jnp.arange(experts, dtype=jnp.int32)[None, :]).astype(jnp.int32)
    earlier = jnp.cumsum(onehot, axis=0) - onehot
    local_rank = jnp.sum(earlier * onehot, axis=1)
    counts = jnp.sum(onehot, axis=0)
    prior_count = carried_in(counts, "expert", add_counts, jnp.zeros_like(counts))
    global_rank = local_rank + jnp.sum(onehot * prior_count[None, :], axis=1)
    route_limit = jnp.sum(onehot * capacity[None, :], axis=1)
    retained_mask = (global_rank < route_limit).astype(jnp.float32)
    weight_of_route = (
        adapter_scale * gate_of_route.reshape(-1).astype(jnp.float32) * retained_mask
    ).astype(jnp.bfloat16)
    slot_index = routes * slot_most + local_rank
    layout = (group_size, resident_experts, slot_most)
    send_hidden = (
        jnp.zeros((experts * slot_most, hidden_width), jnp.bfloat16)
        .at[slot_index]
        .set(hidden_of_route.reshape(-1, hidden_width))
        .reshape(layout + (hidden_width,))
    )
    send_weight = (
        jnp.zeros((experts * slot_most,), jnp.bfloat16)
        .at[slot_index]
        .set(weight_of_route)
        .reshape(layout)
    )
    down_stacked = jnp.concatenate([adapter_down, down_direction], axis=2)
    up_stacked = jnp.concatenate([adapter_up, up_direction], axis=1)

    def spread(token_rows):
        per_route = jnp.repeat(token_rows, top_count, axis=0)
        placed = (
            jnp.zeros((experts * slot_most, model_width), jnp.bfloat16)
            .at[slot_index]
            .set(per_route)
        )
        return placed.reshape(layout + (model_width,))

    send_residual = spread(output_gradient)
    pieces = (
        lax.all_to_all(send_hidden, "expert", split_axis=0, concat_axis=0, tiled=True),
        lax.all_to_all(send_weight, "expert", split_axis=0, concat_axis=0, tiled=True),
    )
    hidden_rows = pieces[0].astype(jnp.float32)
    weight_rows = pieces[1].astype(jnp.float32)[..., None]
    reduced_hidden = jnp.einsum(
        "cjif,jfk->cjik", hidden_rows, down_stacked, precision=finest_precision
    )
    exchanged_rows = jnp.concatenate(
        [reduced_hidden[..., adapter_rank:], reduced_hidden[..., :adapter_rank]], axis=3
    )
    tangent_out = weight_rows * jnp.einsum(
        "cjik,jkd->cjid", exchanged_rows, up_stacked, precision=finest_precision
    )
    returned = lax.all_to_all(
        tangent_out.astype(jnp.bfloat16), "expert", split_axis=0, concat_axis=0, tiled=True
    )
    results = (returned, reduced_hidden) + tuple(pieces)
    returned = results[0]
    reduced_hidden = results[1]
    hidden_rows = results[2]
    weight_rows = results[3]
    route_tangent = returned.reshape(experts * slot_most, model_width)[slot_index]
    out_tangent = jnp.sum(
        route_tangent.reshape(tok_rows, top_count, model_width).astype(jnp.float32), axis=1
    )
    resid_tangent = (curvature[:, None] * out_tangent).astype(jnp.bfloat16)
    send_tangent = spread(resid_tangent)
    residual_rows, tangent_rows = (
        lax.all_to_all(send_residual, "expert", split_axis=0, concat_axis=0, tiled=True),
        lax.all_to_all(send_tangent, "expert", split_axis=0, concat_axis=0, tiled=True),
    )
    residual_full = residual_rows.astype(jnp.float32)
    complete_tangent = tangent_rows.astype(jnp.float32)
    weight_column = weight_rows.astype(jnp.float32)[..., None]
    residual_reduced = jnp.einsum(
        "wyov,yqv->wyoq", residual_full, up_stacked, precision=finest_precision
    )
    reduced_tangent = jnp.einsum(
        "wyov,yqv->wyoq", complete_tangent, adapter_up, precision=finest_precision
    )
    left_terms = jnp.concatenate(
        [
            weight_column * residual_reduced[..., :adapter_rank],
            weight_column * (reduced_tangent + residual_reduced[..., adapter_rank:]),
        ],
        axis=3,
    )
    down_terms = jnp.einsum(
        "cjif,cjik->jfk", hidden_rows.astype(jnp.float32), left_terms, precision=finest_precision
    )
    raised_update = weight_column * reduced_hidden[..., :adapter_rank]
    raised_tangent_update = weight_column * reduced_hidden[..., adapter_rank:]
    up_terms = jnp.einsum(
        "cjik,cjid->jkd",
        jnp.concatenate([raised_update, raised_tangent_update], axis=3),
        residual_full,
        precision=finest_precision,
    )
    curvature_piece = up_terms[:, adapter_rank:] + jnp.einsum(
        "cjik,cjid->jkd", raised_update, complete_tangent, precision=finest_precision
    )
    return (
        down_terms[..., :adapter_rank],
        up_terms[:, :adapter_rank],
        down_terms[..., adapter_rank:],
        curvature_piece,
    )


def local(*arguments):
    adapter_down, adapter_up = arguments[6], arguments[7]
    factor_bytes = 2 * 4 * (adapter_down.size + adapter_up.size) * lax.axis_size("expert")
    plan = gathered_plan if 4 * factor_bytes <= kernel_vmem else routed_plan
    return plan(*arguments)


def solution(mesh):
    return jax.shard_map(
        local,
        mesh=mesh,
        in_specs=(
            P(("groups", "expert"), None, None),
            P(("groups", "expert"), None),
            P(("groups", "expert"), None),
            P("groups"),
            P(("groups", "expert"), None),
            P(("groups", "expert")),
            P("expert", None, None),
            P("expert", None, None),
            P(("groups", "expert"), None, None),
            P(("groups", "expert"), None, None),
        ),
        out_specs=(
            P(("groups", "expert"), None, None),
            P(("groups", "expert"), None, None),
            P(("groups", "expert"), None, None),
            P(("groups", "expert"), None, None),
        ),
        check_vma=False,
    )
```

```python
import functools

import jax
import jax.numpy as jnp
from jax import lax
from jax.experimental import pallas as pl
from jax.experimental.pallas import tpu as pltpu
from jax.sharding import PartitionSpec as P

adapter_scale = 2.0
f32 = jnp.float32
bf16 = jnp.bfloat16
f16 = jnp.float16
lanes = 128
down_scale = 2.0**18
up_scale = 2.0**15
kernel_vmem = 56 * 2**20


def halves(value):
    high = value.astype(bf16)
    return high, (value - high.astype(f32)).astype(bf16)


def dot(a, b, a_dim, b_dim):
    return lax.dot_general(a, b, (((a_dim,), (b_dim,)), ((), ())), preferred_element_type=f32)


def dot_exact_left(a, b, a_dim, b_dim):
    return dot(a, b[0], a_dim, b_dim) + dot(a, b[1], a_dim, b_dim)


def dot_pairs(a, b, a_dim, b_dim):
    return dot(a[0], b[0], a_dim, b_dim) + (dot(a[1], b[0], a_dim, b_dim) + dot(a[0], b[1], a_dim, b_dim))


def token_kernel(
    hidden_width,
    hidden_ref,
    expert_ref,
    gate_ref,
    column_ref,
    prior_ref,
    capacity_ref,
    gradient_ref,
    curvature_ref,
    factor_ref,
    *rest,
):
    slots, _, rank, _ = factor_ref.shape
    out_refs, left_ref = rest[:slots], rest[slots]
    tokens, top = expert_ref.shape
    wide = slots * rank
    model_width = gradient_ref.shape[1]

    named = [expert_ref[:, k : k + 1] == column_ref[...] for k in range(top)]
    gate = jnp.zeros((tokens, wide), f32)
    member = jnp.zeros((tokens, wide), f32)
    for k in range(top):
        gate = jnp.where(named[k], gate_ref[:, k : k + 1], gate)
        member = jnp.where(named[k], 1.0, member)
    below = (
        lax.broadcasted_iota(jnp.int32, (tokens, tokens), 0)
        > lax.broadcasted_iota(jnp.int32, (tokens, tokens), 1)
    )
    local_rank = dot(jnp.where(below, 1.0, 0.0).astype(bf16), member.astype(bf16), 1, 0)
    retained = local_rank + prior_ref[...] < capacity_ref[...]
    weight = jnp.where(retained, adapter_scale * gate, 0.0)

    def factor(kind, start, width):
        block = factor_ref[:, kind, :, start : start + width]
        return halves(block.reshape(wide, width))

    def reduced(kind):
        full = dot_exact_left(hidden_ref[...], factor(kind, 0, hidden_width), 1, 1)
        total = jnp.zeros((tokens, wide), f32)
        for k in range(top):
            total = jnp.where(named[k], full[k * tokens : (k + 1) * tokens], total)
        return halves(weight * total)

    weighted_du = reduced(0)
    weighted_u = reduced(1)

    adapter_up = factor(0, hidden_width, model_width)
    up_direction = factor(1, hidden_width, model_width)
    out_tangent = dot_pairs(weighted_du, adapter_up, 1, 0) + dot_pairs(weighted_u, up_direction, 1, 0)
    resid = halves(curvature_ref[...] * out_tangent)

    def put(kind, start, value):
        for slot in range(slots):
            out_refs[slot][kind, :, start : start + value.shape[1]] = value[slot * rank : (slot + 1) * rank]

    gradient = gradient_ref[...]
    put(1, hidden_width, dot(weighted_u[0], gradient, 0, 0) + dot(weighted_u[1], gradient, 0, 0))
    put(
        0,
        hidden_width,
        dot(weighted_du[0], gradient, 0, 0)
        + dot(weighted_du[1], gradient, 0, 0)
        + dot_pairs(weighted_u, resid, 0, 0),
    )

    to_gradient = weight * dot_exact_left(gradient, adapter_up, 1, 1)
    to_curvature = weight * (
        dot_pairs(resid, adapter_up, 1, 1) + dot_exact_left(gradient, up_direction, 1, 1)
    )
    for kind, terms in ((1, to_gradient), (0, to_curvature)):
        for part, half in enumerate(halves(terms)):
            for k in range(top):
                left_ref[part, k * tokens : (k + 1) * tokens] = jnp.where(
                    named[k], half, jnp.zeros_like(half)
                )
        put(kind, 0, dot(left_ref[0], hidden_ref[...], 0, 0) + dot(left_ref[1], hidden_ref[...], 0, 0))


class Ring:
    def __init__(self, size):
        self.length = size // 2
        rows = self.length // 2
        self.order = [4 * z for z in range(rows)] + [4 * z + 2 for z in reversed(range(rows))]

    def pairs(self, step):
        return [
            (chip + core, self.order[(place + step) % self.length] + core)
            for place, chip in enumerate(self.order)
            for core in range(2)
        ]

    def shift(self, value, step):
        return lax.ppermute(value, "expert", self.pairs(step))

    def swap(self, value):
        return lax.ppermute(value, "expert", [(i, i ^ 1) for i in range(2 * self.length)])

    def members(self):
        me = lax.axis_index("expert")
        rows = self.length // 2
        place = jnp.where(me // 2 % 2 == 0, me // 4, self.length - 1 - me // 4)
        slot = jnp.arange(2 * self.length, dtype=jnp.int32)
        there = (place + slot // 2) % self.length
        chip = jnp.where(there < rows, 4 * there, 4 * (self.length - 1 - there) + 2)
        return chip + (me + slot) % 2

    def gather(self, own):
        half = self.length // 2
        found = {0: own}
        ahead, behind = own, own
        for step in range(1, half):
            behind = self.shift(behind, 1)
            ahead = self.shift(ahead, -1)
            found[self.length - step], found[step] = behind, ahead
        found[half] = jnp.concatenate([self.shift(behind[:1], 1), self.shift(ahead[1:], -1)])
        return [[found[offset], self.swap(found[offset])] for offset in range(self.length)]

    def scatter(self, chunks, encode, decode):
        half = self.length // 2
        mine = {}
        for offset in [half] + [o for step in range(half - 1, 0, -1) for o in (step, -step)] + [0]:
            own, other = chunks[offset % self.length]
            mine[offset] = own + self.swap(other)
        forward = decode(self.shift(encode(mine[half][:1]), 1))
        backward = decode(self.shift(encode(mine[half][1:]), -1))
        onward = jnp.concatenate([forward, jnp.zeros_like(forward)])
        back = jnp.concatenate([jnp.zeros_like(backward), backward])
        for step in range(half - 1, 0, -1):
            onward = decode(self.shift(encode(mine[step] + onward), 1))
            back = decode(self.shift(encode(mine[-step] + back), -1))
        return mine[0] + onward + back


def gathered_plan(
    hidden_of_route,
    expert_of_route,
    gate_of_route,
    capacity,
    output_gradient,
    curvature,
    adapter_down,
    adapter_up,
    down_direction,
    up_direction,
):
    ring = Ring(lax.axis_size("expert"))
    tokens, top = expert_of_route.shape
    hidden_width = hidden_of_route.shape[2]
    _, _, rank = adapter_down.shape
    model_width = output_gradient.shape[1]
    experts = capacity.shape[0]
    width = hidden_width + model_width

    names = jnp.arange(experts, dtype=jnp.int32)
    counts = jnp.sum((expert_of_route[:, :, None] == names).astype(jnp.int32), axis=(0, 1))

    own = jnp.concatenate(
        [
            down_scale * jnp.concatenate([down_direction, adapter_down]).transpose(0, 2, 1),
            up_scale * jnp.concatenate([adapter_up, up_direction]),
            jnp.broadcast_to(jnp.pad(counts.astype(f32), (0, lanes - experts)), (2, rank, lanes)),
        ],
        axis=2,
    ).astype(f16)
    gathered = jnp.stack([piece for pair in ring.gather(own) for piece in pair])
    factors = jnp.concatenate(
        [
            gathered[..., :hidden_width].astype(f32) * (1 / down_scale),
            gathered[..., hidden_width:width].astype(f32) * (1 / up_scale),
        ],
        axis=3,
    )
    members = ring.members()
    all_counts = gathered[:, 0, 0, width : width + experts].astype(f32)
    earlier = members[:, None] < lax.axis_index("expert")
    prior = jnp.sum(jnp.where(earlier, all_counts, 0.0), axis=0)

    def by_column(per_slot):
        return jnp.repeat(per_slot, rank)[None, :]

    def of_slot(per_expert):
        return jnp.sum(jnp.where(members[:, None] == names, per_expert, 0), axis=1)

    hidden_by_position = hidden_of_route.transpose(1, 0, 2).reshape(top * tokens, hidden_width)
    chunk = jax.ShapeDtypeStruct((2, rank, width), f32)
    partial_sums = pl.pallas_call(
        functools.partial(token_kernel, hidden_width),
        out_shape=[chunk] * experts,
        scratch_shapes=[pltpu.VMEM((2, top * tokens, experts * rank), bf16)],
        compiler_params=pltpu.CompilerParams(vmem_limit_bytes=kernel_vmem),
    )(
        hidden_by_position,
        expert_of_route,
        gate_of_route.astype(f32),
        by_column(members),
        by_column(of_slot(prior)),
        by_column(of_slot(capacity).astype(f32)),
        output_gradient,
        curvature[:, None],
        factors,
    )

    def encode(value):
        largest = jnp.max(jnp.abs(value), axis=2, keepdims=True)
        exponent = jnp.ceil(jnp.log2(jnp.maximum(largest, 1e-30)))
        scaled = value * jnp.exp2(15.0 - exponent)
        extra = jnp.broadcast_to(exponent, value.shape[:2] + (lanes,))
        return jnp.concatenate([scaled, extra], axis=2).astype(f16)

    def decode(coded):
        return coded[..., :width].astype(f32) * jnp.exp2(coded[..., width : width + 1].astype(f32) - 15.0)

    pairs = [partial_sums[2 * offset : 2 * offset + 2] for offset in range(ring.length)]
    summed = ring.scatter(pairs, encode, decode)
    down = summed[..., :hidden_width].transpose(0, 2, 1)
    up = summed[..., hidden_width:]
    return down[1:], up[1:], down[:1], up[:1]


def carried_in(value, axis, join, neutral):
    count, mine = (lax.axis_size(axis), lax.axis_index(axis))
    pieces = lax.all_gather(value, axis)
    so_far = jnp.full_like(value, 0) + jnp.asarray(neutral, value.dtype)

    def lap(position, so_far):
        longer = join(so_far, pieces[position])
        return jnp.where(position < mine, longer, so_far)

    return lax.fori_loop(0, count - 1, lap, so_far)


def add_counts(earlier, later):
    return earlier + later


def routed_plan(
    hidden_of_route,
    expert_of_route,
    gate_of_route,
    capacity,
    output_gradient,
    curvature,
    adapter_down,
    adapter_up,
    down_direction,
    up_direction,
):
    finest_precision = lax.Precision.HIGHEST
    group_size = lax.axis_size("expert")
    tok_rows, top_count = expert_of_route.shape
    hidden_width = hidden_of_route.shape[2]
    resident_experts = adapter_down.shape[0]
    adapter_rank = adapter_down.shape[2]
    model_width = output_gradient.shape[1]
    experts = resident_experts * group_size
    slot_most = 2 * tok_rows * top_count // experts
    routes = expert_of_route.reshape(-1)
    onehot = (routes[:, None] == jnp.arange(experts, dtype=jnp.int32)[None, :]).astype(jnp.int32)
    earlier = jnp.cumsum(onehot, axis=0) - onehot
    local_rank = jnp.sum(earlier * onehot, axis=1)
    counts = jnp.sum(onehot, axis=0)
    prior_count = carried_in(counts, "expert", add_counts, jnp.zeros_like(counts))
    global_rank = local_rank + jnp.sum(onehot * prior_count[None, :], axis=1)
    route_limit = jnp.sum(onehot * capacity[None, :], axis=1)
    retained_mask = (global_rank < route_limit).astype(jnp.float32)
    weight_of_route = (
        adapter_scale * gate_of_route.reshape(-1).astype(jnp.float32) * retained_mask
    ).astype(jnp.bfloat16)
    slot_index = routes * slot_most + local_rank
    layout = (group_size, resident_experts, slot_most)
    send_hidden = (
        jnp.zeros((experts * slot_most, hidden_width), jnp.bfloat16)
        .at[slot_index]
        .set(hidden_of_route.reshape(-1, hidden_width))
        .reshape(layout + (hidden_width,))
    )
    send_weight = (
        jnp.zeros((experts * slot_most,), jnp.bfloat16)
        .at[slot_index]
        .set(weight_of_route)
        .reshape(layout)
    )
    down_stacked = jnp.concatenate([adapter_down, down_direction], axis=2)
    up_stacked = jnp.concatenate([adapter_up, up_direction], axis=1)

    def spread(token_rows):
        per_route = jnp.repeat(token_rows, top_count, axis=0)
        placed = (
            jnp.zeros((experts * slot_most, model_width), jnp.bfloat16)
            .at[slot_index]
            .set(per_route)
        )
        return placed.reshape(layout + (model_width,))

    send_residual = spread(output_gradient)
    pieces = (
        lax.all_to_all(send_hidden, "expert", split_axis=0, concat_axis=0, tiled=True),
        lax.all_to_all(send_weight, "expert", split_axis=0, concat_axis=0, tiled=True),
    )
    hidden_rows = pieces[0].astype(jnp.float32)
    weight_rows = pieces[1].astype(jnp.float32)[..., None]
    reduced_hidden = jnp.einsum(
        "cjif,jfk->cjik", hidden_rows, down_stacked, precision=finest_precision
    )
    exchanged_rows = jnp.concatenate(
        [reduced_hidden[..., adapter_rank:], reduced_hidden[..., :adapter_rank]], axis=3
    )
    tangent_out = weight_rows * jnp.einsum(
        "cjik,jkd->cjid", exchanged_rows, up_stacked, precision=finest_precision
    )
    returned = lax.all_to_all(
        tangent_out.astype(jnp.bfloat16), "expert", split_axis=0, concat_axis=0, tiled=True
    )
    results = (returned, reduced_hidden) + tuple(pieces)
    returned = results[0]
    reduced_hidden = results[1]
    hidden_rows = results[2]
    weight_rows = results[3]
    route_tangent = returned.reshape(experts * slot_most, model_width)[slot_index]
    out_tangent = jnp.sum(
        route_tangent.reshape(tok_rows, top_count, model_width).astype(jnp.float32), axis=1
    )
    resid_tangent = (curvature[:, None] * out_tangent).astype(jnp.bfloat16)
    send_tangent = spread(resid_tangent)
    residual_rows, tangent_rows = (
        lax.all_to_all(send_residual, "expert", split_axis=0, concat_axis=0, tiled=True),
        lax.all_to_all(send_tangent, "expert", split_axis=0, concat_axis=0, tiled=True),
    )
    residual_full = residual_rows.astype(jnp.float32)
    complete_tangent = tangent_rows.astype(jnp.float32)
    weight_column = weight_rows.astype(jnp.float32)[..., None]
    residual_reduced = jnp.einsum(
        "wyov,yqv->wyoq", residual_full, up_stacked, precision=finest_precision
    )
    reduced_tangent = jnp.einsum(
        "wyov,yqv->wyoq", complete_tangent, adapter_up, precision=finest_precision
    )
    left_terms = jnp.concatenate(
        [
            weight_column * residual_reduced[..., :adapter_rank],
            weight_column * (reduced_tangent + residual_reduced[..., adapter_rank:]),
        ],
        axis=3,
    )
    down_terms = jnp.einsum(
        "cjif,cjik->jfk", hidden_rows.astype(jnp.float32), left_terms, precision=finest_precision
    )
    raised_update = weight_column * reduced_hidden[..., :adapter_rank]
    raised_tangent_update = weight_column * reduced_hidden[..., adapter_rank:]
    up_terms = jnp.einsum(
        "cjik,cjid->jkd",
        jnp.concatenate([raised_update, raised_tangent_update], axis=3),
        residual_full,
        precision=finest_precision,
    )
    curvature_piece = up_terms[:, adapter_rank:] + jnp.einsum(
        "cjik,cjid->jkd", raised_update, complete_tangent, precision=finest_precision
    )
    return (
        down_terms[..., :adapter_rank],
        up_terms[:, :adapter_rank],
        down_terms[..., adapter_rank:],
        curvature_piece,
    )


def local(*arguments):
    adapter_down, adapter_up = arguments[6], arguments[7]
    factor_bytes = 2 * 4 * (adapter_down.size + adapter_up.size) * lax.axis_size("expert")
    plan = gathered_plan if 4 * factor_bytes <= kernel_vmem else routed_plan
    return plan(*arguments)


def solution(mesh):
    return jax.shard_map(
        local,
        mesh=mesh,
        in_specs=(
            P(("groups", "expert"), None, None),
            P(("groups", "expert"), None),
            P(("groups", "expert"), None),
            P("groups"),
            P(("groups", "expert"), None),
            P(("groups", "expert")),
            P("expert", None, None),
            P("expert", None, None),
            P(("groups", "expert"), None, None),
            P(("groups", "expert"), None, None),
        ),
        out_specs=(
            P(("groups", "expert"), None, None),
            P(("groups", "expert"), None, None),
            P(("groups", "expert"), None, None),
            P(("groups", "expert"), None, None),
        ),
        check_vma=False,
    )
```

```python
import functools

import jax
import jax.numpy as jnp
from jax import lax
from jax.experimental import pallas as pl
from jax.experimental.pallas import tpu as pltpu
from jax.sharding import PartitionSpec as P

adapter_scale = 2.0
f32 = jnp.float32
bf16 = jnp.bfloat16
f16 = jnp.float16
lanes = 128
down_scale = 2.0**18
up_scale = 2.0**15
kernel_vmem = 32 * 2**20


def halves(value):
    high = value.astype(bf16)
    return high, (value - high.astype(f32)).astype(bf16)


def dot(a, b, a_dim, b_dim):
    return lax.dot_general(a, b, (((a_dim,), (b_dim,)), ((), ())), preferred_element_type=f32)


def dot_pairs(a, b, a_dim, b_dim):
    return dot(a[0], b[0], a_dim, b_dim) + (dot(a[1], b[0], a_dim, b_dim) + dot(a[0], b[1], a_dim, b_dim))


def token_columns(small_ref, top):
    small = small_ref[...].T
    experts = [small[:, k : k + 1] for k in range(top)]
    gates = [small[:, top + k : top + k + 1] for k in range(top)]
    return experts, gates, small[:, 2 * top : 2 * top + 1]


def stacked(refs, kind):
    return jnp.concatenate([ref[kind] for ref in refs], axis=0)


def reduce_kernel(top, slots, small_ref, column_ref, own_ref, other_ref, *rest):
    factor_refs, reduced_ref = rest[:slots], rest[slots]
    experts, _, _ = token_columns(small_ref, top)
    high, low = halves(jnp.concatenate([stacked(factor_refs, 0), stacked(factor_refs, 1)], axis=0))
    wide = high.shape[0] // 2
    tokens = own_ref.shape[0] // top
    for block, hidden_ref in enumerate((own_ref, other_ref)):
        rows = slice(block * tokens, (block + 1) * tokens)
        full = dot(hidden_ref[...], high, 1, 1) + dot(hidden_ref[...], low, 1, 1)
        total = jnp.zeros((tokens, 2 * wide), f32)
        for k in range(top):
            named = experts[k][rows] == column_ref[...]
            total = jnp.where(jnp.concatenate([named, named], axis=1), full[k * tokens : (k + 1) * tokens], total)
        reduced_ref[0, rows] = total[:, :wide]
        reduced_ref[1, rows] = total[:, wide:]


def tangent_kernel(top, slots, small_ref, column_ref, limit_ref, reduced_ref, *rest):
    factor_refs = rest[:slots]
    weight_ref, weighted_ref, tangent_ref, high_ref, low_ref = rest[slots:]
    experts, gates, _ = token_columns(small_ref, top)
    tokens, wide = weight_ref.shape
    block = tokens // 2
    gate = jnp.zeros((tokens, wide), f32)
    member = jnp.zeros((tokens, wide), f32)
    for k in range(top):
        named = experts[k] == column_ref[...]
        gate = jnp.where(named, gates[k], gate)
        member = jnp.where(named, 1.0, member)
    below = (
        lax.broadcasted_iota(jnp.int32, (block, block), 0)
        > lax.broadcasted_iota(jnp.int32, (block, block), 1)
    )
    below = jnp.where(below, 1.0, 0.0).astype(bf16)
    weights = []
    for part in range(2):
        rows = slice(part * block, (part + 1) * block)
        local_rank = dot(below, member[rows].astype(bf16), 1, 0)
        weights.append(jnp.where(local_rank < limit_ref[part : part + 1], adapter_scale * gate[rows], 0.0))
    weight = jnp.concatenate(weights, axis=0)
    weight_ref[...] = weight
    weighted = jnp.concatenate([weight * reduced_ref[0], weight * reduced_ref[1]], axis=1)
    weighted_ref[...] = weighted
    factor = halves(jnp.concatenate([stacked(factor_refs, 0), stacked(factor_refs, 1)], axis=0))
    high_ref[...], low_ref[...] = factor
    tangent_ref[...] = dot_pairs(halves(weighted), factor, 1, 0)


def put_left(left_ref, experts, column_ref, terms, top):
    both = jnp.concatenate(halves(terms), axis=1)
    tokens = terms.shape[0] // 2
    for block in range(2):
        rows = slice(block * tokens, (block + 1) * tokens)
        for k in range(top):
            named = experts[k][rows] == column_ref[...]
            named = jnp.concatenate([named, named], axis=1)
            left_ref[block, k * tokens : (k + 1) * tokens] = jnp.where(named, both[rows], jnp.zeros_like(both[rows]))


def add_halves(both, axis):
    middle = both.shape[axis] // 2
    if axis == 0:
        return both[:middle] + both[middle:]
    return both[:, :middle] + both[:, middle:]


def put_chunks(out_refs, start, value):
    rank, width = out_refs[0].shape[0], value.shape[1]
    for slot, out_ref in enumerate(out_refs):
        out_ref[:, start : start + width] = value[slot * rank : (slot + 1) * rank]


def gradient_kernel(
    top,
    small_ref,
    column_ref,
    own_ref,
    other_ref,
    own_gradient_ref,
    other_gradient_ref,
    weight_ref,
    weighted_ref,
    high_ref,
    low_ref,
    *rest,
):
    out_refs, (up_ref, to_ref, left_ref) = rest[:-3], rest[-3:]
    experts, _, _ = token_columns(small_ref, top)
    wide = weight_ref.shape[1]
    hidden_width = own_ref.shape[1]
    gradient = jnp.concatenate([own_gradient_ref[...], other_gradient_ref[...]], axis=0)
    to_both = dot(gradient, high_ref[...], 1, 1) + dot(gradient, low_ref[...], 1, 1)
    to_ref[...] = to_both[:, wide:]
    put_left(left_ref, experts, column_ref, weight_ref[...] * to_both[:, :wide], top)
    down = dot(left_ref[0], own_ref[...], 0, 0) + dot(left_ref[1], other_ref[...], 0, 0)
    put_chunks(out_refs, 0, add_halves(down, 0))
    up = add_halves(dot(jnp.concatenate(halves(weighted_ref[...]), axis=1), gradient, 0, 0), 0)
    up_ref[...] = up[:wide]
    put_chunks(out_refs, hidden_width, up[wide:])


def curvature_kernel(
    top,
    small_ref,
    column_ref,
    own_ref,
    other_ref,
    weight_ref,
    weighted_ref,
    high_ref,
    low_ref,
    up_ref,
    to_ref,
    tangent_ref,
    arrived_ref,
    *rest,
):
    out_refs, left_ref = rest[:-1], rest[-1]
    experts, _, curvature = token_columns(small_ref, top)
    tokens, wide = weight_ref.shape
    block = tokens // 2
    hidden_width = own_ref.shape[1]
    arrived = jnp.concatenate([arrived_ref[block:], arrived_ref[:block]], axis=0)
    resid = halves(curvature * (tangent_ref[...] + arrived))
    adapter_up = high_ref[:wide], low_ref[:wide]
    put_left(
        left_ref, experts, column_ref, weight_ref[...] * (dot_pairs(resid, adapter_up, 1, 1) + to_ref[...]), top
    )
    down = dot(left_ref[0], own_ref[...], 0, 0) + dot(left_ref[1], other_ref[...], 0, 0)
    put_chunks(out_refs, 0, add_halves(down, 0))
    weighted_u = halves(weighted_ref[:, wide:])
    up = add_halves(dot(jnp.concatenate(weighted_u, axis=1), resid[0], 0, 0), 0) + dot(weighted_u[0], resid[1], 0, 0)
    put_chunks(out_refs, hidden_width, up_ref[...] + up)


class Ring:
    def __init__(self, size):
        self.length = size // 2
        rows = self.length // 2
        self.order = [4 * z for z in range(rows)] + [4 * z + 2 for z in reversed(range(rows))]

    def shift(self, value, step):
        pairs = [
            (chip + core, self.order[(place + step) % self.length] + core)
            for place, chip in enumerate(self.order)
            for core in range(2)
        ]
        return lax.ppermute(value, "expert", pairs)

    def swap(self, value):
        return lax.ppermute(value, "expert", [(i, i ^ 1) for i in range(2 * self.length)])

    def members(self):
        me = lax.axis_index("expert")
        rows = self.length // 2
        place = jnp.where(me // 2 % 2 == 0, me // 4, self.length - 1 - me // 4)
        there = (place + jnp.arange(self.length, dtype=jnp.int32)) % self.length
        return jnp.where(there < rows, 4 * there, 4 * (self.length - 1 - there) + 2) + me % 2

    def gather(self, own):
        half = self.length // 2
        found = {0: own}
        ahead, behind = own, own
        for step in range(1, half):
            behind = self.shift(behind, 1)
            ahead = self.shift(ahead, -1)
            found[self.length - step], found[step] = behind, ahead
        found[half] = jnp.concatenate([self.shift(behind[:1], 1), self.shift(ahead[1:], -1)])
        return [found[offset] for offset in range(self.length)]

    def scatter(self, chunks, longer):
        half = self.length // 2
        total = chunks[0]
        for way in (longer, -longer):
            start = half if way == longer else half - 1
            moving = chunks[way * start % self.length]
            for step in range(start, 0, -1):
                arrived = decode(self.shift(encode(moving), way))
                moving = arrived if step == 1 else chunks[way * (step - 1) % self.length] + arrived
            total = total + moving
        return total


def encode(value):
    largest = jnp.max(jnp.abs(value), axis=1, keepdims=True)
    exponent = jnp.ceil(jnp.log2(jnp.maximum(largest, 1e-30)))
    scaled = value * jnp.exp2(15.0 - exponent)
    extra = jnp.broadcast_to(exponent, (value.shape[0], lanes))
    return jnp.concatenate([scaled, extra], axis=1).astype(f16)


def decode(coded):
    width = coded.shape[1] - lanes
    return coded[:, :width].astype(f32) * jnp.exp2(coded[:, width : width + 1].astype(f32) - 15.0)


def gathered_plan(
    hidden_of_route,
    expert_of_route,
    gate_of_route,
    capacity,
    output_gradient,
    curvature,
    adapter_down,
    adapter_up,
    down_direction,
    up_direction,
):
    ring = Ring(lax.axis_size("expert"))
    slots = ring.length
    me = lax.axis_index("expert")
    tokens, top = expert_of_route.shape
    hidden_width = hidden_of_route.shape[2]
    rank = adapter_down.shape[2]
    model_width = output_gradient.shape[1]
    experts = capacity.shape[0]
    wide = slots * rank
    names = jnp.arange(experts, dtype=jnp.int32)

    counts = jnp.sum((expert_of_route[:, :, None] == names).astype(f32), axis=(0, 1))
    own_down = jnp.concatenate(
        [
            down_scale * jnp.concatenate([down_direction, adapter_down]).transpose(0, 2, 1),
            jnp.broadcast_to(jnp.pad(counts, (0, lanes - experts)), (2, rank, lanes)),
        ],
        axis=2,
    ).astype(f16)
    own_up = (up_scale * jnp.concatenate([adapter_up, up_direction])).astype(f16)
    down_pieces = ring.gather(own_down)
    up_pieces = ring.gather(own_up)

    small = jnp.concatenate(
        [
            expert_of_route.T.astype(f32),
            gate_of_route.T.astype(f32),
            curvature[None, :],
            jnp.zeros((-(2 * top + 1) % 8, tokens), f32),
        ]
    )
    small = jnp.concatenate([small, ring.swap(small)], axis=1)
    hidden = hidden_of_route.transpose(1, 0, 2).reshape(top * tokens, hidden_width)
    hidden_other = ring.swap(hidden)
    gradient_other = ring.swap(output_gradient)

    members = ring.members()
    all_counts = jnp.stack([piece[0, 0, hidden_width : hidden_width + experts] for piece in down_pieces]).astype(f32)
    blocks = jnp.stack([me, me ^ 1])
    prior = jnp.sum(jnp.where(members[None, :, None] < blocks[:, None, None], all_counts, 0.0), axis=1)
    prior = prior + ring.swap(prior)[::-1]
    of_slot = members[:, None] == names
    limit = jnp.sum(jnp.where(of_slot, capacity.astype(f32) - prior[:, None, :], 0.0), axis=2)
    limit = jnp.repeat(limit, rank, axis=1)
    column = jnp.repeat(members.astype(f32), rank)[None, :]

    def call(kernel, outs, *operands, scratch=()):
        return pl.pallas_call(
            kernel,
            out_shape=[jax.ShapeDtypeStruct(shape, dtype) for shape, dtype in outs],
            scratch_shapes=scratch,
            compiler_params=pltpu.CompilerParams(vmem_limit_bytes=kernel_vmem),
        )(*operands)

    (reduced,) = call(
        functools.partial(reduce_kernel, top, slots),
        [((2, 2 * tokens, wide), f32)],
        small,
        column,
        hidden,
        hidden_other,
        *[piece[..., :hidden_width].astype(f32) * (1 / down_scale) for piece in down_pieces],
    )
    weight, weighted, tangent, high, low = call(
        functools.partial(tangent_kernel, top, slots),
        [
            ((2 * tokens, wide), f32),
            ((2 * tokens, 2 * wide), f32),
            ((2 * tokens, model_width), f32),
            ((2 * wide, model_width), bf16),
            ((2 * wide, model_width), bf16),
        ],
        small,
        column,
        limit,
        reduced,
        *[piece.astype(f32) * (1 / up_scale) for piece in up_pieces],
    )
    arrived = ring.swap(tangent)
    left = [pltpu.VMEM((2, top * tokens, 2 * wide), bf16)]
    chunk = ((rank, hidden_width + model_width), f32)
    *gradients, up, to = call(
        functools.partial(gradient_kernel, top),
        [chunk] * slots + [((wide, model_width), f32), ((2 * tokens, wide), f32)],
        small,
        column,
        hidden,
        hidden_other,
        output_gradient,
        gradient_other,
        weight,
        weighted,
        high,
        low,
        scratch=left,
    )
    curvatures = call(
        functools.partial(curvature_kernel, top),
        [chunk] * slots,
        small,
        column,
        hidden,
        hidden_other,
        weight,
        weighted,
        high,
        low,
        up,
        to,
        tangent,
        arrived,
        scratch=left,
    )
    gradient_sum = ring.scatter(gradients, 1)
    curvature_sum = ring.scatter(curvatures, -1)
    return (
        gradient_sum[:, :hidden_width].T[None],
        gradient_sum[None, :, hidden_width:],
        curvature_sum[:, :hidden_width].T[None],
        curvature_sum[None, :, hidden_width:],
    )


def carried_in(value, axis, join, neutral):
    count, mine = (lax.axis_size(axis), lax.axis_index(axis))
    pieces = lax.all_gather(value, axis)
    so_far = jnp.full_like(value, 0) + jnp.asarray(neutral, value.dtype)

    def lap(position, so_far):
        longer = join(so_far, pieces[position])
        return jnp.where(position < mine, longer, so_far)

    return lax.fori_loop(0, count - 1, lap, so_far)


def add_counts(earlier, later):
    return earlier + later


def routed_plan(
    hidden_of_route,
    expert_of_route,
    gate_of_route,
    capacity,
    output_gradient,
    curvature,
    adapter_down,
    adapter_up,
    down_direction,
    up_direction,
):
    finest_precision = lax.Precision.HIGHEST
    group_size = lax.axis_size("expert")
    tok_rows, top_count = expert_of_route.shape
    hidden_width = hidden_of_route.shape[2]
    resident_experts = adapter_down.shape[0]
    adapter_rank = adapter_down.shape[2]
    model_width = output_gradient.shape[1]
    experts = resident_experts * group_size
    slot_most = 2 * tok_rows * top_count // experts
    routes = expert_of_route.reshape(-1)
    onehot = (routes[:, None] == jnp.arange(experts, dtype=jnp.int32)[None, :]).astype(jnp.int32)
    earlier = jnp.cumsum(onehot, axis=0) - onehot
    local_rank = jnp.sum(earlier * onehot, axis=1)
    counts = jnp.sum(onehot, axis=0)
    prior_count = carried_in(counts, "expert", add_counts, jnp.zeros_like(counts))
    global_rank = local_rank + jnp.sum(onehot * prior_count[None, :], axis=1)
    route_limit = jnp.sum(onehot * capacity[None, :], axis=1)
    retained_mask = (global_rank < route_limit).astype(jnp.float32)
    weight_of_route = (
        adapter_scale * gate_of_route.reshape(-1).astype(jnp.float32) * retained_mask
    ).astype(jnp.bfloat16)
    slot_index = routes * slot_most + local_rank
    layout = (group_size, resident_experts, slot_most)
    send_hidden = (
        jnp.zeros((experts * slot_most, hidden_width), jnp.bfloat16)
        .at[slot_index]
        .set(hidden_of_route.reshape(-1, hidden_width))
        .reshape(layout + (hidden_width,))
    )
    send_weight = (
        jnp.zeros((experts * slot_most,), jnp.bfloat16)
        .at[slot_index]
        .set(weight_of_route)
        .reshape(layout)
    )
    down_stacked = jnp.concatenate([adapter_down, down_direction], axis=2)
    up_stacked = jnp.concatenate([adapter_up, up_direction], axis=1)

    def spread(token_rows):
        per_route = jnp.repeat(token_rows, top_count, axis=0)
        placed = (
            jnp.zeros((experts * slot_most, model_width), jnp.bfloat16)
            .at[slot_index]
            .set(per_route)
        )
        return placed.reshape(layout + (model_width,))

    send_residual = spread(output_gradient)
    pieces = (
        lax.all_to_all(send_hidden, "expert", split_axis=0, concat_axis=0, tiled=True),
        lax.all_to_all(send_weight, "expert", split_axis=0, concat_axis=0, tiled=True),
    )
    hidden_rows = pieces[0].astype(jnp.float32)
    weight_rows = pieces[1].astype(jnp.float32)[..., None]
    reduced_hidden = jnp.einsum(
        "cjif,jfk->cjik", hidden_rows, down_stacked, precision=finest_precision
    )
    exchanged_rows = jnp.concatenate(
        [reduced_hidden[..., adapter_rank:], reduced_hidden[..., :adapter_rank]], axis=3
    )
    tangent_out = weight_rows * jnp.einsum(
        "cjik,jkd->cjid", exchanged_rows, up_stacked, precision=finest_precision
    )
    returned = lax.all_to_all(
        tangent_out.astype(jnp.bfloat16), "expert", split_axis=0, concat_axis=0, tiled=True
    )
    results = (returned, reduced_hidden) + tuple(pieces)
    returned = results[0]
    reduced_hidden = results[1]
    hidden_rows = results[2]
    weight_rows = results[3]
    route_tangent = returned.reshape(experts * slot_most, model_width)[slot_index]
    out_tangent = jnp.sum(
        route_tangent.reshape(tok_rows, top_count, model_width).astype(jnp.float32), axis=1
    )
    resid_tangent = (curvature[:, None] * out_tangent).astype(jnp.bfloat16)
    send_tangent = spread(resid_tangent)
    residual_rows, tangent_rows = (
        lax.all_to_all(send_residual, "expert", split_axis=0, concat_axis=0, tiled=True),
        lax.all_to_all(send_tangent, "expert", split_axis=0, concat_axis=0, tiled=True),
    )
    residual_full = residual_rows.astype(jnp.float32)
    complete_tangent = tangent_rows.astype(jnp.float32)
    weight_column = weight_rows.astype(jnp.float32)[..., None]
    residual_reduced = jnp.einsum(
        "wyov,yqv->wyoq", residual_full, up_stacked, precision=finest_precision
    )
    reduced_tangent = jnp.einsum(
        "wyov,yqv->wyoq", complete_tangent, adapter_up, precision=finest_precision
    )
    left_terms = jnp.concatenate(
        [
            weight_column * residual_reduced[..., :adapter_rank],
            weight_column * (reduced_tangent + residual_reduced[..., adapter_rank:]),
        ],
        axis=3,
    )
    down_terms = jnp.einsum(
        "cjif,cjik->jfk", hidden_rows.astype(jnp.float32), left_terms, precision=finest_precision
    )
    raised_update = weight_column * reduced_hidden[..., :adapter_rank]
    raised_tangent_update = weight_column * reduced_hidden[..., adapter_rank:]
    up_terms = jnp.einsum(
        "cjik,cjid->jkd",
        jnp.concatenate([raised_update, raised_tangent_update], axis=3),
        residual_full,
        precision=finest_precision,
    )
    curvature_piece = up_terms[:, adapter_rank:] + jnp.einsum(
        "cjik,cjid->jkd", raised_update, complete_tangent, precision=finest_precision
    )
    return (
        down_terms[..., :adapter_rank],
        up_terms[:, :adapter_rank],
        down_terms[..., adapter_rank:],
        curvature_piece,
    )


def local(*arguments):
    adapter_down, adapter_up = arguments[6], arguments[7]
    factor_bytes = 2 * 4 * (adapter_down.size + adapter_up.size) * lax.axis_size("expert")
    plan = gathered_plan if 4 * factor_bytes <= kernel_vmem else routed_plan
    return plan(*arguments)


def solution(mesh):
    return jax.shard_map(
        local,
        mesh=mesh,
        in_specs=(
            P(("groups", "expert"), None, None),
            P(("groups", "expert"), None),
            P(("groups", "expert"), None),
            P("groups"),
            P(("groups", "expert"), None),
            P(("groups", "expert")),
            P("expert", None, None),
            P("expert", None, None),
            P(("groups", "expert"), None, None),
            P(("groups", "expert"), None, None),
        ),
        out_specs=(
            P(("groups", "expert"), None, None),
            P(("groups", "expert"), None, None),
            P(("groups", "expert"), None, None),
            P(("groups", "expert"), None, None),
        ),
        check_vma=False,
    )
```

```python
import functools

import jax
import jax.numpy as jnp
from jax import lax
from jax.experimental import pallas as pl
from jax.experimental.pallas import tpu as pltpu
from jax.sharding import PartitionSpec as P

adapter_scale = 2.0
f32 = jnp.float32
bf16 = jnp.bfloat16
f16 = jnp.float16
lanes = 128
down_scale = 2.0**18
up_scale = 2.0**15
kernel_vmem = 32 * 2**20


def halves(value):
    high = value.astype(bf16)
    return high, (value - high.astype(f32)).astype(bf16)


def dot(a, b, a_dim, b_dim):
    return lax.dot_general(a, b, (((a_dim,), (b_dim,)), ((), ())), preferred_element_type=f32)


def dot_pairs(a, b, a_dim, b_dim):
    return dot(a[0], b[0], a_dim, b_dim) + (dot(a[1], b[0], a_dim, b_dim) + dot(a[0], b[1], a_dim, b_dim))


def token_columns(small_ref, top):
    small = small_ref[...].T
    experts = [small[:, k : k + 1] for k in range(top)]
    gates = [small[:, top + k : top + k + 1] for k in range(top)]
    return experts, gates, small[:, 2 * top : 2 * top + 1]


def stacked(refs, width):
    rows = [ref[:, kind, :, :width].reshape(-1, width) for kind in range(2) for ref in refs]
    return halves(jnp.concatenate(rows, axis=0))


def reduce_kernel(top, small_ref, column_ref, own_ref, other_ref, factor_ref, reduced_ref):
    experts, _, _ = token_columns(small_ref, top)
    high, low = stacked([factor_ref], own_ref.shape[1])
    wide = high.shape[0] // 2
    tokens = own_ref.shape[0] // top
    for block, hidden_ref in enumerate((own_ref, other_ref)):
        rows = slice(block * tokens, (block + 1) * tokens)
        full = dot(hidden_ref[...], high, 1, 1) + dot(hidden_ref[...], low, 1, 1)
        total = jnp.zeros((tokens, 2 * wide), f32)
        for k in range(top):
            named = experts[k][rows] == column_ref[...]
            total = jnp.where(jnp.concatenate([named, named], axis=1), full[k * tokens : (k + 1) * tokens], total)
        reduced_ref[0, rows] = total[:, :wide]
        reduced_ref[1, rows] = total[:, wide:]


def rank_limits(rank, column_ref, capacity_ref, factor_refs):
    wide = column_ref.shape[1]
    member = [column_ref[:, start : start + 1] for start in range(0, wide, rank)]
    me = member[0]
    across = 1.0 - 2.0 * (me - 2.0 * jnp.floor(me * 0.5))
    left = []
    for block in (me, me + across):
        total = capacity_ref[...]
        slot = 0
        for ref in factor_refs:
            for piece in range(ref.shape[0]):
                own = ref[piece, 0, 0:1, ref.shape[3] - lanes :]
                other = ref[piece, 0, 1:2, ref.shape[3] - lanes :]
                total = total - jnp.where(member[slot] < block, own, 0.0)
                total = total - jnp.where(member[slot] + across < block, other, 0.0)
                slot += 1
        left.append(total)
    lane = lax.broadcasted_iota(jnp.int32, (1, lanes), 1).astype(f32)
    slot_of = lax.broadcasted_iota(jnp.int32, (1, wide), 1) // rank
    limits = []
    for total in left:
        limit = jnp.zeros((1, wide), f32)
        for slot, expert in enumerate(member):
            value = jnp.sum(jnp.where(lane == expert, total, 0.0), axis=1, keepdims=True)
            limit = jnp.where(slot_of == slot, value, limit)
        limits.append(limit)
    return limits


def tangent_kernel(top, small_ref, column_ref, capacity_ref, reduced_ref, near_ref, far_ref, *outs):
    weight_ref, weighted_ref, tangent_ref, high_ref, low_ref = outs
    experts, gates, _ = token_columns(small_ref, top)
    tokens, wide = weight_ref.shape
    block = tokens // 2
    limits = rank_limits(near_ref.shape[2], column_ref, capacity_ref, (near_ref, far_ref))
    gate = jnp.zeros((tokens, wide), f32)
    member = jnp.zeros((tokens, wide), f32)
    for k in range(top):
        named = experts[k] == column_ref[...]
        gate = jnp.where(named, gates[k], gate)
        member = jnp.where(named, 1.0, member)
    below = (
        lax.broadcasted_iota(jnp.int32, (block, block), 0)
        > lax.broadcasted_iota(jnp.int32, (block, block), 1)
    )
    below = jnp.where(below, 1.0, 0.0).astype(bf16)
    weights = []
    for part in range(2):
        rows = slice(part * block, (part + 1) * block)
        local_rank = dot(below, member[rows].astype(bf16), 1, 0)
        weights.append(jnp.where(local_rank < limits[part], adapter_scale * gate[rows], 0.0))
    weight = jnp.concatenate(weights, axis=0)
    weight_ref[...] = weight
    weighted = jnp.concatenate([weight * reduced_ref[0], weight * reduced_ref[1]], axis=1)
    weighted_ref[...] = weighted
    factor = stacked([near_ref, far_ref], high_ref.shape[1])
    high_ref[...], low_ref[...] = factor
    tangent_ref[...] = dot_pairs(halves(weighted), factor, 1, 0)


def put_left(left_ref, experts, column_ref, terms, top):
    both = jnp.concatenate(halves(terms), axis=1)
    tokens = terms.shape[0] // 2
    for block in range(2):
        rows = slice(block * tokens, (block + 1) * tokens)
        for k in range(top):
            named = experts[k][rows] == column_ref[...]
            named = jnp.concatenate([named, named], axis=1)
            left_ref[block, k * tokens : (k + 1) * tokens] = jnp.where(named, both[rows], jnp.zeros_like(both[rows]))


def add_halves(both, axis):
    middle = both.shape[axis] // 2
    if axis == 0:
        return both[:middle] + both[middle:]
    return both[:, :middle] + both[:, middle:]


def put_chunks(out_refs, start, value):
    for place, out_ref in enumerate(out_refs):
        count, rank, _ = out_ref.shape
        rows = value[place * count * rank : (place + 1) * count * rank]
        out_ref[:, :, start : start + value.shape[1]] = rows.reshape(count, rank, value.shape[1])


def gradient_kernel(
    top,
    small_ref,
    column_ref,
    own_ref,
    other_ref,
    own_gradient_ref,
    other_gradient_ref,
    weight_ref,
    weighted_ref,
    high_ref,
    low_ref,
    *rest,
):
    out_refs, (up_ref, to_ref, left_ref) = rest[:-3], rest[-3:]
    experts, _, _ = token_columns(small_ref, top)
    wide = weight_ref.shape[1]
    hidden_width = own_ref.shape[1]
    gradient = jnp.concatenate([own_gradient_ref[...], other_gradient_ref[...]], axis=0)
    to_both = dot(gradient, high_ref[...], 1, 1) + dot(gradient, low_ref[...], 1, 1)
    to_ref[...] = to_both[:, wide:]
    put_left(left_ref, experts, column_ref, weight_ref[...] * to_both[:, :wide], top)
    down = dot(left_ref[0], own_ref[...], 0, 0) + dot(left_ref[1], other_ref[...], 0, 0)
    put_chunks(out_refs, 0, add_halves(down, 0))
    up = add_halves(dot(jnp.concatenate(halves(weighted_ref[...]), axis=1), gradient, 0, 0), 0)
    up_ref[...] = up[:wide]
    put_chunks(out_refs, hidden_width, up[wide:])


def curvature_kernel(
    top,
    small_ref,
    column_ref,
    own_ref,
    other_ref,
    weight_ref,
    weighted_ref,
    high_ref,
    low_ref,
    up_ref,
    to_ref,
    tangent_ref,
    arrived_ref,
    *rest,
):
    out_refs, left_ref = rest[:-1], rest[-1]
    experts, _, curvature = token_columns(small_ref, top)
    tokens, wide = weight_ref.shape
    block = tokens // 2
    hidden_width = own_ref.shape[1]
    arrived = jnp.concatenate([arrived_ref[block:], arrived_ref[:block]], axis=0)
    resid = halves(curvature * (tangent_ref[...] + arrived))
    adapter_up = high_ref[:wide], low_ref[:wide]
    put_left(
        left_ref, experts, column_ref, weight_ref[...] * (dot_pairs(resid, adapter_up, 1, 1) + to_ref[...]), top
    )
    down = dot(left_ref[0], own_ref[...], 0, 0) + dot(left_ref[1], other_ref[...], 0, 0)
    put_chunks(out_refs, 0, add_halves(down, 0))
    weighted_u = halves(weighted_ref[:, wide:])
    up = add_halves(dot(jnp.concatenate(weighted_u, axis=1), resid[0], 0, 0), 0) + dot(weighted_u[0], resid[1], 0, 0)
    put_chunks(out_refs, hidden_width, up_ref[...] + up)


def exchange(value, mask):
    size = lax.axis_size("expert")
    return lax.ppermute(value, "expert", [(device, device ^ mask) for device in range(size)])


def encode(value):
    largest = jnp.max(jnp.abs(value), axis=-1, keepdims=True)
    exponent = jnp.ceil(jnp.log2(jnp.maximum(largest, 1e-30)))
    scaled = value * jnp.exp2(15.0 - exponent)
    extra = jnp.broadcast_to(exponent, value.shape[:-1] + (lanes,))
    return jnp.concatenate([scaled, extra], axis=-1).astype(f16)


def decode(coded):
    width = coded.shape[-1] - lanes
    return coded[..., :width].astype(f32) * jnp.exp2(coded[..., width : width + 1].astype(f32) - 15.0)


def gathered_plan(
    hidden_of_route,
    expert_of_route,
    gate_of_route,
    capacity,
    output_gradient,
    curvature,
    adapter_down,
    adapter_up,
    down_direction,
    up_direction,
):
    rows = lax.axis_size("expert") // 4
    masks = [4 * z for z in range(rows)] + [4 * z + 2 for z in range(rows)]
    me = lax.axis_index("expert")
    tokens, top = expert_of_route.shape
    hidden_width = hidden_of_route.shape[2]
    rank = adapter_down.shape[2]
    model_width = output_gradient.shape[1]
    experts = capacity.shape[0]
    wide = 2 * rows * rank
    names = jnp.arange(experts, dtype=f32)

    def gather(own):
        near = [own] + [exchange(own, 4 * z) for z in range(1, rows)]
        return near, [exchange(piece, 2) for piece in near]

    own_down = (down_scale * jnp.concatenate([down_direction, adapter_down]).transpose(0, 2, 1)).astype(f16)
    down_near, down_far = gather(own_down)

    small = jnp.concatenate(
        [
            expert_of_route.T.astype(f32),
            gate_of_route.T.astype(f32),
            curvature[None, :],
            jnp.zeros((-(2 * top + 1) % 8, tokens), f32),
        ]
    )
    small_other = exchange(small, 1)
    counts = jnp.stack(
        [jnp.sum((part[:top, :, None] == names).astype(f32), axis=(0, 1)) for part in (small, small_other)]
    )
    counts = jnp.pad(counts, ((0, rank - 2), (0, lanes - experts)))
    own_up = jnp.concatenate(
        [
            up_scale * jnp.concatenate([adapter_up, up_direction]),
            jnp.broadcast_to(counts, (2, rank, lanes)),
        ],
        axis=2,
    ).astype(f16)
    up_near, up_far = gather(own_up)

    hidden_of_route, _ = lax.optimization_barrier((hidden_of_route, own_up))
    small = jnp.concatenate([small, small_other], axis=1)
    hidden = hidden_of_route.transpose(1, 0, 2).reshape(top * tokens, hidden_width)
    hidden_other = exchange(hidden, 1)
    gradient_other = exchange(output_gradient, 1)
    column = jnp.repeat((me ^ jnp.array(masks, jnp.int32)).astype(f32), rank)[None, :]
    capacity_row = jnp.pad(capacity.astype(f32), (0, lanes - experts))[None, :]

    def call(kernel, outs, *operands, scratch=()):
        return pl.pallas_call(
            functools.partial(kernel, top),
            out_shape=[jax.ShapeDtypeStruct(shape, dtype) for shape, dtype in outs],
            scratch_shapes=scratch,
            compiler_params=pltpu.CompilerParams(vmem_limit_bytes=kernel_vmem),
        )(*operands)

    down_factors = jnp.stack(down_near + down_far).astype(f32) * (1 / down_scale)
    down_factors, *_ = lax.optimization_barrier((down_factors, *up_near))
    (reduced,) = call(
        reduce_kernel, [((2, 2 * tokens, wide), f32)], small, column, hidden, hidden_other, down_factors
    )
    unscale = jnp.concatenate([jnp.full((model_width,), 1 / up_scale, f32), jnp.ones((lanes,), f32)])
    weight, weighted, tangent, high, low = call(
        tangent_kernel,
        [
            ((2 * tokens, wide), f32),
            ((2 * tokens, 2 * wide), f32),
            ((2 * tokens, model_width), f32),
            ((2 * wide, model_width), bf16),
            ((2 * wide, model_width), bf16),
        ],
        small,
        column,
        capacity_row,
        reduced,
        jnp.stack(up_near).astype(f32) * unscale,
        jnp.stack(up_far).astype(f32) * unscale,
    )
    arrived = exchange(tangent, 1)
    left = [pltpu.VMEM((2, top * tokens, 2 * wide), bf16)]
    chunks = [((rows // 2, rank, hidden_width + model_width), f32)] * 4
    *gradients, up, to = call(
        gradient_kernel,
        chunks + [((wide, model_width), f32), ((2 * tokens, wide), f32)],
        small,
        column,
        hidden,
        hidden_other,
        output_gradient,
        gradient_other,
        weight,
        weighted,
        high,
        low,
        scratch=left,
    )
    curvatures = call(
        curvature_kernel,
        chunks,
        small,
        column,
        hidden,
        hidden_other,
        weight,
        weighted,
        high,
        low,
        up,
        to,
        tangent,
        arrived,
        scratch=left,
    )

    def along_x(parts):
        later = exchange(encode(parts[3]), 2)
        sooner = exchange(encode(parts[2]), 2)
        return sooner, later

    def along_z(parts, moved):
        later = encode(parts[1] + decode(moved[1]))
        arrived = [exchange(later[z - rows // 2], 4 * z) for z in range(rows // 2, rows)]
        sooner = parts[0] + decode(moved[0])
        arrived += [exchange(encode(sooner[z]), 4 * z) for z in range(1, rows // 2)]
        return sooner[0] + sum(decode(piece) for piece in arrived)

    gradients_moved = along_x(gradients)
    gradients_moved, curvatures = lax.optimization_barrier((gradients_moved, curvatures))
    curvatures_moved = along_x(curvatures)
    gradient_sum = along_z(gradients, gradients_moved)
    curvature_sum = along_z(curvatures, curvatures_moved)
    return (
        gradient_sum[:, :hidden_width].T[None],
        gradient_sum[None, :, hidden_width:],
        curvature_sum[:, :hidden_width].T[None],
        curvature_sum[None, :, hidden_width:],
    )


def carried_in(value, axis, join, neutral):
    count, mine = (lax.axis_size(axis), lax.axis_index(axis))
    pieces = lax.all_gather(value, axis)
    so_far = jnp.full_like(value, 0) + jnp.asarray(neutral, value.dtype)

    def lap(position, so_far):
        longer = join(so_far, pieces[position])
        return jnp.where(position < mine, longer, so_far)

    return lax.fori_loop(0, count - 1, lap, so_far)


def add_counts(earlier, later):
    return earlier + later


def routed_plan(
    hidden_of_route,
    expert_of_route,
    gate_of_route,
    capacity,
    output_gradient,
    curvature,
    adapter_down,
    adapter_up,
    down_direction,
    up_direction,
):
    finest_precision = lax.Precision.HIGHEST
    group_size = lax.axis_size("expert")
    tok_rows, top_count = expert_of_route.shape
    hidden_width = hidden_of_route.shape[2]
    resident_experts = adapter_down.shape[0]
    adapter_rank = adapter_down.shape[2]
    model_width = output_gradient.shape[1]
    experts = resident_experts * group_size
    slot_most = 2 * tok_rows * top_count // experts
    routes = expert_of_route.reshape(-1)
    onehot = (routes[:, None] == jnp.arange(experts, dtype=jnp.int32)[None, :]).astype(jnp.int32)
    earlier = jnp.cumsum(onehot, axis=0) - onehot
    local_rank = jnp.sum(earlier * onehot, axis=1)
    counts = jnp.sum(onehot, axis=0)
    prior_count = carried_in(counts, "expert", add_counts, jnp.zeros_like(counts))
    global_rank = local_rank + jnp.sum(onehot * prior_count[None, :], axis=1)
    route_limit = jnp.sum(onehot * capacity[None, :], axis=1)
    retained_mask = (global_rank < route_limit).astype(jnp.float32)
    weight_of_route = (
        adapter_scale * gate_of_route.reshape(-1).astype(jnp.float32) * retained_mask
    ).astype(jnp.bfloat16)
    slot_index = routes * slot_most + local_rank
    layout = (group_size, resident_experts, slot_most)
    send_hidden = (
        jnp.zeros((experts * slot_most, hidden_width), jnp.bfloat16)
        .at[slot_index]
        .set(hidden_of_route.reshape(-1, hidden_width))
        .reshape(layout + (hidden_width,))
    )
    send_weight = (
        jnp.zeros((experts * slot_most,), jnp.bfloat16)
        .at[slot_index]
        .set(weight_of_route)
        .reshape(layout)
    )
    down_stacked = jnp.concatenate([adapter_down, down_direction], axis=2)
    up_stacked = jnp.concatenate([adapter_up, up_direction], axis=1)

    def spread(token_rows):
        per_route = jnp.repeat(token_rows, top_count, axis=0)
        placed = (
            jnp.zeros((experts * slot_most, model_width), jnp.bfloat16)
            .at[slot_index]
            .set(per_route)
        )
        return placed.reshape(layout + (model_width,))

    send_residual = spread(output_gradient)
    pieces = (
        lax.all_to_all(send_hidden, "expert", split_axis=0, concat_axis=0, tiled=True),
        lax.all_to_all(send_weight, "expert", split_axis=0, concat_axis=0, tiled=True),
    )
    hidden_rows = pieces[0].astype(jnp.float32)
    weight_rows = pieces[1].astype(jnp.float32)[..., None]
    reduced_hidden = jnp.einsum(
        "cjif,jfk->cjik", hidden_rows, down_stacked, precision=finest_precision
    )
    exchanged_rows = jnp.concatenate(
        [reduced_hidden[..., adapter_rank:], reduced_hidden[..., :adapter_rank]], axis=3
    )
    tangent_out = weight_rows * jnp.einsum(
        "cjik,jkd->cjid", exchanged_rows, up_stacked, precision=finest_precision
    )
    returned = lax.all_to_all(
        tangent_out.astype(jnp.bfloat16), "expert", split_axis=0, concat_axis=0, tiled=True
    )
    results = (returned, reduced_hidden) + tuple(pieces)
    returned = results[0]
    reduced_hidden = results[1]
    hidden_rows = results[2]
    weight_rows = results[3]
    route_tangent = returned.reshape(experts * slot_most, model_width)[slot_index]
    out_tangent = jnp.sum(
        route_tangent.reshape(tok_rows, top_count, model_width).astype(jnp.float32), axis=1
    )
    resid_tangent = (curvature[:, None] * out_tangent).astype(jnp.bfloat16)
    send_tangent = spread(resid_tangent)
    residual_rows, tangent_rows = (
        lax.all_to_all(send_residual, "expert", split_axis=0, concat_axis=0, tiled=True),
        lax.all_to_all(send_tangent, "expert", split_axis=0, concat_axis=0, tiled=True),
    )
    residual_full = residual_rows.astype(jnp.float32)
    complete_tangent = tangent_rows.astype(jnp.float32)
    weight_column = weight_rows.astype(jnp.float32)[..., None]
    residual_reduced = jnp.einsum(
        "wyov,yqv->wyoq", residual_full, up_stacked, precision=finest_precision
    )
    reduced_tangent = jnp.einsum(
        "wyov,yqv->wyoq", complete_tangent, adapter_up, precision=finest_precision
    )
    left_terms = jnp.concatenate(
        [
            weight_column * residual_reduced[..., :adapter_rank],
            weight_column * (reduced_tangent + residual_reduced[..., adapter_rank:]),
        ],
        axis=3,
    )
    down_terms = jnp.einsum(
        "cjif,cjik->jfk", hidden_rows.astype(jnp.float32), left_terms, precision=finest_precision
    )
    raised_update = weight_column * reduced_hidden[..., :adapter_rank]
    raised_tangent_update = weight_column * reduced_hidden[..., adapter_rank:]
    up_terms = jnp.einsum(
        "cjik,cjid->jkd",
        jnp.concatenate([raised_update, raised_tangent_update], axis=3),
        residual_full,
        precision=finest_precision,
    )
    curvature_piece = up_terms[:, adapter_rank:] + jnp.einsum(
        "cjik,cjid->jkd", raised_update, complete_tangent, precision=finest_precision
    )
    return (
        down_terms[..., :adapter_rank],
        up_terms[:, :adapter_rank],
        down_terms[..., adapter_rank:],
        curvature_piece,
    )


def local(*arguments):
    adapter_down, adapter_up = arguments[6], arguments[7]
    factor_bytes = 2 * 4 * (adapter_down.size + adapter_up.size) * lax.axis_size("expert")
    plan = gathered_plan if 4 * factor_bytes <= kernel_vmem else routed_plan
    return plan(*arguments)


def solution(mesh):
    return jax.shard_map(
        local,
        mesh=mesh,
        in_specs=(
            P(("groups", "expert"), None, None),
            P(("groups", "expert"), None),
            P(("groups", "expert"), None),
            P("groups"),
            P(("groups", "expert"), None),
            P(("groups", "expert")),
            P("expert", None, None),
            P("expert", None, None),
            P(("groups", "expert"), None, None),
            P(("groups", "expert"), None, None),
        ),
        out_specs=(
            P(("groups", "expert"), None, None),
            P(("groups", "expert"), None, None),
            P(("groups", "expert"), None, None),
            P(("groups", "expert"), None, None),
        ),
        check_vma=False,
    )
```

```python
import functools

import jax
import jax.numpy as jnp
from jax import lax
from jax.experimental import pallas as pl
from jax.experimental.pallas import tpu as pltpu
from jax.sharding import PartitionSpec as P

adapter_scale = 2.0
f32 = jnp.float32
bf16 = jnp.bfloat16
f16 = jnp.float16
lanes = 128
down_scale = 2.0**18
up_scale = 2.0**15
kernel_vmem = 32 * 2**20


def halves(value):
    high = value.astype(bf16)
    return high, (value - high.astype(f32)).astype(bf16)


def dot(a, b, a_dim, b_dim):
    return lax.dot_general(a, b, (((a_dim,), (b_dim,)), ((), ())), preferred_element_type=f32)


def dot_pairs(a, b, a_dim, b_dim):
    return dot(a[0], b[0], a_dim, b_dim) + (dot(a[1], b[0], a_dim, b_dim) + dot(a[0], b[1], a_dim, b_dim))


def token_columns(small_ref, top):
    small = small_ref[...].T
    experts = [small[:, k : k + 1] for k in range(top)]
    gates = [small[:, top + k : top + k + 1] for k in range(top)]
    return experts, gates, small[:, 2 * top : 2 * top + 1]


def stacked(chip_ref, masks, factor_ref, width):
    rows = [factor_ref[chip_ref[0] ^ mask, kind, :, :width] for kind in range(2) for mask in masks]
    return halves(jnp.concatenate(rows, axis=0))


def reduce_kernel(top, masks, chip_ref, small_ref, column_ref, own_ref, other_ref, factor_ref, reduced_ref):
    experts, _, _ = token_columns(small_ref, top)
    high, low = stacked(chip_ref, masks, factor_ref, own_ref.shape[1])
    wide = high.shape[0] // 2
    tokens = own_ref.shape[0] // top
    for block, hidden_ref in enumerate((own_ref, other_ref)):
        rows = slice(block * tokens, (block + 1) * tokens)
        full = dot(hidden_ref[...], high, 1, 1) + dot(hidden_ref[...], low, 1, 1)
        total = jnp.zeros((tokens, 2 * wide), f32)
        for k in range(top):
            named = experts[k][rows] == column_ref[...]
            total = jnp.where(jnp.concatenate([named, named], axis=1), full[k * tokens : (k + 1) * tokens], total)
        reduced_ref[0, rows] = total[:, :wide]
        reduced_ref[1, rows] = total[:, wide:]


def rank_limits(rank, column_ref, capacity_ref, factor_ref):
    wide = column_ref.shape[1]
    member = [column_ref[:, start : start + 1] for start in range(0, wide, rank)]
    me = member[0]
    core = me - 2.0 * jnp.floor(me * 0.5)
    across = 1.0 - 2.0 * core
    left = []
    for block in (me, me + across):
        total = capacity_ref[...]
        for chip in range(factor_ref.shape[0]):
            own = factor_ref[chip, 0, 0:1, factor_ref.shape[3] - lanes :]
            other = factor_ref[chip, 0, 1:2, factor_ref.shape[3] - lanes :]
            device = 2.0 * chip + core
            total = total - jnp.where(device < block, own, 0.0)
            total = total - jnp.where(device + across < block, other, 0.0)
        left.append(total)
    lane = lax.broadcasted_iota(jnp.int32, (1, lanes), 1).astype(f32)
    slot_of = lax.broadcasted_iota(jnp.int32, (1, wide), 1) // rank
    limits = []
    for total in left:
        limit = jnp.zeros((1, wide), f32)
        for slot, expert in enumerate(member):
            value = jnp.sum(jnp.where(lane == expert, total, 0.0), axis=1, keepdims=True)
            limit = jnp.where(slot_of == slot, value, limit)
        limits.append(limit)
    return limits


def tangent_kernel(top, masks, chip_ref, small_ref, column_ref, capacity_ref, reduced_ref, factor_ref, *outs):
    weight_ref, weighted_ref, tangent_ref, high_ref, low_ref = outs
    experts, gates, _ = token_columns(small_ref, top)
    tokens, wide = weight_ref.shape
    block = tokens // 2
    limits = rank_limits(factor_ref.shape[2], column_ref, capacity_ref, factor_ref)
    gate = jnp.zeros((tokens, wide), f32)
    member = jnp.zeros((tokens, wide), f32)
    for k in range(top):
        named = experts[k] == column_ref[...]
        gate = jnp.where(named, gates[k], gate)
        member = jnp.where(named, 1.0, member)
    below = (
        lax.broadcasted_iota(jnp.int32, (block, block), 0)
        > lax.broadcasted_iota(jnp.int32, (block, block), 1)
    )
    below = jnp.where(below, 1.0, 0.0).astype(bf16)
    weights = []
    for part in range(2):
        rows = slice(part * block, (part + 1) * block)
        local_rank = dot(below, member[rows].astype(bf16), 1, 0)
        weights.append(jnp.where(local_rank < limits[part], adapter_scale * gate[rows], 0.0))
    weight = jnp.concatenate(weights, axis=0)
    weight_ref[...] = weight
    weighted = jnp.concatenate([weight * reduced_ref[0], weight * reduced_ref[1]], axis=1)
    weighted_ref[...] = weighted
    factor = stacked(chip_ref, masks, factor_ref, high_ref.shape[1])
    high_ref[...], low_ref[...] = factor
    tangent_ref[...] = dot_pairs(halves(weighted), factor, 1, 0)


def put_left(left_ref, experts, column_ref, terms, top):
    both = jnp.concatenate(halves(terms), axis=1)
    tokens = terms.shape[0] // 2
    for block in range(2):
        rows = slice(block * tokens, (block + 1) * tokens)
        for k in range(top):
            named = experts[k][rows] == column_ref[...]
            named = jnp.concatenate([named, named], axis=1)
            left_ref[block, k * tokens : (k + 1) * tokens] = jnp.where(named, both[rows], jnp.zeros_like(both[rows]))


def add_halves(both, axis):
    middle = both.shape[axis] // 2
    if axis == 0:
        return both[:middle] + both[middle:]
    return both[:, :middle] + both[:, middle:]


def put_chunks(out_refs, start, value):
    for place, out_ref in enumerate(out_refs):
        count, rank, _ = out_ref.shape
        rows = value[place * count * rank : (place + 1) * count * rank]
        out_ref[:, :, start : start + value.shape[1]] = rows.reshape(count, rank, value.shape[1])


def gradient_kernel(
    top,
    small_ref,
    column_ref,
    own_ref,
    other_ref,
    own_gradient_ref,
    other_gradient_ref,
    weight_ref,
    weighted_ref,
    high_ref,
    low_ref,
    *rest,
):
    out_refs, (up_ref, to_ref, left_ref) = rest[:-3], rest[-3:]
    experts, _, _ = token_columns(small_ref, top)
    wide = weight_ref.shape[1]
    hidden_width = own_ref.shape[1]
    gradient = jnp.concatenate([own_gradient_ref[...], other_gradient_ref[...]], axis=0)
    to_both = dot(gradient, high_ref[...], 1, 1) + dot(gradient, low_ref[...], 1, 1)
    to_ref[...] = to_both[:, wide:]
    put_left(left_ref, experts, column_ref, weight_ref[...] * to_both[:, :wide], top)
    down = dot(left_ref[0], own_ref[...], 0, 0) + dot(left_ref[1], other_ref[...], 0, 0)
    put_chunks(out_refs, 0, add_halves(down, 0))
    up = add_halves(dot(jnp.concatenate(halves(weighted_ref[...]), axis=1), gradient, 0, 0), 0)
    up_ref[...] = up[:wide]
    put_chunks(out_refs, hidden_width, up[wide:])


def curvature_kernel(
    top,
    small_ref,
    column_ref,
    own_ref,
    other_ref,
    weight_ref,
    weighted_ref,
    high_ref,
    low_ref,
    up_ref,
    to_ref,
    tangent_ref,
    arrived_ref,
    *rest,
):
    out_refs, left_ref = rest[:-1], rest[-1]
    experts, _, curvature = token_columns(small_ref, top)
    tokens, wide = weight_ref.shape
    block = tokens // 2
    hidden_width = own_ref.shape[1]
    arrived = jnp.concatenate([arrived_ref[block:], arrived_ref[:block]], axis=0)
    resid = halves(curvature * (tangent_ref[...] + arrived))
    adapter_up = high_ref[:wide], low_ref[:wide]
    put_left(
        left_ref, experts, column_ref, weight_ref[...] * (dot_pairs(resid, adapter_up, 1, 1) + to_ref[...]), top
    )
    down = dot(left_ref[0], own_ref[...], 0, 0) + dot(left_ref[1], other_ref[...], 0, 0)
    put_chunks(out_refs, 0, add_halves(down, 0))
    weighted_u = halves(weighted_ref[:, wide:])
    up = add_halves(dot(jnp.concatenate(weighted_u, axis=1), resid[0], 0, 0), 0) + dot(weighted_u[0], resid[1], 0, 0)
    put_chunks(out_refs, hidden_width, up_ref[...] + up)


def exchange(value, mask):
    size = lax.axis_size("expert")
    return lax.ppermute(value, "expert", [(device, device ^ mask) for device in range(size)])


def encode(value):
    largest = jnp.max(jnp.abs(value), axis=-1, keepdims=True)
    exponent = jnp.ceil(jnp.log2(jnp.maximum(largest, 1e-30)))
    scaled = value * jnp.exp2(15.0 - exponent)
    extra = jnp.broadcast_to(exponent, value.shape[:-1] + (lanes,))
    return jnp.concatenate([scaled, extra], axis=-1).astype(f16)


def decode(coded):
    width = coded.shape[-1] - lanes
    return coded[..., :width].astype(f32) * jnp.exp2(coded[..., width : width + 1].astype(f32) - 15.0)


def gathered_plan(
    hidden_of_route,
    expert_of_route,
    gate_of_route,
    capacity,
    output_gradient,
    curvature,
    adapter_down,
    adapter_up,
    down_direction,
    up_direction,
):
    size = lax.axis_size("expert")
    rows = size // 4
    masks = [2 * z for z in range(rows)] + [2 * z + 1 for z in range(rows)]
    cores = [list(range(core, size, 2)) for core in range(2)]
    me = lax.axis_index("expert")
    tokens, top = expert_of_route.shape
    hidden_width = hidden_of_route.shape[2]
    rank = adapter_down.shape[2]
    model_width = output_gradient.shape[1]
    experts = capacity.shape[0]
    wide = 2 * rows * rank
    names = jnp.arange(experts, dtype=f32)

    def gather(own):
        return lax.all_gather(own, "expert", axis_index_groups=cores)

    own_down = (down_scale * jnp.concatenate([down_direction, adapter_down]).transpose(0, 2, 1)).astype(f16)
    down_factors = gather(own_down).astype(f32) * (1 / down_scale)

    small = jnp.concatenate(
        [
            expert_of_route.T.astype(f32),
            gate_of_route.T.astype(f32),
            curvature[None, :],
            jnp.zeros((-(2 * top + 1) % 8, tokens), f32),
        ]
    )
    small_other = exchange(small, 1)
    counts = jnp.stack(
        [jnp.sum((part[:top, :, None] == names).astype(f32), axis=(0, 1)) for part in (small, small_other)]
    )
    counts = jnp.pad(counts, ((0, rank - 2), (0, lanes - experts)))
    own_up = jnp.concatenate(
        [
            up_scale * jnp.concatenate([adapter_up, up_direction]),
            jnp.broadcast_to(counts, (2, rank, lanes)),
        ],
        axis=2,
    ).astype(f16)
    unscale = jnp.concatenate([jnp.full((model_width,), 1 / up_scale, f32), jnp.ones((lanes,), f32)])
    up_factors = gather(own_up).astype(f32) * unscale

    hidden_of_route, _ = lax.optimization_barrier((hidden_of_route, own_up))
    small = jnp.concatenate([small, small_other], axis=1)
    hidden = hidden_of_route.transpose(1, 0, 2).reshape(top * tokens, hidden_width)
    hidden_other = exchange(hidden, 1)
    gradient_other = exchange(output_gradient, 1)
    chip = (me // 2)[None]
    column = jnp.repeat((me ^ (2 * jnp.array(masks, jnp.int32))).astype(f32), rank)[None, :]
    capacity_row = jnp.pad(capacity.astype(f32), (0, lanes - experts))[None, :]

    def call(kernel, outs, *operands, scratch=()):
        places = [
            pl.BlockSpec(memory_space=pltpu.SMEM if operand is chip else pltpu.VMEM) for operand in operands
        ]
        return pl.pallas_call(
            kernel,
            out_shape=[jax.ShapeDtypeStruct(shape, dtype) for shape, dtype in outs],
            in_specs=places,
            scratch_shapes=scratch,
            compiler_params=pltpu.CompilerParams(vmem_limit_bytes=kernel_vmem),
        )(*operands)

    (reduced,) = call(
        functools.partial(reduce_kernel, top, masks),
        [((2, 2 * tokens, wide), f32)],
        chip,
        small,
        column,
        hidden,
        hidden_other,
        down_factors,
    )
    weight, weighted, tangent, high, low = call(
        functools.partial(tangent_kernel, top, masks),
        [
            ((2 * tokens, wide), f32),
            ((2 * tokens, 2 * wide), f32),
            ((2 * tokens, model_width), f32),
            ((2 * wide, model_width), bf16),
            ((2 * wide, model_width), bf16),
        ],
        chip,
        small,
        column,
        capacity_row,
        reduced,
        up_factors,
    )
    arrived = exchange(tangent, 1)
    left = [pltpu.VMEM((2, top * tokens, 2 * wide), bf16)]
    chunks = [((rows // 2, rank, hidden_width + model_width), f32)] * 4
    *gradients, up, to = call(
        functools.partial(gradient_kernel, top),
        chunks + [((wide, model_width), f32), ((2 * tokens, wide), f32)],
        small,
        column,
        hidden,
        hidden_other,
        output_gradient,
        gradient_other,
        weight,
        weighted,
        high,
        low,
        scratch=left,
    )
    coded = encode(gradients[3]), encode(gradients[2])
    gradients_far, gradients_near = [exchange(part, 2) for part in coded]
    arrived, _ = lax.optimization_barrier((arrived, coded))
    curvatures = call(
        functools.partial(curvature_kernel, top),
        chunks,
        small,
        column,
        hidden,
        hidden_other,
        weight,
        weighted,
        high,
        low,
        up,
        to,
        tangent,
        arrived,
        scratch=left,
    )

    coded = encode(curvatures[3]), encode(curvatures[2])
    curvatures_far, curvatures_near = [exchange(part, 2) for part in coded]

    def along_z(parts):
        return [exchange(parts[z - rows // 2], 4 * z) for z in range(rows // 2, rows)]

    gradients_far, _ = lax.optimization_barrier((gradients_far, coded))
    gradients_far = along_z(encode(gradients[1] + decode(gradients_far)))
    curvatures_far = along_z(encode(curvatures[1] + decode(curvatures_far)))
    near = jnp.stack([gradients[0] + decode(gradients_near), curvatures[0] + decode(curvatures_near)])
    total = near[:, 0]
    for z in range(1, rows // 2):
        total = total + decode(exchange(encode(near[:, z]), 4 * z))
    gradient_sum = total[0] + sum(decode(part) for part in gradients_far)
    curvature_sum = total[1] + sum(decode(part) for part in curvatures_far)
    return (
        gradient_sum[:, :hidden_width].T[None],
        gradient_sum[None, :, hidden_width:],
        curvature_sum[:, :hidden_width].T[None],
        curvature_sum[None, :, hidden_width:],
    )


def carried_in(value, axis, join, neutral):
    count, mine = (lax.axis_size(axis), lax.axis_index(axis))
    pieces = lax.all_gather(value, axis)
    so_far = jnp.full_like(value, 0) + jnp.asarray(neutral, value.dtype)

    def lap(position, so_far):
        longer = join(so_far, pieces[position])
        return jnp.where(position < mine, longer, so_far)

    return lax.fori_loop(0, count - 1, lap, so_far)


def add_counts(earlier, later):
    return earlier + later


def routed_plan(
    hidden_of_route,
    expert_of_route,
    gate_of_route,
    capacity,
    output_gradient,
    curvature,
    adapter_down,
    adapter_up,
    down_direction,
    up_direction,
):
    finest_precision = lax.Precision.HIGHEST
    group_size = lax.axis_size("expert")
    tok_rows, top_count = expert_of_route.shape
    hidden_width = hidden_of_route.shape[2]
    resident_experts = adapter_down.shape[0]
    adapter_rank = adapter_down.shape[2]
    model_width = output_gradient.shape[1]
    experts = resident_experts * group_size
    slot_most = 2 * tok_rows * top_count // experts
    routes = expert_of_route.reshape(-1)
    onehot = (routes[:, None] == jnp.arange(experts, dtype=jnp.int32)[None, :]).astype(jnp.int32)
    earlier = jnp.cumsum(onehot, axis=0) - onehot
    local_rank = jnp.sum(earlier * onehot, axis=1)
    counts = jnp.sum(onehot, axis=0)
    prior_count = carried_in(counts, "expert", add_counts, jnp.zeros_like(counts))
    global_rank = local_rank + jnp.sum(onehot * prior_count[None, :], axis=1)
    route_limit = jnp.sum(onehot * capacity[None, :], axis=1)
    retained_mask = (global_rank < route_limit).astype(jnp.float32)
    weight_of_route = (
        adapter_scale * gate_of_route.reshape(-1).astype(jnp.float32) * retained_mask
    ).astype(jnp.bfloat16)
    slot_index = routes * slot_most + local_rank
    layout = (group_size, resident_experts, slot_most)
    send_hidden = (
        jnp.zeros((experts * slot_most, hidden_width), jnp.bfloat16)
        .at[slot_index]
        .set(hidden_of_route.reshape(-1, hidden_width))
        .reshape(layout + (hidden_width,))
    )
    send_weight = (
        jnp.zeros((experts * slot_most,), jnp.bfloat16)
        .at[slot_index]
        .set(weight_of_route)
        .reshape(layout)
    )
    down_stacked = jnp.concatenate([adapter_down, down_direction], axis=2)
    up_stacked = jnp.concatenate([adapter_up, up_direction], axis=1)

    def spread(token_rows):
        per_route = jnp.repeat(token_rows, top_count, axis=0)
        placed = (
            jnp.zeros((experts * slot_most, model_width), jnp.bfloat16)
            .at[slot_index]
            .set(per_route)
        )
        return placed.reshape(layout + (model_width,))

    send_residual = spread(output_gradient)
    pieces = (
        lax.all_to_all(send_hidden, "expert", split_axis=0, concat_axis=0, tiled=True),
        lax.all_to_all(send_weight, "expert", split_axis=0, concat_axis=0, tiled=True),
    )
    hidden_rows = pieces[0].astype(jnp.float32)
    weight_rows = pieces[1].astype(jnp.float32)[..., None]
    reduced_hidden = jnp.einsum(
        "cjif,jfk->cjik", hidden_rows, down_stacked, precision=finest_precision
    )
    exchanged_rows = jnp.concatenate(
        [reduced_hidden[..., adapter_rank:], reduced_hidden[..., :adapter_rank]], axis=3
    )
    tangent_out = weight_rows * jnp.einsum(
        "cjik,jkd->cjid", exchanged_rows, up_stacked, precision=finest_precision
    )
    returned = lax.all_to_all(
        tangent_out.astype(jnp.bfloat16), "expert", split_axis=0, concat_axis=0, tiled=True
    )
    results = (returned, reduced_hidden) + tuple(pieces)
    returned = results[0]
    reduced_hidden = results[1]
    hidden_rows = results[2]
    weight_rows = results[3]
    route_tangent = returned.reshape(experts * slot_most, model_width)[slot_index]
    out_tangent = jnp.sum(
        route_tangent.reshape(tok_rows, top_count, model_width).astype(jnp.float32), axis=1
    )
    resid_tangent = (curvature[:, None] * out_tangent).astype(jnp.bfloat16)
    send_tangent = spread(resid_tangent)
    residual_rows, tangent_rows = (
        lax.all_to_all(send_residual, "expert", split_axis=0, concat_axis=0, tiled=True),
        lax.all_to_all(send_tangent, "expert", split_axis=0, concat_axis=0, tiled=True),
    )
    residual_full = residual_rows.astype(jnp.float32)
    complete_tangent = tangent_rows.astype(jnp.float32)
    weight_column = weight_rows.astype(jnp.float32)[..., None]
    residual_reduced = jnp.einsum(
        "wyov,yqv->wyoq", residual_full, up_stacked, precision=finest_precision
    )
    reduced_tangent = jnp.einsum(
        "wyov,yqv->wyoq", complete_tangent, adapter_up, precision=finest_precision
    )
    left_terms = jnp.concatenate(
        [
            weight_column * residual_reduced[..., :adapter_rank],
            weight_column * (reduced_tangent + residual_reduced[..., adapter_rank:]),
        ],
        axis=3,
    )
    down_terms = jnp.einsum(
        "cjif,cjik->jfk", hidden_rows.astype(jnp.float32), left_terms, precision=finest_precision
    )
    raised_update = weight_column * reduced_hidden[..., :adapter_rank]
    raised_tangent_update = weight_column * reduced_hidden[..., adapter_rank:]
    up_terms = jnp.einsum(
        "cjik,cjid->jkd",
        jnp.concatenate([raised_update, raised_tangent_update], axis=3),
        residual_full,
        precision=finest_precision,
    )
    curvature_piece = up_terms[:, adapter_rank:] + jnp.einsum(
        "cjik,cjid->jkd", raised_update, complete_tangent, precision=finest_precision
    )
    return (
        down_terms[..., :adapter_rank],
        up_terms[:, :adapter_rank],
        down_terms[..., adapter_rank:],
        curvature_piece,
    )


def local(*arguments):
    adapter_down, adapter_up = arguments[6], arguments[7]
    factor_bytes = 2 * 4 * (adapter_down.size + adapter_up.size) * lax.axis_size("expert")
    plan = gathered_plan if 4 * factor_bytes <= kernel_vmem else routed_plan
    return plan(*arguments)


def solution(mesh):
    return jax.shard_map(
        local,
        mesh=mesh,
        in_specs=(
            P(("groups", "expert"), None, None),
            P(("groups", "expert"), None),
            P(("groups", "expert"), None),
            P("groups"),
            P(("groups", "expert"), None),
            P(("groups", "expert")),
            P("expert", None, None),
            P("expert", None, None),
            P(("groups", "expert"), None, None),
            P(("groups", "expert"), None, None),
        ),
        out_specs=(
            P(("groups", "expert"), None, None),
            P(("groups", "expert"), None, None),
            P(("groups", "expert"), None, None),
            P(("groups", "expert"), None, None),
        ),
        check_vma=False,
    )
```

```python
import functools

import jax
import jax.numpy as jnp
from jax import lax
from jax.experimental import pallas as pl
from jax.experimental.pallas import tpu as pltpu
from jax.sharding import PartitionSpec as P

adapter_scale = 2.0
f32 = jnp.float32
bf16 = jnp.bfloat16
f16 = jnp.float16
lanes = 128
kernel_vmem = 32 * 2**20


def halves(value):
    high = value.astype(bf16)
    return high, (value - high.astype(f32)).astype(bf16)


def dot(a, b, a_dim, b_dim):
    return lax.dot_general(a, b, (((a_dim,), (b_dim,)), ((), ())), preferred_element_type=f32)


def dot_pairs(a, b, a_dim, b_dim):
    return dot(a[0], b[0], a_dim, b_dim) + (dot(a[1], b[0], a_dim, b_dim) + dot(a[0], b[1], a_dim, b_dim))


def token_columns(small_ref, top):
    small = small_ref[...].T
    experts = [small[:, k : k + 1] for k in range(top)]
    gates = [small[:, top + k : top + k + 1] for k in range(top)]
    return experts, gates, small[:, 2 * top : 2 * top + 1]


def stacked(chip_ref, masks, factor_ref, width):
    rows = [factor_ref[chip_ref[0] ^ mask, kind, :, :width] for kind in range(2) for mask in masks]
    return halves(jnp.concatenate(rows, axis=0))


def reduce_kernel(top, masks, chip_ref, small_ref, column_ref, own_ref, other_ref, factor_ref, reduced_ref):
    experts, _, _ = token_columns(small_ref, top)
    high, low = stacked(chip_ref, masks, factor_ref, own_ref.shape[1])
    wide = high.shape[0] // 2
    tokens = own_ref.shape[0] // top
    for block, hidden_ref in enumerate((own_ref, other_ref)):
        rows = slice(block * tokens, (block + 1) * tokens)
        full = dot(hidden_ref[...], high, 1, 1) + dot(hidden_ref[...], low, 1, 1)
        total = jnp.zeros((tokens, 2 * wide), f32)
        for k in range(top):
            named = experts[k][rows] == column_ref[...]
            total = jnp.where(jnp.concatenate([named, named], axis=1), full[k * tokens : (k + 1) * tokens], total)
        reduced_ref[0, rows] = total[:, :wide]
        reduced_ref[1, rows] = total[:, wide:]


def rank_limits(rank, column_ref, capacity_ref, factor_ref):
    wide = column_ref.shape[1]
    member = [column_ref[:, start : start + 1] for start in range(0, wide, rank)]
    me = member[0]
    core = me - 2.0 * jnp.floor(me * 0.5)
    across = 1.0 - 2.0 * core
    left = []
    for block in (me, me + across):
        total = capacity_ref[...]
        for chip in range(factor_ref.shape[0]):
            own = factor_ref[chip, 0, 0:1, factor_ref.shape[3] - lanes :]
            other = factor_ref[chip, 0, 1:2, factor_ref.shape[3] - lanes :]
            device = 2.0 * chip + core
            total = total - jnp.where(device < block, own, 0.0)
            total = total - jnp.where(device + across < block, other, 0.0)
        left.append(total)
    lane = lax.broadcasted_iota(jnp.int32, (1, lanes), 1).astype(f32)
    slot_of = lax.broadcasted_iota(jnp.int32, (1, wide), 1) // rank
    limits = []
    for total in left:
        limit = jnp.zeros((1, wide), f32)
        for slot, expert in enumerate(member):
            value = jnp.sum(jnp.where(lane == expert, total, 0.0), axis=1, keepdims=True)
            limit = jnp.where(slot_of == slot, value, limit)
        limits.append(limit)
    return limits


def tangent_kernel(top, masks, chip_ref, small_ref, column_ref, capacity_ref, reduced_ref, factor_ref, *outs):
    weight_ref, weighted_ref, tangent_ref, high_ref, low_ref = outs
    experts, gates, _ = token_columns(small_ref, top)
    tokens, wide = weight_ref.shape
    block = tokens // 2
    limits = rank_limits(factor_ref.shape[2], column_ref, capacity_ref, factor_ref)
    gate = jnp.zeros((tokens, wide), f32)
    member = jnp.zeros((tokens, wide), f32)
    for k in range(top):
        named = experts[k] == column_ref[...]
        gate = jnp.where(named, gates[k], gate)
        member = jnp.where(named, 1.0, member)
    below = (
        lax.broadcasted_iota(jnp.int32, (block, block), 0)
        > lax.broadcasted_iota(jnp.int32, (block, block), 1)
    )
    below = jnp.where(below, 1.0, 0.0).astype(bf16)
    weights = []
    for part in range(2):
        rows = slice(part * block, (part + 1) * block)
        local_rank = dot(below, member[rows].astype(bf16), 1, 0)
        weights.append(jnp.where(local_rank < limits[part], adapter_scale * gate[rows], 0.0))
    weight = jnp.concatenate(weights, axis=0)
    weight_ref[...] = weight
    weighted = jnp.concatenate([weight * reduced_ref[0], weight * reduced_ref[1]], axis=1)
    weighted_ref[...] = weighted
    factor = stacked(chip_ref, masks, factor_ref, high_ref.shape[1])
    high_ref[...], low_ref[...] = factor
    tangent_ref[...] = dot_pairs(halves(weighted), factor, 1, 0)


def put_left(left_ref, experts, column_ref, terms, top):
    both = jnp.concatenate(halves(terms), axis=1)
    tokens = terms.shape[0] // 2
    for block in range(2):
        rows = slice(block * tokens, (block + 1) * tokens)
        for k in range(top):
            named = experts[k][rows] == column_ref[...]
            named = jnp.concatenate([named, named], axis=1)
            left_ref[block, k * tokens : (k + 1) * tokens] = jnp.where(named, both[rows], jnp.zeros_like(both[rows]))


def add_halves(both, axis):
    middle = both.shape[axis] // 2
    if axis == 0:
        return both[:middle] + both[middle:]
    return both[:, :middle] + both[:, middle:]


def put_chunks(out_refs, start, value):
    for place, out_ref in enumerate(out_refs):
        count, rank, _ = out_ref.shape
        rows = value[place * count * rank : (place + 1) * count * rank]
        out_ref[:, :, start : start + value.shape[1]] = rows.reshape(count, rank, value.shape[1])


def gradient_kernel(
    top,
    small_ref,
    column_ref,
    own_ref,
    other_ref,
    own_gradient_ref,
    other_gradient_ref,
    weight_ref,
    weighted_ref,
    high_ref,
    low_ref,
    *rest,
):
    out_refs, (up_ref, to_ref, left_ref) = rest[:-3], rest[-3:]
    experts, _, _ = token_columns(small_ref, top)
    wide = weight_ref.shape[1]
    hidden_width = own_ref.shape[1]
    gradient = jnp.concatenate([own_gradient_ref[...], other_gradient_ref[...]], axis=0)
    to_both = dot(gradient, high_ref[...], 1, 1) + dot(gradient, low_ref[...], 1, 1)
    to_ref[...] = to_both[:, wide:]
    put_left(left_ref, experts, column_ref, weight_ref[...] * to_both[:, :wide], top)
    down = dot(left_ref[0], own_ref[...], 0, 0) + dot(left_ref[1], other_ref[...], 0, 0)
    put_chunks(out_refs, 0, add_halves(down, 0))
    up = add_halves(dot(jnp.concatenate(halves(weighted_ref[...]), axis=1), gradient, 0, 0), 0)
    up_ref[...] = up[:wide]
    put_chunks(out_refs, hidden_width, up[wide:])


def curvature_kernel(
    top,
    small_ref,
    column_ref,
    own_ref,
    other_ref,
    weight_ref,
    weighted_ref,
    high_ref,
    low_ref,
    up_ref,
    to_ref,
    tangent_ref,
    arrived_ref,
    *rest,
):
    out_refs, left_ref = rest[:-1], rest[-1]
    experts, _, curvature = token_columns(small_ref, top)
    tokens, wide = weight_ref.shape
    block = tokens // 2
    hidden_width = own_ref.shape[1]
    arrived = jnp.concatenate([arrived_ref[block:], arrived_ref[:block]], axis=0)
    resid = halves(curvature * (tangent_ref[...] + arrived))
    adapter_up = high_ref[:wide], low_ref[:wide]
    put_left(
        left_ref, experts, column_ref, weight_ref[...] * (dot_pairs(resid, adapter_up, 1, 1) + to_ref[...]), top
    )
    down = dot(left_ref[0], own_ref[...], 0, 0) + dot(left_ref[1], other_ref[...], 0, 0)
    put_chunks(out_refs, 0, add_halves(down, 0))
    weighted_u = halves(weighted_ref[:, wide:])
    up = add_halves(dot(jnp.concatenate(weighted_u, axis=1), resid[0], 0, 0), 0) + dot(weighted_u[0], resid[1], 0, 0)
    put_chunks(out_refs, hidden_width, up_ref[...] + up)


def exchange(value, mask):
    size = lax.axis_size("chip") * 2
    return lax.ppermute(value, ("chip", "core"), [(device, device ^ mask) for device in range(size)])


def encode(value):
    largest = jnp.max(jnp.abs(value), axis=-1, keepdims=True)
    exponent = jnp.ceil(jnp.log2(jnp.maximum(largest, 1e-30)))
    scaled = value * jnp.exp2(15.0 - exponent)
    extra = jnp.broadcast_to(exponent, value.shape[:-1] + (lanes,))
    return jnp.concatenate([scaled, extra], axis=-1).astype(f16)


def decode(coded):
    width = coded.shape[-1] - lanes
    return coded[..., :width].astype(f32) * jnp.exp2(coded[..., width : width + 1].astype(f32) - 15.0)


def gathered_plan(
    hidden_of_route,
    expert_of_route,
    gate_of_route,
    capacity,
    output_gradient,
    curvature,
    adapter_down,
    adapter_up,
    down_direction,
    up_direction,
):
    size = lax.axis_size("chip") * 2
    rows = size // 4
    masks = [2 * z for z in range(rows)] + [2 * z + 1 for z in range(rows)]
    me = 2 * lax.axis_index("chip") + lax.axis_index("core")
    tokens, top = expert_of_route.shape
    hidden_width = hidden_of_route.shape[2]
    rank = adapter_down.shape[2]
    model_width = output_gradient.shape[1]
    experts = capacity.shape[0]
    wide = 2 * rows * rank
    names = jnp.arange(experts, dtype=f32)

    def gather(own):
        return lax.all_gather(own, "chip")

    down_factors = gather(jnp.concatenate([down_direction, adapter_down]).transpose(0, 2, 1))

    small = jnp.concatenate(
        [
            expert_of_route.T.astype(f32),
            gate_of_route.T.astype(f32),
            curvature[None, :],
            jnp.zeros((-(2 * top + 1) % 8, tokens), f32),
        ]
    )
    small_other = exchange(small, 1)
    counts = jnp.stack(
        [jnp.sum((part[:top, :, None] == names).astype(f32), axis=(0, 1)) for part in (small, small_other)]
    )
    counts = jnp.pad(counts, ((0, rank - 2), (0, lanes - experts)))
    own_up = jnp.concatenate(
        [jnp.concatenate([adapter_up, up_direction]), jnp.broadcast_to(counts, (2, rank, lanes))], axis=2
    )
    up_factors = gather(own_up)

    hidden_of_route, _ = lax.optimization_barrier((hidden_of_route, own_up))
    small = jnp.concatenate([small, small_other], axis=1)
    hidden = hidden_of_route.transpose(1, 0, 2).reshape(top * tokens, hidden_width)
    hidden_other = exchange(hidden, 1)
    gradient_other = exchange(output_gradient, 1)
    chip = (me // 2)[None]
    column = jnp.repeat((me ^ (2 * jnp.array(masks, jnp.int32))).astype(f32), rank)[None, :]
    capacity_row = jnp.pad(capacity.astype(f32), (0, lanes - experts))[None, :]

    def call(kernel, multiplies, outs, *operands, scratch=()):
        places = [
            pl.BlockSpec(memory_space=pltpu.SMEM if operand is chip else pltpu.VMEM) for operand in operands
        ]
        return pl.pallas_call(
            kernel,
            out_shape=[jax.ShapeDtypeStruct(shape, dtype) for shape, dtype in outs],
            in_specs=places,
            scratch_shapes=scratch,
            compiler_params=pltpu.CompilerParams(vmem_limit_bytes=kernel_vmem),
            cost_estimate=pl.CostEstimate(flops=2 * multiplies, bytes_accessed=2**23, transcendentals=0),
        )(*operands)

    both = 2 * tokens
    (reduced,) = call(
        functools.partial(reduce_kernel, top, masks),
        4 * top * both * hidden_width * wide,
        [((2, 2 * tokens, wide), f32)],
        chip,
        small,
        column,
        hidden,
        hidden_other,
        down_factors,
    )
    weight, weighted, tangent, high, low = call(
        functools.partial(tangent_kernel, top, masks),
        6 * both * model_width * wide,
        [
            ((2 * tokens, wide), f32),
            ((2 * tokens, 2 * wide), f32),
            ((2 * tokens, model_width), f32),
            ((2 * wide, model_width), bf16),
            ((2 * wide, model_width), bf16),
        ],
        chip,
        small,
        column,
        capacity_row,
        reduced,
        up_factors,
    )
    arrived = exchange(tangent, 1)
    left = [pltpu.VMEM((2, top * tokens, 2 * wide), bf16)]
    chunks = [((rows // 2, rank, hidden_width + model_width), f32)] * 4
    *gradients, up, to = call(
        functools.partial(gradient_kernel, top),
        2 * top * both * hidden_width * wide + 8 * both * model_width * wide,
        chunks + [((wide, model_width), f32), ((2 * tokens, wide), f32)],
        small,
        column,
        hidden,
        hidden_other,
        output_gradient,
        gradient_other,
        weight,
        weighted,
        high,
        low,
        scratch=left,
    )
    coded = encode(gradients[3]), encode(gradients[2])
    gradients_far, gradients_near = [exchange(part, 2) for part in coded]
    arrived, _ = lax.optimization_barrier((arrived, coded))
    curvatures = call(
        functools.partial(curvature_kernel, top),
        2 * top * both * hidden_width * wide + 6 * both * model_width * wide,
        chunks,
        small,
        column,
        hidden,
        hidden_other,
        weight,
        weighted,
        high,
        low,
        up,
        to,
        tangent,
        arrived,
        scratch=left,
    )

    coded = encode(curvatures[3]), encode(curvatures[2])
    curvatures_far, curvatures_near = [exchange(part, 2) for part in coded]

    def along_z(parts):
        return [exchange(parts[z - rows // 2], 4 * z) for z in range(rows // 2, rows)]

    gradients_far, _ = lax.optimization_barrier((gradients_far, coded))
    gradients_far = along_z(encode(gradients[1] + decode(gradients_far)))
    curvatures_far = along_z(encode(curvatures[1] + decode(curvatures_far)))
    near = jnp.stack([gradients[0] + decode(gradients_near), curvatures[0] + decode(curvatures_near)])
    total = near[:, 0]
    for z in range(1, rows // 2):
        total = total + decode(exchange(encode(near[:, z]), 4 * z))
    gradient_sum = total[0] + sum(decode(part) for part in gradients_far)
    curvature_sum = total[1] + sum(decode(part) for part in curvatures_far)
    return (
        gradient_sum[:, :hidden_width].T[None],
        gradient_sum[None, :, hidden_width:],
        curvature_sum[:, :hidden_width].T[None],
        curvature_sum[None, :, hidden_width:],
    )


def carried_in(value, axis, join, neutral):
    count, mine = (lax.axis_size(axis), lax.axis_index(axis))
    pieces = lax.all_gather(value, axis)
    so_far = jnp.full_like(value, 0) + jnp.asarray(neutral, value.dtype)

    def lap(position, so_far):
        longer = join(so_far, pieces[position])
        return jnp.where(position < mine, longer, so_far)

    return lax.fori_loop(0, count - 1, lap, so_far)


def add_counts(earlier, later):
    return earlier + later


def routed_plan(
    hidden_of_route,
    expert_of_route,
    gate_of_route,
    capacity,
    output_gradient,
    curvature,
    adapter_down,
    adapter_up,
    down_direction,
    up_direction,
):
    finest_precision = lax.Precision.HIGHEST
    group_size = lax.axis_size("expert")
    tok_rows, top_count = expert_of_route.shape
    hidden_width = hidden_of_route.shape[2]
    resident_experts = adapter_down.shape[0]
    adapter_rank = adapter_down.shape[2]
    model_width = output_gradient.shape[1]
    experts = resident_experts * group_size
    slot_most = 2 * tok_rows * top_count // experts
    routes = expert_of_route.reshape(-1)
    onehot = (routes[:, None] == jnp.arange(experts, dtype=jnp.int32)[None, :]).astype(jnp.int32)
    earlier = jnp.cumsum(onehot, axis=0) - onehot
    local_rank = jnp.sum(earlier * onehot, axis=1)
    counts = jnp.sum(onehot, axis=0)
    prior_count = carried_in(counts, "expert", add_counts, jnp.zeros_like(counts))
    global_rank = local_rank + jnp.sum(onehot * prior_count[None, :], axis=1)
    route_limit = jnp.sum(onehot * capacity[None, :], axis=1)
    retained_mask = (global_rank < route_limit).astype(jnp.float32)
    weight_of_route = (
        adapter_scale * gate_of_route.reshape(-1).astype(jnp.float32) * retained_mask
    ).astype(jnp.bfloat16)
    slot_index = routes * slot_most + local_rank
    layout = (group_size, resident_experts, slot_most)
    send_hidden = (
        jnp.zeros((experts * slot_most, hidden_width), jnp.bfloat16)
        .at[slot_index]
        .set(hidden_of_route.reshape(-1, hidden_width))
        .reshape(layout + (hidden_width,))
    )
    send_weight = (
        jnp.zeros((experts * slot_most,), jnp.bfloat16)
        .at[slot_index]
        .set(weight_of_route)
        .reshape(layout)
    )
    down_stacked = jnp.concatenate([adapter_down, down_direction], axis=2)
    up_stacked = jnp.concatenate([adapter_up, up_direction], axis=1)

    def spread(token_rows):
        per_route = jnp.repeat(token_rows, top_count, axis=0)
        placed = (
            jnp.zeros((experts * slot_most, model_width), jnp.bfloat16)
            .at[slot_index]
            .set(per_route)
        )
        return placed.reshape(layout + (model_width,))

    send_residual = spread(output_gradient)
    pieces = (
        lax.all_to_all(send_hidden, "expert", split_axis=0, concat_axis=0, tiled=True),
        lax.all_to_all(send_weight, "expert", split_axis=0, concat_axis=0, tiled=True),
    )
    hidden_rows = pieces[0].astype(jnp.float32)
    weight_rows = pieces[1].astype(jnp.float32)[..., None]
    reduced_hidden = jnp.einsum(
        "cjif,jfk->cjik", hidden_rows, down_stacked, precision=finest_precision
    )
    exchanged_rows = jnp.concatenate(
        [reduced_hidden[..., adapter_rank:], reduced_hidden[..., :adapter_rank]], axis=3
    )
    tangent_out = weight_rows * jnp.einsum(
        "cjik,jkd->cjid", exchanged_rows, up_stacked, precision=finest_precision
    )
    returned = lax.all_to_all(
        tangent_out.astype(jnp.bfloat16), "expert", split_axis=0, concat_axis=0, tiled=True
    )
    results = (returned, reduced_hidden) + tuple(pieces)
    returned = results[0]
    reduced_hidden = results[1]
    hidden_rows = results[2]
    weight_rows = results[3]
    route_tangent = returned.reshape(experts * slot_most, model_width)[slot_index]
    out_tangent = jnp.sum(
        route_tangent.reshape(tok_rows, top_count, model_width).astype(jnp.float32), axis=1
    )
    resid_tangent = (curvature[:, None] * out_tangent).astype(jnp.bfloat16)
    send_tangent = spread(resid_tangent)
    residual_rows, tangent_rows = (
        lax.all_to_all(send_residual, "expert", split_axis=0, concat_axis=0, tiled=True),
        lax.all_to_all(send_tangent, "expert", split_axis=0, concat_axis=0, tiled=True),
    )
    residual_full = residual_rows.astype(jnp.float32)
    complete_tangent = tangent_rows.astype(jnp.float32)
    weight_column = weight_rows.astype(jnp.float32)[..., None]
    residual_reduced = jnp.einsum(
        "wyov,yqv->wyoq", residual_full, up_stacked, precision=finest_precision
    )
    reduced_tangent = jnp.einsum(
        "wyov,yqv->wyoq", complete_tangent, adapter_up, precision=finest_precision
    )
    left_terms = jnp.concatenate(
        [
            weight_column * residual_reduced[..., :adapter_rank],
            weight_column * (reduced_tangent + residual_reduced[..., adapter_rank:]),
        ],
        axis=3,
    )
    down_terms = jnp.einsum(
        "cjif,cjik->jfk", hidden_rows.astype(jnp.float32), left_terms, precision=finest_precision
    )
    raised_update = weight_column * reduced_hidden[..., :adapter_rank]
    raised_tangent_update = weight_column * reduced_hidden[..., adapter_rank:]
    up_terms = jnp.einsum(
        "cjik,cjid->jkd",
        jnp.concatenate([raised_update, raised_tangent_update], axis=3),
        residual_full,
        precision=finest_precision,
    )
    curvature_piece = up_terms[:, adapter_rank:] + jnp.einsum(
        "cjik,cjid->jkd", raised_update, complete_tangent, precision=finest_precision
    )
    return (
        down_terms[..., :adapter_rank],
        up_terms[:, :adapter_rank],
        down_terms[..., adapter_rank:],
        curvature_piece,
    )


def solution(mesh):
    def whole(*arguments):
        factor_bytes = 2 * 4 * (arguments[6].size + arguments[7].size)
        devices, plan, part = mesh, routed_plan, "expert"
        if 4 * factor_bytes <= kernel_vmem:
            devices = jax.sharding.Mesh(
                mesh.devices.reshape(mesh.shape["groups"], mesh.shape["expert"] // 2, 2), ("groups", "chip", "core")
            )
            plan, part = gathered_plan, ("chip", "core")
        every = P(("groups",) + part if isinstance(part, tuple) else ("groups", part))
        return jax.shard_map(
            plan,
            mesh=devices,
            in_specs=(every, every, every, P("groups"), every, every, P(part), P(part), every, every),
            out_specs=(every,) * 4,
            check_vma=False,
        )(*arguments)

    return whole
```

```python
import functools

import jax
import jax.numpy as jnp
from jax import lax
from jax.experimental import pallas as pl
from jax.experimental.pallas import tpu as pltpu
from jax.sharding import PartitionSpec as P

adapter_scale = 2.0
f32 = jnp.float32
bf16 = jnp.bfloat16
i16 = jnp.int16
lanes = 128
counts_lane = 64
kernel_vmem = 32 * 2**20


def halves(value):
    high = value.astype(bf16)
    return high, (value - high.astype(f32)).astype(bf16)


def dot(a, b, a_dim, b_dim):
    return lax.dot_general(a, b, (((a_dim,), (b_dim,)), ((), ())), preferred_element_type=f32)


def dot_pairs(a, b, a_dim, b_dim):
    return dot(a[0], b[0], a_dim, b_dim) + (dot(a[1], b[0], a_dim, b_dim) + dot(a[0], b[1], a_dim, b_dim))


def encode(down, up, counts=0.0):
    def scaled(value):
        largest = jnp.max(jnp.abs(value), axis=-1, keepdims=True)
        exponent = jnp.ceil(jnp.log2(jnp.maximum(largest, 1e-30)))
        coded = jnp.round(value * jnp.exp2(15.0 - exponent))
        return jnp.clip(coded, -32767.0, 32767.0), exponent

    down, down_exponent = scaled(down)
    up, up_exponent = scaled(up)
    lane = lax.broadcasted_iota(jnp.int32, down.shape[:-1] + (lanes,), down.ndim - 1)
    tail = jnp.where(lane < counts_lane // 2, down_exponent, up_exponent)
    tail = jnp.where(lane < counts_lane, tail, counts)
    return jnp.concatenate([down, up, tail], axis=-1).astype(jnp.int32).astype(i16)


def decode(coded, hidden_width):
    width = coded.shape[-1] - lanes
    value = coded.astype(jnp.int32).astype(f32)
    down_scale = jnp.exp2(value[..., width : width + 1] - 15.0)
    up_scale = jnp.exp2(value[..., width + counts_lane // 2 : width + counts_lane // 2 + 1] - 15.0)
    return value[..., :hidden_width] * down_scale, value[..., hidden_width:width] * up_scale


def prepare_kernel(expert_ref, gate_ref, curvature_ref, *rest):
    (down_direction_ref, adapter_down_ref, adapter_up_ref, up_direction_ref, piece_ref, small_ref) = rest
    top = expert_ref.shape[0]
    small_ref[...] = jnp.zeros_like(small_ref)
    small_ref[:top] = expert_ref[...].astype(f32)
    small_ref[top : 2 * top] = gate_ref[...].astype(f32)
    small_ref[2 * top : 2 * top + 1] = curvature_ref[...]
    lane = lax.broadcasted_iota(jnp.int32, (1, lanes), 1)
    counts = jnp.zeros((1, lanes), f32)
    for expert in range(lanes - counts_lane):
        named = jnp.where(expert_ref[...] == expert, 1.0, 0.0)
        total = jnp.sum(jnp.sum(named, axis=0, keepdims=True), axis=1, keepdims=True)
        counts = jnp.where(lane == counts_lane + expert, total, counts)
    piece_ref[0] = encode(down_direction_ref[...], adapter_up_ref[...], counts)
    piece_ref[1] = encode(adapter_down_ref[...], up_direction_ref[...], counts)


def token_columns(own_ref, other_ref, top):
    small = jnp.concatenate([own_ref[...], other_ref[...]], axis=1).T
    experts = [small[:, k : k + 1] for k in range(top)]
    gates = [small[:, top + k : top + k + 1] for k in range(top)]
    return experts, gates, small[:, 2 * top : 2 * top + 1]


def members(place_ref, wide, masks):
    slot_of = lax.broadcasted_iota(jnp.int32, (1, wide), 1) // (wide // len(masks))
    found = jnp.zeros((1, wide), jnp.int32)
    for slot, mask in enumerate(masks):
        found = jnp.where(slot_of == slot, place_ref[0] ^ mask, found)
    return found.astype(f32)


def prior_kernel(masks, place_ref, *rest):
    piece_refs, prior_ref = rest[:-1], rest[-1]
    me = place_ref[0]
    slots = len(masks)
    prior_ref[...] = jnp.zeros_like(prior_ref)
    for block, number in enumerate((me, me ^ 1)):
        total = jnp.zeros((1, lanes), f32)
        for offset in range(slots):
            device = place_ref[1 + slots + offset]
            tail = piece_refs[offset][0, :, piece_refs[offset].shape[2] - lanes :]
            counts = tail.astype(jnp.int32).astype(f32)[0:1]
            total = total + jnp.where(device < number, counts, 0.0)
        prior_ref[block : block + 1] = total


def piece_part(refs, offset, kind):
    last = len(refs) - 2
    half = last // 2 + 1
    if offset == half:
        return refs[last + kind][0]
    return refs[offset if offset < half else offset - 1][kind]


def reduce_kernel(top, masks, place_ref, small_ref, small_other_ref, own_ref, other_ref, *rest):
    slots = len(masks)
    piece_refs, (_, reduced_ref, high_ref, low_ref) = rest[: slots + 1], rest[slots + 1 :]
    hidden_width = own_ref.shape[1]
    for offset in range(slots):
        slot = place_ref[1 + offset]
        for kind in range(2):
            down, _ = decode(piece_part(piece_refs, offset, kind), hidden_width)
            high_ref[kind, slot], low_ref[kind, slot] = halves(down)
    experts, _, _ = token_columns(small_ref, small_other_ref, top)
    wide = reduced_ref.shape[2]
    column = members(place_ref, wide, masks)
    high = high_ref[...].reshape(2 * wide, hidden_width)
    low = low_ref[...].reshape(2 * wide, hidden_width)
    tokens = own_ref.shape[0] // top
    for block, hidden_ref in enumerate((own_ref, other_ref)):
        rows = slice(block * tokens, (block + 1) * tokens)
        full = dot(hidden_ref[...], high, 1, 1) + dot(hidden_ref[...], low, 1, 1)
        total = jnp.zeros((tokens, 2 * wide), f32)
        for k in range(top):
            named = experts[k][rows] == column
            total = jnp.where(jnp.concatenate([named, named], axis=1), full[k * tokens : (k + 1) * tokens], total)
        reduced_ref[0, rows] = total[:, :wide]
        reduced_ref[1, rows] = total[:, wide:]


def rank_limits(place_ref, masks, wide, capacity_ref, prior_ref, arrived_ref):
    lane = lax.broadcasted_iota(jnp.int32, (1, lanes), 1)
    slot_of = lax.broadcasted_iota(jnp.int32, (1, wide), 1) // (wide // len(masks))
    limits = []
    for block in range(2):
        total = capacity_ref[...] - prior_ref[block : block + 1] - arrived_ref[1 - block : 2 - block]
        limit = jnp.zeros((1, wide), f32)
        for slot, mask in enumerate(masks):
            picked = jnp.where(lane == counts_lane + (place_ref[0] ^ mask), total, 0.0)
            limit = jnp.where(slot_of == slot, jnp.sum(picked, axis=1, keepdims=True), limit)
        limits.append(limit)
    return limits


def tangent_kernel(
    top, masks, place_ref, small_ref, small_other_ref, capacity_ref, prior_ref, arrived_ref, reduced_ref, *rest
):
    slots = len(masks)
    piece_refs = rest[: slots + 1]
    weight_ref, weighted_ref, tangent_ref, coded_ref, high_ref, low_ref = rest[slots + 1 :]
    experts, gates, _ = token_columns(small_ref, small_other_ref, top)
    tokens, wide = weight_ref.shape
    model_width = tangent_ref.shape[1]
    hidden_width = piece_refs[0].shape[2] - model_width - lanes
    block = tokens // 2
    column = members(place_ref, wide, masks)
    limits = rank_limits(place_ref, masks, wide, capacity_ref, prior_ref, arrived_ref)
    gate = jnp.zeros((tokens, wide), f32)
    member = jnp.zeros((tokens, wide), f32)
    for k in range(top):
        named = experts[k] == column
        gate = jnp.where(named, gates[k], gate)
        member = jnp.where(named, 1.0, member)
    below = (
        lax.broadcasted_iota(jnp.int32, (block, block), 0)
        > lax.broadcasted_iota(jnp.int32, (block, block), 1)
    )
    below = jnp.where(below, 1.0, 0.0).astype(bf16)
    weights = []
    for part in range(2):
        rows = slice(part * block, (part + 1) * block)
        local_rank = dot(below, member[rows].astype(bf16), 1, 0)
        weights.append(jnp.where(local_rank < limits[part], adapter_scale * gate[rows], 0.0))
    weight = jnp.concatenate(weights, axis=0)
    weight_ref[...] = weight
    weighted = jnp.concatenate([weight * reduced_ref[0], weight * reduced_ref[1]], axis=1)
    weighted_ref[...] = weighted
    for offset in range(slots):
        slot = place_ref[1 + offset]
        for kind in range(2):
            _, up = decode(piece_part(piece_refs, offset, kind), hidden_width)
            high_ref[kind, slot], low_ref[kind, slot] = halves(up)
    factor = high_ref[...].reshape(2 * wide, model_width), low_ref[...].reshape(2 * wide, model_width)
    tangent = dot_pairs(halves(weighted), factor, 1, 0)
    tangent_ref[...] = tangent
    coded_ref[...] = tangent.astype(bf16)


def put_left(left_ref, experts, column, terms, top):
    both = jnp.concatenate(halves(terms), axis=1)
    tokens = terms.shape[0] // 2
    for block in range(2):
        rows = slice(block * tokens, (block + 1) * tokens)
        for k in range(top):
            named = experts[k][rows] == column
            named = jnp.concatenate([named, named], axis=1)
            left_ref[block, k * tokens : (k + 1) * tokens] = jnp.where(named, both[rows], jnp.zeros_like(both[rows]))


def add_halves(both):
    middle = both.shape[0] // 2
    return both[:middle] + both[middle:]


def put_chunks(own_ref, near_ref, far_ref, down, up):
    count, rank, _ = own_ref.shape
    hidden_width = down.shape[1]
    own_ref[:, :, :hidden_width] = down[: count * rank].reshape(count, rank, -1)
    own_ref[:, :, hidden_width:] = up[: count * rank].reshape(count, rank, -1)
    start = count * rank
    for out_ref in (near_ref, far_ref):
        stop = start + out_ref.shape[0] * rank
        out_ref[...] = encode(down[start:stop], up[start:stop]).reshape(out_ref.shape)
        start = stop


def gradient_kernel(
    top,
    masks,
    place_ref,
    small_ref,
    small_other_ref,
    own_ref,
    other_ref,
    own_gradient_ref,
    other_gradient_ref,
    weight_ref,
    weighted_ref,
    high_ref,
    low_ref,
    chunk_ref,
    near_ref,
    far_ref,
    up_ref,
    to_ref,
    left_ref,
):
    experts, _, _ = token_columns(small_ref, small_other_ref, top)
    wide = weight_ref.shape[1]
    model_width = up_ref.shape[1]
    column = members(place_ref, wide, masks)
    gradient = jnp.concatenate([own_gradient_ref[...], other_gradient_ref[...]], axis=0)
    high = high_ref[...].reshape(2 * wide, model_width)
    low = low_ref[...].reshape(2 * wide, model_width)
    to_both = dot(gradient, high, 1, 1) + dot(gradient, low, 1, 1)
    to_ref[...] = to_both[:, wide:]
    put_left(left_ref, experts, column, weight_ref[...] * to_both[:, :wide], top)
    down = dot(left_ref[0], own_ref[...], 0, 0) + dot(left_ref[1], other_ref[...], 0, 0)
    up = add_halves(dot(jnp.concatenate(halves(weighted_ref[...]), axis=1), gradient, 0, 0))
    up_ref[...] = up[:wide]
    put_chunks(chunk_ref, near_ref, far_ref, add_halves(down), up[wide:])


def curvature_kernel(
    top,
    masks,
    place_ref,
    small_ref,
    small_other_ref,
    own_ref,
    other_ref,
    weight_ref,
    weighted_ref,
    high_ref,
    low_ref,
    up_ref,
    to_ref,
    tangent_ref,
    arrived_ref,
    chunk_ref,
    near_ref,
    far_ref,
    left_ref,
):
    experts, _, curvature = token_columns(small_ref, small_other_ref, top)
    tokens, wide = weight_ref.shape
    block = tokens // 2
    model_width = up_ref.shape[1]
    column = members(place_ref, wide, masks)
    arrived = jnp.concatenate([arrived_ref[block:], arrived_ref[:block]], axis=0).astype(f32)
    resid = halves(curvature * (tangent_ref[...] + arrived))
    adapter_up = high_ref[0].reshape(wide, model_width), low_ref[0].reshape(wide, model_width)
    put_left(
        left_ref, experts, column, weight_ref[...] * (dot_pairs(resid, adapter_up, 1, 1) + to_ref[...]), top
    )
    down = dot(left_ref[0], own_ref[...], 0, 0) + dot(left_ref[1], other_ref[...], 0, 0)
    weighted_u = halves(weighted_ref[:, wide:])
    up = add_halves(dot(jnp.concatenate(weighted_u, axis=1), resid[0], 0, 0)) + dot(weighted_u[0], resid[1], 0, 0)
    put_chunks(chunk_ref, near_ref, far_ref, add_halves(down), up_ref[...] + up)


def far_kernel(hidden_width, arrived_ref, chunk_ref, _, *out_refs):
    count = len(out_refs)
    for place, out_ref in enumerate(out_refs):
        down, up = decode(arrived_ref[place], hidden_width)
        own = chunk_ref[chunk_ref.shape[0] - count + place]
        out_ref[...] = encode(own[:, :hidden_width] + down, own[:, hidden_width:] + up)


def near_kernel(hidden_width, gradient_ref, curvature_ref, gradient_chunk_ref, curvature_chunk_ref, out_ref, total_ref):
    pairs = ((gradient_ref, gradient_chunk_ref), (curvature_ref, curvature_chunk_ref))
    for kind, (arrived_ref, chunk_ref) in enumerate(pairs):
        for place in range(arrived_ref.shape[0]):
            down, up = decode(arrived_ref[place], hidden_width)
            own = chunk_ref[place]
            down, up = own[:, :hidden_width] + down, own[:, hidden_width:] + up
            if place == 0:
                total_ref[kind] = jnp.concatenate([down, up], axis=1)
            else:
                out_ref[place - 1, kind] = encode(down, up)


def total_kernel(hidden_width, far, total_ref, *rest):
    near_refs, far_refs, out_refs = rest[: -2 * far - 4], rest[-2 * far - 4 : -4], rest[-4:]
    for kind in range(2):
        down = total_ref[kind, :, :hidden_width]
        up = total_ref[kind, :, hidden_width:]
        arrived = [ref[kind] for ref in near_refs] + [ref[...] for ref in far_refs[kind * far : (kind + 1) * far]]
        for coded in arrived:
            more = decode(coded, hidden_width)
            down, up = down + more[0], up + more[1]
        out_refs[2 * kind][...] = down
        out_refs[2 * kind + 1][...] = up


class Ring:
    def __init__(self, size):
        self.length = size // 2
        rows = self.length // 2
        self.order = [4 * z for z in range(rows)] + [4 * z + 2 for z in reversed(range(rows))]

    def shift(self, value, step):
        pairs = [
            (chip + core, self.order[(place + step) % self.length] + core)
            for place, chip in enumerate(self.order)
            for core in range(2)
        ]
        return lax.ppermute(value, "expert", pairs)

    def members(self, me):
        rows = self.length // 2
        place = jnp.where(me // 2 % 2 == 0, me // 4, self.length - 1 - me // 4)
        there = (place + jnp.arange(self.length, dtype=jnp.int32)) % self.length
        return jnp.where(there < rows, 4 * there, 4 * (self.length - 1 - there) + 2) + me % 2

    def gather(self, own):
        half = self.length // 2
        found = {0: own}
        ahead, behind = own, own
        for step in range(1, half):
            behind = self.shift(behind, 1)
            ahead = self.shift(ahead, -1)
            found[self.length - step], found[step] = behind, ahead
        last = [self.shift(behind[:1], 1), self.shift(ahead[1:], -1)]
        return [found[offset] for offset in sorted(found)] + last


def exchange(value, mask):
    size = lax.axis_size("expert")
    return lax.ppermute(value, "expert", [(device, device ^ mask) for device in range(size)])


def gathered_plan(
    hidden_of_route,
    expert_of_route,
    gate_of_route,
    capacity,
    output_gradient,
    curvature,
    adapter_down,
    adapter_up,
    down_direction,
    up_direction,
):
    ring = Ring(lax.axis_size("expert"))
    slots = ring.length
    rows = slots // 2
    far = rows // 2
    masks = [4 * z for z in range(rows)] + [4 * z + 2 for z in range(rows)]
    me = lax.axis_index("expert")
    tokens, top = expert_of_route.shape
    both = 2 * tokens
    hidden_width = hidden_of_route.shape[2]
    rank = adapter_down.shape[2]
    model_width = output_gradient.shape[1]
    experts = capacity.shape[0]
    wide = slots * rank
    coded_width = hidden_width + model_width + lanes

    ring_members = ring.members(me)
    differs = ring_members ^ me
    slot_of_offset = differs // 4 + rows * (differs // 2 % 2)
    place = jnp.concatenate([me[None], slot_of_offset, ring_members]).astype(jnp.int32)

    def call(kernel, multiplies, outs, *operands, scratch=(), after=()):
        places = [
            pl.BlockSpec(memory_space=pltpu.SMEM if operand is place else pltpu.VMEM) for operand in operands
        ] + [pl.BlockSpec(memory_space=pl.ANY) for _ in after]
        return pl.pallas_call(
            kernel,
            out_shape=[jax.ShapeDtypeStruct(shape, dtype) for shape, dtype in outs],
            in_specs=places,
            scratch_shapes=scratch,
            compiler_params=pltpu.CompilerParams(vmem_limit_bytes=kernel_vmem),
            cost_estimate=pl.CostEstimate(flops=2 * multiplies, bytes_accessed=2**20, transcendentals=0),
        )(*operands, *after)

    down_multiplies = 2 * top * both * hidden_width * wide
    up_multiplies = both * model_width * wide

    piece, small = call(
        prepare_kernel,
        10**8,
        [((2, rank, coded_width), i16), (((2 * top + 8) // 8 * 8, tokens), f32)],
        expert_of_route.T,
        gate_of_route.T,
        curvature[None],
        down_direction[0].T,
        adapter_down[0].T,
        adapter_up[0],
        up_direction[0],
    )
    pieces = ring.gather(piece)
    small_other = exchange(small, 1)
    hidden = hidden_of_route.transpose(1, 0, 2).reshape(top * tokens, hidden_width)
    hidden_other = exchange(hidden, 1)
    gradient_other = exchange(output_gradient, 1)
    capacity_row = jnp.pad(capacity.astype(f32), (counts_lane, lanes - counts_lane - experts))[None, :]

    by_offset = pieces[:rows] + [pieces[-2]] + pieces[rows:-2]
    (prior,) = call(functools.partial(prior_kernel, masks), 10**8, [((8, lanes), f32)], place, *by_offset)
    prior_arrived = exchange(prior, 1)
    factor_halves = [pltpu.VMEM((2, slots, rank, hidden_width), bf16)] * 2
    (reduced,) = call(
        functools.partial(reduce_kernel, top, masks),
        2 * down_multiplies,
        [((2, both, wide), f32)],
        place,
        small,
        small_other,
        hidden,
        hidden_other,
        *pieces,
        scratch=factor_halves,
        after=[prior],
    )
    weight, weighted, tangent, coded, high, low = call(
        functools.partial(tangent_kernel, top, masks),
        6 * up_multiplies,
        [
            ((both, wide), f32),
            ((both, 2 * wide), f32),
            ((both, model_width), f32),
            ((both, model_width), bf16),
            ((2, slots, rank, model_width), bf16),
            ((2, slots, rank, model_width), bf16),
        ],
        place,
        small,
        small_other,
        capacity_row,
        prior,
        prior_arrived,
        reduced,
        *pieces,
    )
    arrived = exchange(coded, 1)
    left = [pltpu.VMEM((2, top * tokens, 2 * wide), bf16)]
    chunks = [
        ((rows, rank, hidden_width + model_width), f32),
        ((rows - far, rank, coded_width), i16),
        ((far, rank, coded_width), i16),
    ]
    gradient_own, gradient_near, gradient_far, up, to = call(
        functools.partial(gradient_kernel, top, masks),
        down_multiplies + 8 * up_multiplies,
        chunks + [((wide, model_width), f32), ((both, wide), f32)],
        place,
        small,
        small_other,
        hidden,
        hidden_other,
        output_gradient,
        gradient_other,
        weight,
        weighted,
        high,
        low,
        scratch=left,
    )
    gradient_far = exchange(gradient_far, 2)
    gradient_near = exchange(gradient_near, 2)
    curvature_own, curvature_near, curvature_far = call(
        functools.partial(curvature_kernel, top, masks),
        down_multiplies + 6 * up_multiplies,
        chunks,
        place,
        small,
        small_other,
        hidden,
        hidden_other,
        weight,
        weighted,
        high,
        low,
        up,
        to,
        tangent,
        arrived,
        scratch=left,
    )

    def along_z(arrived, own, after):
        sums = call(
            functools.partial(far_kernel, hidden_width),
            10**8,
            [((rank, coded_width), i16)] * far,
            arrived,
            own,
            after=[after],
        )
        return [exchange(part, 4 * z) for z, part in zip(range(rows - far, rows), sums)]

    gradient_parts = along_z(gradient_far, gradient_own, curvature_far)
    curvature_far = exchange(curvature_far, 2)
    curvature_near = exchange(curvature_near, 2)
    curvature_parts = along_z(curvature_far, curvature_own, gradient_near)
    near, total = call(
        functools.partial(near_kernel, hidden_width),
        10**8,
        [((rows - far - 1, 2, rank, coded_width), i16), ((2, rank, hidden_width + model_width), f32)],
        gradient_near,
        curvature_near,
        gradient_own,
        curvature_own,
    )
    near_parts = [exchange(near[z - 1], 4 * z) for z in range(1, rows - far)]
    down_gradient, up_gradient, curvature_down, curvature_up = call(
        functools.partial(total_kernel, hidden_width, far),
        10**8,
        [((rank, hidden_width), f32), ((rank, model_width), f32)] * 2,
        total,
        *near_parts,
        *gradient_parts,
        *curvature_parts,
    )
    return down_gradient.T[None], up_gradient[None], curvature_down.T[None], curvature_up[None]


def carried_in(value, axis, join, neutral):
    count, mine = (lax.axis_size(axis), lax.axis_index(axis))
    pieces = lax.all_gather(value, axis)
    so_far = jnp.full_like(value, 0) + jnp.asarray(neutral, value.dtype)

    def lap(position, so_far):
        longer = join(so_far, pieces[position])
        return jnp.where(position < mine, longer, so_far)

    return lax.fori_loop(0, count - 1, lap, so_far)


def add_counts(earlier, later):
    return earlier + later


def routed_plan(
    hidden_of_route,
    expert_of_route,
    gate_of_route,
    capacity,
    output_gradient,
    curvature,
    adapter_down,
    adapter_up,
    down_direction,
    up_direction,
):
    finest_precision = lax.Precision.HIGHEST
    group_size = lax.axis_size("expert")
    tok_rows, top_count = expert_of_route.shape
    hidden_width = hidden_of_route.shape[2]
    resident_experts = adapter_down.shape[0]
    adapter_rank = adapter_down.shape[2]
    model_width = output_gradient.shape[1]
    experts = resident_experts * group_size
    slot_most = 2 * tok_rows * top_count // experts
    routes = expert_of_route.reshape(-1)
    onehot = (routes[:, None] == jnp.arange(experts, dtype=jnp.int32)[None, :]).astype(jnp.int32)
    earlier = jnp.cumsum(onehot, axis=0) - onehot
    local_rank = jnp.sum(earlier * onehot, axis=1)
    counts = jnp.sum(onehot, axis=0)
    prior_count = carried_in(counts, "expert", add_counts, jnp.zeros_like(counts))
    global_rank = local_rank + jnp.sum(onehot * prior_count[None, :], axis=1)
    route_limit = jnp.sum(onehot * capacity[None, :], axis=1)
    retained_mask = (global_rank < route_limit).astype(jnp.float32)
    weight_of_route = (
        adapter_scale * gate_of_route.reshape(-1).astype(jnp.float32) * retained_mask
    ).astype(jnp.bfloat16)
    slot_index = routes * slot_most + local_rank
    layout = (group_size, resident_experts, slot_most)
    send_hidden = (
        jnp.zeros((experts * slot_most, hidden_width), jnp.bfloat16)
        .at[slot_index]
        .set(hidden_of_route.reshape(-1, hidden_width))
        .reshape(layout + (hidden_width,))
    )
    send_weight = (
        jnp.zeros((experts * slot_most,), jnp.bfloat16)
        .at[slot_index]
        .set(weight_of_route)
        .reshape(layout)
    )
    down_stacked = jnp.concatenate([adapter_down, down_direction], axis=2)
    up_stacked = jnp.concatenate([adapter_up, up_direction], axis=1)

    def spread(token_rows):
        per_route = jnp.repeat(token_rows, top_count, axis=0)
        placed = (
            jnp.zeros((experts * slot_most, model_width), jnp.bfloat16)
            .at[slot_index]
            .set(per_route)
        )
        return placed.reshape(layout + (model_width,))

    send_residual = spread(output_gradient)
    pieces = (
        lax.all_to_all(send_hidden, "expert", split_axis=0, concat_axis=0, tiled=True),
        lax.all_to_all(send_weight, "expert", split_axis=0, concat_axis=0, tiled=True),
    )
    hidden_rows = pieces[0].astype(jnp.float32)
    weight_rows = pieces[1].astype(jnp.float32)[..., None]
    reduced_hidden = jnp.einsum(
        "cjif,jfk->cjik", hidden_rows, down_stacked, precision=finest_precision
    )
    exchanged_rows = jnp.concatenate(
        [reduced_hidden[..., adapter_rank:], reduced_hidden[..., :adapter_rank]], axis=3
    )
    tangent_out = weight_rows * jnp.einsum(
        "cjik,jkd->cjid", exchanged_rows, up_stacked, precision=finest_precision
    )
    returned = lax.all_to_all(
        tangent_out.astype(jnp.bfloat16), "expert", split_axis=0, concat_axis=0, tiled=True
    )
    results = (returned, reduced_hidden) + tuple(pieces)
    returned = results[0]
    reduced_hidden = results[1]
    hidden_rows = results[2]
    weight_rows = results[3]
    route_tangent = returned.reshape(experts * slot_most, model_width)[slot_index]
    out_tangent = jnp.sum(
        route_tangent.reshape(tok_rows, top_count, model_width).astype(jnp.float32), axis=1
    )
    resid_tangent = (curvature[:, None] * out_tangent).astype(jnp.bfloat16)
    send_tangent = spread(resid_tangent)
    residual_rows, tangent_rows = (
        lax.all_to_all(send_residual, "expert", split_axis=0, concat_axis=0, tiled=True),
        lax.all_to_all(send_tangent, "expert", split_axis=0, concat_axis=0, tiled=True),
    )
    residual_full = residual_rows.astype(jnp.float32)
    complete_tangent = tangent_rows.astype(jnp.float32)
    weight_column = weight_rows.astype(jnp.float32)[..., None]
    residual_reduced = jnp.einsum(
        "wyov,yqv->wyoq", residual_full, up_stacked, precision=finest_precision
    )
    reduced_tangent = jnp.einsum(
        "wyov,yqv->wyoq", complete_tangent, adapter_up, precision=finest_precision
    )
    left_terms = jnp.concatenate(
        [
            weight_column * residual_reduced[..., :adapter_rank],
            weight_column * (reduced_tangent + residual_reduced[..., adapter_rank:]),
        ],
        axis=3,
    )
    down_terms = jnp.einsum(
        "cjif,cjik->jfk", hidden_rows.astype(jnp.float32), left_terms, precision=finest_precision
    )
    raised_update = weight_column * reduced_hidden[..., :adapter_rank]
    raised_tangent_update = weight_column * reduced_hidden[..., adapter_rank:]
    up_terms = jnp.einsum(
        "cjik,cjid->jkd",
        jnp.concatenate([raised_update, raised_tangent_update], axis=3),
        residual_full,
        precision=finest_precision,
    )
    curvature_piece = up_terms[:, adapter_rank:] + jnp.einsum(
        "cjik,cjid->jkd", raised_update, complete_tangent, precision=finest_precision
    )
    return (
        down_terms[..., :adapter_rank],
        up_terms[:, :adapter_rank],
        down_terms[..., adapter_rank:],
        curvature_piece,
    )


def local(*arguments):
    factor_bytes = 2 * 4 * (arguments[6].size + arguments[7].size) * lax.axis_size("expert")
    plan = gathered_plan if 4 * factor_bytes <= kernel_vmem else routed_plan
    return plan(*arguments)


def solution(mesh):
    return jax.shard_map(
        local,
        mesh=mesh,
        in_specs=(
            P(("groups", "expert"), None, None),
            P(("groups", "expert"), None),
            P(("groups", "expert"), None),
            P("groups"),
            P(("groups", "expert"), None),
            P(("groups", "expert")),
            P("expert", None, None),
            P("expert", None, None),
            P(("groups", "expert"), None, None),
            P(("groups", "expert"), None, None),
        ),
        out_specs=(
            P(("groups", "expert"), None, None),
            P(("groups", "expert"), None, None),
            P(("groups", "expert"), None, None),
            P(("groups", "expert"), None, None),
        ),
        check_vma=False,
    )
```

```python
import functools

import jax
import jax.numpy as jnp
from jax import lax
from jax.experimental import pallas as pl
from jax.experimental.pallas import tpu as pltpu
from jax.sharding import PartitionSpec as P

adapter_scale = 2.0
f32 = jnp.float32
bf16 = jnp.bfloat16
i16 = jnp.int16
lanes = 128
counts_lane = 64
kernel_vmem = 32 * 2**20


def halves(value):
    high = value.astype(bf16)
    return high, (value - high.astype(f32)).astype(bf16)


def dot(a, b, a_dim, b_dim):
    return lax.dot_general(a, b, (((a_dim,), (b_dim,)), ((), ())), preferred_element_type=f32)


def dot_pairs(a, b, a_dim, b_dim):
    return dot(a[0], b[0], a_dim, b_dim) + (dot(a[1], b[0], a_dim, b_dim) + dot(a[0], b[1], a_dim, b_dim))


def encode(down, up, counts=0.0):
    def scaled(value):
        largest = jnp.max(jnp.abs(value), axis=-1, keepdims=True)
        exponent = jnp.ceil(jnp.log2(jnp.maximum(largest, 1e-30)))
        coded = jnp.round(value * jnp.exp2(15.0 - exponent))
        return jnp.clip(coded, -32767.0, 32767.0), exponent

    down, down_exponent = scaled(down)
    up, up_exponent = scaled(up)
    lane = lax.broadcasted_iota(jnp.int32, down.shape[:-1] + (lanes,), down.ndim - 1)
    tail = jnp.where(lane < counts_lane // 2, down_exponent, up_exponent)
    tail = jnp.where(lane < counts_lane, tail, counts)
    return jnp.concatenate([down, up, tail], axis=-1).astype(jnp.int32).astype(i16)


def decode(coded, hidden_width):
    width = coded.shape[-1] - lanes
    value = coded.astype(jnp.int32).astype(f32)
    down_scale = jnp.exp2(value[..., width : width + 1] - 15.0)
    up_scale = jnp.exp2(value[..., width + counts_lane // 2 : width + counts_lane // 2 + 1] - 15.0)
    return value[..., :hidden_width] * down_scale, value[..., hidden_width:width] * up_scale


def prepare_kernel(expert_ref, gate_ref, curvature_ref, *rest):
    (down_direction_ref, adapter_down_ref, adapter_up_ref, up_direction_ref, *piece_refs, small_ref) = rest
    top = expert_ref.shape[0]
    small_ref[...] = jnp.zeros_like(small_ref)
    small_ref[:top] = expert_ref[...].astype(f32)
    small_ref[top : 2 * top] = gate_ref[...].astype(f32)
    small_ref[2 * top : 2 * top + 1] = curvature_ref[...]
    lane = lax.broadcasted_iota(jnp.int32, (1, lanes), 1)
    counts = jnp.zeros((1, lanes), f32)
    for expert in range(lanes - counts_lane):
        named = jnp.where(expert_ref[...] == expert, 1.0, 0.0)
        total = jnp.sum(jnp.sum(named, axis=0, keepdims=True), axis=1, keepdims=True)
        counts = jnp.where(lane == counts_lane + expert, total, counts)
    piece_refs[0][...] = encode(down_direction_ref[...], adapter_up_ref[...], counts)
    piece_refs[1][...] = encode(adapter_down_ref[...], up_direction_ref[...], counts)


def token_columns(own_ref, other_ref, top):
    small = jnp.concatenate([own_ref[...], other_ref[...]], axis=1).T
    experts = [small[:, k : k + 1] for k in range(top)]
    gates = [small[:, top + k : top + k + 1] for k in range(top)]
    return experts, gates, small[:, 2 * top : 2 * top + 1]


def members(place_ref, wide, masks):
    slot_of = lax.broadcasted_iota(jnp.int32, (1, wide), 1) // (wide // len(masks))
    found = jnp.zeros((1, wide), jnp.int32)
    for slot, mask in enumerate(masks):
        found = jnp.where(slot_of == slot, place_ref[0] ^ mask, found)
    return found.astype(f32)


def prior_kernel(masks, place_ref, *rest):
    piece_refs, prior_ref = rest[:-1], rest[-1]
    me = place_ref[0]
    slots = len(masks)
    prior_ref[...] = jnp.zeros_like(prior_ref)
    for block, number in enumerate((me, me ^ 1)):
        total = jnp.zeros((1, lanes), f32)
        for offset in range(slots):
            device = place_ref[1 + slots + offset]
            tail = piece_refs[offset][:, piece_refs[offset].shape[1] - lanes :]
            counts = tail.astype(jnp.int32).astype(f32)[0:1]
            total = total + jnp.where(device < number, counts, 0.0)
        prior_ref[block : block + 1] = total


def rows_kernel(
    top,
    masks,
    place_ref,
    small_ref,
    small_other_ref,
    hidden_other_ref,
    gradient_ref,
    gradient_other_ref,
    piece_ref,
    same_ref,
    mask_ref,
    hidden_ref,
    both_ref,
    onward_ref,
):
    onward_ref[...] = piece_ref[...]
    rows, tokens = same_ref.shape
    wide = mask_ref.shape[2]
    row = lax.broadcasted_iota(jnp.int32, (rows, tokens), 0)
    same = jnp.where(row // top == lax.broadcasted_iota(jnp.int32, (rows, tokens), 1), 1.0, 0.0).astype(bf16)
    same_ref[...] = same
    column = members(place_ref, wide, masks)
    for core, ref in enumerate((small_ref, small_other_ref)):
        small = ref[...].T
        experts = dot(same, small.astype(bf16), 1, 0)
        position = lax.broadcasted_iota(jnp.int32, experts.shape, 0) % top
        own = lax.broadcasted_iota(jnp.int32, experts.shape, 1) == position
        expert = jnp.sum(jnp.where(own, experts, 0.0), axis=1, keepdims=True)
        mask_ref[core] = jnp.where(expert == column, 1.0, 0.0).astype(bf16)
    hidden_ref[...] = hidden_other_ref[...]
    both_ref[:tokens] = gradient_ref[...]
    both_ref[tokens:] = gradient_other_ref[...]


def reduce_kernel(masks, place_ref, same_ref, mask_ref, own_ref, other_ref, *rest):
    slots = len(masks)
    piece_refs, (_, reduced_ref, high_ref, low_ref) = rest[: 2 * slots], rest[2 * slots :]
    hidden_width = own_ref.shape[1]
    for offset in range(slots):
        slot = place_ref[1 + offset]
        for kind in range(2):
            down, _ = decode(piece_refs[kind * slots + offset][...], hidden_width)
            high_ref[kind, slot], low_ref[kind, slot] = halves(down)
    wide = reduced_ref.shape[2]
    high = high_ref[...].reshape(2 * wide, hidden_width)
    low = low_ref[...].reshape(2 * wide, hidden_width)
    tokens = same_ref.shape[1]
    for core, hidden_ref in enumerate((own_ref, other_ref)):
        full = dot(hidden_ref[...], high, 1, 1) + dot(hidden_ref[...], low, 1, 1)
        mask = mask_ref[core].astype(f32)
        named = halves(full * jnp.concatenate([mask, mask], axis=1))
        total = dot(same_ref[...], named[0], 0, 0) + dot(same_ref[...], named[1], 0, 0)
        reduced_ref[0, core * tokens : (core + 1) * tokens] = total[:, :wide]
        reduced_ref[1, core * tokens : (core + 1) * tokens] = total[:, wide:]


def rank_limits(place_ref, masks, wide, capacity_ref, prior_ref, arrived_ref):
    lane = lax.broadcasted_iota(jnp.int32, (1, lanes), 1)
    slot_of = lax.broadcasted_iota(jnp.int32, (1, wide), 1) // (wide // len(masks))
    limits = []
    for block in range(2):
        total = capacity_ref[...] - prior_ref[block : block + 1] - arrived_ref[1 - block : 2 - block]
        limit = jnp.zeros((1, wide), f32)
        for slot, mask in enumerate(masks):
            picked = jnp.where(lane == counts_lane + (place_ref[0] ^ mask), total, 0.0)
            limit = jnp.where(slot_of == slot, jnp.sum(picked, axis=1, keepdims=True), limit)
        limits.append(limit)
    return limits


def tangent_kernel(
    top, masks, place_ref, small_ref, small_other_ref, capacity_ref, prior_ref, arrived_ref, reduced_ref, *rest
):
    slots = len(masks)
    piece_refs = rest[: 2 * slots]
    weight_ref, weighted_ref, tangent_ref, coded_ref, high_ref, low_ref = rest[2 * slots :]
    experts, gates, _ = token_columns(small_ref, small_other_ref, top)
    tokens, wide = weight_ref.shape
    model_width = tangent_ref.shape[1]
    hidden_width = piece_refs[0].shape[1] - model_width - lanes
    block = tokens // 2
    column = members(place_ref, wide, masks)
    limits = rank_limits(place_ref, masks, wide, capacity_ref, prior_ref, arrived_ref)
    gate = jnp.zeros((tokens, wide), f32)
    member = jnp.zeros((tokens, wide), f32)
    for k in range(top):
        named = experts[k] == column
        gate = jnp.where(named, gates[k], gate)
        member = jnp.where(named, 1.0, member)
    below = (
        lax.broadcasted_iota(jnp.int32, (block, block), 0)
        > lax.broadcasted_iota(jnp.int32, (block, block), 1)
    )
    below = jnp.where(below, 1.0, 0.0).astype(bf16)
    weights = []
    for part in range(2):
        rows = slice(part * block, (part + 1) * block)
        local_rank = dot(below, member[rows].astype(bf16), 1, 0)
        weights.append(jnp.where(local_rank < limits[part], adapter_scale * gate[rows], 0.0))
    weight = jnp.concatenate(weights, axis=0)
    weight_ref[...] = weight
    weighted = jnp.concatenate([weight * reduced_ref[0], weight * reduced_ref[1]], axis=1)
    weighted_ref[...] = weighted
    for offset in range(slots):
        slot = place_ref[1 + offset]
        for kind in range(2):
            _, up = decode(piece_refs[kind * slots + offset][...], hidden_width)
            high_ref[kind, slot], low_ref[kind, slot] = halves(up)
    factor = high_ref[...].reshape(2 * wide, model_width), low_ref[...].reshape(2 * wide, model_width)
    tangent = dot_pairs(halves(weighted), factor, 1, 0)
    tangent_ref[...] = tangent
    coded_ref[...] = tangent.astype(bf16)


def put_left(left_ref, same_ref, mask_ref, terms):
    both = jnp.concatenate(halves(terms), axis=1)
    tokens = terms.shape[0] // 2
    for core in range(2):
        repeated = dot(same_ref[...], both[core * tokens : (core + 1) * tokens], 1, 0).astype(bf16)
        mask = mask_ref[core]
        left_ref[core] = repeated * jnp.concatenate([mask, mask], axis=1)


def add_halves(both):
    middle = both.shape[0] // 2
    return both[:middle] + both[middle:]


def put_chunks(own_ref, near_ref, far_ref, down, up):
    count, rank, _ = own_ref.shape
    hidden_width = down.shape[1]
    own_ref[:, :, :hidden_width] = down[: count * rank].reshape(count, rank, -1)
    own_ref[:, :, hidden_width:] = up[: count * rank].reshape(count, rank, -1)
    start = count * rank
    for out_ref in (near_ref, far_ref):
        stop = start + out_ref.shape[0] * rank
        out_ref[...] = encode(down[start:stop], up[start:stop]).reshape(out_ref.shape)
        start = stop


def gradient_kernel(
    same_ref,
    mask_ref,
    own_ref,
    other_ref,
    gradient_ref,
    weight_ref,
    weighted_ref,
    high_ref,
    low_ref,
    chunk_ref,
    near_ref,
    far_ref,
    up_ref,
    to_ref,
    left_ref,
):
    wide = weight_ref.shape[1]
    model_width = up_ref.shape[1]
    gradient = gradient_ref[...]
    high = high_ref[...].reshape(2 * wide, model_width)
    low = low_ref[...].reshape(2 * wide, model_width)
    to_both = dot(gradient, high, 1, 1) + dot(gradient, low, 1, 1)
    to_ref[...] = to_both[:, wide:]
    put_left(left_ref, same_ref, mask_ref, weight_ref[...] * to_both[:, :wide])
    down = dot(left_ref[0], own_ref[...], 0, 0) + dot(left_ref[1], other_ref[...], 0, 0)
    up = add_halves(dot(jnp.concatenate(halves(weighted_ref[...]), axis=1), gradient, 0, 0))
    up_ref[...] = up[:wide]
    put_chunks(chunk_ref, near_ref, far_ref, add_halves(down), up[wide:])


def curvature_kernel(
    top,
    small_ref,
    small_other_ref,
    same_ref,
    mask_ref,
    own_ref,
    other_ref,
    weight_ref,
    weighted_ref,
    high_ref,
    low_ref,
    up_ref,
    to_ref,
    tangent_ref,
    arrived_ref,
    chunk_ref,
    near_ref,
    far_ref,
    left_ref,
):
    _, _, curvature = token_columns(small_ref, small_other_ref, top)
    tokens, wide = weight_ref.shape
    block = tokens // 2
    model_width = up_ref.shape[1]
    arrived = jnp.concatenate([arrived_ref[block:], arrived_ref[:block]], axis=0).astype(f32)
    resid = halves(curvature * (tangent_ref[...] + arrived))
    adapter_up = high_ref[0].reshape(wide, model_width), low_ref[0].reshape(wide, model_width)
    put_left(left_ref, same_ref, mask_ref, weight_ref[...] * (dot_pairs(resid, adapter_up, 1, 1) + to_ref[...]))
    down = dot(left_ref[0], own_ref[...], 0, 0) + dot(left_ref[1], other_ref[...], 0, 0)
    weighted_u = halves(weighted_ref[:, wide:])
    up = add_halves(dot(jnp.concatenate(weighted_u, axis=1), resid[0], 0, 0)) + dot(weighted_u[0], resid[1], 0, 0)
    put_chunks(chunk_ref, near_ref, far_ref, add_halves(down), up_ref[...] + up)


def far_kernel(hidden_width, arrived_ref, chunk_ref, _, *out_refs):
    count = len(out_refs)
    for place, out_ref in enumerate(out_refs):
        down, up = decode(arrived_ref[place], hidden_width)
        own = chunk_ref[chunk_ref.shape[0] - count + place]
        out_ref[...] = encode(own[:, :hidden_width] + down, own[:, hidden_width:] + up)


def near_kernel(
    hidden_width, gradient_ref, curvature_ref, gradient_chunk_ref, curvature_chunk_ref, _, out_ref, total_ref
):
    pairs = ((gradient_ref, gradient_chunk_ref), (curvature_ref, curvature_chunk_ref))
    for kind, (arrived_ref, chunk_ref) in enumerate(pairs):
        for place in range(arrived_ref.shape[0]):
            down, up = decode(arrived_ref[place], hidden_width)
            own = chunk_ref[place]
            down, up = own[:, :hidden_width] + down, own[:, hidden_width:] + up
            if place == 0:
                total_ref[kind] = jnp.concatenate([down, up], axis=1)
            else:
                out_ref[place - 1, kind] = encode(down, up)


def add_kernel(hidden_width, *refs):
    coded_refs, total_ref = refs[:-2], refs[-1]
    parts = [decode(ref[...], hidden_width) for ref in coded_refs]
    total_ref[:, :hidden_width] = sum(part[0] for part in parts)
    total_ref[:, hidden_width:] = sum(part[1] for part in parts)


def total_kernel(hidden_width, own_ref, gradient_ref, curvature_ref, *rest):
    near_refs, out_refs = rest[:-4], rest[-4:]
    for kind, far_ref in enumerate((gradient_ref, curvature_ref)):
        total = own_ref[kind] + far_ref[...]
        down, up = total[:, :hidden_width], total[:, hidden_width:]
        for ref in near_refs:
            more = decode(ref[kind], hidden_width)
            down, up = down + more[0], up + more[1]
        out_refs[2 * kind][...] = down
        out_refs[2 * kind + 1][...] = up


class Ring:
    def __init__(self, size):
        self.length = size // 2
        rows = self.length // 2
        self.order = [4 * z for z in range(rows)] + [4 * z + 2 for z in reversed(range(rows))]

    def shift(self, value, step):
        pairs = [
            (chip + core, self.order[(place + step) % self.length] + core)
            for place, chip in enumerate(self.order)
            for core in range(2)
        ]
        return lax.ppermute(value, "expert", pairs)

    def members(self, me):
        rows = self.length // 2
        place = jnp.where(me // 2 % 2 == 0, me // 4, self.length - 1 - me // 4)
        there = (place + jnp.arange(self.length, dtype=jnp.int32)) % self.length
        return jnp.where(there < rows, 4 * there, 4 * (self.length - 1 - there) + 2) + me % 2

    def gather(self, own, way, passing=lambda piece: piece):
        half = self.length // 2
        found = {0: own}
        for direction in (way, -way):
            moving = own
            for step in range(1, half + (direction == way)):
                moving = self.shift(moving, direction)
                if step == 1 and direction != way:
                    moving = passing(moving)
                found[-direction * step % self.length] = moving
        return [found[offset] for offset in range(self.length)]


def exchange(value, mask):
    size = lax.axis_size("expert")
    return lax.ppermute(value, "expert", [(device, device ^ mask) for device in range(size)])


def gathered_plan(
    hidden_of_route,
    expert_of_route,
    gate_of_route,
    capacity,
    output_gradient,
    curvature,
    adapter_down,
    adapter_up,
    down_direction,
    up_direction,
):
    ring = Ring(lax.axis_size("expert"))
    slots = ring.length
    rows = slots // 2
    far = rows // 2
    masks = [4 * z for z in range(rows)] + [4 * z + 2 for z in range(rows)]
    me = lax.axis_index("expert")
    tokens, top = expert_of_route.shape
    both = 2 * tokens
    hidden_width = hidden_of_route.shape[2]
    rank = adapter_down.shape[2]
    model_width = output_gradient.shape[1]
    experts = capacity.shape[0]
    wide = slots * rank
    coded_width = hidden_width + model_width + lanes

    ring_members = ring.members(me)
    differs = ring_members ^ me
    slot_of_offset = differs // 4 + rows * (differs // 2 % 2)
    place = jnp.concatenate([me[None], slot_of_offset, ring_members]).astype(jnp.int32)

    def call(kernel, multiplies, outs, *operands, scratch=(), after=()):
        places = [
            pl.BlockSpec(memory_space=pltpu.SMEM if operand is place else pltpu.VMEM) for operand in operands
        ] + [pl.BlockSpec(memory_space=pl.ANY) for _ in after]
        return pl.pallas_call(
            kernel,
            out_shape=[jax.ShapeDtypeStruct(shape, dtype) for shape, dtype in outs],
            in_specs=places,
            scratch_shapes=scratch,
            compiler_params=pltpu.CompilerParams(vmem_limit_bytes=kernel_vmem),
            cost_estimate=pl.CostEstimate(flops=2 * multiplies, bytes_accessed=2**20, transcendentals=0),
        )(*operands, *after)

    down_multiplies = 2 * top * both * hidden_width * wide
    up_multiplies = both * model_width * wide

    *own_pieces, small = call(
        prepare_kernel,
        10**8,
        [((rank, coded_width), i16)] * 2 + [(((2 * top + 8) // 8 * 8, tokens), f32)],
        expert_of_route.T,
        gate_of_route.T,
        curvature[None],
        down_direction[0].T,
        adapter_down[0].T,
        adapter_up[0],
        up_direction[0],
    )
    small_other = exchange(small, 1)
    hidden = hidden_of_route.reshape(tokens * top, hidden_width)
    beside = []

    def passing(piece):
        *made, onward = call(
            functools.partial(rows_kernel, top, masks),
            10**9,
            [
                ((tokens * top, tokens), bf16),
                ((2, tokens * top, wide), bf16),
                ((tokens * top, hidden_width), bf16),
                ((both, model_width), bf16),
                ((rank, coded_width), i16),
            ],
            place,
            small,
            small_other,
            exchange(hidden, 1),
            output_gradient,
            exchange(output_gradient, 1),
            piece,
        )
        beside.extend(made)
        return onward

    pieces = ring.gather(own_pieces[0], 1, passing) + ring.gather(own_pieces[1], -1)
    same, mask, hidden_other, gradient = beside
    capacity_row = jnp.pad(capacity.astype(f32), (counts_lane, lanes - counts_lane - experts))[None, :]

    (prior,) = call(functools.partial(prior_kernel, masks), 10**8, [((8, lanes), f32)], place, *pieces[:slots])
    prior_arrived = exchange(prior, 1)
    factor_halves = [pltpu.VMEM((2, slots, rank, hidden_width), bf16)] * 2
    (reduced,) = call(
        functools.partial(reduce_kernel, masks),
        2 * down_multiplies,
        [((2, both, wide), f32)],
        place,
        same,
        mask,
        hidden,
        hidden_other,
        *pieces,
        scratch=factor_halves,
        after=[prior],
    )
    weight, weighted, tangent, coded, high, low = call(
        functools.partial(tangent_kernel, top, masks),
        6 * up_multiplies,
        [
            ((both, wide), f32),
            ((both, 2 * wide), f32),
            ((both, model_width), f32),
            ((both, model_width), bf16),
            ((2, slots, rank, model_width), bf16),
            ((2, slots, rank, model_width), bf16),
        ],
        place,
        small,
        small_other,
        capacity_row,
        prior,
        prior_arrived,
        reduced,
        *pieces,
    )
    arrived = exchange(coded, 1)
    left = [pltpu.VMEM((2, top * tokens, 2 * wide), bf16)]
    chunks = [
        ((rows, rank, hidden_width + model_width), f32),
        ((rows - far, rank, coded_width), i16),
        ((far, rank, coded_width), i16),
    ]
    gradient_own, gradient_near, gradient_far, up, to = call(
        gradient_kernel,
        down_multiplies + 8 * up_multiplies,
        chunks + [((wide, model_width), f32), ((both, wide), f32)],
        same,
        mask,
        hidden,
        hidden_other,
        gradient,
        weight,
        weighted,
        high,
        low,
        scratch=left,
    )
    gradient_far = exchange(gradient_far, 2)
    gradient_near = exchange(gradient_near, 2)
    curvature_own, curvature_near, curvature_far = call(
        functools.partial(curvature_kernel, top),
        down_multiplies + 6 * up_multiplies,
        chunks,
        small,
        small_other,
        same,
        mask,
        hidden,
        hidden_other,
        weight,
        weighted,
        high,
        low,
        up,
        to,
        tangent,
        arrived,
        scratch=left,
    )

    hop = 2 * 10**9

    def along_z(arrived, own, after):
        sums = call(
            functools.partial(far_kernel, hidden_width),
            hop,
            [((rank, coded_width), i16)] * far,
            arrived,
            own,
            after=[after],
        )
        return sums, [exchange(part, 4 * z) for z, part in zip(range(rows - far, rows), sums)]

    def added(parts, after):
        return call(
            functools.partial(add_kernel, hidden_width),
            hop,
            [((rank, hidden_width + model_width), f32)],
            *parts,
            after=[after],
        )[0]

    sums, gradient_parts = along_z(gradient_far, gradient_own, curvature_far)
    curvature_far = exchange(curvature_far, 2)
    curvature_near = exchange(curvature_near, 2)
    sums, curvature_parts = along_z(curvature_far, curvature_own, sums[0])
    near, total = call(
        functools.partial(near_kernel, hidden_width),
        hop,
        [((rows - far - 1, 2, rank, coded_width), i16), ((2, rank, hidden_width + model_width), f32)],
        gradient_near,
        curvature_near,
        gradient_own,
        curvature_own,
        after=[sums[0]],
    )
    near_parts = [exchange(near[z - 1], 4 * z) for z in range(1, rows - far)]
    gradient_total = added(gradient_parts, near)
    curvature_total = added(curvature_parts, gradient_total)
    down_gradient, up_gradient, curvature_down, curvature_up = call(
        functools.partial(total_kernel, hidden_width),
        hop,
        [((rank, hidden_width), f32), ((rank, model_width), f32)] * 2,
        total,
        gradient_total,
        curvature_total,
        *near_parts,
    )
    return down_gradient.T[None], up_gradient[None], curvature_down.T[None], curvature_up[None]


def carried_in(value, axis, join, neutral):
    count, mine = (lax.axis_size(axis), lax.axis_index(axis))
    pieces = lax.all_gather(value, axis)
    so_far = jnp.full_like(value, 0) + jnp.asarray(neutral, value.dtype)

    def lap(position, so_far):
        longer = join(so_far, pieces[position])
        return jnp.where(position < mine, longer, so_far)

    return lax.fori_loop(0, count - 1, lap, so_far)


def add_counts(earlier, later):
    return earlier + later


def routed_plan(
    hidden_of_route,
    expert_of_route,
    gate_of_route,
    capacity,
    output_gradient,
    curvature,
    adapter_down,
    adapter_up,
    down_direction,
    up_direction,
):
    finest_precision = lax.Precision.HIGHEST
    group_size = lax.axis_size("expert")
    tok_rows, top_count = expert_of_route.shape
    hidden_width = hidden_of_route.shape[2]
    resident_experts = adapter_down.shape[0]
    adapter_rank = adapter_down.shape[2]
    model_width = output_gradient.shape[1]
    experts = resident_experts * group_size
    slot_most = 2 * tok_rows * top_count // experts
    routes = expert_of_route.reshape(-1)
    onehot = (routes[:, None] == jnp.arange(experts, dtype=jnp.int32)[None, :]).astype(jnp.int32)
    earlier = jnp.cumsum(onehot, axis=0) - onehot
    local_rank = jnp.sum(earlier * onehot, axis=1)
    counts = jnp.sum(onehot, axis=0)
    prior_count = carried_in(counts, "expert", add_counts, jnp.zeros_like(counts))
    global_rank = local_rank + jnp.sum(onehot * prior_count[None, :], axis=1)
    route_limit = jnp.sum(onehot * capacity[None, :], axis=1)
    retained_mask = (global_rank < route_limit).astype(jnp.float32)
    weight_of_route = (
        adapter_scale * gate_of_route.reshape(-1).astype(jnp.float32) * retained_mask
    ).astype(jnp.bfloat16)
    slot_index = routes * slot_most + local_rank
    layout = (group_size, resident_experts, slot_most)
    send_hidden = (
        jnp.zeros((experts * slot_most, hidden_width), jnp.bfloat16)
        .at[slot_index]
        .set(hidden_of_route.reshape(-1, hidden_width))
        .reshape(layout + (hidden_width,))
    )
    send_weight = (
        jnp.zeros((experts * slot_most,), jnp.bfloat16)
        .at[slot_index]
        .set(weight_of_route)
        .reshape(layout)
    )
    down_stacked = jnp.concatenate([adapter_down, down_direction], axis=2)
    up_stacked = jnp.concatenate([adapter_up, up_direction], axis=1)

    def spread(token_rows):
        per_route = jnp.repeat(token_rows, top_count, axis=0)
        placed = (
            jnp.zeros((experts * slot_most, model_width), jnp.bfloat16)
            .at[slot_index]
            .set(per_route)
        )
        return placed.reshape(layout + (model_width,))

    send_residual = spread(output_gradient)
    pieces = (
        lax.all_to_all(send_hidden, "expert", split_axis=0, concat_axis=0, tiled=True),
        lax.all_to_all(send_weight, "expert", split_axis=0, concat_axis=0, tiled=True),
    )
    hidden_rows = pieces[0].astype(jnp.float32)
    weight_rows = pieces[1].astype(jnp.float32)[..., None]
    reduced_hidden = jnp.einsum(
        "cjif,jfk->cjik", hidden_rows, down_stacked, precision=finest_precision
    )
    exchanged_rows = jnp.concatenate(
        [reduced_hidden[..., adapter_rank:], reduced_hidden[..., :adapter_rank]], axis=3
    )
    tangent_out = weight_rows * jnp.einsum(
        "cjik,jkd->cjid", exchanged_rows, up_stacked, precision=finest_precision
    )
    returned = lax.all_to_all(
        tangent_out.astype(jnp.bfloat16), "expert", split_axis=0, concat_axis=0, tiled=True
    )
    results = (returned, reduced_hidden) + tuple(pieces)
    returned = results[0]
    reduced_hidden = results[1]
    hidden_rows = results[2]
    weight_rows = results[3]
    route_tangent = returned.reshape(experts * slot_most, model_width)[slot_index]
    out_tangent = jnp.sum(
        route_tangent.reshape(tok_rows, top_count, model_width).astype(jnp.float32), axis=1
    )
    resid_tangent = (curvature[:, None] * out_tangent).astype(jnp.bfloat16)
    send_tangent = spread(resid_tangent)
    residual_rows, tangent_rows = (
        lax.all_to_all(send_residual, "expert", split_axis=0, concat_axis=0, tiled=True),
        lax.all_to_all(send_tangent, "expert", split_axis=0, concat_axis=0, tiled=True),
    )
    residual_full = residual_rows.astype(jnp.float32)
    complete_tangent = tangent_rows.astype(jnp.float32)
    weight_column = weight_rows.astype(jnp.float32)[..., None]
    residual_reduced = jnp.einsum(
        "wyov,yqv->wyoq", residual_full, up_stacked, precision=finest_precision
    )
    reduced_tangent = jnp.einsum(
        "wyov,yqv->wyoq", complete_tangent, adapter_up, precision=finest_precision
    )
    left_terms = jnp.concatenate(
        [
            weight_column * residual_reduced[..., :adapter_rank],
            weight_column * (reduced_tangent + residual_reduced[..., adapter_rank:]),
        ],
        axis=3,
    )
    down_terms = jnp.einsum(
        "cjif,cjik->jfk", hidden_rows.astype(jnp.float32), left_terms, precision=finest_precision
    )
    raised_update = weight_column * reduced_hidden[..., :adapter_rank]
    raised_tangent_update = weight_column * reduced_hidden[..., adapter_rank:]
    up_terms = jnp.einsum(
        "cjik,cjid->jkd",
        jnp.concatenate([raised_update, raised_tangent_update], axis=3),
        residual_full,
        precision=finest_precision,
    )
    curvature_piece = up_terms[:, adapter_rank:] + jnp.einsum(
        "cjik,cjid->jkd", raised_update, complete_tangent, precision=finest_precision
    )
    return (
        down_terms[..., :adapter_rank],
        up_terms[:, :adapter_rank],
        down_terms[..., adapter_rank:],
        curvature_piece,
    )


def local(*arguments):
    factor_bytes = 2 * 4 * (arguments[6].size + arguments[7].size) * lax.axis_size("expert")
    plan = gathered_plan if 4 * factor_bytes <= kernel_vmem else routed_plan
    return plan(*arguments)


def solution(mesh):
    return jax.shard_map(
        local,
        mesh=mesh,
        in_specs=(
            P(("groups", "expert"), None, None),
            P(("groups", "expert"), None),
            P(("groups", "expert"), None),
            P("groups"),
            P(("groups", "expert"), None),
            P(("groups", "expert")),
            P("expert", None, None),
            P("expert", None, None),
            P(("groups", "expert"), None, None),
            P(("groups", "expert"), None, None),
        ),
        out_specs=(
            P(("groups", "expert"), None, None),
            P(("groups", "expert"), None, None),
            P(("groups", "expert"), None, None),
            P(("groups", "expert"), None, None),
        ),
        check_vma=False,
    )
```

```python
import functools

import jax
import jax.numpy as jnp
from jax import lax
from jax.experimental import pallas as pl
from jax.experimental.pallas import tpu as pltpu
from jax.sharding import PartitionSpec as P

adapter_scale = 2.0
f32 = jnp.float32
bf16 = jnp.bfloat16
i16 = jnp.int16
lanes = 128
counts_lane = 64
kernel_vmem = 32 * 2**20
whole_vmem = 60 * 2**20


def halves(value):
    high = value.astype(bf16)
    return high, (value - high.astype(f32)).astype(bf16)


def dot(a, b, a_dim, b_dim):
    return lax.dot_general(a, b, (((a_dim,), (b_dim,)), ((), ())), preferred_element_type=f32)


def dot_pairs(a, b, a_dim, b_dim):
    return dot(a[0], b[0], a_dim, b_dim) + (dot(a[1], b[0], a_dim, b_dim) + dot(a[0], b[1], a_dim, b_dim))


def encode(down, up, counts=0.0):
    def scaled(value):
        largest = jnp.max(jnp.abs(value), axis=-1, keepdims=True)
        exponent = jnp.ceil(jnp.log2(jnp.maximum(largest, 1e-30)))
        coded = jnp.round(value * jnp.exp2(15.0 - exponent))
        return jnp.clip(coded, -32767.0, 32767.0), exponent

    down, down_exponent = scaled(down)
    up, up_exponent = scaled(up)
    lane = lax.broadcasted_iota(jnp.int32, down.shape[:-1] + (lanes,), down.ndim - 1)
    tail = jnp.where(lane < counts_lane // 2, down_exponent, up_exponent)
    tail = jnp.where(lane < counts_lane, tail, counts)
    return jnp.concatenate([down, up, tail], axis=-1).astype(jnp.int32).astype(i16)


def decode(coded, hidden_width):
    width = coded.shape[-1] - lanes
    value = coded.astype(jnp.int32).astype(f32)
    down_scale = jnp.exp2(value[..., width : width + 1] - 15.0)
    up_scale = jnp.exp2(value[..., width + counts_lane // 2 : width + counts_lane // 2 + 1] - 15.0)
    return value[..., :hidden_width] * down_scale, value[..., hidden_width:width] * up_scale


def prepare_kernel(*refs):
    (piece_ref, small_ref), sem, refs = refs[7:9], refs[-1], refs[:7] + refs[9:-1]
    copies = [pltpu.make_async_copy(refs[i], refs[7 + i], sem.at[i]) for i in range(7)]
    for copy in copies:
        copy.start()
    for copy in copies:
        copy.wait()
    expert, gate, curvature, down_direction, adapter_down, adapter_up, up_direction = [ref[...] for ref in refs[7:]]
    top = expert.shape[0]
    small_ref[...] = jnp.zeros_like(small_ref)
    small_ref[:top] = expert.astype(f32)
    small_ref[top : 2 * top] = gate.astype(f32)
    small_ref[2 * top : 2 * top + 1] = curvature
    lane = lax.broadcasted_iota(jnp.int32, (1, lanes), 1)
    counts = jnp.zeros((1, lanes), f32)
    for number in range(lanes - counts_lane):
        named = jnp.where(expert == number, 1.0, 0.0)
        total = jnp.sum(jnp.sum(named, axis=0, keepdims=True), axis=1, keepdims=True)
        counts = jnp.where(lane == counts_lane + number, total, counts)
    piece_ref[0] = encode(down_direction, adapter_up, counts)
    piece_ref[1] = encode(adapter_down, up_direction, counts)


def token_columns(own_ref, other_ref, top):
    small = jnp.concatenate([own_ref[...], other_ref[...]], axis=1).T
    experts = [small[:, k : k + 1] for k in range(top)]
    gates = [small[:, top + k : top + k + 1] for k in range(top)]
    return experts, gates, small[:, 2 * top : 2 * top + 1]


def members(place_ref, wide, masks):
    slot_of = lax.broadcasted_iota(jnp.int32, (1, wide), 1) // (wide // len(masks))
    found = jnp.zeros((1, wide), jnp.int32)
    for slot, mask in enumerate(masks):
        found = jnp.where(slot_of == slot, place_ref[0] ^ mask, found)
    return found.astype(f32)


def prior_kernel(masks, place_ref, *rest):
    piece_refs, prior_ref = rest[:-1], rest[-1]
    me = place_ref[0]
    slots = len(masks)
    prior_ref[...] = jnp.zeros_like(prior_ref)
    for block, number in enumerate((me, me ^ 1)):
        total = jnp.zeros((1, lanes), f32)
        for offset in range(slots):
            device = place_ref[1 + slots + offset]
            tail = piece_refs[offset][0, :, piece_refs[offset].shape[2] - lanes :]
            counts = tail.astype(jnp.int32).astype(f32)[0:1]
            total = total + jnp.where(device < number, counts, 0.0)
        prior_ref[block : block + 1] = total


def piece_part(refs, offset, kind):
    last = len(refs) - 2
    half = last // 2 + 1
    if offset == half:
        return refs[last + kind][0]
    return refs[offset if offset < half else offset - 1][kind]


def rows_kernel(top, masks, place_ref, small_ref, small_other_ref, hidden_other_ref, gradient_other_ref, piece_ref, *outs):
    same_ref, same_turned_ref, mask_ref, rank_ref, gate_ref, hidden_ref, gradient_ref, onward_ref = outs
    onward_ref[...] = piece_ref[...]
    hidden_ref[...] = hidden_other_ref[...]
    gradient_ref[...] = gradient_other_ref[...]
    rows, tokens = same_ref.shape
    wide = mask_ref.shape[2]

    def ones(row_dim):
        row = lax.broadcasted_iota(jnp.int32, (rows, tokens) if row_dim == 0 else (tokens, rows), row_dim)
        token = lax.broadcasted_iota(jnp.int32, row.shape, 1 - row_dim)
        return jnp.where(row // top == token, 1.0, 0.0).astype(bf16)

    same = ones(0)
    same_ref[...] = same
    same_turned_ref[...] = ones(1)
    column = members(place_ref, wide, masks)
    below = (
        lax.broadcasted_iota(jnp.int32, (tokens, tokens), 0)
        > lax.broadcasted_iota(jnp.int32, (tokens, tokens), 1)
    )
    below = jnp.where(below, 1.0, 0.0).astype(bf16)
    for core, ref in enumerate((small_ref, small_other_ref)):
        small = ref[...].T
        experts = dot(same, small.astype(bf16), 1, 0)
        position = lax.broadcasted_iota(jnp.int32, experts.shape, 0) % top
        own = lax.broadcasted_iota(jnp.int32, experts.shape, 1) == position
        expert = jnp.sum(jnp.where(own, experts, 0.0), axis=1, keepdims=True)
        mask_ref[core] = jnp.where(expert == column, 1.0, 0.0).astype(bf16)
        gate = jnp.zeros((tokens, wide), f32)
        member = jnp.zeros((tokens, wide), f32)
        for k in range(top):
            named = small[:, k : k + 1] == column
            gate = jnp.where(named, small[:, top + k : top + k + 1], gate)
            member = jnp.where(named, 1.0, member)
        gate_ref[core] = gate
        rank_ref[core] = dot(below, member.astype(bf16), 1, 0)


def reduce_kernel(masks, place_ref, same_turned_ref, mask_ref, own_ref, other_ref, *rest):
    slots = len(masks)
    piece_refs, (_, reduced_ref, high_ref, low_ref) = rest[: slots + 1], rest[slots + 1 :]
    hidden_width = own_ref.shape[1]
    for offset in range(slots):
        slot = place_ref[1 + offset]
        for kind in range(2):
            down, _ = decode(piece_part(piece_refs, offset, kind), hidden_width)
            high_ref[kind, slot], low_ref[kind, slot] = halves(down)
    wide = reduced_ref.shape[2]
    high = high_ref[...].reshape(2 * wide, hidden_width)
    low = low_ref[...].reshape(2 * wide, hidden_width)
    tokens = same_turned_ref.shape[0]
    for core, hidden_ref in enumerate((own_ref, other_ref)):
        full = dot(hidden_ref[...], high, 1, 1) + dot(hidden_ref[...], low, 1, 1)
        mask = mask_ref[core].astype(f32)
        named = halves(full * jnp.concatenate([mask, mask], axis=1))
        total = dot(same_turned_ref[...], named[0], 1, 0) + dot(same_turned_ref[...], named[1], 1, 0)
        reduced_ref[0, core * tokens : (core + 1) * tokens] = total[:, :wide]
        reduced_ref[1, core * tokens : (core + 1) * tokens] = total[:, wide:]


def rank_limits(place_ref, masks, wide, capacity_ref, prior_ref, arrived_ref):
    lane = lax.broadcasted_iota(jnp.int32, (1, lanes), 1)
    slot_of = lax.broadcasted_iota(jnp.int32, (1, wide), 1) // (wide // len(masks))
    limits = []
    for block in range(2):
        total = capacity_ref[...] - prior_ref[block : block + 1] - arrived_ref[1 - block : 2 - block]
        limit = jnp.zeros((1, wide), f32)
        for slot, mask in enumerate(masks):
            picked = jnp.where(lane == counts_lane + (place_ref[0] ^ mask), total, 0.0)
            limit = jnp.where(slot_of == slot, jnp.sum(picked, axis=1, keepdims=True), limit)
        limits.append(limit)
    return limits


def tangent_kernel(masks, place_ref, rank_ref, gate_ref, capacity_ref, prior_ref, arrived_ref, reduced_ref, *rest):
    slots = len(masks)
    piece_refs = rest[: slots + 1]
    weight_ref, weighted_ref, tangent_ref, coded_ref, high_ref, low_ref = rest[slots + 1 :]
    _, wide = weight_ref.shape
    model_width = tangent_ref.shape[1]
    hidden_width = piece_refs[0].shape[2] - model_width - lanes
    limits = rank_limits(place_ref, masks, wide, capacity_ref, prior_ref, arrived_ref)
    weights = [
        jnp.where(rank_ref[core] < limits[core], adapter_scale * gate_ref[core], 0.0) for core in range(2)
    ]
    weight = jnp.concatenate(weights, axis=0)
    weight_ref[...] = weight
    weighted = jnp.concatenate([weight * reduced_ref[0], weight * reduced_ref[1]], axis=1)
    weighted_ref[...] = weighted
    for offset in range(slots):
        slot = place_ref[1 + offset]
        for kind in range(2):
            _, up = decode(piece_part(piece_refs, offset, kind), hidden_width)
            high_ref[kind, slot], low_ref[kind, slot] = halves(up)
    factor = high_ref[...].reshape(2 * wide, model_width), low_ref[...].reshape(2 * wide, model_width)
    tangent = dot_pairs(halves(weighted), factor, 1, 0)
    tangent_ref[...] = tangent
    coded_ref[...] = tangent.astype(bf16)


def put_left(left_ref, same_ref, mask_ref, terms):
    both = jnp.concatenate(halves(terms), axis=1)
    tokens = terms.shape[0] // 2
    for core in range(2):
        repeated = dot(same_ref[...], both[core * tokens : (core + 1) * tokens], 1, 0).astype(bf16)
        mask = mask_ref[core]
        left_ref[core] = repeated * jnp.concatenate([mask, mask], axis=1)


def add_halves(both):
    middle = both.shape[0] // 2
    return both[:middle] + both[middle:]


def put_chunks(own_ref, near_ref, far_ref, down, up):
    count, rank, _ = own_ref.shape
    hidden_width = down.shape[1]
    own_ref[:, :, :hidden_width] = down[: count * rank].reshape(count, rank, -1)
    own_ref[:, :, hidden_width:] = up[: count * rank].reshape(count, rank, -1)
    start = count * rank
    for out_ref in (near_ref, far_ref):
        stop = start + out_ref.shape[0] * rank
        out_ref[...] = encode(down[start:stop], up[start:stop]).reshape(out_ref.shape)
        start = stop


def gradient_kernel(
    same_ref,
    mask_ref,
    own_ref,
    other_ref,
    own_gradient_ref,
    other_gradient_ref,
    weight_ref,
    weighted_ref,
    high_ref,
    low_ref,
    chunk_ref,
    near_ref,
    far_ref,
    up_ref,
    to_ref,
    left_ref,
):
    wide = weight_ref.shape[1]
    model_width = up_ref.shape[1]
    gradient = jnp.concatenate([own_gradient_ref[...], other_gradient_ref[...]], axis=0)
    high = high_ref[...].reshape(2 * wide, model_width)
    low = low_ref[...].reshape(2 * wide, model_width)
    to_both = dot(gradient, high, 1, 1) + dot(gradient, low, 1, 1)
    to_ref[...] = to_both[:, wide:]
    put_left(left_ref, same_ref, mask_ref, weight_ref[...] * to_both[:, :wide])
    down = dot(left_ref[0], own_ref[...], 0, 0) + dot(left_ref[1], other_ref[...], 0, 0)
    up = add_halves(dot(jnp.concatenate(halves(weighted_ref[...]), axis=1), gradient, 0, 0))
    up_ref[...] = up[:wide]
    put_chunks(chunk_ref, near_ref, far_ref, add_halves(down), up[wide:])


def curvature_kernel(
    top,
    small_ref,
    small_other_ref,
    same_ref,
    mask_ref,
    own_ref,
    other_ref,
    weight_ref,
    weighted_ref,
    high_ref,
    low_ref,
    up_ref,
    to_ref,
    tangent_ref,
    arrived_ref,
    chunk_ref,
    near_ref,
    far_ref,
    left_ref,
):
    _, _, curvature = token_columns(small_ref, small_other_ref, top)
    tokens, wide = weight_ref.shape
    block = tokens // 2
    model_width = up_ref.shape[1]
    arrived = jnp.concatenate([arrived_ref[block:], arrived_ref[:block]], axis=0).astype(f32)
    resid = halves(curvature * (tangent_ref[...] + arrived))
    adapter_up = high_ref[0].reshape(wide, model_width), low_ref[0].reshape(wide, model_width)
    put_left(left_ref, same_ref, mask_ref, weight_ref[...] * (dot_pairs(resid, adapter_up, 1, 1) + to_ref[...]))
    down = dot(left_ref[0], own_ref[...], 0, 0) + dot(left_ref[1], other_ref[...], 0, 0)
    weighted_u = halves(weighted_ref[:, wide:])
    up = add_halves(dot(jnp.concatenate(weighted_u, axis=1), resid[0], 0, 0)) + dot(weighted_u[0], resid[1], 0, 0)
    put_chunks(chunk_ref, near_ref, far_ref, add_halves(down), up_ref[...] + up)


def far_kernel(hidden_width, arrived_ref, chunk_ref, near_ref, _, onward_ref, *out_refs):
    onward_ref[...] = near_ref[...]
    count = len(out_refs)
    for place, out_ref in enumerate(out_refs):
        down, up = decode(arrived_ref[place], hidden_width)
        own = chunk_ref[chunk_ref.shape[0] - count + place]
        out_ref[...] = encode(own[:, :hidden_width] + down, own[:, hidden_width:] + up)


def near_kernel(
    hidden_width, gradient_ref, curvature_ref, gradient_chunk_ref, curvature_chunk_ref, _, out_ref, total_ref
):
    pairs = ((gradient_ref, gradient_chunk_ref), (curvature_ref, curvature_chunk_ref))
    for kind, (arrived_ref, chunk_ref) in enumerate(pairs):
        for place in range(arrived_ref.shape[0]):
            down, up = decode(arrived_ref[place], hidden_width)
            own = chunk_ref[place]
            down, up = own[:, :hidden_width] + down, own[:, hidden_width:] + up
            if place == 0:
                total_ref[kind] = jnp.concatenate([down, up], axis=1)
            else:
                out_ref[place - 1, kind] = encode(down, up)


def add_kernel(hidden_width, *refs):
    coded_refs, total_ref = refs[:-2], refs[-1]
    parts = [decode(ref[...], hidden_width) for ref in coded_refs]
    total_ref[:, :hidden_width] = sum(part[0] for part in parts)
    total_ref[:, hidden_width:] = sum(part[1] for part in parts)


def total_kernel(hidden_width, own_ref, gradient_ref, curvature_ref, *rest):
    near_refs, out_refs = rest[:-4], rest[-4:]
    for kind, far_ref in enumerate((gradient_ref, curvature_ref)):
        total = own_ref[kind] + far_ref[...]
        down, up = total[:, :hidden_width], total[:, hidden_width:]
        for ref in near_refs:
            more = decode(ref[kind], hidden_width)
            down, up = down + more[0], up + more[1]
        out_refs[2 * kind][...] = down
        out_refs[2 * kind + 1][...] = up


class Ring:
    def __init__(self, size):
        self.length = size // 2
        rows = self.length // 2
        self.order = [4 * z for z in range(rows)] + [4 * z + 2 for z in reversed(range(rows))]

    def shift(self, value, step):
        pairs = [
            (chip + core, self.order[(place + step) % self.length] + core)
            for place, chip in enumerate(self.order)
            for core in range(2)
        ]
        return lax.ppermute(value, "expert", pairs)

    def members(self, me):
        rows = self.length // 2
        place = jnp.where(me // 2 % 2 == 0, me // 4, self.length - 1 - me // 4)
        there = (place + jnp.arange(self.length, dtype=jnp.int32)) % self.length
        return jnp.where(there < rows, 4 * there, 4 * (self.length - 1 - there) + 2) + me % 2

    def gather(self, own, passing):
        half = self.length // 2
        found = {0: own}
        ahead, behind = own, own
        for step in range(1, half):
            behind = self.shift(behind, 1)
            ahead = self.shift(ahead, -1)
            if step == 1:
                ahead = passing(ahead)
            found[self.length - step], found[step] = behind, ahead
        last = [self.shift(behind[:1], 1), self.shift(ahead[1:], -1)]
        return [found[offset] for offset in sorted(found)] + last


def exchange(value, mask):
    size = lax.axis_size("expert")
    return lax.ppermute(value, "expert", [(device, device ^ mask) for device in range(size)])


def gathered_plan(
    hidden_of_route,
    expert_of_route,
    gate_of_route,
    capacity,
    output_gradient,
    curvature,
    adapter_down,
    adapter_up,
    down_direction,
    up_direction,
):
    ring = Ring(lax.axis_size("expert"))
    slots = ring.length
    rows = slots // 2
    far = rows // 2
    masks = [4 * z for z in range(rows)] + [4 * z + 2 for z in range(rows)]
    me = lax.axis_index("expert")
    tokens, top = expert_of_route.shape
    both = 2 * tokens
    hidden_width = hidden_of_route.shape[2]
    rank = adapter_down.shape[2]
    model_width = output_gradient.shape[1]
    experts = capacity.shape[0]
    wide = slots * rank
    coded_width = hidden_width + model_width + lanes

    ring_members = ring.members(me)
    differs = ring_members ^ me
    slot_of_offset = differs // 4 + rows * (differs // 2 % 2)
    place = jnp.concatenate([me[None], slot_of_offset, ring_members]).astype(jnp.int32)

    def call(kernel, multiplies, outs, *operands, scratch=(), after=(), grant=kernel_vmem):
        space = pltpu.HBM if kernel is prepare_kernel else pltpu.VMEM
        places = [
            pl.BlockSpec(memory_space=pltpu.SMEM if operand is place else space) for operand in operands
        ] + [pl.BlockSpec(memory_space=pl.ANY) for _ in after]
        return pl.pallas_call(
            kernel,
            out_shape=[jax.ShapeDtypeStruct(shape, dtype) for shape, dtype in outs],
            in_specs=places,
            scratch_shapes=scratch,
            compiler_params=pltpu.CompilerParams(vmem_limit_bytes=grant),
            cost_estimate=pl.CostEstimate(flops=2 * multiplies, bytes_accessed=2**20, transcendentals=0),
        )(*operands, *after)

    down_multiplies = 2 * top * both * hidden_width * wide
    up_multiplies = both * model_width * wide

    first = (
        expert_of_route.T,
        gate_of_route.T,
        curvature[None],
        down_direction[0].T,
        adapter_down[0].T,
        adapter_up[0],
        up_direction[0],
    )
    piece, small = call(
        prepare_kernel,
        10**8,
        [((2, rank, coded_width), i16), (((2 * top + 8) // 8 * 8, tokens), f32)],
        *first,
        scratch=[pltpu.VMEM(operand.shape, operand.dtype) for operand in first]
        + [pltpu.SemaphoreType.DMA((len(first),))],
        grant=whole_vmem,
    )
    small_other = exchange(small, 1)
    hidden = hidden_of_route.reshape(tokens * top, hidden_width)
    beside = []

    def passing(piece):
        *made, onward = call(
            functools.partial(rows_kernel, top, masks),
            10**9,
            [
                ((tokens * top, tokens), bf16),
                ((tokens, tokens * top), bf16),
                ((2, tokens * top, wide), bf16),
                ((2, tokens, wide), f32),
                ((2, tokens, wide), f32),
                ((tokens * top, hidden_width), bf16),
                ((tokens, model_width), bf16),
                (piece.shape, i16),
            ],
            place,
            small,
            small_other,
            exchange(hidden, 1),
            exchange(output_gradient, 1),
            piece,
        )
        beside.extend(made)
        return onward

    pieces = ring.gather(piece, passing)
    same, same_turned, mask, local_rank, gate, hidden_other, gradient_other = beside
    capacity_row = jnp.pad(capacity.astype(f32), (counts_lane, lanes - counts_lane - experts))[None, :]

    by_offset = pieces[:rows] + [pieces[-2]] + pieces[rows:-2]
    (prior,) = call(functools.partial(prior_kernel, masks), 10**8, [((8, lanes), f32)], place, *by_offset)
    prior_arrived = exchange(prior, 1)
    factor_halves = [pltpu.VMEM((2, slots, rank, hidden_width), bf16)] * 2
    (reduced,) = call(
        functools.partial(reduce_kernel, masks),
        2 * down_multiplies,
        [((2, both, wide), f32)],
        place,
        same_turned,
        mask,
        hidden,
        hidden_other,
        *pieces,
        scratch=factor_halves,
        after=[prior],
    )
    weight, weighted, tangent, coded, high, low = call(
        functools.partial(tangent_kernel, masks),
        6 * up_multiplies,
        [
            ((both, wide), f32),
            ((both, 2 * wide), f32),
            ((both, model_width), f32),
            ((both, model_width), bf16),
            ((2, slots, rank, model_width), bf16),
            ((2, slots, rank, model_width), bf16),
        ],
        place,
        local_rank,
        gate,
        capacity_row,
        prior,
        prior_arrived,
        reduced,
        *pieces,
    )
    arrived = exchange(coded, 1)
    left = [pltpu.VMEM((2, top * tokens, 2 * wide), bf16)]
    chunks = [
        ((rows, rank, hidden_width + model_width), f32),
        ((rows - far, rank, coded_width), i16),
        ((far, rank, coded_width), i16),
    ]
    gradient_own, gradient_near, gradient_far, up, to = call(
        gradient_kernel,
        down_multiplies + 8 * up_multiplies,
        chunks + [((wide, model_width), f32), ((both, wide), f32)],
        same,
        mask,
        hidden,
        hidden_other,
        output_gradient,
        gradient_other,
        weight,
        weighted,
        high,
        low,
        scratch=left,
    )
    gradient_far = exchange(gradient_far, 2)
    curvature_own, curvature_near, curvature_far = call(
        functools.partial(curvature_kernel, top),
        down_multiplies + 6 * up_multiplies,
        chunks,
        small,
        small_other,
        same,
        mask,
        hidden,
        hidden_other,
        weight,
        weighted,
        high,
        low,
        up,
        to,
        tangent,
        arrived,
        scratch=left,
    )

    hop = 2 * 10**9

    def along_z(arrived, own, near, after):
        onward, *sums = call(
            functools.partial(far_kernel, hidden_width),
            hop,
            [(near.shape, i16)] + [((rank, coded_width), i16)] * far,
            arrived,
            own,
            near,
            after=[after],
        )
        return exchange(onward, 2), sums, [exchange(part, 4 * z) for z, part in zip(range(rows - far, rows), sums)]

    def added(parts, after):
        return call(
            functools.partial(add_kernel, hidden_width),
            hop,
            [((rank, hidden_width + model_width), f32)],
            *parts,
            after=[after],
        )[0]

    gradient_near, sums, gradient_parts = along_z(gradient_far, gradient_own, gradient_near, curvature_far)
    curvature_far = exchange(curvature_far, 2)
    curvature_near, sums, curvature_parts = along_z(curvature_far, curvature_own, curvature_near, sums[0])
    gradient_total = added(gradient_parts, sums[0])
    near, total = call(
        functools.partial(near_kernel, hidden_width),
        hop,
        [((rows - far - 1, 2, rank, coded_width), i16), ((2, rank, hidden_width + model_width), f32)],
        gradient_near,
        curvature_near,
        gradient_own,
        curvature_own,
        after=[gradient_total],
    )
    near_parts = [exchange(near[z - 1], 4 * z) for z in range(1, rows - far)]
    curvature_total = added(curvature_parts, near)
    down_gradient, up_gradient, curvature_down, curvature_up = call(
        functools.partial(total_kernel, hidden_width),
        hop,
        [((rank, hidden_width), f32), ((rank, model_width), f32)] * 2,
        total,
        gradient_total,
        curvature_total,
        *near_parts,
    )
    return down_gradient.T[None], up_gradient[None], curvature_down.T[None], curvature_up[None]


def carried_in(value, axis, join, neutral):
    count, mine = (lax.axis_size(axis), lax.axis_index(axis))
    pieces = lax.all_gather(value, axis)
    so_far = jnp.full_like(value, 0) + jnp.asarray(neutral, value.dtype)

    def lap(position, so_far):
        longer = join(so_far, pieces[position])
        return jnp.where(position < mine, longer, so_far)

    return lax.fori_loop(0, count - 1, lap, so_far)


def add_counts(earlier, later):
    return earlier + later


def routed_plan(
    hidden_of_route,
    expert_of_route,
    gate_of_route,
    capacity,
    output_gradient,
    curvature,
    adapter_down,
    adapter_up,
    down_direction,
    up_direction,
):
    finest_precision = lax.Precision.HIGHEST
    group_size = lax.axis_size("expert")
    tok_rows, top_count = expert_of_route.shape
    hidden_width = hidden_of_route.shape[2]
    resident_experts = adapter_down.shape[0]
    adapter_rank = adapter_down.shape[2]
    model_width = output_gradient.shape[1]
    experts = resident_experts * group_size
    slot_most = 2 * tok_rows * top_count // experts
    routes = expert_of_route.reshape(-1)
    onehot = (routes[:, None] == jnp.arange(experts, dtype=jnp.int32)[None, :]).astype(jnp.int32)
    earlier = jnp.cumsum(onehot, axis=0) - onehot
    local_rank = jnp.sum(earlier * onehot, axis=1)
    counts = jnp.sum(onehot, axis=0)
    prior_count = carried_in(counts, "expert", add_counts, jnp.zeros_like(counts))
    global_rank = local_rank + jnp.sum(onehot * prior_count[None, :], axis=1)
    route_limit = jnp.sum(onehot * capacity[None, :], axis=1)
    retained_mask = (global_rank < route_limit).astype(jnp.float32)
    weight_of_route = (
        adapter_scale * gate_of_route.reshape(-1).astype(jnp.float32) * retained_mask
    ).astype(jnp.bfloat16)
    slot_index = routes * slot_most + local_rank
    layout = (group_size, resident_experts, slot_most)
    send_hidden = (
        jnp.zeros((experts * slot_most, hidden_width), jnp.bfloat16)
        .at[slot_index]
        .set(hidden_of_route.reshape(-1, hidden_width))
        .reshape(layout + (hidden_width,))
    )
    send_weight = (
        jnp.zeros((experts * slot_most,), jnp.bfloat16)
        .at[slot_index]
        .set(weight_of_route)
        .reshape(layout)
    )
    down_stacked = jnp.concatenate([adapter_down, down_direction], axis=2)
    up_stacked = jnp.concatenate([adapter_up, up_direction], axis=1)

    def spread(token_rows):
        per_route = jnp.repeat(token_rows, top_count, axis=0)
        placed = (
            jnp.zeros((experts * slot_most, model_width), jnp.bfloat16)
            .at[slot_index]
            .set(per_route)
        )
        return placed.reshape(layout + (model_width,))

    send_residual = spread(output_gradient)
    pieces = (
        lax.all_to_all(send_hidden, "expert", split_axis=0, concat_axis=0, tiled=True),
        lax.all_to_all(send_weight, "expert", split_axis=0, concat_axis=0, tiled=True),
    )
    hidden_rows = pieces[0].astype(jnp.float32)
    weight_rows = pieces[1].astype(jnp.float32)[..., None]
    reduced_hidden = jnp.einsum(
        "cjif,jfk->cjik", hidden_rows, down_stacked, precision=finest_precision
    )
    exchanged_rows = jnp.concatenate(
        [reduced_hidden[..., adapter_rank:], reduced_hidden[..., :adapter_rank]], axis=3
    )
    tangent_out = weight_rows * jnp.einsum(
        "cjik,jkd->cjid", exchanged_rows, up_stacked, precision=finest_precision
    )
    returned = lax.all_to_all(
        tangent_out.astype(jnp.bfloat16), "expert", split_axis=0, concat_axis=0, tiled=True
    )
    results = (returned, reduced_hidden) + tuple(pieces)
    returned = results[0]
    reduced_hidden = results[1]
    hidden_rows = results[2]
    weight_rows = results[3]
    route_tangent = returned.reshape(experts * slot_most, model_width)[slot_index]
    out_tangent = jnp.sum(
        route_tangent.reshape(tok_rows, top_count, model_width).astype(jnp.float32), axis=1
    )
    resid_tangent = (curvature[:, None] * out_tangent).astype(jnp.bfloat16)
    send_tangent = spread(resid_tangent)
    residual_rows, tangent_rows = (
        lax.all_to_all(send_residual, "expert", split_axis=0, concat_axis=0, tiled=True),
        lax.all_to_all(send_tangent, "expert", split_axis=0, concat_axis=0, tiled=True),
    )
    residual_full = residual_rows.astype(jnp.float32)
    complete_tangent = tangent_rows.astype(jnp.float32)
    weight_column = weight_rows.astype(jnp.float32)[..., None]
    residual_reduced = jnp.einsum(
        "wyov,yqv->wyoq", residual_full, up_stacked, precision=finest_precision
    )
    reduced_tangent = jnp.einsum(
        "wyov,yqv->wyoq", complete_tangent, adapter_up, precision=finest_precision
    )
    left_terms = jnp.concatenate(
        [
            weight_column * residual_reduced[..., :adapter_rank],
            weight_column * (reduced_tangent + residual_reduced[..., adapter_rank:]),
        ],
        axis=3,
    )
    down_terms = jnp.einsum(
        "cjif,cjik->jfk", hidden_rows.astype(jnp.float32), left_terms, precision=finest_precision
    )
    raised_update = weight_column * reduced_hidden[..., :adapter_rank]
    raised_tangent_update = weight_column * reduced_hidden[..., adapter_rank:]
    up_terms = jnp.einsum(
        "cjik,cjid->jkd",
        jnp.concatenate([raised_update, raised_tangent_update], axis=3),
        residual_full,
        precision=finest_precision,
    )
    curvature_piece = up_terms[:, adapter_rank:] + jnp.einsum(
        "cjik,cjid->jkd", raised_update, complete_tangent, precision=finest_precision
    )
    return (
        down_terms[..., :adapter_rank],
        up_terms[:, :adapter_rank],
        down_terms[..., adapter_rank:],
        curvature_piece,
    )


def local(*arguments):
    factor_bytes = 2 * 4 * (arguments[6].size + arguments[7].size) * lax.axis_size("expert")
    plan = gathered_plan if 4 * factor_bytes <= kernel_vmem else routed_plan
    return plan(*arguments)


def solution(mesh):
    return jax.shard_map(
        local,
        mesh=mesh,
        in_specs=(
            P(("groups", "expert"), None, None),
            P(("groups", "expert"), None),
            P(("groups", "expert"), None),
            P("groups"),
            P(("groups", "expert"), None),
            P(("groups", "expert")),
            P("expert", None, None),
            P("expert", None, None),
            P(("groups", "expert"), None, None),
            P(("groups", "expert"), None, None),
        ),
        out_specs=(
            P(("groups", "expert"), None, None),
            P(("groups", "expert"), None, None),
            P(("groups", "expert"), None, None),
            P(("groups", "expert"), None, None),
        ),
        check_vma=False,
    )
```

```python
import functools

import jax
import jax.numpy as jnp
from jax import lax
from jax.experimental import pallas as pl
from jax.experimental.pallas import tpu as pltpu
from jax.sharding import PartitionSpec as P

adapter_scale = 2.0
f32 = jnp.float32
bf16 = jnp.bfloat16
i16 = jnp.int16
lanes = 128
counts_lane = 64
kernel_vmem = 32 * 2**20
whole_vmem = 60 * 2**20


def halves(value):
    high = value.astype(bf16)
    return high, (value - high.astype(f32)).astype(bf16)


def dot(a, b, a_dim, b_dim):
    return lax.dot_general(a, b, (((a_dim,), (b_dim,)), ((), ())), preferred_element_type=f32)


def dot_pairs(a, b, a_dim, b_dim):
    return dot(a[0], b[0], a_dim, b_dim) + (dot(a[1], b[0], a_dim, b_dim) + dot(a[0], b[1], a_dim, b_dim))


def encode(down, up, counts=0.0):
    def scaled(value):
        largest = jnp.max(jnp.abs(value), axis=-1, keepdims=True)
        exponent = jnp.ceil(jnp.log2(jnp.maximum(largest, 1e-30)))
        coded = jnp.round(value * jnp.exp2(15.0 - exponent))
        return jnp.clip(coded, -32767.0, 32767.0), exponent

    down, down_exponent = scaled(down)
    up, up_exponent = scaled(up)
    lane = lax.broadcasted_iota(jnp.int32, down.shape[:-1] + (lanes,), down.ndim - 1)
    tail = jnp.where(lane < counts_lane // 2, down_exponent, up_exponent)
    tail = jnp.where(lane < counts_lane, tail, counts)
    return jnp.concatenate([down, up, tail], axis=-1).astype(jnp.int32).astype(i16)


def decode(coded, hidden_width):
    width = coded.shape[-1] - lanes
    value = coded.astype(jnp.int32).astype(f32)
    down_scale = jnp.exp2(value[..., width : width + 1] - 15.0)
    up_scale = jnp.exp2(value[..., width + counts_lane // 2 : width + counts_lane // 2 + 1] - 15.0)
    return value[..., :hidden_width] * down_scale, value[..., hidden_width:width] * up_scale


def prepare_kernel(*refs):
    (piece_ref, small_ref), sem, refs = refs[7:9], refs[-1], refs[:7] + refs[9:-1]
    copies = [pltpu.make_async_copy(refs[i], refs[7 + i], sem.at[i]) for i in range(7)]
    for copy in copies:
        copy.start()
    for copy in copies:
        copy.wait()
    expert, gate, curvature, down_direction, adapter_down, adapter_up, up_direction = [ref[...] for ref in refs[7:]]
    top = expert.shape[0]
    small_ref[...] = jnp.zeros_like(small_ref)
    small_ref[:top] = expert.astype(f32)
    small_ref[top : 2 * top] = gate.astype(f32)
    small_ref[2 * top : 2 * top + 1] = curvature
    lane = lax.broadcasted_iota(jnp.int32, (1, lanes), 1)
    counts = jnp.zeros((1, lanes), f32)
    for number in range(lanes - counts_lane):
        named = jnp.where(expert == number, 1.0, 0.0)
        total = jnp.sum(jnp.sum(named, axis=0, keepdims=True), axis=1, keepdims=True)
        counts = jnp.where(lane == counts_lane + number, total, counts)
    piece_ref[0] = encode(down_direction, adapter_up, counts)
    piece_ref[1] = encode(adapter_down, up_direction, counts)


def token_columns(own_ref, other_ref, top):
    small = jnp.concatenate([own_ref[...], other_ref[...]], axis=1).T
    experts = [small[:, k : k + 1] for k in range(top)]
    gates = [small[:, top + k : top + k + 1] for k in range(top)]
    return experts, gates, small[:, 2 * top : 2 * top + 1]


def members(place_ref, wide, masks):
    slot_of = lax.broadcasted_iota(jnp.int32, (1, wide), 1) // (wide // len(masks))
    found = jnp.zeros((1, wide), jnp.int32)
    for slot, mask in enumerate(masks):
        found = jnp.where(slot_of == slot, place_ref[0] ^ mask, found)
    return found.astype(f32)


def prior_kernel(masks, place_ref, *rest):
    piece_refs, prior_ref = rest[:-1], rest[-1]
    me = place_ref[0]
    slots = len(masks)
    prior_ref[...] = jnp.zeros_like(prior_ref)
    for block, number in enumerate((me, me ^ 1)):
        total = jnp.zeros((1, lanes), f32)
        for offset in range(slots):
            device = place_ref[1 + slots + offset]
            tail = piece_refs[offset][0, :, piece_refs[offset].shape[2] - lanes :]
            counts = tail.astype(jnp.int32).astype(f32)[0:1]
            total = total + jnp.where(device < number, counts, 0.0)
        prior_ref[block : block + 1] = total


def piece_part(refs, offset, kind):
    last = len(refs) - 2
    half = last // 2 + 1
    if offset == half:
        return refs[last + kind][0]
    return refs[offset if offset < half else offset - 1][kind]


def rows_kernel(top, masks, place_ref, small_ref, small_other_ref, hidden_other_ref, gradient_other_ref, piece_ref, *outs):
    same_ref, mask_ref, rank_ref, gate_ref, hidden_ref, gradient_ref, onward_ref, sem = outs
    copies = [
        pltpu.make_async_copy(hidden_other_ref, hidden_ref, sem.at[0]),
        pltpu.make_async_copy(gradient_other_ref, gradient_ref, sem.at[1]),
        pltpu.make_async_copy(piece_ref, onward_ref, sem.at[2]),
    ]
    for copy in copies:
        copy.start()
    rows, tokens = same_ref.shape
    wide = mask_ref.shape[2]
    row = lax.broadcasted_iota(jnp.int32, (rows, tokens), 0)
    same = jnp.where(row // top == lax.broadcasted_iota(jnp.int32, (rows, tokens), 1), 1.0, 0.0).astype(bf16)
    same_ref[...] = same
    column = members(place_ref, wide, masks)
    below = (
        lax.broadcasted_iota(jnp.int32, (tokens, tokens), 0)
        > lax.broadcasted_iota(jnp.int32, (tokens, tokens), 1)
    )
    below = jnp.where(below, 1.0, 0.0).astype(bf16)
    for core, ref in enumerate((small_ref, small_other_ref)):
        small = ref[...].T
        experts = dot(same, small.astype(bf16), 1, 0)
        position = lax.broadcasted_iota(jnp.int32, experts.shape, 0) % top
        own = lax.broadcasted_iota(jnp.int32, experts.shape, 1) == position
        expert = jnp.sum(jnp.where(own, experts, 0.0), axis=1, keepdims=True)
        mask_ref[core] = jnp.where(expert == column, 1.0, 0.0).astype(bf16)
        gate = jnp.zeros((tokens, wide), f32)
        member = jnp.zeros((tokens, wide), f32)
        for k in range(top):
            named = small[:, k : k + 1] == column
            gate = jnp.where(named, small[:, top + k : top + k + 1], gate)
            member = jnp.where(named, 1.0, member)
        gate_ref[core] = gate
        rank_ref[core] = dot(below, member.astype(bf16), 1, 0)
    for copy in copies:
        copy.wait()


def reduce_kernel(top, masks, place_ref, small_ref, small_other_ref, own_ref, other_ref, *rest):
    slots = len(masks)
    piece_refs, (_, reduced_ref, high_ref, low_ref, full_ref) = rest[: slots + 1], rest[slots + 1 :]
    hidden_width = own_ref.shape[1]
    for offset in range(slots):
        slot = place_ref[1 + offset]
        for kind in range(2):
            down, _ = decode(piece_part(piece_refs, offset, kind), hidden_width)
            high_ref[kind, slot], low_ref[kind, slot] = halves(down)
    experts, _, _ = token_columns(small_ref, small_other_ref, top)
    wide = reduced_ref.shape[2]
    column = members(place_ref, wide, masks)
    high = high_ref[...].reshape(2 * wide, hidden_width)
    low = low_ref[...].reshape(2 * wide, hidden_width)
    tokens = own_ref.shape[0] // top
    for core, hidden_ref in enumerate((own_ref, other_ref)):
        full = dot(hidden_ref[...], high, 1, 1) + dot(hidden_ref[...], low, 1, 1)
        full_ref[0], full_ref[1] = full[:, :wide], full[:, wide:]
        tokens_of = slice(core * tokens, (core + 1) * tokens)
        for kind in range(2):
            total = jnp.zeros((tokens, wide), f32)
            for k in range(top):
                here = full_ref[kind, pl.ds(k, tokens, stride=top), :]
                total = jnp.where(experts[k][tokens_of] == column, here, total)
            reduced_ref[kind, tokens_of] = total


def rank_limits(place_ref, masks, wide, capacity_ref, prior_ref, arrived_ref):
    lane = lax.broadcasted_iota(jnp.int32, (1, lanes), 1)
    slot_of = lax.broadcasted_iota(jnp.int32, (1, wide), 1) // (wide // len(masks))
    limits = []
    for block in range(2):
        total = capacity_ref[...] - prior_ref[block : block + 1] - arrived_ref[1 - block : 2 - block]
        limit = jnp.zeros((1, wide), f32)
        for slot, mask in enumerate(masks):
            picked = jnp.where(lane == counts_lane + (place_ref[0] ^ mask), total, 0.0)
            limit = jnp.where(slot_of == slot, jnp.sum(picked, axis=1, keepdims=True), limit)
        limits.append(limit)
    return limits


def tangent_kernel(masks, place_ref, rank_ref, gate_ref, capacity_ref, prior_ref, arrived_ref, reduced_ref, *rest):
    slots = len(masks)
    piece_refs = rest[: slots + 1]
    weight_ref, weighted_ref, tangent_ref, coded_ref, high_ref, low_ref = rest[slots + 1 :]
    _, wide = weight_ref.shape
    model_width = tangent_ref.shape[1]
    hidden_width = piece_refs[0].shape[2] - model_width - lanes
    limits = rank_limits(place_ref, masks, wide, capacity_ref, prior_ref, arrived_ref)
    weights = [
        jnp.where(rank_ref[core] < limits[core], adapter_scale * gate_ref[core], 0.0) for core in range(2)
    ]
    weight = jnp.concatenate(weights, axis=0)
    weight_ref[...] = weight
    weighted = jnp.concatenate([weight * reduced_ref[0], weight * reduced_ref[1]], axis=1)
    weighted_ref[...] = weighted
    for offset in range(slots):
        slot = place_ref[1 + offset]
        for kind in range(2):
            _, up = decode(piece_part(piece_refs, offset, kind), hidden_width)
            high_ref[kind, slot], low_ref[kind, slot] = halves(up)
    factor = high_ref[...].reshape(2 * wide, model_width), low_ref[...].reshape(2 * wide, model_width)
    tangent = dot_pairs(halves(weighted), factor, 1, 0)
    tangent_ref[...] = tangent
    coded_ref[...] = tangent.astype(bf16)


def put_left(left_ref, same_ref, mask_ref, terms):
    both = jnp.concatenate(halves(terms), axis=1)
    tokens = terms.shape[0] // 2
    for core in range(2):
        repeated = dot(same_ref[...], both[core * tokens : (core + 1) * tokens], 1, 0).astype(bf16)
        mask = mask_ref[core]
        left_ref[core] = repeated * jnp.concatenate([mask, mask], axis=1)


def add_halves(both):
    middle = both.shape[0] // 2
    return both[:middle] + both[middle:]


def put_chunks(keep_ref, chunk_ref, far_ref, near_ref, kind, down, up):
    far, rank, _ = chunk_ref.shape
    rows = down.shape[0] // rank // 2

    def slot(number):
        start = number * rank
        return down[start : start + rank], up[start : start + rank]

    for x in range(2):
        keep_ref[x] = jnp.concatenate(slot(x * rows), axis=1)
        for z in range(1, rows - far):
            near_ref[z - 1, kind, x] = encode(*slot(x * rows + z))
    for place in range(far):
        chunk_ref[place] = jnp.concatenate(slot(rows - far + place), axis=1)
        far_ref[place] = encode(*slot(2 * rows - far + place))


def gradient_kernel(
    same_ref,
    mask_ref,
    own_ref,
    other_ref,
    own_gradient_ref,
    other_gradient_ref,
    weight_ref,
    weighted_ref,
    high_ref,
    low_ref,
    keep_ref,
    chunk_ref,
    far_ref,
    near_ref,
    up_ref,
    to_ref,
    left_ref,
):
    wide = weight_ref.shape[1]
    model_width = up_ref.shape[1]
    gradient = jnp.concatenate([own_gradient_ref[...], other_gradient_ref[...]], axis=0)
    high = high_ref[...].reshape(2 * wide, model_width)
    low = low_ref[...].reshape(2 * wide, model_width)
    to_both = dot(gradient, high, 1, 1) + dot(gradient, low, 1, 1)
    to_ref[...] = to_both[:, wide:]
    put_left(left_ref, same_ref, mask_ref, weight_ref[...] * to_both[:, :wide])
    down = dot(left_ref[0], own_ref[...], 0, 0) + dot(left_ref[1], other_ref[...], 0, 0)
    up = add_halves(dot(jnp.concatenate(halves(weighted_ref[...]), axis=1), gradient, 0, 0))
    up_ref[...] = up[:wide]
    put_chunks(keep_ref, chunk_ref, far_ref, near_ref, 0, add_halves(down), up[wide:])


def curvature_kernel(
    top,
    small_ref,
    small_other_ref,
    same_ref,
    mask_ref,
    own_ref,
    other_ref,
    weight_ref,
    weighted_ref,
    high_ref,
    low_ref,
    up_ref,
    to_ref,
    tangent_ref,
    arrived_ref,
    gradient_near_ref,
    keep_ref,
    chunk_ref,
    far_ref,
    near_ref,
    left_ref,
):
    near_ref[:, 0:1] = gradient_near_ref[...]
    _, _, curvature = token_columns(small_ref, small_other_ref, top)
    tokens, wide = weight_ref.shape
    block = tokens // 2
    model_width = up_ref.shape[1]
    arrived = jnp.concatenate([arrived_ref[block:], arrived_ref[:block]], axis=0).astype(f32)
    resid = halves(curvature * (tangent_ref[...] + arrived))
    adapter_up = high_ref[0].reshape(wide, model_width), low_ref[0].reshape(wide, model_width)
    put_left(left_ref, same_ref, mask_ref, weight_ref[...] * (dot_pairs(resid, adapter_up, 1, 1) + to_ref[...]))
    down = dot(left_ref[0], own_ref[...], 0, 0) + dot(left_ref[1], other_ref[...], 0, 0)
    weighted_u = halves(weighted_ref[:, wide:])
    up = add_halves(dot(jnp.concatenate(weighted_u, axis=1), resid[0], 0, 0)) + dot(weighted_u[0], resid[1], 0, 0)
    put_chunks(keep_ref, chunk_ref, far_ref, near_ref, 1, add_halves(down), up_ref[...] + up)


def far_kernel(hidden_width, arrived_ref, chunk_ref, _, *out_refs):
    for place, out_ref in enumerate(out_refs):
        down, up = decode(arrived_ref[place], hidden_width)
        own = chunk_ref[place]
        out_ref[...] = encode(own[:, :hidden_width] + down, own[:, hidden_width:] + up)


def near_kernel(hidden_width, gradient_ref, curvature_ref, *rest):
    arrived_refs, (_, across_ref, total_ref) = rest[:-3], rest[-3:]
    for kind, keep_ref in enumerate((gradient_ref, curvature_ref)):
        for x in range(2):
            down, up = keep_ref[x, :, :hidden_width], keep_ref[x, :, hidden_width:]
            for ref in arrived_refs:
                more = decode(ref[kind, x], hidden_width)
                down, up = down + more[0], up + more[1]
            if x == 0:
                total_ref[kind] = jnp.concatenate([down, up], axis=1)
            else:
                across_ref[kind] = encode(down, up)


def add_kernel(hidden_width, *refs):
    coded_refs, total_ref = refs[:-2], refs[-1]
    parts = [decode(ref[...], hidden_width) for ref in coded_refs]
    total_ref[:, :hidden_width] = sum(part[0] for part in parts)
    total_ref[:, hidden_width:] = sum(part[1] for part in parts)


def total_kernel(hidden_width, own_ref, gradient_ref, curvature_ref, across_ref, *out_refs):
    for kind, far_ref in enumerate((gradient_ref, curvature_ref)):
        total = own_ref[kind] + far_ref[...]
        down, up = decode(across_ref[kind], hidden_width)
        out_refs[2 * kind][...] = total[:, :hidden_width] + down
        out_refs[2 * kind + 1][...] = total[:, hidden_width:] + up


class Ring:
    def __init__(self, size):
        self.length = size // 2
        rows = self.length // 2
        self.order = [4 * z for z in range(rows)] + [4 * z + 2 for z in reversed(range(rows))]

    def shift(self, value, step):
        pairs = [
            (chip + core, self.order[(place + step) % self.length] + core)
            for place, chip in enumerate(self.order)
            for core in range(2)
        ]
        return lax.ppermute(value, "expert", pairs)

    def members(self, me):
        rows = self.length // 2
        place = jnp.where(me // 2 % 2 == 0, me // 4, self.length - 1 - me // 4)
        there = (place + jnp.arange(self.length, dtype=jnp.int32)) % self.length
        return jnp.where(there < rows, 4 * there, 4 * (self.length - 1 - there) + 2) + me % 2

    def gather(self, own, passing):
        half = self.length // 2
        found = {0: own}
        ahead, behind = own, own
        for step in range(1, half):
            behind = self.shift(behind, 1)
            ahead = self.shift(ahead, -1)
            if step == 1:
                ahead = passing(ahead)
            found[self.length - step], found[step] = behind, ahead
        last = [self.shift(behind[:1], 1), self.shift(ahead[1:], -1)]
        return [found[offset] for offset in sorted(found)] + last


def exchange(value, mask):
    size = lax.axis_size("expert")
    return lax.ppermute(value, "expert", [(device, device ^ mask) for device in range(size)])


def gathered_plan(
    hidden_of_route,
    expert_of_route,
    gate_of_route,
    capacity,
    output_gradient,
    curvature,
    adapter_down,
    adapter_up,
    down_direction,
    up_direction,
):
    ring = Ring(lax.axis_size("expert"))
    slots = ring.length
    rows = slots // 2
    far = rows // 2
    masks = [4 * z for z in range(rows)] + [4 * z + 2 for z in range(rows)]
    me = lax.axis_index("expert")
    tokens, top = expert_of_route.shape
    both = 2 * tokens
    hidden_width = hidden_of_route.shape[2]
    rank = adapter_down.shape[2]
    model_width = output_gradient.shape[1]
    experts = capacity.shape[0]
    wide = slots * rank
    coded_width = hidden_width + model_width + lanes

    ring_members = ring.members(me)
    differs = ring_members ^ me
    slot_of_offset = differs // 4 + rows * (differs // 2 % 2)
    place = jnp.concatenate([me[None], slot_of_offset, ring_members]).astype(jnp.int32)

    def call(kernel, multiplies, outs, *operands, scratch=(), after=(), grant=kernel_vmem):
        space = pltpu.HBM if kernel is prepare_kernel else pltpu.VMEM
        places = [
            pl.BlockSpec(memory_space=pltpu.SMEM if operand is place else space) for operand in operands
        ] + [pl.BlockSpec(memory_space=pl.ANY) for _ in after]
        return pl.pallas_call(
            kernel,
            out_shape=[jax.ShapeDtypeStruct(shape, dtype) for shape, dtype in outs],
            in_specs=places,
            scratch_shapes=scratch,
            compiler_params=pltpu.CompilerParams(vmem_limit_bytes=grant),
            cost_estimate=pl.CostEstimate(flops=2 * multiplies, bytes_accessed=2**20, transcendentals=0),
        )(*operands, *after)

    down_multiplies = 2 * top * both * hidden_width * wide
    up_multiplies = both * model_width * wide

    first = (
        expert_of_route.T,
        gate_of_route.T,
        curvature[None],
        down_direction[0].T,
        adapter_down[0].T,
        adapter_up[0],
        up_direction[0],
    )
    piece, small = call(
        prepare_kernel,
        10**8,
        [((2, rank, coded_width), i16), (((2 * top + 8) // 8 * 8, tokens), f32)],
        *first,
        scratch=[pltpu.VMEM(operand.shape, operand.dtype) for operand in first]
        + [pltpu.SemaphoreType.DMA((len(first),))],
        grant=whole_vmem,
    )
    small_other = exchange(small, 1)
    hidden = hidden_of_route.reshape(tokens * top, hidden_width)
    beside = []

    def passing(piece):
        *made, onward = call(
            functools.partial(rows_kernel, top, masks),
            10**9,
            [
                ((tokens * top, tokens), bf16),
                ((2, tokens * top, wide), bf16),
                ((2, tokens, wide), f32),
                ((2, tokens, wide), f32),
                ((tokens * top, hidden_width), bf16),
                ((tokens, model_width), bf16),
                (piece.shape, i16),
            ],
            place,
            small,
            small_other,
            exchange(hidden, 1),
            exchange(output_gradient, 1),
            piece,
            scratch=[pltpu.SemaphoreType.DMA((3,))],
        )
        beside.extend(made)
        return onward

    pieces = ring.gather(piece, passing)
    same, mask, local_rank, gate, hidden_other, gradient_other = beside
    capacity_row = jnp.pad(capacity.astype(f32), (counts_lane, lanes - counts_lane - experts))[None, :]

    by_offset = pieces[:rows] + [pieces[-2]] + pieces[rows:-2]
    (prior,) = call(functools.partial(prior_kernel, masks), 10**8, [((8, lanes), f32)], place, *by_offset)
    prior_arrived = exchange(prior, 1)
    factor_halves = [pltpu.VMEM((2, slots, rank, hidden_width), bf16)] * 2
    (reduced,) = call(
        functools.partial(reduce_kernel, top, masks),
        2 * down_multiplies,
        [((2, both, wide), f32)],
        place,
        small,
        small_other,
        hidden,
        hidden_other,
        *pieces,
        scratch=factor_halves + [pltpu.VMEM((2, tokens * top, wide), f32)],
        after=[prior],
    )
    weight, weighted, tangent, coded, high, low = call(
        functools.partial(tangent_kernel, masks),
        6 * up_multiplies,
        [
            ((both, wide), f32),
            ((both, 2 * wide), f32),
            ((both, model_width), f32),
            ((both, model_width), bf16),
            ((2, slots, rank, model_width), bf16),
            ((2, slots, rank, model_width), bf16),
        ],
        place,
        local_rank,
        gate,
        capacity_row,
        prior,
        prior_arrived,
        reduced,
        *pieces,
    )
    arrived = exchange(coded, 1)
    left = [pltpu.VMEM((2, top * tokens, 2 * wide), bf16)]
    def chunks(kinds):
        return [
            ((2, rank, hidden_width + model_width), f32),
            ((far, rank, hidden_width + model_width), f32),
            ((far, rank, coded_width), i16),
            ((rows - far - 1, kinds, 2, rank, coded_width), i16),
        ]

    gradient_keep, gradient_chunk, gradient_far, near, up, to = call(
        gradient_kernel,
        down_multiplies + 8 * up_multiplies,
        chunks(1) + [((wide, model_width), f32), ((both, wide), f32)],
        same,
        mask,
        hidden,
        hidden_other,
        output_gradient,
        gradient_other,
        weight,
        weighted,
        high,
        low,
        scratch=left,
    )
    gradient_far = exchange(gradient_far, 2)
    curvature_keep, curvature_chunk, curvature_far, near = call(
        functools.partial(curvature_kernel, top),
        down_multiplies + 6 * up_multiplies,
        chunks(2),
        small,
        small_other,
        same,
        mask,
        hidden,
        hidden_other,
        weight,
        weighted,
        high,
        low,
        up,
        to,
        tangent,
        arrived,
        near,
        scratch=left,
    )

    hop = 2 * 10**9

    def along_z(arrived, own, after):
        sums = call(
            functools.partial(far_kernel, hidden_width),
            hop,
            [((rank, coded_width), i16)] * far,
            arrived,
            own,
            after=[after],
        )
        return sums[0], [exchange(part, 4 * z) for z, part in zip(range(rows - far, rows), sums)]

    def added(parts, after):
        return call(
            functools.partial(add_kernel, hidden_width),
            hop,
            [((rank, hidden_width + model_width), f32)],
            *parts,
            after=[after],
        )[0]

    curvature_far = exchange(curvature_far, 2)
    near_parts = [exchange(near[z - 1], 4 * z) for z in range(1, rows - far)]
    done, gradient_parts = along_z(gradient_far, gradient_chunk, near)
    done, curvature_parts = along_z(curvature_far, curvature_chunk, done)
    across, total = call(
        functools.partial(near_kernel, hidden_width),
        hop,
        [((2, rank, coded_width), i16), ((2, rank, hidden_width + model_width), f32)],
        gradient_keep,
        curvature_keep,
        *near_parts,
        after=[done],
    )
    gradient_total = added(gradient_parts, across)
    curvature_total = added(curvature_parts, gradient_total)
    down_gradient, up_gradient, curvature_down, curvature_up = call(
        functools.partial(total_kernel, hidden_width),
        hop,
        [((rank, hidden_width), f32), ((rank, model_width), f32)] * 2,
        total,
        gradient_total,
        curvature_total,
        exchange(across, 2),
    )
    return down_gradient.T[None], up_gradient[None], curvature_down.T[None], curvature_up[None]


def carried_in(value, axis, join, neutral):
    count, mine = (lax.axis_size(axis), lax.axis_index(axis))
    pieces = lax.all_gather(value, axis)
    so_far = jnp.full_like(value, 0) + jnp.asarray(neutral, value.dtype)

    def lap(position, so_far):
        longer = join(so_far, pieces[position])
        return jnp.where(position < mine, longer, so_far)

    return lax.fori_loop(0, count - 1, lap, so_far)


def add_counts(earlier, later):
    return earlier + later


def routed_plan(
    hidden_of_route,
    expert_of_route,
    gate_of_route,
    capacity,
    output_gradient,
    curvature,
    adapter_down,
    adapter_up,
    down_direction,
    up_direction,
):
    finest_precision = lax.Precision.HIGHEST
    group_size = lax.axis_size("expert")
    tok_rows, top_count = expert_of_route.shape
    hidden_width = hidden_of_route.shape[2]
    resident_experts = adapter_down.shape[0]
    adapter_rank = adapter_down.shape[2]
    model_width = output_gradient.shape[1]
    experts = resident_experts * group_size
    slot_most = 2 * tok_rows * top_count // experts
    routes = expert_of_route.reshape(-1)
    onehot = (routes[:, None] == jnp.arange(experts, dtype=jnp.int32)[None, :]).astype(jnp.int32)
    earlier = jnp.cumsum(onehot, axis=0) - onehot
    local_rank = jnp.sum(earlier * onehot, axis=1)
    counts = jnp.sum(onehot, axis=0)
    prior_count = carried_in(counts, "expert", add_counts, jnp.zeros_like(counts))
    global_rank = local_rank + jnp.sum(onehot * prior_count[None, :], axis=1)
    route_limit = jnp.sum(onehot * capacity[None, :], axis=1)
    retained_mask = (global_rank < route_limit).astype(jnp.float32)
    weight_of_route = (
        adapter_scale * gate_of_route.reshape(-1).astype(jnp.float32) * retained_mask
    ).astype(jnp.bfloat16)
    slot_index = routes * slot_most + local_rank
    layout = (group_size, resident_experts, slot_most)
    send_hidden = (
        jnp.zeros((experts * slot_most, hidden_width), jnp.bfloat16)
        .at[slot_index]
        .set(hidden_of_route.reshape(-1, hidden_width))
        .reshape(layout + (hidden_width,))
    )
    send_weight = (
        jnp.zeros((experts * slot_most,), jnp.bfloat16)
        .at[slot_index]
        .set(weight_of_route)
        .reshape(layout)
    )
    down_stacked = jnp.concatenate([adapter_down, down_direction], axis=2)
    up_stacked = jnp.concatenate([adapter_up, up_direction], axis=1)

    def spread(token_rows):
        per_route = jnp.repeat(token_rows, top_count, axis=0)
        placed = (
            jnp.zeros((experts * slot_most, model_width), jnp.bfloat16)
            .at[slot_index]
            .set(per_route)
        )
        return placed.reshape(layout + (model_width,))

    send_residual = spread(output_gradient)
    pieces = (
        lax.all_to_all(send_hidden, "expert", split_axis=0, concat_axis=0, tiled=True),
        lax.all_to_all(send_weight, "expert", split_axis=0, concat_axis=0, tiled=True),
    )
    hidden_rows = pieces[0].astype(jnp.float32)
    weight_rows = pieces[1].astype(jnp.float32)[..., None]
    reduced_hidden = jnp.einsum(
        "cjif,jfk->cjik", hidden_rows, down_stacked, precision=finest_precision
    )
    exchanged_rows = jnp.concatenate(
        [reduced_hidden[..., adapter_rank:], reduced_hidden[..., :adapter_rank]], axis=3
    )
    tangent_out = weight_rows * jnp.einsum(
        "cjik,jkd->cjid", exchanged_rows, up_stacked, precision=finest_precision
    )
    returned = lax.all_to_all(
        tangent_out.astype(jnp.bfloat16), "expert", split_axis=0, concat_axis=0, tiled=True
    )
    results = (returned, reduced_hidden) + tuple(pieces)
    returned = results[0]
    reduced_hidden = results[1]
    hidden_rows = results[2]
    weight_rows = results[3]
    route_tangent = returned.reshape(experts * slot_most, model_width)[slot_index]
    out_tangent = jnp.sum(
        route_tangent.reshape(tok_rows, top_count, model_width).astype(jnp.float32), axis=1
    )
    resid_tangent = (curvature[:, None] * out_tangent).astype(jnp.bfloat16)
    send_tangent = spread(resid_tangent)
    residual_rows, tangent_rows = (
        lax.all_to_all(send_residual, "expert", split_axis=0, concat_axis=0, tiled=True),
        lax.all_to_all(send_tangent, "expert", split_axis=0, concat_axis=0, tiled=True),
    )
    residual_full = residual_rows.astype(jnp.float32)
    complete_tangent = tangent_rows.astype(jnp.float32)
    weight_column = weight_rows.astype(jnp.float32)[..., None]
    residual_reduced = jnp.einsum(
        "wyov,yqv->wyoq", residual_full, up_stacked, precision=finest_precision
    )
    reduced_tangent = jnp.einsum(
        "wyov,yqv->wyoq", complete_tangent, adapter_up, precision=finest_precision
    )
    left_terms = jnp.concatenate(
        [
            weight_column * residual_reduced[..., :adapter_rank],
            weight_column * (reduced_tangent + residual_reduced[..., adapter_rank:]),
        ],
        axis=3,
    )
    down_terms = jnp.einsum(
        "cjif,cjik->jfk", hidden_rows.astype(jnp.float32), left_terms, precision=finest_precision
    )
    raised_update = weight_column * reduced_hidden[..., :adapter_rank]
    raised_tangent_update = weight_column * reduced_hidden[..., adapter_rank:]
    up_terms = jnp.einsum(
        "cjik,cjid->jkd",
        jnp.concatenate([raised_update, raised_tangent_update], axis=3),
        residual_full,
        precision=finest_precision,
    )
    curvature_piece = up_terms[:, adapter_rank:] + jnp.einsum(
        "cjik,cjid->jkd", raised_update, complete_tangent, precision=finest_precision
    )
    return (
        down_terms[..., :adapter_rank],
        up_terms[:, :adapter_rank],
        down_terms[..., adapter_rank:],
        curvature_piece,
    )


def local(*arguments):
    factor_bytes = 2 * 4 * (arguments[6].size + arguments[7].size) * lax.axis_size("expert")
    plan = gathered_plan if 4 * factor_bytes <= kernel_vmem else routed_plan
    return plan(*arguments)


def solution(mesh):
    return jax.shard_map(
        local,
        mesh=mesh,
        in_specs=(
            P(("groups", "expert"), None, None),
            P(("groups", "expert"), None),
            P(("groups", "expert"), None),
            P("groups"),
            P(("groups", "expert"), None),
            P(("groups", "expert")),
            P("expert", None, None),
            P("expert", None, None),
            P(("groups", "expert"), None, None),
            P(("groups", "expert"), None, None),
        ),
        out_specs=(
            P(("groups", "expert"), None, None),
            P(("groups", "expert"), None, None),
            P(("groups", "expert"), None, None),
            P(("groups", "expert"), None, None),
        ),
        check_vma=False,
    )
```

```python
import functools

import jax
import jax.numpy as jnp
from jax import lax
from jax.experimental import pallas as pl
from jax.experimental.pallas import tpu as pltpu
from jax.sharding import PartitionSpec as P

adapter_scale = 2.0
f32 = jnp.float32
bf16 = jnp.bfloat16
i16 = jnp.int16
lanes = 128
counts_lane = 64
kernel_vmem = 32 * 2**20
whole_vmem = 60 * 2**20


def halves(value):
    high = value.astype(bf16)
    return high, (value - high.astype(f32)).astype(bf16)


def dot(a, b, a_dim, b_dim):
    return lax.dot_general(a, b, (((a_dim,), (b_dim,)), ((), ())), preferred_element_type=f32)


def dot_pairs(a, b, a_dim, b_dim):
    return dot(a[0], b[0], a_dim, b_dim) + (dot(a[1], b[0], a_dim, b_dim) + dot(a[0], b[1], a_dim, b_dim))


def encode(down, up, counts=0.0):
    def scaled(value):
        largest = jnp.max(jnp.abs(value), axis=-1, keepdims=True)
        exponent = jnp.ceil(jnp.log2(jnp.maximum(largest, 1e-30)))
        coded = jnp.round(value * jnp.exp2(15.0 - exponent))
        return jnp.clip(coded, -32767.0, 32767.0), exponent

    down, down_exponent = scaled(down)
    up, up_exponent = scaled(up)
    lane = lax.broadcasted_iota(jnp.int32, down.shape[:-1] + (lanes,), down.ndim - 1)
    tail = jnp.where(lane < counts_lane // 2, down_exponent, up_exponent)
    tail = jnp.where(lane < counts_lane, tail, counts)
    return jnp.concatenate([down, up, tail], axis=-1).astype(jnp.int32).astype(i16)


def decode(coded, hidden_width):
    width = coded.shape[-1] - lanes
    value = coded.astype(jnp.int32).astype(f32)
    down_scale = jnp.exp2(value[..., width : width + 1] - 15.0)
    up_scale = jnp.exp2(value[..., width + counts_lane // 2 : width + counts_lane // 2 + 1] - 15.0)
    return value[..., :hidden_width] * down_scale, value[..., hidden_width:width] * up_scale


def prepare_kernel(*refs):
    (piece_ref, small_ref), sem, refs = refs[7:9], refs[-1], refs[:7] + refs[9:-1]
    copies = [pltpu.make_async_copy(refs[i], refs[7 + i], sem.at[i]) for i in range(7)]
    for copy in copies:
        copy.start()
    for copy in copies:
        copy.wait()
    expert, gate, curvature, down_direction, adapter_down, adapter_up, up_direction = [ref[...] for ref in refs[7:]]
    top = expert.shape[0]
    small_ref[...] = jnp.zeros_like(small_ref)
    small_ref[:top] = expert.astype(f32)
    small_ref[top : 2 * top] = gate.astype(f32)
    small_ref[2 * top : 2 * top + 1] = curvature
    lane = lax.broadcasted_iota(jnp.int32, (1, lanes), 1)
    counts = jnp.zeros((1, lanes), f32)
    for number in range(lanes - counts_lane):
        named = jnp.where(expert == number, 1.0, 0.0)
        total = jnp.sum(jnp.sum(named, axis=0, keepdims=True), axis=1, keepdims=True)
        counts = jnp.where(lane == counts_lane + number, total, counts)
    piece_ref[0] = encode(down_direction, adapter_up, counts)
    piece_ref[1] = encode(adapter_down, up_direction, counts)


def token_columns(small_ref, top):
    experts = [small_ref[:, k : k + 1] for k in range(top)]
    gates = [small_ref[:, top + k : top + k + 1] for k in range(top)]
    return experts, gates, small_ref[:, 2 * top : 2 * top + 1]


def members(place_ref, wide, masks):
    slot_of = lax.broadcasted_iota(jnp.int32, (1, wide), 1) // (wide // len(masks))
    found = jnp.zeros((1, wide), jnp.int32)
    for slot, mask in enumerate(masks):
        found = jnp.where(slot_of == slot, place_ref[0] ^ mask, found)
    return found.astype(f32)


def prior_kernel(masks, place_ref, *rest):
    piece_refs, prior_ref = rest[:-1], rest[-1]
    me = place_ref[0]
    slots = len(masks)
    prior_ref[...] = jnp.zeros_like(prior_ref)
    for block, number in enumerate((me, me ^ 1)):
        total = jnp.zeros((1, lanes), f32)
        for offset in range(slots):
            device = place_ref[1 + slots + offset]
            tail = piece_refs[offset][0, :, piece_refs[offset].shape[2] - lanes :]
            counts = tail.astype(jnp.int32).astype(f32)[0:1]
            total = total + jnp.where(device < number, counts, 0.0)
        prior_ref[block : block + 1] = total


def piece_part(refs, offset, kind):
    last = len(refs) - 2
    half = last // 2 + 1
    if offset == half:
        return refs[last + kind][0]
    return refs[offset if offset < half else offset - 1][kind]


def tokens_kernel(top, masks, place_ref, own_ref, other_ref, piece_ref, *rest):
    small_ref, rank_ref, gate_ref, onward_ref = rest[-4:]
    onward_ref[...] = piece_ref[...]
    small_ref[...] = jnp.concatenate([own_ref[...], other_ref[...]], axis=1).T
    experts, gates, _ = token_columns(small_ref, top)
    _, tokens, wide = rank_ref.shape
    column = members(place_ref, wide, masks)
    below = (
        lax.broadcasted_iota(jnp.int32, (tokens, tokens), 0)
        > lax.broadcasted_iota(jnp.int32, (tokens, tokens), 1)
    )
    below = jnp.where(below, 1.0, 0.0).astype(bf16)
    for core in range(2):
        tokens_of = slice(core * tokens, (core + 1) * tokens)
        gate = jnp.zeros((tokens, wide), f32)
        member = jnp.zeros((tokens, wide), f32)
        for k in range(top):
            named = experts[k][tokens_of] == column
            gate = jnp.where(named, gates[k][tokens_of], gate)
            member = jnp.where(named, 1.0, member)
        gate_ref[core] = gate
        rank_ref[core] = dot(below, member.astype(bf16), 1, 0)


def reduce_kernel(top, masks, place_ref, small_ref, own_ref, other_ref, *rest):
    slots = len(masks)
    piece_refs, (_, reduced_ref, high_ref, low_ref, full_ref) = rest[: slots + 1], rest[slots + 1 :]
    hidden_width = own_ref.shape[1]
    for offset in range(slots):
        slot = place_ref[1 + offset]
        for kind in range(2):
            down, _ = decode(piece_part(piece_refs, offset, kind), hidden_width)
            high_ref[kind, slot], low_ref[kind, slot] = halves(down)
    experts, _, _ = token_columns(small_ref, top)
    wide = reduced_ref.shape[2]
    column = members(place_ref, wide, masks)
    high = high_ref[...].reshape(2 * wide, hidden_width)
    low = low_ref[...].reshape(2 * wide, hidden_width)
    tokens = own_ref.shape[0] // top
    for core, hidden_ref in enumerate((own_ref, other_ref)):
        full = dot(hidden_ref[...], high, 1, 1) + dot(hidden_ref[...], low, 1, 1)
        full_ref[0], full_ref[1] = full[:, :wide], full[:, wide:]
        tokens_of = slice(core * tokens, (core + 1) * tokens)
        for kind in range(2):
            total = jnp.zeros((tokens, wide), f32)
            for k in range(top):
                here = full_ref[kind, pl.ds(k, tokens, stride=top), :]
                total = jnp.where(experts[k][tokens_of] == column, here, total)
            reduced_ref[kind, tokens_of] = total


def rank_limits(place_ref, masks, wide, capacity_ref, prior_ref, arrived_ref):
    lane = lax.broadcasted_iota(jnp.int32, (1, lanes), 1)
    slot_of = lax.broadcasted_iota(jnp.int32, (1, wide), 1) // (wide // len(masks))
    limits = []
    for block in range(2):
        total = capacity_ref[...] - prior_ref[block : block + 1] - arrived_ref[1 - block : 2 - block]
        limit = jnp.zeros((1, wide), f32)
        for slot, mask in enumerate(masks):
            picked = jnp.where(lane == counts_lane + (place_ref[0] ^ mask), total, 0.0)
            limit = jnp.where(slot_of == slot, jnp.sum(picked, axis=1, keepdims=True), limit)
        limits.append(limit)
    return limits


def tangent_kernel(masks, place_ref, rank_ref, gate_ref, capacity_ref, prior_ref, arrived_ref, reduced_ref, *rest):
    slots = len(masks)
    piece_refs = rest[: slots + 1]
    weight_ref, weighted_ref, tangent_ref, coded_ref, high_ref, low_ref = rest[slots + 1 :]
    _, wide = weight_ref.shape
    model_width = tangent_ref.shape[1]
    hidden_width = piece_refs[0].shape[2] - model_width - lanes
    limits = rank_limits(place_ref, masks, wide, capacity_ref, prior_ref, arrived_ref)
    weights = [
        jnp.where(rank_ref[core] < limits[core], adapter_scale * gate_ref[core], 0.0) for core in range(2)
    ]
    weight = jnp.concatenate(weights, axis=0)
    weight_ref[...] = weight
    weighted = jnp.concatenate([weight * reduced_ref[0], weight * reduced_ref[1]], axis=1)
    weighted_ref[...] = weighted
    for offset in range(slots):
        slot = place_ref[1 + offset]
        for kind in range(2):
            _, up = decode(piece_part(piece_refs, offset, kind), hidden_width)
            high_ref[kind, slot], low_ref[kind, slot] = halves(up)
    factor = high_ref[...].reshape(2 * wide, model_width), low_ref[...].reshape(2 * wide, model_width)
    tangent = dot_pairs(halves(weighted), factor, 1, 0)
    tangent_ref[...] = tangent
    coded_ref[...] = tangent.astype(bf16)


def put_left(left_ref, wide_ref, top, masks, place_ref, small_ref, terms):
    experts, _, _ = token_columns(small_ref, top)
    tokens, wide = terms.shape[0] // 2, terms.shape[1]
    column = members(place_ref, wide, masks)
    for core in range(2):
        tokens_of = slice(core * tokens, (core + 1) * tokens)
        for k in range(top):
            named = experts[k][tokens_of] == column
            wide_ref[core, pl.ds(k, tokens, stride=top), :] = jnp.where(named, terms[tokens_of], 0.0)
        left_ref[core] = jnp.concatenate(halves(wide_ref[core]), axis=1)


def add_halves(both):
    middle = both.shape[0] // 2
    return both[:middle] + both[middle:]


def put_chunks(keep_ref, chunk_ref, far_ref, near_ref, kind, down, up):
    rank = keep_ref.shape[1]
    rows = down.shape[0] // rank // 2

    def slot(number):
        start = number * rank
        return down[start : start + rank], up[start : start + rank]

    for x in range(2):
        keep_ref[x] = jnp.concatenate(slot(x * rows), axis=1)
        chunk_ref[x] = jnp.concatenate(slot(x * rows + 2), axis=1)
        far_ref[x] = encode(*slot(x * rows + 3))
        near_ref[kind, x] = encode(*slot(x * rows + 1))


def gradient_kernel(
    top,
    masks,
    place_ref,
    small_ref,
    own_ref,
    other_ref,
    own_gradient_ref,
    other_gradient_ref,
    weight_ref,
    weighted_ref,
    high_ref,
    low_ref,
    keep_ref,
    chunk_ref,
    far_ref,
    near_ref,
    up_ref,
    to_ref,
    left_ref,
    wide_ref,
):
    wide = weight_ref.shape[1]
    model_width = up_ref.shape[1]
    gradient = jnp.concatenate([own_gradient_ref[...], other_gradient_ref[...]], axis=0)
    high = high_ref[...].reshape(2 * wide, model_width)
    low = low_ref[...].reshape(2 * wide, model_width)
    to_both = dot(gradient, high, 1, 1) + dot(gradient, low, 1, 1)
    to_ref[...] = to_both[:, wide:]
    put_left(left_ref, wide_ref, top, masks, place_ref, small_ref, weight_ref[...] * to_both[:, :wide])
    down = dot(left_ref[0], own_ref[...], 0, 0) + dot(left_ref[1], other_ref[...], 0, 0)
    up = add_halves(dot(jnp.concatenate(halves(weighted_ref[...]), axis=1), gradient, 0, 0))
    up_ref[...] = up[:wide]
    put_chunks(keep_ref, chunk_ref, far_ref, near_ref, 0, add_halves(down), up[wide:])


def curvature_kernel(
    top,
    masks,
    place_ref,
    small_ref,
    own_ref,
    other_ref,
    weight_ref,
    weighted_ref,
    high_ref,
    low_ref,
    up_ref,
    to_ref,
    tangent_ref,
    arrived_ref,
    gradient_near_ref,
    keep_ref,
    chunk_ref,
    far_ref,
    near_ref,
    left_ref,
    wide_ref,
):
    near_ref[0:1] = gradient_near_ref[...]
    _, _, curvature = token_columns(small_ref, top)
    tokens, wide = weight_ref.shape
    block = tokens // 2
    model_width = up_ref.shape[1]
    arrived = jnp.concatenate([arrived_ref[block:], arrived_ref[:block]], axis=0).astype(f32)
    resid = halves(curvature * (tangent_ref[...] + arrived))
    adapter_up = high_ref[0].reshape(wide, model_width), low_ref[0].reshape(wide, model_width)
    terms = weight_ref[...] * (dot_pairs(resid, adapter_up, 1, 1) + to_ref[...])
    put_left(left_ref, wide_ref, top, masks, place_ref, small_ref, terms)
    down = dot(left_ref[0], own_ref[...], 0, 0) + dot(left_ref[1], other_ref[...], 0, 0)
    weighted_u = halves(weighted_ref[:, wide:])
    up = add_halves(dot(jnp.concatenate(weighted_u, axis=1), resid[0], 0, 0)) + dot(weighted_u[0], resid[1], 0, 0)
    put_chunks(keep_ref, chunk_ref, far_ref, near_ref, 1, add_halves(down), up_ref[...] + up)


def pair_kernel(hidden_width, arrived_ref, chunk_ref, _, across_ref, keep_ref):
    for x in range(2):
        down, up = decode(arrived_ref[x], hidden_width)
        down, up = chunk_ref[x, :, :hidden_width] + down, chunk_ref[x, :, hidden_width:] + up
        if x == 0:
            keep_ref[...] = jnp.concatenate([down, up], axis=1)
        else:
            across_ref[...] = encode(down, up)


def far_kernel(hidden_width, arrived_ref, keep_ref, _, out_ref):
    down, up = decode(arrived_ref[...], hidden_width)
    out_ref[...] = encode(keep_ref[:, :hidden_width] + down, keep_ref[:, hidden_width:] + up)


def near_kernel(hidden_width, arrived_ref, gradient_ref, curvature_ref, _, across_ref, total_ref):
    for kind, keep_ref in enumerate((gradient_ref, curvature_ref)):
        for x in range(2):
            down, up = decode(arrived_ref[kind, x], hidden_width)
            down, up = keep_ref[x, :, :hidden_width] + down, keep_ref[x, :, hidden_width:] + up
            if x == 0:
                total_ref[kind] = jnp.concatenate([down, up], axis=1)
            else:
                across_ref[kind] = encode(down, up)


def add_kernel(hidden_width, total_ref, arrived_ref, _, out_ref):
    down, up = decode(arrived_ref[...], hidden_width)
    out_ref[:, :hidden_width] = total_ref[0, :, :hidden_width] + down
    out_ref[:, hidden_width:] = total_ref[0, :, hidden_width:] + up


def total_kernel(hidden_width, gradient_ref, total_ref, far_ref, across_ref, *out_refs):
    far = decode(far_ref[...], hidden_width)
    totals = [
        (gradient_ref[:, :hidden_width], gradient_ref[:, hidden_width:]),
        (total_ref[1, :, :hidden_width] + far[0], total_ref[1, :, hidden_width:] + far[1]),
    ]
    for kind in range(2):
        down, up = decode(across_ref[kind], hidden_width)
        out_refs[2 * kind][...] = totals[kind][0] + down
        out_refs[2 * kind + 1][...] = totals[kind][1] + up


class Ring:
    def __init__(self, size):
        self.length = size // 2
        rows = self.length // 2
        self.order = [4 * z for z in range(rows)] + [4 * z + 2 for z in reversed(range(rows))]

    def shift(self, value, step):
        pairs = [
            (chip + core, self.order[(place + step) % self.length] + core)
            for place, chip in enumerate(self.order)
            for core in range(2)
        ]
        return lax.ppermute(value, "expert", pairs)

    def members(self, me):
        rows = self.length // 2
        place = jnp.where(me // 2 % 2 == 0, me // 4, self.length - 1 - me // 4)
        there = (place + jnp.arange(self.length, dtype=jnp.int32)) % self.length
        return jnp.where(there < rows, 4 * there, 4 * (self.length - 1 - there) + 2) + me % 2

    def gather(self, own, passing):
        half = self.length // 2
        found = {0: own}
        ahead, behind = own, own
        for step in range(1, half):
            behind = self.shift(behind, 1)
            ahead = self.shift(ahead, -1)
            if step == 1:
                ahead = passing(ahead)
            found[self.length - step], found[step] = behind, ahead
        last = [self.shift(behind[:1], 1), self.shift(ahead[1:], -1)]
        return [found[offset] for offset in sorted(found)] + last


def exchange(value, mask):
    size = lax.axis_size("expert")
    return lax.ppermute(value, "expert", [(device, device ^ mask) for device in range(size)])


def gathered_plan(
    hidden_of_route,
    expert_of_route,
    gate_of_route,
    capacity,
    output_gradient,
    curvature,
    adapter_down,
    adapter_up,
    down_direction,
    up_direction,
):
    ring = Ring(lax.axis_size("expert"))
    slots = ring.length
    rows = slots // 2
    masks = [4 * z for z in range(rows)] + [4 * z + 2 for z in range(rows)]
    me = lax.axis_index("expert")
    tokens, top = expert_of_route.shape
    both = 2 * tokens
    hidden_width = hidden_of_route.shape[2]
    rank = adapter_down.shape[2]
    model_width = output_gradient.shape[1]
    experts = capacity.shape[0]
    wide = slots * rank
    coded_width = hidden_width + model_width + lanes

    ring_members = ring.members(me)
    differs = ring_members ^ me
    slot_of_offset = differs // 4 + rows * (differs // 2 % 2)
    place = jnp.concatenate([me[None], slot_of_offset, ring_members]).astype(jnp.int32)

    def call(kernel, multiplies, outs, *operands, scratch=(), after=(), grant=kernel_vmem):
        space = pltpu.HBM if kernel is prepare_kernel else pltpu.VMEM
        places = [
            pl.BlockSpec(memory_space=pltpu.SMEM if operand is place else space) for operand in operands
        ] + [pl.BlockSpec(memory_space=pl.ANY) for _ in after]
        return pl.pallas_call(
            kernel,
            out_shape=[jax.ShapeDtypeStruct(shape, dtype) for shape, dtype in outs],
            in_specs=places,
            scratch_shapes=scratch,
            compiler_params=pltpu.CompilerParams(vmem_limit_bytes=grant),
            cost_estimate=pl.CostEstimate(flops=2 * multiplies, bytes_accessed=2**20, transcendentals=0),
        )(*operands, *after)

    down_multiplies = 2 * top * both * hidden_width * wide
    up_multiplies = both * model_width * wide

    first = (
        expert_of_route.T,
        gate_of_route.T,
        curvature[None],
        down_direction[0].T,
        adapter_down[0].T,
        adapter_up[0],
        up_direction[0],
    )
    piece, small = call(
        prepare_kernel,
        10**8,
        [((2, rank, coded_width), i16), (((2 * top + 8) // 8 * 8, tokens), f32)],
        *first,
        scratch=[pltpu.VMEM(operand.shape, operand.dtype) for operand in first]
        + [pltpu.SemaphoreType.DMA((len(first),))],
        grant=whole_vmem,
    )
    small_other = exchange(small, 1)
    hidden = hidden_of_route.reshape(tokens * top, hidden_width)
    beside = []

    hidden_other = exchange(hidden, 1)
    gradient_other = exchange(output_gradient, 1)

    def passing(piece):
        *made, onward = call(
            functools.partial(tokens_kernel, top, masks),
            10**9,
            [
                ((both, small.shape[0]), f32),
                ((2, tokens, wide), f32),
                ((2, tokens, wide), f32),
                (piece.shape, i16),
            ],
            place,
            small,
            small_other,
            piece,
            after=[hidden_other, gradient_other],
        )
        beside.extend(made)
        return onward

    pieces = ring.gather(piece, passing)
    small_columns, local_rank, gate = beside
    capacity_row = jnp.pad(capacity.astype(f32), (counts_lane, lanes - counts_lane - experts))[None, :]

    by_offset = pieces[:rows] + [pieces[-2]] + pieces[rows:-2]
    (prior,) = call(functools.partial(prior_kernel, masks), 10**8, [((8, lanes), f32)], place, *by_offset)
    prior_arrived = exchange(prior, 1)
    factor_halves = [pltpu.VMEM((2, slots, rank, hidden_width), bf16)] * 2
    (reduced,) = call(
        functools.partial(reduce_kernel, top, masks),
        2 * down_multiplies,
        [((2, both, wide), f32)],
        place,
        small_columns,
        hidden,
        hidden_other,
        *pieces,
        scratch=factor_halves + [pltpu.VMEM((2, tokens * top, wide), f32)],
        after=[prior],
    )
    weight, weighted, tangent, coded, high, low = call(
        functools.partial(tangent_kernel, masks),
        6 * up_multiplies,
        [
            ((both, wide), f32),
            ((both, 2 * wide), f32),
            ((both, model_width), f32),
            ((both, model_width), bf16),
            ((2, slots, rank, model_width), bf16),
            ((2, slots, rank, model_width), bf16),
        ],
        place,
        local_rank,
        gate,
        capacity_row,
        prior,
        prior_arrived,
        reduced,
        *pieces,
    )
    arrived = exchange(coded, 1)
    left = [pltpu.VMEM((2, top * tokens, 2 * wide), bf16), pltpu.VMEM((2, top * tokens, wide), f32)]
    def chunks(kinds):
        return [
            ((2, rank, hidden_width + model_width), f32),
            ((2, rank, hidden_width + model_width), f32),
            ((2, rank, coded_width), i16),
            ((kinds, 2, rank, coded_width), i16),
        ]

    gradient_keep, gradient_chunk, gradient_far, near, up, to = call(
        functools.partial(gradient_kernel, top, masks),
        down_multiplies + 8 * up_multiplies,
        chunks(1) + [((wide, model_width), f32), ((both, wide), f32)],
        place,
        small_columns,
        hidden,
        hidden_other,
        output_gradient,
        gradient_other,
        weight,
        weighted,
        high,
        low,
        scratch=left,
    )
    gradient_far = exchange(gradient_far, 4)
    curvature_keep, curvature_chunk, curvature_far, near = call(
        functools.partial(curvature_kernel, top, masks),
        down_multiplies + 6 * up_multiplies,
        chunks(2),
        place,
        small_columns,
        hidden,
        hidden_other,
        weight,
        weighted,
        high,
        low,
        up,
        to,
        tangent,
        arrived,
        near,
        scratch=left,
    )

    hop = 2 * 10**9

    one = (rank, hidden_width + model_width)
    one_coded = (rank, coded_width)

    def hop_call(kernel, outs, *operands, after=()):
        return call(functools.partial(kernel, hidden_width), hop, outs, *operands, after=after)

    curvature_far = exchange(curvature_far, 4)
    near_arrived = exchange(near, 4)
    gradient_across, gradient_pair = hop_call(
        pair_kernel, [(one_coded, i16), (one, f32)], gradient_far, gradient_chunk, after=[near]
    )
    curvature_across, curvature_pair = hop_call(
        pair_kernel, [(one_coded, i16), (one, f32)], curvature_far, curvature_chunk, after=[gradient_across]
    )
    (gradient_beyond,) = hop_call(
        far_kernel, [(one_coded, i16)], exchange(gradient_across, 2), gradient_pair, after=[curvature_across]
    )
    (curvature_beyond,) = hop_call(
        far_kernel, [(one_coded, i16)], exchange(curvature_across, 2), curvature_pair, after=[gradient_beyond]
    )
    near_across, total = hop_call(
        near_kernel,
        [((2,) + one_coded, i16), ((2,) + one, f32)],
        near_arrived,
        gradient_keep,
        curvature_keep,
        after=[curvature_beyond],
    )
    (gradient_total,) = hop_call(
        add_kernel, [(one, f32)], total, exchange(gradient_beyond, 8), after=[near_across]
    )
    down_gradient, up_gradient, curvature_down, curvature_up = hop_call(
        total_kernel,
        [((rank, hidden_width), f32), ((rank, model_width), f32)] * 2,
        gradient_total,
        total,
        exchange(curvature_beyond, 8),
        exchange(near_across, 2),
    )
    return down_gradient.T[None], up_gradient[None], curvature_down.T[None], curvature_up[None]


def carried_in(value, axis, join, neutral):
    count, mine = (lax.axis_size(axis), lax.axis_index(axis))
    pieces = lax.all_gather(value, axis)
    so_far = jnp.full_like(value, 0) + jnp.asarray(neutral, value.dtype)

    def lap(position, so_far):
        longer = join(so_far, pieces[position])
        return jnp.where(position < mine, longer, so_far)

    return lax.fori_loop(0, count - 1, lap, so_far)


def add_counts(earlier, later):
    return earlier + later


def routed_plan(
    hidden_of_route,
    expert_of_route,
    gate_of_route,
    capacity,
    output_gradient,
    curvature,
    adapter_down,
    adapter_up,
    down_direction,
    up_direction,
):
    finest_precision = lax.Precision.HIGHEST
    group_size = lax.axis_size("expert")
    tok_rows, top_count = expert_of_route.shape
    hidden_width = hidden_of_route.shape[2]
    resident_experts = adapter_down.shape[0]
    adapter_rank = adapter_down.shape[2]
    model_width = output_gradient.shape[1]
    experts = resident_experts * group_size
    slot_most = 2 * tok_rows * top_count // experts
    routes = expert_of_route.reshape(-1)
    onehot = (routes[:, None] == jnp.arange(experts, dtype=jnp.int32)[None, :]).astype(jnp.int32)
    earlier = jnp.cumsum(onehot, axis=0) - onehot
    local_rank = jnp.sum(earlier * onehot, axis=1)
    counts = jnp.sum(onehot, axis=0)
    prior_count = carried_in(counts, "expert", add_counts, jnp.zeros_like(counts))
    global_rank = local_rank + jnp.sum(onehot * prior_count[None, :], axis=1)
    route_limit = jnp.sum(onehot * capacity[None, :], axis=1)
    retained_mask = (global_rank < route_limit).astype(jnp.float32)
    weight_of_route = (
        adapter_scale * gate_of_route.reshape(-1).astype(jnp.float32) * retained_mask
    ).astype(jnp.bfloat16)
    slot_index = routes * slot_most + local_rank
    layout = (group_size, resident_experts, slot_most)
    send_hidden = (
        jnp.zeros((experts * slot_most, hidden_width), jnp.bfloat16)
        .at[slot_index]
        .set(hidden_of_route.reshape(-1, hidden_width))
        .reshape(layout + (hidden_width,))
    )
    send_weight = (
        jnp.zeros((experts * slot_most,), jnp.bfloat16)
        .at[slot_index]
        .set(weight_of_route)
        .reshape(layout)
    )
    down_stacked = jnp.concatenate([adapter_down, down_direction], axis=2)
    up_stacked = jnp.concatenate([adapter_up, up_direction], axis=1)

    def spread(token_rows):
        per_route = jnp.repeat(token_rows, top_count, axis=0)
        placed = (
            jnp.zeros((experts * slot_most, model_width), jnp.bfloat16)
            .at[slot_index]
            .set(per_route)
        )
        return placed.reshape(layout + (model_width,))

    send_residual = spread(output_gradient)
    pieces = (
        lax.all_to_all(send_hidden, "expert", split_axis=0, concat_axis=0, tiled=True),
        lax.all_to_all(send_weight, "expert", split_axis=0, concat_axis=0, tiled=True),
    )
    hidden_rows = pieces[0].astype(jnp.float32)
    weight_rows = pieces[1].astype(jnp.float32)[..., None]
    reduced_hidden = jnp.einsum(
        "cjif,jfk->cjik", hidden_rows, down_stacked, precision=finest_precision
    )
    exchanged_rows = jnp.concatenate(
        [reduced_hidden[..., adapter_rank:], reduced_hidden[..., :adapter_rank]], axis=3
    )
    tangent_out = weight_rows * jnp.einsum(
        "cjik,jkd->cjid", exchanged_rows, up_stacked, precision=finest_precision
    )
    returned = lax.all_to_all(
        tangent_out.astype(jnp.bfloat16), "expert", split_axis=0, concat_axis=0, tiled=True
    )
    results = (returned, reduced_hidden) + tuple(pieces)
    returned = results[0]
    reduced_hidden = results[1]
    hidden_rows = results[2]
    weight_rows = results[3]
    route_tangent = returned.reshape(experts * slot_most, model_width)[slot_index]
    out_tangent = jnp.sum(
        route_tangent.reshape(tok_rows, top_count, model_width).astype(jnp.float32), axis=1
    )
    resid_tangent = (curvature[:, None] * out_tangent).astype(jnp.bfloat16)
    send_tangent = spread(resid_tangent)
    residual_rows, tangent_rows = (
        lax.all_to_all(send_residual, "expert", split_axis=0, concat_axis=0, tiled=True),
        lax.all_to_all(send_tangent, "expert", split_axis=0, concat_axis=0, tiled=True),
    )
    residual_full = residual_rows.astype(jnp.float32)
    complete_tangent = tangent_rows.astype(jnp.float32)
    weight_column = weight_rows.astype(jnp.float32)[..., None]
    residual_reduced = jnp.einsum(
        "wyov,yqv->wyoq", residual_full, up_stacked, precision=finest_precision
    )
    reduced_tangent = jnp.einsum(
        "wyov,yqv->wyoq", complete_tangent, adapter_up, precision=finest_precision
    )
    left_terms = jnp.concatenate(
        [
            weight_column * residual_reduced[..., :adapter_rank],
            weight_column * (reduced_tangent + residual_reduced[..., adapter_rank:]),
        ],
        axis=3,
    )
    down_terms = jnp.einsum(
        "cjif,cjik->jfk", hidden_rows.astype(jnp.float32), left_terms, precision=finest_precision
    )
    raised_update = weight_column * reduced_hidden[..., :adapter_rank]
    raised_tangent_update = weight_column * reduced_hidden[..., adapter_rank:]
    up_terms = jnp.einsum(
        "cjik,cjid->jkd",
        jnp.concatenate([raised_update, raised_tangent_update], axis=3),
        residual_full,
        precision=finest_precision,
    )
    curvature_piece = up_terms[:, adapter_rank:] + jnp.einsum(
        "cjik,cjid->jkd", raised_update, complete_tangent, precision=finest_precision
    )
    return (
        down_terms[..., :adapter_rank],
        up_terms[:, :adapter_rank],
        down_terms[..., adapter_rank:],
        curvature_piece,
    )


def local(*arguments):
    factor_bytes = 2 * 4 * (arguments[6].size + arguments[7].size) * lax.axis_size("expert")
    fits = lax.axis_size("expert") == 16 and 4 * factor_bytes <= kernel_vmem
    plan = gathered_plan if fits else routed_plan
    return plan(*arguments)


def solution(mesh):
    return jax.shard_map(
        local,
        mesh=mesh,
        in_specs=(
            P(("groups", "expert"), None, None),
            P(("groups", "expert"), None),
            P(("groups", "expert"), None),
            P("groups"),
            P(("groups", "expert"), None),
            P(("groups", "expert")),
            P("expert", None, None),
            P("expert", None, None),
            P(("groups", "expert"), None, None),
            P(("groups", "expert"), None, None),
        ),
        out_specs=(
            P(("groups", "expert"), None, None),
            P(("groups", "expert"), None, None),
            P(("groups", "expert"), None, None),
            P(("groups", "expert"), None, None),
        ),
        check_vma=False,
    )
```

```python
import functools

import jax
import jax.numpy as jnp
from jax import lax
from jax.experimental import pallas as pl
from jax.experimental.pallas import tpu as pltpu
from jax.sharding import PartitionSpec as P

adapter_scale = 2.0
f32 = jnp.float32
bf16 = jnp.bfloat16
i16 = jnp.int16
lanes = 128
counts_lane = 64
kernel_vmem = 32 * 2**20
whole_vmem = 60 * 2**20


def halves(value):
    high = value.astype(bf16)
    return high, (value - high.astype(f32)).astype(bf16)


def dot(a, b, a_dim, b_dim):
    return lax.dot_general(a, b, (((a_dim,), (b_dim,)), ((), ())), preferred_element_type=f32)


def dot_pairs(a, b, a_dim, b_dim):
    return dot(a[0], b[0], a_dim, b_dim) + (dot(a[1], b[0], a_dim, b_dim) + dot(a[0], b[1], a_dim, b_dim))


def encode(down, up, counts=0.0):
    def scaled(value):
        largest = jnp.max(jnp.abs(value), axis=-1, keepdims=True)
        exponent = jnp.ceil(jnp.log2(jnp.maximum(largest, 1e-30)))
        coded = jnp.round(value * jnp.exp2(15.0 - exponent))
        return jnp.clip(coded, -32767.0, 32767.0), exponent

    down, down_exponent = scaled(down)
    up, up_exponent = scaled(up)
    lane = lax.broadcasted_iota(jnp.int32, down.shape[:-1] + (lanes,), down.ndim - 1)
    tail = jnp.where(lane < counts_lane // 2, down_exponent, up_exponent)
    tail = jnp.where(lane < counts_lane, tail, counts)
    return jnp.concatenate([down, up, tail], axis=-1).astype(jnp.int32).astype(i16)


def decode(coded, hidden_width):
    width = coded.shape[-1] - lanes
    value = coded.astype(jnp.int32).astype(f32)
    down_scale = jnp.exp2(value[..., width : width + 1] - 15.0)
    up_scale = jnp.exp2(value[..., width + counts_lane // 2 : width + counts_lane // 2 + 1] - 15.0)
    return value[..., :hidden_width] * down_scale, value[..., hidden_width:width] * up_scale


def prepare_kernel(*refs):
    (piece_ref, small_ref), sem, refs = refs[7:9], refs[-1], refs[:7] + refs[9:-1]
    copies = [pltpu.make_async_copy(refs[i], refs[7 + i], sem.at[i]) for i in range(7)]
    for copy in copies:
        copy.start()
    for copy in copies:
        copy.wait()
    expert, gate, curvature, down_direction, adapter_down, adapter_up, up_direction = [ref[...] for ref in refs[7:]]
    top = expert.shape[0]
    small_ref[...] = jnp.zeros_like(small_ref)
    small_ref[:top] = expert.astype(f32)
    small_ref[top : 2 * top] = gate.astype(f32)
    small_ref[2 * top : 2 * top + 1] = curvature
    lane = lax.broadcasted_iota(jnp.int32, (1, lanes), 1)
    counts = jnp.zeros((1, lanes), f32)
    for number in range(lanes - counts_lane):
        named = jnp.where(expert == number, 1.0, 0.0)
        total = jnp.sum(jnp.sum(named, axis=0, keepdims=True), axis=1, keepdims=True)
        counts = jnp.where(lane == counts_lane + number, total, counts)
    piece_ref[0] = encode(down_direction, adapter_up, counts)
    piece_ref[1] = encode(adapter_down, up_direction, counts)


def token_columns(small_ref, top):
    experts = [small_ref[:, k : k + 1] for k in range(top)]
    gates = [small_ref[:, top + k : top + k + 1] for k in range(top)]
    return experts, gates, small_ref[:, 2 * top : 2 * top + 1]


def members(place_ref, wide, masks):
    slot_of = lax.broadcasted_iota(jnp.int32, (1, wide), 1) // (wide // len(masks))
    found = jnp.zeros((1, wide), jnp.int32)
    for slot, mask in enumerate(masks):
        found = jnp.where(slot_of == slot, place_ref[0] ^ mask, found)
    return found.astype(f32)


def prior_kernel(masks, place_ref, *rest):
    piece_refs, prior_ref = rest[:-1], rest[-1]
    me = place_ref[0]
    slots = len(masks)
    prior_ref[...] = jnp.zeros_like(prior_ref)
    for block, number in enumerate((me, me ^ 1)):
        total = jnp.zeros((1, lanes), f32)
        for offset, piece_ref in enumerate(piece_refs):
            device = place_ref[1 + slots + offset]
            tail = piece_ref[0, :, piece_ref.shape[2] - lanes :]
            counts = tail.astype(jnp.int32).astype(f32)[0:1]
            total = total + jnp.where(device < number, counts, 0.0)
        prior_ref[block : block + 1] = total


def tokens_kernel(top, masks, place_ref, own_ref, other_ref, piece_ref, *outs):
    small_ref, rank_ref, gate_ref, same_ref, mask_ref, onward_ref = outs
    onward_ref[...] = piece_ref[...]
    small_ref[...] = jnp.concatenate([own_ref[...], other_ref[...]], axis=1).T
    experts, gates, _ = token_columns(small_ref, top)
    _, tokens, wide = rank_ref.shape
    column = members(place_ref, wide, masks)
    below = (
        lax.broadcasted_iota(jnp.int32, (tokens, tokens), 0)
        > lax.broadcasted_iota(jnp.int32, (tokens, tokens), 1)
    )
    below = jnp.where(below, 1.0, 0.0).astype(bf16)
    rows = same_ref.shape[0]
    row = lax.broadcasted_iota(jnp.int32, (rows, tokens), 0)
    same = jnp.where(row // top == lax.broadcasted_iota(jnp.int32, (rows, tokens), 1), 1.0, 0.0).astype(bf16)
    same_ref[...] = same
    for core in range(2):
        tokens_of = slice(core * tokens, (core + 1) * tokens)
        gate = jnp.zeros((tokens, wide), f32)
        member = jnp.zeros((tokens, wide), f32)
        for k in range(top):
            named = experts[k][tokens_of] == column
            gate = jnp.where(named, gates[k][tokens_of], gate)
            member = jnp.where(named, 1.0, member)
        gate_ref[core] = gate
        rank_ref[core] = dot(below, member.astype(bf16), 1, 0)
        named = dot(same, small_ref[tokens_of].astype(bf16), 1, 0)
        position = lax.broadcasted_iota(jnp.int32, named.shape, 0) % top
        own = lax.broadcasted_iota(jnp.int32, named.shape, 1) == position
        expert = jnp.sum(jnp.where(own, named, 0.0), axis=1, keepdims=True)
        mask_ref[core] = jnp.where(expert == column, 1.0, 0.0).astype(bf16)


def reduce_kernel(top, masks, place_ref, small_ref, own_ref, other_ref, *rest):
    slots = len(masks)
    piece_refs, (reduced_ref, high_ref, low_ref, full_ref) = rest[:slots], rest[slots:]
    hidden_width = own_ref.shape[1]
    for offset in range(slots):
        slot = place_ref[1 + offset]
        for kind in range(2):
            down, _ = decode(piece_refs[offset][kind], hidden_width)
            high_ref[kind, slot], low_ref[kind, slot] = halves(down)
    experts, _, _ = token_columns(small_ref, top)
    wide = reduced_ref.shape[2]
    column = members(place_ref, wide, masks)
    high = high_ref[...].reshape(2 * wide, hidden_width)
    low = low_ref[...].reshape(2 * wide, hidden_width)
    tokens = own_ref.shape[0] // top
    for core, hidden_ref in enumerate((own_ref, other_ref)):
        full = dot(hidden_ref[...], high, 1, 1) + dot(hidden_ref[...], low, 1, 1)
        full_ref[0], full_ref[1] = full[:, :wide], full[:, wide:]
        tokens_of = slice(core * tokens, (core + 1) * tokens)
        for kind in range(2):
            total = jnp.zeros((tokens, wide), f32)
            for k in range(top):
                here = full_ref[kind, pl.ds(k, tokens, stride=top), :]
                total = jnp.where(experts[k][tokens_of] == column, here, total)
            reduced_ref[kind, tokens_of] = total


def rank_limits(place_ref, masks, wide, capacity_ref, prior_ref, arrived_ref):
    lane = lax.broadcasted_iota(jnp.int32, (1, lanes), 1)
    slot_of = lax.broadcasted_iota(jnp.int32, (1, wide), 1) // (wide // len(masks))
    limits = []
    for block in range(2):
        total = capacity_ref[...] - prior_ref[block : block + 1] - arrived_ref[1 - block : 2 - block]
        limit = jnp.zeros((1, wide), f32)
        for slot, mask in enumerate(masks):
            picked = jnp.where(lane == counts_lane + (place_ref[0] ^ mask), total, 0.0)
            limit = jnp.where(slot_of == slot, jnp.sum(picked, axis=1, keepdims=True), limit)
        limits.append(limit)
    return limits


def tangent_kernel(masks, place_ref, rank_ref, gate_ref, capacity_ref, prior_ref, arrived_ref, reduced_ref, *rest):
    slots = len(masks)
    piece_refs = rest[:slots]
    weight_ref, weighted_ref, tangent_ref, coded_ref, high_ref, low_ref = rest[slots:]
    _, wide = weight_ref.shape
    model_width = tangent_ref.shape[1]
    hidden_width = piece_refs[0].shape[2] - model_width - lanes
    limits = rank_limits(place_ref, masks, wide, capacity_ref, prior_ref, arrived_ref)
    weights = [
        jnp.where(rank_ref[core] < limits[core], adapter_scale * gate_ref[core], 0.0) for core in range(2)
    ]
    weight = jnp.concatenate(weights, axis=0)
    weight_ref[...] = weight
    weighted = jnp.concatenate([weight * reduced_ref[0], weight * reduced_ref[1]], axis=1)
    weighted_ref[...] = weighted
    for offset in range(slots):
        slot = place_ref[1 + offset]
        for kind in range(2):
            _, up = decode(piece_refs[offset][kind], hidden_width)
            high_ref[kind, slot], low_ref[kind, slot] = halves(up)
    factor = high_ref[...].reshape(2 * wide, model_width), low_ref[...].reshape(2 * wide, model_width)
    tangent = dot_pairs(halves(weighted), factor, 1, 0)
    tangent_ref[...] = tangent
    coded_ref[...] = tangent.astype(bf16)


def put_left(left_ref, same_ref, mask_ref, terms):
    both = jnp.concatenate(halves(terms), axis=1)
    tokens = terms.shape[0] // 2
    for core in range(2):
        repeated = dot(same_ref[...], both[core * tokens : (core + 1) * tokens], 1, 0).astype(bf16)
        mask = mask_ref[core]
        left_ref[core] = repeated * jnp.concatenate([mask, mask], axis=1)


def add_halves(both):
    middle = both.shape[0] // 2
    return both[:middle] + both[middle:]


def put_chunks(keep_ref, near_ref, chunk_ref, far_ref, down, up):
    rank = keep_ref.shape[1]
    rows = down.shape[0] // rank // 2

    def slot(number):
        start = number * rank
        return down[start : start + rank], up[start : start + rank]

    for place in range(2):
        keep_ref[place] = jnp.concatenate(slot(place), axis=1)
        near_ref[place] = encode(*slot(rows + place))
        chunk_ref[place] = jnp.concatenate(slot(place * rows + 2), axis=1)
        far_ref[place] = encode(*slot(place * rows + 3))


def gradient_kernel(
    same_ref,
    mask_ref,
    own_ref,
    other_ref,
    own_gradient_ref,
    other_gradient_ref,
    weight_ref,
    weighted_ref,
    high_ref,
    low_ref,
    keep_ref,
    near_ref,
    chunk_ref,
    far_ref,
    up_ref,
    to_ref,
    left_ref,
):
    wide = weight_ref.shape[1]
    model_width = up_ref.shape[1]
    gradient = jnp.concatenate([own_gradient_ref[...], other_gradient_ref[...]], axis=0)
    high = high_ref[...].reshape(2 * wide, model_width)
    low = low_ref[...].reshape(2 * wide, model_width)
    to_both = dot(gradient, high, 1, 1) + dot(gradient, low, 1, 1)
    to_ref[...] = to_both[:, wide:]
    put_left(left_ref, same_ref, mask_ref, weight_ref[...] * to_both[:, :wide])
    down = dot(left_ref[0], own_ref[...], 0, 0) + dot(left_ref[1], other_ref[...], 0, 0)
    up = add_halves(dot(jnp.concatenate(halves(weighted_ref[...]), axis=1), gradient, 0, 0))
    up_ref[...] = up[:wide]
    put_chunks(keep_ref, near_ref, chunk_ref, far_ref, add_halves(down), up[wide:])


def curvature_kernel(
    top,
    small_ref,
    same_ref,
    mask_ref,
    own_ref,
    other_ref,
    weight_ref,
    weighted_ref,
    high_ref,
    low_ref,
    up_ref,
    to_ref,
    tangent_ref,
    arrived_ref,
    keep_ref,
    near_ref,
    chunk_ref,
    far_ref,
    left_ref,
):
    _, _, curvature = token_columns(small_ref, top)
    tokens, wide = weight_ref.shape
    block = tokens // 2
    model_width = up_ref.shape[1]
    arrived = jnp.concatenate([arrived_ref[block:], arrived_ref[:block]], axis=0).astype(f32)
    resid = halves(curvature * (tangent_ref[...] + arrived))
    adapter_up = high_ref[0].reshape(wide, model_width), low_ref[0].reshape(wide, model_width)
    terms = weight_ref[...] * (dot_pairs(resid, adapter_up, 1, 1) + to_ref[...])
    put_left(left_ref, same_ref, mask_ref, terms)
    down = dot(left_ref[0], own_ref[...], 0, 0) + dot(left_ref[1], other_ref[...], 0, 0)
    weighted_u = halves(weighted_ref[:, wide:])
    up = add_halves(dot(jnp.concatenate(weighted_u, axis=1), resid[0], 0, 0)) + dot(weighted_u[0], resid[1], 0, 0)
    put_chunks(keep_ref, near_ref, chunk_ref, far_ref, add_halves(down), up_ref[...] + up)


def pair_kernel(hidden_width, arrived_ref, chunk_ref, across_ref, keep_ref):
    for x in range(2):
        down, up = decode(arrived_ref[x], hidden_width)
        down, up = chunk_ref[x, :, :hidden_width] + down, chunk_ref[x, :, hidden_width:] + up
        if x == 0:
            keep_ref[...] = jnp.concatenate([down, up], axis=1)
        else:
            across_ref[...] = encode(down, up)


def far_kernel(hidden_width, arrived_ref, keep_ref, out_ref):
    down, up = decode(arrived_ref[...], hidden_width)
    out_ref[...] = encode(keep_ref[:, :hidden_width] + down, keep_ref[:, hidden_width:] + up)


def near_kernel(
    hidden_width, gradient_ref, curvature_ref, gradient_keep_ref, curvature_keep_ref, onward_ref, total_ref
):
    pairs = ((gradient_ref, gradient_keep_ref), (curvature_ref, curvature_keep_ref))
    for kind, (arrived_ref, keep_ref) in enumerate(pairs):
        for z in range(2):
            down, up = decode(arrived_ref[z], hidden_width)
            down, up = keep_ref[z, :, :hidden_width] + down, keep_ref[z, :, hidden_width:] + up
            if z == 0:
                total_ref[kind] = jnp.concatenate([down, up], axis=1)
            else:
                onward_ref[kind] = encode(down, up)


def add_kernel(hidden_width, total_ref, arrived_ref, out_ref):
    down, up = decode(arrived_ref[...], hidden_width)
    out_ref[:, :hidden_width] = total_ref[0, :, :hidden_width] + down
    out_ref[:, hidden_width:] = total_ref[0, :, hidden_width:] + up


def total_kernel(hidden_width, gradient_ref, total_ref, far_ref, pair_ref, *out_refs):
    far = decode(far_ref[...], hidden_width)
    totals = [
        (gradient_ref[:, :hidden_width], gradient_ref[:, hidden_width:]),
        (total_ref[1, :, :hidden_width] + far[0], total_ref[1, :, hidden_width:] + far[1]),
    ]
    for kind in range(2):
        down, up = decode(pair_ref[kind], hidden_width)
        out_refs[2 * kind][...] = totals[kind][0] + down
        out_refs[2 * kind + 1][...] = totals[kind][1] + up


class Ring:
    def __init__(self, size):
        self.length = size // 2
        rows = self.length // 2
        self.order = [4 * z for z in range(rows)] + [4 * z + 2 for z in reversed(range(rows))]

    def shift(self, value, step):
        pairs = [
            (chip + core, self.order[(place + step) % self.length] + core)
            for place, chip in enumerate(self.order)
            for core in range(2)
        ]
        return lax.ppermute(value, "expert", pairs)

    def members(self, me):
        rows = self.length // 2
        place = jnp.where(me // 2 % 2 == 0, me // 4, self.length - 1 - me // 4)
        there = (place + jnp.arange(self.length, dtype=jnp.int32)) % self.length
        return jnp.where(there < rows, 4 * there, 4 * (self.length - 1 - there) + 2) + me % 2

    def gather(self, own, passing):
        half = self.length // 2
        found = {0: own}
        ahead, behind = own, own
        for step in range(1, half + 1):
            behind = found[self.length - step] = self.shift(behind, 1)
            if step < half:
                ahead = self.shift(ahead, -1)
                ahead = found[step] = passing(ahead) if step == 1 else ahead
        return [found[offset] for offset in range(self.length)]


def exchange(value, mask):
    size = lax.axis_size("expert")
    return lax.ppermute(value, "expert", [(device, device ^ mask) for device in range(size)])


def gathered_plan(
    hidden_of_route,
    expert_of_route,
    gate_of_route,
    capacity,
    output_gradient,
    curvature,
    adapter_down,
    adapter_up,
    down_direction,
    up_direction,
):
    ring = Ring(lax.axis_size("expert"))
    slots = ring.length
    rows = slots // 2
    masks = [4 * z for z in range(rows)] + [4 * z + 2 for z in range(rows)]
    me = lax.axis_index("expert")
    tokens, top = expert_of_route.shape
    both = 2 * tokens
    hidden_width = hidden_of_route.shape[2]
    rank = adapter_down.shape[2]
    model_width = output_gradient.shape[1]
    experts = capacity.shape[0]
    wide = slots * rank
    coded_width = hidden_width + model_width + lanes

    ring_members = ring.members(me)
    differs = ring_members ^ me
    slot_of_offset = differs // 4 + rows * (differs // 2 % 2)
    place = jnp.concatenate([me[None], slot_of_offset, ring_members]).astype(jnp.int32)

    def call(kernel, multiplies, outs, *operands, scratch=(), after=(), grant=kernel_vmem):
        space = pltpu.HBM if kernel is prepare_kernel else pltpu.VMEM
        places = [pl.BlockSpec(memory_space=pl.ANY) for _ in after] + [
            pl.BlockSpec(memory_space=pltpu.SMEM if operand is place else space) for operand in operands
        ]
        return pl.pallas_call(
            lambda *refs: kernel(*refs[len(after) :]),
            out_shape=[jax.ShapeDtypeStruct(shape, dtype) for shape, dtype in outs],
            in_specs=places,
            scratch_shapes=scratch,
            compiler_params=pltpu.CompilerParams(vmem_limit_bytes=grant),
            cost_estimate=pl.CostEstimate(flops=2 * multiplies, bytes_accessed=2**20, transcendentals=0),
        )(*after, *operands)

    down_multiplies = 2 * top * both * hidden_width * wide
    up_multiplies = both * model_width * wide

    first = (
        expert_of_route.T,
        gate_of_route.T,
        curvature[None],
        down_direction[0].T,
        adapter_down[0].T,
        adapter_up[0],
        up_direction[0],
    )
    piece, small = call(
        prepare_kernel,
        10**8,
        [((2, rank, coded_width), i16), (((2 * top + 8) // 8 * 8, tokens), f32)],
        *first,
        scratch=[pltpu.VMEM(operand.shape, operand.dtype) for operand in first]
        + [pltpu.SemaphoreType.DMA((len(first),))],
        grant=whole_vmem,
    )
    small_other = exchange(small, 1)
    hidden = hidden_of_route.reshape(tokens * top, hidden_width)
    beside = []

    hidden_other = exchange(hidden, 1)
    gradient_other = exchange(output_gradient, 1)

    def passing(piece):
        *made, onward = call(
            functools.partial(tokens_kernel, top, masks),
            10**9,
            [
                ((both, small.shape[0]), f32),
                ((2, tokens, wide), f32),
                ((2, tokens, wide), f32),
                ((top * tokens, tokens), bf16),
                ((2, top * tokens, wide), bf16),
                (piece.shape, i16),
            ],
            place,
            small,
            small_other,
            piece,
            after=[hidden_other, gradient_other],
        )
        beside.extend(made)
        return onward

    pieces = ring.gather(piece, passing)
    small_columns, local_rank, gate, same, mask = beside
    capacity_row = jnp.pad(capacity.astype(f32), (counts_lane, lanes - counts_lane - experts))[None, :]

    (prior,) = call(functools.partial(prior_kernel, masks), 10**8, [((8, lanes), f32)], place, *pieces)
    prior_arrived = exchange(prior, 1)
    factor_halves = [pltpu.VMEM((2, slots, rank, hidden_width), bf16)] * 2
    (reduced,) = call(
        functools.partial(reduce_kernel, top, masks),
        2 * down_multiplies,
        [((2, both, wide), f32)],
        place,
        small_columns,
        hidden,
        hidden_other,
        *pieces,
        scratch=factor_halves + [pltpu.VMEM((2, tokens * top, wide), f32)],
        after=[prior],
    )
    weight, weighted, tangent, coded, high, low = call(
        functools.partial(tangent_kernel, masks),
        6 * up_multiplies,
        [
            ((both, wide), f32),
            ((both, 2 * wide), f32),
            ((both, model_width), f32),
            ((both, model_width), bf16),
            ((2, slots, rank, model_width), bf16),
            ((2, slots, rank, model_width), bf16),
        ],
        place,
        local_rank,
        gate,
        capacity_row,
        prior,
        prior_arrived,
        reduced,
        *pieces,
    )
    arrived = exchange(coded, 1)
    left = [pltpu.VMEM((2, top * tokens, 2 * wide), bf16)]
    chunks = [((2, rank, hidden_width + model_width), f32), ((2, rank, coded_width), i16)] * 2
    gradient_keep, gradient_near, gradient_chunk, gradient_far, up, to = call(
        gradient_kernel,
        down_multiplies + 8 * up_multiplies,
        chunks + [((wide, model_width), f32), ((both, wide), f32)],
        same,
        mask,
        hidden,
        hidden_other,
        output_gradient,
        gradient_other,
        weight,
        weighted,
        high,
        low,
        scratch=left,
    )
    gradient_far = exchange(gradient_far, 4)
    gradient_near = exchange(gradient_near, 2)
    curvature_keep, curvature_near, curvature_chunk, curvature_far = call(
        functools.partial(curvature_kernel, top),
        down_multiplies + 6 * up_multiplies,
        chunks,
        small_columns,
        same,
        mask,
        hidden,
        hidden_other,
        weight,
        weighted,
        high,
        low,
        up,
        to,
        tangent,
        arrived,
        scratch=left,
    )

    hop = 2 * 10**9

    one = (rank, hidden_width + model_width)
    one_coded = (rank, coded_width)

    def hop_call(kernel, outs, *operands, after=()):
        return call(functools.partial(kernel, hidden_width), hop, outs, *operands, after=after)

    curvature_far = exchange(curvature_far, 4)
    curvature_near = exchange(curvature_near, 2)
    gradient_across, gradient_pair = hop_call(
        pair_kernel,
        [(one_coded, i16), (one, f32)],
        gradient_far,
        gradient_chunk,
        after=[curvature_keep],
    )
    curvature_across, curvature_pair = hop_call(
        pair_kernel,
        [(one_coded, i16), (one, f32)],
        curvature_far,
        curvature_chunk,
        after=[gradient_across, gradient_near],
    )
    (gradient_beyond,) = hop_call(
        far_kernel,
        [(one_coded, i16)],
        exchange(gradient_across, 2),
        gradient_pair,
        after=[curvature_across, curvature_near],
    )
    onward, total = hop_call(
        near_kernel,
        [((2,) + one_coded, i16), ((2,) + one, f32)],
        gradient_near,
        curvature_near,
        gradient_keep,
        curvature_keep,
        after=[gradient_beyond],
    )
    (curvature_beyond,) = hop_call(
        far_kernel, [(one_coded, i16)], exchange(curvature_across, 2), curvature_pair, after=[onward]
    )
    (gradient_total,) = hop_call(
        add_kernel, [(one, f32)], total, exchange(gradient_beyond, 8), after=[curvature_beyond]
    )
    down_gradient, up_gradient, curvature_down, curvature_up = hop_call(
        total_kernel,
        [((rank, hidden_width), f32), ((rank, model_width), f32)] * 2,
        gradient_total,
        total,
        exchange(curvature_beyond, 8),
        exchange(onward, 4),
    )
    return down_gradient.T[None], up_gradient[None], curvature_down.T[None], curvature_up[None]


def carried_in(value, axis, join, neutral):
    count, mine = (lax.axis_size(axis), lax.axis_index(axis))
    pieces = lax.all_gather(value, axis)
    so_far = jnp.full_like(value, 0) + jnp.asarray(neutral, value.dtype)

    def lap(position, so_far):
        longer = join(so_far, pieces[position])
        return jnp.where(position < mine, longer, so_far)

    return lax.fori_loop(0, count - 1, lap, so_far)


def add_counts(earlier, later):
    return earlier + later


def routed_plan(
    hidden_of_route,
    expert_of_route,
    gate_of_route,
    capacity,
    output_gradient,
    curvature,
    adapter_down,
    adapter_up,
    down_direction,
    up_direction,
):
    finest_precision = lax.Precision.HIGHEST
    group_size = lax.axis_size("expert")
    tok_rows, top_count = expert_of_route.shape
    hidden_width = hidden_of_route.shape[2]
    resident_experts = adapter_down.shape[0]
    adapter_rank = adapter_down.shape[2]
    model_width = output_gradient.shape[1]
    experts = resident_experts * group_size
    slot_most = 2 * tok_rows * top_count // experts
    routes = expert_of_route.reshape(-1)
    onehot = (routes[:, None] == jnp.arange(experts, dtype=jnp.int32)[None, :]).astype(jnp.int32)
    earlier = jnp.cumsum(onehot, axis=0) - onehot
    local_rank = jnp.sum(earlier * onehot, axis=1)
    counts = jnp.sum(onehot, axis=0)
    prior_count = carried_in(counts, "expert", add_counts, jnp.zeros_like(counts))
    global_rank = local_rank + jnp.sum(onehot * prior_count[None, :], axis=1)
    route_limit = jnp.sum(onehot * capacity[None, :], axis=1)
    retained_mask = (global_rank < route_limit).astype(jnp.float32)
    weight_of_route = (
        adapter_scale * gate_of_route.reshape(-1).astype(jnp.float32) * retained_mask
    ).astype(jnp.bfloat16)
    slot_index = routes * slot_most + local_rank
    layout = (group_size, resident_experts, slot_most)
    send_hidden = (
        jnp.zeros((experts * slot_most, hidden_width), jnp.bfloat16)
        .at[slot_index]
        .set(hidden_of_route.reshape(-1, hidden_width))
        .reshape(layout + (hidden_width,))
    )
    send_weight = (
        jnp.zeros((experts * slot_most,), jnp.bfloat16)
        .at[slot_index]
        .set(weight_of_route)
        .reshape(layout)
    )
    down_stacked = jnp.concatenate([adapter_down, down_direction], axis=2)
    up_stacked = jnp.concatenate([adapter_up, up_direction], axis=1)

    def spread(token_rows):
        per_route = jnp.repeat(token_rows, top_count, axis=0)
        placed = (
            jnp.zeros((experts * slot_most, model_width), jnp.bfloat16)
            .at[slot_index]
            .set(per_route)
        )
        return placed.reshape(layout + (model_width,))

    send_residual = spread(output_gradient)
    pieces = (
        lax.all_to_all(send_hidden, "expert", split_axis=0, concat_axis=0, tiled=True),
        lax.all_to_all(send_weight, "expert", split_axis=0, concat_axis=0, tiled=True),
    )
    hidden_rows = pieces[0].astype(jnp.float32)
    weight_rows = pieces[1].astype(jnp.float32)[..., None]
    reduced_hidden = jnp.einsum(
        "cjif,jfk->cjik", hidden_rows, down_stacked, precision=finest_precision
    )
    exchanged_rows = jnp.concatenate(
        [reduced_hidden[..., adapter_rank:], reduced_hidden[..., :adapter_rank]], axis=3
    )
    tangent_out = weight_rows * jnp.einsum(
        "cjik,jkd->cjid", exchanged_rows, up_stacked, precision=finest_precision
    )
    returned = lax.all_to_all(
        tangent_out.astype(jnp.bfloat16), "expert", split_axis=0, concat_axis=0, tiled=True
    )
    results = (returned, reduced_hidden) + tuple(pieces)
    returned = results[0]
    reduced_hidden = results[1]
    hidden_rows = results[2]
    weight_rows = results[3]
    route_tangent = returned.reshape(experts * slot_most, model_width)[slot_index]
    out_tangent = jnp.sum(
        route_tangent.reshape(tok_rows, top_count, model_width).astype(jnp.float32), axis=1
    )
    resid_tangent = (curvature[:, None] * out_tangent).astype(jnp.bfloat16)
    send_tangent = spread(resid_tangent)
    residual_rows, tangent_rows = (
        lax.all_to_all(send_residual, "expert", split_axis=0, concat_axis=0, tiled=True),
        lax.all_to_all(send_tangent, "expert", split_axis=0, concat_axis=0, tiled=True),
    )
    residual_full = residual_rows.astype(jnp.float32)
    complete_tangent = tangent_rows.astype(jnp.float32)
    weight_column = weight_rows.astype(jnp.float32)[..., None]
    residual_reduced = jnp.einsum(
        "wyov,yqv->wyoq", residual_full, up_stacked, precision=finest_precision
    )
    reduced_tangent = jnp.einsum(
        "wyov,yqv->wyoq", complete_tangent, adapter_up, precision=finest_precision
    )
    left_terms = jnp.concatenate(
        [
            weight_column * residual_reduced[..., :adapter_rank],
            weight_column * (reduced_tangent + residual_reduced[..., adapter_rank:]),
        ],
        axis=3,
    )
    down_terms = jnp.einsum(
        "cjif,cjik->jfk", hidden_rows.astype(jnp.float32), left_terms, precision=finest_precision
    )
    raised_update = weight_column * reduced_hidden[..., :adapter_rank]
    raised_tangent_update = weight_column * reduced_hidden[..., adapter_rank:]
    up_terms = jnp.einsum(
        "cjik,cjid->jkd",
        jnp.concatenate([raised_update, raised_tangent_update], axis=3),
        residual_full,
        precision=finest_precision,
    )
    curvature_piece = up_terms[:, adapter_rank:] + jnp.einsum(
        "cjik,cjid->jkd", raised_update, complete_tangent, precision=finest_precision
    )
    return (
        down_terms[..., :adapter_rank],
        up_terms[:, :adapter_rank],
        down_terms[..., adapter_rank:],
        curvature_piece,
    )


def local(*arguments):
    factor_bytes = 2 * 4 * (arguments[6].size + arguments[7].size) * lax.axis_size("expert")
    fits = lax.axis_size("expert") == 16 and 4 * factor_bytes <= kernel_vmem
    plan = gathered_plan if fits else routed_plan
    return plan(*arguments)


def solution(mesh):
    return jax.shard_map(
        local,
        mesh=mesh,
        in_specs=(
            P(("groups", "expert"), None, None),
            P(("groups", "expert"), None),
            P(("groups", "expert"), None),
            P("groups"),
            P(("groups", "expert"), None),
            P(("groups", "expert")),
            P("expert", None, None),
            P("expert", None, None),
            P(("groups", "expert"), None, None),
            P(("groups", "expert"), None, None),
        ),
        out_specs=(
            P(("groups", "expert"), None, None),
            P(("groups", "expert"), None, None),
            P(("groups", "expert"), None, None),
            P(("groups", "expert"), None, None),
        ),
        check_vma=False,
    )
```

```python
import functools

import jax
import jax.numpy as jnp
from jax import lax
from jax.experimental import pallas as pl
from jax.experimental.pallas import tpu as pltpu
from jax.sharding import PartitionSpec as P

adapter_scale = 2.0
f32 = jnp.float32
bf16 = jnp.bfloat16
i16 = jnp.int16
lanes = 128
counts_lane = 64
kernel_vmem = 32 * 2**20
whole_vmem = 60 * 2**20


def halves(value):
    high = value.astype(bf16)
    return high, (value - high.astype(f32)).astype(bf16)


def dot(a, b, a_dim, b_dim):
    return lax.dot_general(a, b, (((a_dim,), (b_dim,)), ((), ())), preferred_element_type=f32)


def dot_pairs(a, b, a_dim, b_dim):
    return dot(a[0], b[0], a_dim, b_dim) + (dot(a[1], b[0], a_dim, b_dim) + dot(a[0], b[1], a_dim, b_dim))


def encode(down, up, counts=0.0):
    def scaled(value):
        largest = jnp.max(jnp.abs(value), axis=-1, keepdims=True)
        exponent = jnp.ceil(jnp.log2(jnp.maximum(largest, 1e-30)))
        coded = jnp.round(value * jnp.exp2(15.0 - exponent))
        return jnp.clip(coded, -32767.0, 32767.0), exponent

    down, down_exponent = scaled(down)
    up, up_exponent = scaled(up)
    lane = lax.broadcasted_iota(jnp.int32, down.shape[:-1] + (lanes,), down.ndim - 1)
    tail = jnp.where(lane < counts_lane // 2, down_exponent, up_exponent)
    tail = jnp.where(lane < counts_lane, tail, counts)
    return jnp.concatenate([down, up, tail], axis=-1).astype(jnp.int32).astype(i16)


def decode(coded, hidden_width):
    width = coded.shape[-1] - lanes
    value = coded.astype(jnp.int32).astype(f32)
    down_scale = jnp.exp2(value[..., width : width + 1] - 15.0)
    up_scale = jnp.exp2(value[..., width + counts_lane // 2 : width + counts_lane // 2 + 1] - 15.0)
    return value[..., :hidden_width] * down_scale, value[..., hidden_width:width] * up_scale


def prepare_kernel(*refs):
    (piece_ref, small_ref), sem, refs = refs[7:9], refs[-1], refs[:7] + refs[9:-1]
    copies = [pltpu.make_async_copy(refs[i], refs[7 + i], sem.at[i]) for i in range(7)]
    for copy in copies:
        copy.start()
    for copy in copies:
        copy.wait()
    expert, gate, curvature, down_direction, adapter_down, adapter_up, up_direction = [ref[...] for ref in refs[7:]]
    top = expert.shape[0]
    small_ref[...] = jnp.zeros_like(small_ref)
    small_ref[:top] = expert.astype(f32)
    small_ref[top : 2 * top] = gate.astype(f32)
    small_ref[2 * top : 2 * top + 1] = curvature
    lane = lax.broadcasted_iota(jnp.int32, (1, lanes), 1)
    counts = jnp.zeros((1, lanes), f32)
    for number in range(lanes - counts_lane):
        named = jnp.where(expert == number, 1.0, 0.0)
        total = jnp.sum(jnp.sum(named, axis=0, keepdims=True), axis=1, keepdims=True)
        counts = jnp.where(lane == counts_lane + number, total, counts)
    piece_ref[0] = encode(down_direction, adapter_up, counts)
    piece_ref[1] = encode(adapter_down, up_direction, counts)


def token_columns(small_ref, top):
    experts = [small_ref[:, k : k + 1] for k in range(top)]
    gates = [small_ref[:, top + k : top + k + 1] for k in range(top)]
    return experts, gates, small_ref[:, 2 * top : 2 * top + 1]


def members(place_ref, wide, masks):
    slot_of = lax.broadcasted_iota(jnp.int32, (1, wide), 1) // (wide // len(masks))
    found = jnp.zeros((1, wide), jnp.int32)
    for slot, mask in enumerate(masks):
        found = jnp.where(slot_of == slot, place_ref[0] ^ mask, found)
    return found.astype(f32)


def prior_kernel(masks, place_ref, *rest):
    piece_refs, prior_ref = rest[:-1], rest[-1]
    me = place_ref[0]
    slots = len(masks)
    prior_ref[...] = jnp.zeros_like(prior_ref)
    for block, number in enumerate((me, me ^ 1)):
        total = jnp.zeros((1, lanes), f32)
        for offset in range(slots):
            piece_ref = piece_refs[offset]
            device = place_ref[1 + slots + offset]
            tail = piece_ref[0, :, piece_ref.shape[2] - lanes :]
            counts = tail.astype(jnp.int32).astype(f32)[0:1]
            total = total + jnp.where(device < number, counts, 0.0)
        prior_ref[block : block + 1] = total


def piece_part(refs, offset, kind):
    last = len(refs) - 2
    half = last // 2 + 1
    if offset == half:
        return refs[last + kind][0]
    return refs[offset if offset < half else offset - 1][kind]


def tokens_kernel(top, masks, place_ref, own_ref, other_ref, hidden_other_ref, gradient_other_ref, *outs):
    small_ref, rank_ref, gate_ref, same_ref, mask_ref, hidden_ref, gradient_ref, sem = outs
    copies = [
        pltpu.make_async_copy(hidden_other_ref, hidden_ref, sem.at[0]),
        pltpu.make_async_copy(gradient_other_ref, gradient_ref, sem.at[1]),
    ]
    for copy in copies:
        copy.start()
    small_ref[...] = jnp.concatenate([own_ref[...], other_ref[...]], axis=1).T
    experts, gates, _ = token_columns(small_ref, top)
    _, tokens, wide = rank_ref.shape
    column = members(place_ref, wide, masks)
    below = (
        lax.broadcasted_iota(jnp.int32, (tokens, tokens), 0)
        > lax.broadcasted_iota(jnp.int32, (tokens, tokens), 1)
    )
    below = jnp.where(below, 1.0, 0.0).astype(bf16)
    rows = same_ref.shape[0]
    row = lax.broadcasted_iota(jnp.int32, (rows, tokens), 0)
    same = jnp.where(row // top == lax.broadcasted_iota(jnp.int32, (rows, tokens), 1), 1.0, 0.0).astype(bf16)
    same_ref[...] = same
    for core in range(2):
        tokens_of = slice(core * tokens, (core + 1) * tokens)
        gate = jnp.zeros((tokens, wide), f32)
        member = jnp.zeros((tokens, wide), f32)
        for k in range(top):
            named = experts[k][tokens_of] == column
            gate = jnp.where(named, gates[k][tokens_of], gate)
            member = jnp.where(named, 1.0, member)
        gate_ref[core] = gate
        rank_ref[core] = dot(below, member.astype(bf16), 1, 0)
        named = dot(same, small_ref[tokens_of].astype(bf16), 1, 0)
        position = lax.broadcasted_iota(jnp.int32, named.shape, 0) % top
        own = lax.broadcasted_iota(jnp.int32, named.shape, 1) == position
        expert = jnp.sum(jnp.where(own, named, 0.0), axis=1, keepdims=True)
        mask_ref[core] = jnp.where(expert == column, 1.0, 0.0).astype(bf16)
    for copy in copies:
        copy.wait()


def reduce_kernel(top, masks, place_ref, small_ref, own_ref, other_ref, *rest):
    slots = len(masks)
    piece_refs, (reduced_ref, high_ref, low_ref, full_ref) = rest[: slots + 1], rest[slots + 1 :]
    hidden_width = own_ref.shape[1]
    for offset in range(slots):
        slot = place_ref[1 + offset]
        for kind in range(2):
            down, _ = decode(piece_part(piece_refs, offset, kind), hidden_width)
            high_ref[kind, slot], low_ref[kind, slot] = halves(down)
    experts, _, _ = token_columns(small_ref, top)
    wide = reduced_ref.shape[2]
    column = members(place_ref, wide, masks)
    high = high_ref[...].reshape(2 * wide, hidden_width)
    low = low_ref[...].reshape(2 * wide, hidden_width)
    tokens = own_ref.shape[0] // top
    for core, hidden_ref in enumerate((own_ref, other_ref)):
        full = dot(hidden_ref[...], high, 1, 1) + dot(hidden_ref[...], low, 1, 1)
        full_ref[0], full_ref[1] = full[:, :wide], full[:, wide:]
        tokens_of = slice(core * tokens, (core + 1) * tokens)
        for kind in range(2):
            total = jnp.zeros((tokens, wide), f32)
            for k in range(top):
                here = full_ref[kind, pl.ds(k, tokens, stride=top), :]
                total = jnp.where(experts[k][tokens_of] == column, here, total)
            reduced_ref[kind, tokens_of] = total


def rank_limits(place_ref, masks, wide, capacity_ref, prior_ref, arrived_ref):
    lane = lax.broadcasted_iota(jnp.int32, (1, lanes), 1)
    slot_of = lax.broadcasted_iota(jnp.int32, (1, wide), 1) // (wide // len(masks))
    limits = []
    for block in range(2):
        total = capacity_ref[...] - prior_ref[block : block + 1] - arrived_ref[1 - block : 2 - block]
        limit = jnp.zeros((1, wide), f32)
        for slot, mask in enumerate(masks):
            picked = jnp.where(lane == counts_lane + (place_ref[0] ^ mask), total, 0.0)
            limit = jnp.where(slot_of == slot, jnp.sum(picked, axis=1, keepdims=True), limit)
        limits.append(limit)
    return limits


def tangent_kernel(masks, place_ref, rank_ref, gate_ref, capacity_ref, prior_ref, arrived_ref, reduced_ref, *rest):
    slots = len(masks)
    piece_refs = rest[: slots + 1]
    weight_ref, weighted_ref, tangent_ref, coded_ref, high_ref, low_ref = rest[slots + 1 :]
    _, wide = weight_ref.shape
    model_width = tangent_ref.shape[1]
    hidden_width = piece_refs[0].shape[2] - model_width - lanes
    limits = rank_limits(place_ref, masks, wide, capacity_ref, prior_ref, arrived_ref)
    weights = [
        jnp.where(rank_ref[core] < limits[core], adapter_scale * gate_ref[core], 0.0) for core in range(2)
    ]
    weight = jnp.concatenate(weights, axis=0)
    weight_ref[...] = weight
    weighted = jnp.concatenate([weight * reduced_ref[0], weight * reduced_ref[1]], axis=1)
    weighted_ref[...] = weighted
    for offset in range(slots):
        slot = place_ref[1 + offset]
        for kind in range(2):
            _, up = decode(piece_part(piece_refs, offset, kind), hidden_width)
            high_ref[kind, slot], low_ref[kind, slot] = halves(up)
    factor = high_ref[...].reshape(2 * wide, model_width), low_ref[...].reshape(2 * wide, model_width)
    tangent = dot_pairs(halves(weighted), factor, 1, 0)
    tangent_ref[...] = tangent
    coded_ref[...] = tangent.astype(bf16)


def put_left(left_ref, same_ref, mask_ref, terms):
    both = jnp.concatenate(halves(terms), axis=1)
    tokens = terms.shape[0] // 2
    for core in range(2):
        repeated = dot(same_ref[...], both[core * tokens : (core + 1) * tokens], 1, 0).astype(bf16)
        mask = mask_ref[core]
        left_ref[core] = repeated * jnp.concatenate([mask, mask], axis=1)


def add_halves(both):
    middle = both.shape[0] // 2
    return both[:middle] + both[middle:]


def put_chunks(keep_ref, near_ref, chunk_ref, far_ref, down, up):
    rank = keep_ref.shape[1]
    rows = down.shape[0] // rank // 2

    def slot(number):
        start = number * rank
        return down[start : start + rank], up[start : start + rank]

    for place in range(2):
        keep_ref[place] = jnp.concatenate(slot(place), axis=1)
        near_ref[place] = encode(*slot(rows + place))
        chunk_ref[place] = jnp.concatenate(slot(place * rows + 2), axis=1)
        far_ref[place] = encode(*slot(place * rows + 3))


def gradient_kernel(
    same_ref,
    mask_ref,
    own_ref,
    other_ref,
    own_gradient_ref,
    other_gradient_ref,
    weight_ref,
    weighted_ref,
    high_ref,
    low_ref,
    keep_ref,
    near_ref,
    chunk_ref,
    far_ref,
    up_ref,
    to_ref,
    left_ref,
):
    wide = weight_ref.shape[1]
    model_width = up_ref.shape[1]
    gradient = jnp.concatenate([own_gradient_ref[...], other_gradient_ref[...]], axis=0)
    high = high_ref[...].reshape(2 * wide, model_width)
    low = low_ref[...].reshape(2 * wide, model_width)
    to_both = dot(gradient, high, 1, 1) + dot(gradient, low, 1, 1)
    to_ref[...] = to_both[:, wide:]
    put_left(left_ref, same_ref, mask_ref, weight_ref[...] * to_both[:, :wide])
    down = dot(left_ref[0], own_ref[...], 0, 0) + dot(left_ref[1], other_ref[...], 0, 0)
    up = add_halves(dot(jnp.concatenate(halves(weighted_ref[...]), axis=1), gradient, 0, 0))
    up_ref[...] = up[:wide]
    put_chunks(keep_ref, near_ref, chunk_ref, far_ref, add_halves(down), up[wide:])


def curvature_kernel(
    top,
    small_ref,
    same_ref,
    mask_ref,
    own_ref,
    other_ref,
    weight_ref,
    weighted_ref,
    high_ref,
    low_ref,
    up_ref,
    to_ref,
    tangent_ref,
    arrived_ref,
    keep_ref,
    near_ref,
    chunk_ref,
    far_ref,
    left_ref,
):
    _, _, curvature = token_columns(small_ref, top)
    tokens, wide = weight_ref.shape
    block = tokens // 2
    model_width = up_ref.shape[1]
    arrived = jnp.concatenate([arrived_ref[block:], arrived_ref[:block]], axis=0).astype(f32)
    resid = halves(curvature * (tangent_ref[...] + arrived))
    adapter_up = high_ref[0].reshape(wide, model_width), low_ref[0].reshape(wide, model_width)
    terms = weight_ref[...] * (dot_pairs(resid, adapter_up, 1, 1) + to_ref[...])
    put_left(left_ref, same_ref, mask_ref, terms)
    down = dot(left_ref[0], own_ref[...], 0, 0) + dot(left_ref[1], other_ref[...], 0, 0)
    weighted_u = halves(weighted_ref[:, wide:])
    up = add_halves(dot(jnp.concatenate(weighted_u, axis=1), resid[0], 0, 0)) + dot(weighted_u[0], resid[1], 0, 0)
    put_chunks(keep_ref, near_ref, chunk_ref, far_ref, add_halves(down), up_ref[...] + up)


def pair_kernel(hidden_width, arrived_ref, chunk_ref, near_ref, across_ref, keep_ref, onward_ref):
    onward_ref[...] = near_ref[...]
    for x in range(2):
        down, up = decode(arrived_ref[x], hidden_width)
        down, up = chunk_ref[x, :, :hidden_width] + down, chunk_ref[x, :, hidden_width:] + up
        if x == 0:
            keep_ref[...] = jnp.concatenate([down, up], axis=1)
        else:
            across_ref[...] = encode(down, up)


def far_kernel(hidden_width, arrived_ref, keep_ref, out_ref):
    down, up = decode(arrived_ref[...], hidden_width)
    out_ref[...] = encode(keep_ref[:, :hidden_width] + down, keep_ref[:, hidden_width:] + up)


def near_kernel(
    hidden_width, gradient_ref, curvature_ref, gradient_keep_ref, curvature_keep_ref, onward_ref, total_ref
):
    pairs = ((gradient_ref, gradient_keep_ref), (curvature_ref, curvature_keep_ref))
    for kind, (arrived_ref, keep_ref) in enumerate(pairs):
        for z in range(2):
            down, up = decode(arrived_ref[z], hidden_width)
            down, up = keep_ref[z, :, :hidden_width] + down, keep_ref[z, :, hidden_width:] + up
            if z == 0:
                total_ref[kind] = jnp.concatenate([down, up], axis=1)
            else:
                onward_ref[kind] = encode(down, up)


def add_kernel(hidden_width, total_ref, arrived_ref, out_ref):
    down, up = decode(arrived_ref[...], hidden_width)
    out_ref[:, :hidden_width] = total_ref[0, :, :hidden_width] + down
    out_ref[:, hidden_width:] = total_ref[0, :, hidden_width:] + up


def total_kernel(hidden_width, gradient_ref, total_ref, far_ref, pair_ref, *out_refs):
    far = decode(far_ref[...], hidden_width)
    totals = [
        (gradient_ref[:, :hidden_width], gradient_ref[:, hidden_width:]),
        (total_ref[1, :, :hidden_width] + far[0], total_ref[1, :, hidden_width:] + far[1]),
    ]
    for kind in range(2):
        down, up = decode(pair_ref[kind], hidden_width)
        out_refs[2 * kind][...] = totals[kind][0] + down
        out_refs[2 * kind + 1][...] = totals[kind][1] + up


class Ring:
    def __init__(self, size):
        self.length = size // 2
        rows = self.length // 2
        self.order = [4 * z for z in range(rows)] + [4 * z + 2 for z in reversed(range(rows))]

    def shift(self, value, step):
        pairs = [
            (chip + core, self.order[(place + step) % self.length] + core)
            for place, chip in enumerate(self.order)
            for core in range(2)
        ]
        return lax.ppermute(value, "expert", pairs)

    def members(self, me):
        rows = self.length // 2
        place = jnp.where(me // 2 % 2 == 0, me // 4, self.length - 1 - me // 4)
        there = (place + jnp.arange(self.length, dtype=jnp.int32)) % self.length
        return jnp.where(there < rows, 4 * there, 4 * (self.length - 1 - there) + 2) + me % 2

    def gather(self, own):
        half = self.length // 2
        found = {0: own}
        ahead, behind = own, own
        for step in range(1, half):
            behind = self.shift(behind, 1)
            ahead = self.shift(ahead, -1)
            found[self.length - step], found[step] = behind, ahead
        last = [self.shift(behind[:1], 1), self.shift(ahead[1:], -1)]
        return [found[offset] for offset in sorted(found)] + last


def exchange(value, mask):
    size = lax.axis_size("expert")
    return lax.ppermute(value, "expert", [(device, device ^ mask) for device in range(size)])


def gathered_plan(
    hidden_of_route,
    expert_of_route,
    gate_of_route,
    capacity,
    output_gradient,
    curvature,
    adapter_down,
    adapter_up,
    down_direction,
    up_direction,
):
    ring = Ring(lax.axis_size("expert"))
    slots = ring.length
    rows = slots // 2
    masks = [4 * z for z in range(rows)] + [4 * z + 2 for z in range(rows)]
    me = lax.axis_index("expert")
    tokens, top = expert_of_route.shape
    both = 2 * tokens
    hidden_width = hidden_of_route.shape[2]
    rank = adapter_down.shape[2]
    model_width = output_gradient.shape[1]
    experts = capacity.shape[0]
    wide = slots * rank
    coded_width = hidden_width + model_width + lanes

    ring_members = ring.members(me)
    differs = ring_members ^ me
    slot_of_offset = differs // 4 + rows * (differs // 2 % 2)
    place = jnp.concatenate([me[None], slot_of_offset, ring_members]).astype(jnp.int32)

    def call(kernel, multiplies, outs, *operands, scratch=(), after=(), grant=kernel_vmem):
        space = pltpu.HBM if kernel is prepare_kernel else pltpu.VMEM
        places = [pl.BlockSpec(memory_space=pl.ANY) for _ in after] + [
            pl.BlockSpec(memory_space=pltpu.SMEM if operand is place else space) for operand in operands
        ]
        return pl.pallas_call(
            lambda *refs: kernel(*refs[len(after) :]),
            out_shape=[jax.ShapeDtypeStruct(shape, dtype) for shape, dtype in outs],
            in_specs=places,
            scratch_shapes=scratch,
            compiler_params=pltpu.CompilerParams(vmem_limit_bytes=grant),
            cost_estimate=pl.CostEstimate(flops=2 * multiplies, bytes_accessed=2**20, transcendentals=0),
        )(*after, *operands)

    down_multiplies = 2 * top * both * hidden_width * wide
    up_multiplies = both * model_width * wide

    first = (
        expert_of_route.T,
        gate_of_route.T,
        curvature[None],
        down_direction[0].T,
        adapter_down[0].T,
        adapter_up[0],
        up_direction[0],
    )
    piece, small = call(
        prepare_kernel,
        10**8,
        [((2, rank, coded_width), i16), (((2 * top + 8) // 8 * 8, tokens), f32)],
        *first,
        scratch=[pltpu.VMEM(operand.shape, operand.dtype) for operand in first]
        + [pltpu.SemaphoreType.DMA((len(first),))],
        grant=whole_vmem,
    )
    small_other = exchange(small, 1)
    hidden = hidden_of_route.reshape(tokens * top, hidden_width)
    small_columns, local_rank, gate, same, mask, hidden_other, gradient_other = call(
        functools.partial(tokens_kernel, top, masks),
        10**9,
        [
            ((both, small.shape[0]), f32),
            ((2, tokens, wide), f32),
            ((2, tokens, wide), f32),
            ((top * tokens, tokens), bf16),
            ((2, top * tokens, wide), bf16),
            (hidden.shape, bf16),
            (output_gradient.shape, bf16),
        ],
        place,
        small,
        small_other,
        exchange(hidden, 1),
        exchange(output_gradient, 1),
        scratch=[pltpu.SemaphoreType.DMA((2,))],
    )
    pieces = ring.gather(piece)
    capacity_row = jnp.pad(capacity.astype(f32), (counts_lane, lanes - counts_lane - experts))[None, :]

    by_offset = pieces[:rows] + [pieces[-2]] + pieces[rows:-2]
    (prior,) = call(
        functools.partial(prior_kernel, masks), 10**8, [((8, lanes), f32)], place, *by_offset, after=[same]
    )
    prior_arrived = exchange(prior, 1)
    factor_halves = [pltpu.VMEM((2, slots, rank, hidden_width), bf16)] * 2
    (reduced,) = call(
        functools.partial(reduce_kernel, top, masks),
        2 * down_multiplies,
        [((2, both, wide), f32)],
        place,
        small_columns,
        hidden,
        hidden_other,
        *pieces,
        scratch=factor_halves + [pltpu.VMEM((2, tokens * top, wide), f32)],
        after=[prior],
    )
    weight, weighted, tangent, coded, high, low = call(
        functools.partial(tangent_kernel, masks),
        6 * up_multiplies,
        [
            ((both, wide), f32),
            ((both, 2 * wide), f32),
            ((both, model_width), f32),
            ((both, model_width), bf16),
            ((2, slots, rank, model_width), bf16),
            ((2, slots, rank, model_width), bf16),
        ],
        place,
        local_rank,
        gate,
        capacity_row,
        prior,
        prior_arrived,
        reduced,
        *pieces,
    )
    arrived = exchange(coded, 1)
    left = [pltpu.VMEM((2, top * tokens, 2 * wide), bf16)]
    chunks = [((2, rank, hidden_width + model_width), f32), ((2, rank, coded_width), i16)] * 2
    gradient_keep, gradient_near, gradient_chunk, gradient_far, up, to = call(
        gradient_kernel,
        down_multiplies + 8 * up_multiplies,
        chunks + [((wide, model_width), f32), ((both, wide), f32)],
        same,
        mask,
        hidden,
        hidden_other,
        output_gradient,
        gradient_other,
        weight,
        weighted,
        high,
        low,
        scratch=left,
    )
    gradient_far = exchange(gradient_far, 4)
    gradient_near = exchange(gradient_near, 2)
    curvature_keep, curvature_near, curvature_chunk, curvature_far = call(
        functools.partial(curvature_kernel, top),
        down_multiplies + 6 * up_multiplies,
        chunks,
        small_columns,
        same,
        mask,
        hidden,
        hidden_other,
        weight,
        weighted,
        high,
        low,
        up,
        to,
        tangent,
        arrived,
        scratch=left,
    )

    hop = 2 * 10**9

    one = (rank, hidden_width + model_width)
    one_coded = (rank, coded_width)

    def hop_call(kernel, outs, *operands, after=()):
        return call(functools.partial(kernel, hidden_width), hop, outs, *operands, after=after)

    curvature_far = exchange(curvature_far, 4)
    pair = [(one_coded, i16), (one, f32), ((2,) + one_coded, i16)]
    gradient_across, gradient_pair, curvature_near = hop_call(
        pair_kernel, pair, gradient_far, gradient_chunk, curvature_near, after=[curvature_keep]
    )
    curvature_near = exchange(curvature_near, 2)
    curvature_across, curvature_pair, gradient_near = hop_call(
        pair_kernel, pair, curvature_far, curvature_chunk, gradient_near, after=[gradient_across]
    )
    (gradient_beyond,) = hop_call(
        far_kernel,
        [(one_coded, i16)],
        exchange(gradient_across, 2),
        gradient_pair,
        after=[curvature_across],
    )
    onward, total = hop_call(
        near_kernel,
        [((2,) + one_coded, i16), ((2,) + one, f32)],
        gradient_near,
        curvature_near,
        gradient_keep,
        curvature_keep,
        after=[gradient_beyond],
    )
    (curvature_beyond,) = hop_call(
        far_kernel, [(one_coded, i16)], exchange(curvature_across, 2), curvature_pair, after=[onward]
    )
    (gradient_total,) = hop_call(
        add_kernel, [(one, f32)], total, exchange(gradient_beyond, 8), after=[curvature_beyond]
    )
    down_gradient, up_gradient, curvature_down, curvature_up = hop_call(
        total_kernel,
        [((rank, hidden_width), f32), ((rank, model_width), f32)] * 2,
        gradient_total,
        total,
        exchange(curvature_beyond, 8),
        exchange(onward, 4),
    )
    return down_gradient.T[None], up_gradient[None], curvature_down.T[None], curvature_up[None]


def carried_in(value, axis, join, neutral):
    count, mine = (lax.axis_size(axis), lax.axis_index(axis))
    pieces = lax.all_gather(value, axis)
    so_far = jnp.full_like(value, 0) + jnp.asarray(neutral, value.dtype)

    def lap(position, so_far):
        longer = join(so_far, pieces[position])
        return jnp.where(position < mine, longer, so_far)

    return lax.fori_loop(0, count - 1, lap, so_far)


def add_counts(earlier, later):
    return earlier + later


def routed_plan(
    hidden_of_route,
    expert_of_route,
    gate_of_route,
    capacity,
    output_gradient,
    curvature,
    adapter_down,
    adapter_up,
    down_direction,
    up_direction,
):
    finest_precision = lax.Precision.HIGHEST
    group_size = lax.axis_size("expert")
    tok_rows, top_count = expert_of_route.shape
    hidden_width = hidden_of_route.shape[2]
    resident_experts = adapter_down.shape[0]
    adapter_rank = adapter_down.shape[2]
    model_width = output_gradient.shape[1]
    experts = resident_experts * group_size
    slot_most = 2 * tok_rows * top_count // experts
    routes = expert_of_route.reshape(-1)
    onehot = (routes[:, None] == jnp.arange(experts, dtype=jnp.int32)[None, :]).astype(jnp.int32)
    earlier = jnp.cumsum(onehot, axis=0) - onehot
    local_rank = jnp.sum(earlier * onehot, axis=1)
    counts = jnp.sum(onehot, axis=0)
    prior_count = carried_in(counts, "expert", add_counts, jnp.zeros_like(counts))
    global_rank = local_rank + jnp.sum(onehot * prior_count[None, :], axis=1)
    route_limit = jnp.sum(onehot * capacity[None, :], axis=1)
    retained_mask = (global_rank < route_limit).astype(jnp.float32)
    weight_of_route = (
        adapter_scale * gate_of_route.reshape(-1).astype(jnp.float32) * retained_mask
    ).astype(jnp.bfloat16)
    slot_index = routes * slot_most + local_rank
    layout = (group_size, resident_experts, slot_most)
    send_hidden = (
        jnp.zeros((experts * slot_most, hidden_width), jnp.bfloat16)
        .at[slot_index]
        .set(hidden_of_route.reshape(-1, hidden_width))
        .reshape(layout + (hidden_width,))
    )
    send_weight = (
        jnp.zeros((experts * slot_most,), jnp.bfloat16)
        .at[slot_index]
        .set(weight_of_route)
        .reshape(layout)
    )
    down_stacked = jnp.concatenate([adapter_down, down_direction], axis=2)
    up_stacked = jnp.concatenate([adapter_up, up_direction], axis=1)

    def spread(token_rows):
        per_route = jnp.repeat(token_rows, top_count, axis=0)
        placed = (
            jnp.zeros((experts * slot_most, model_width), jnp.bfloat16)
            .at[slot_index]
            .set(per_route)
        )
        return placed.reshape(layout + (model_width,))

    send_residual = spread(output_gradient)
    pieces = (
        lax.all_to_all(send_hidden, "expert", split_axis=0, concat_axis=0, tiled=True),
        lax.all_to_all(send_weight, "expert", split_axis=0, concat_axis=0, tiled=True),
    )
    hidden_rows = pieces[0].astype(jnp.float32)
    weight_rows = pieces[1].astype(jnp.float32)[..., None]
    reduced_hidden = jnp.einsum(
        "cjif,jfk->cjik", hidden_rows, down_stacked, precision=finest_precision
    )
    exchanged_rows = jnp.concatenate(
        [reduced_hidden[..., adapter_rank:], reduced_hidden[..., :adapter_rank]], axis=3
    )
    tangent_out = weight_rows * jnp.einsum(
        "cjik,jkd->cjid", exchanged_rows, up_stacked, precision=finest_precision
    )
    returned = lax.all_to_all(
        tangent_out.astype(jnp.bfloat16), "expert", split_axis=0, concat_axis=0, tiled=True
    )
    results = (returned, reduced_hidden) + tuple(pieces)
    returned = results[0]
    reduced_hidden = results[1]
    hidden_rows = results[2]
    weight_rows = results[3]
    route_tangent = returned.reshape(experts * slot_most, model_width)[slot_index]
    out_tangent = jnp.sum(
        route_tangent.reshape(tok_rows, top_count, model_width).astype(jnp.float32), axis=1
    )
    resid_tangent = (curvature[:, None] * out_tangent).astype(jnp.bfloat16)
    send_tangent = spread(resid_tangent)
    residual_rows, tangent_rows = (
        lax.all_to_all(send_residual, "expert", split_axis=0, concat_axis=0, tiled=True),
        lax.all_to_all(send_tangent, "expert", split_axis=0, concat_axis=0, tiled=True),
    )
    residual_full = residual_rows.astype(jnp.float32)
    complete_tangent = tangent_rows.astype(jnp.float32)
    weight_column = weight_rows.astype(jnp.float32)[..., None]
    residual_reduced = jnp.einsum(
        "wyov,yqv->wyoq", residual_full, up_stacked, precision=finest_precision
    )
    reduced_tangent = jnp.einsum(
        "wyov,yqv->wyoq", complete_tangent, adapter_up, precision=finest_precision
    )
    left_terms = jnp.concatenate(
        [
            weight_column * residual_reduced[..., :adapter_rank],
            weight_column * (reduced_tangent + residual_reduced[..., adapter_rank:]),
        ],
        axis=3,
    )
    down_terms = jnp.einsum(
        "cjif,cjik->jfk", hidden_rows.astype(jnp.float32), left_terms, precision=finest_precision
    )
    raised_update = weight_column * reduced_hidden[..., :adapter_rank]
    raised_tangent_update = weight_column * reduced_hidden[..., adapter_rank:]
    up_terms = jnp.einsum(
        "cjik,cjid->jkd",
        jnp.concatenate([raised_update, raised_tangent_update], axis=3),
        residual_full,
        precision=finest_precision,
    )
    curvature_piece = up_terms[:, adapter_rank:] + jnp.einsum(
        "cjik,cjid->jkd", raised_update, complete_tangent, precision=finest_precision
    )
    return (
        down_terms[..., :adapter_rank],
        up_terms[:, :adapter_rank],
        down_terms[..., adapter_rank:],
        curvature_piece,
    )


def local(*arguments):
    factor_bytes = 2 * 4 * (arguments[6].size + arguments[7].size) * lax.axis_size("expert")
    fits = lax.axis_size("expert") == 16 and 4 * factor_bytes <= kernel_vmem
    plan = gathered_plan if fits else routed_plan
    return plan(*arguments)


def solution(mesh):
    return jax.shard_map(
        local,
        mesh=mesh,
        in_specs=(
            P(("groups", "expert"), None, None),
            P(("groups", "expert"), None),
            P(("groups", "expert"), None),
            P("groups"),
            P(("groups", "expert"), None),
            P(("groups", "expert")),
            P("expert", None, None),
            P("expert", None, None),
            P(("groups", "expert"), None, None),
            P(("groups", "expert"), None, None),
        ),
        out_specs=(
            P(("groups", "expert"), None, None),
            P(("groups", "expert"), None, None),
            P(("groups", "expert"), None, None),
            P(("groups", "expert"), None, None),
        ),
        check_vma=False,
    )
```

```python
import functools

import jax
import jax.numpy as jnp
from jax import lax
from jax.experimental import pallas as pl
from jax.experimental.pallas import tpu as pltpu
from jax.sharding import PartitionSpec as P

adapter_scale = 2.0
f32 = jnp.float32
bf16 = jnp.bfloat16
i16 = jnp.int16
lanes = 128
counts_lane = 64
kernel_vmem = 32 * 2**20
whole_vmem = 60 * 2**20


def halves(value):
    high = value.astype(bf16)
    return high, (value - high.astype(f32)).astype(bf16)


def dot(a, b, a_dim, b_dim):
    return lax.dot_general(a, b, (((a_dim,), (b_dim,)), ((), ())), preferred_element_type=f32)


def dot_pairs(a, b, a_dim, b_dim):
    return dot(a[0], b[0], a_dim, b_dim) + (dot(a[1], b[0], a_dim, b_dim) + dot(a[0], b[1], a_dim, b_dim))


def encode(down, up, counts=0.0):
    def scaled(value):
        largest = jnp.max(jnp.abs(value), axis=-1, keepdims=True)
        exponent = jnp.ceil(jnp.log2(jnp.maximum(largest, 1e-30)))
        coded = jnp.round(value * jnp.exp2(15.0 - exponent))
        return jnp.clip(coded, -32767.0, 32767.0), exponent

    down, down_exponent = scaled(down)
    up, up_exponent = scaled(up)
    lane = lax.broadcasted_iota(jnp.int32, down.shape[:-1] + (lanes,), down.ndim - 1)
    tail = jnp.where(lane < counts_lane // 2, down_exponent, up_exponent)
    tail = jnp.where(lane < counts_lane, tail, counts)
    return jnp.concatenate([down, up, tail], axis=-1).astype(jnp.int32).astype(i16)


def decode(coded, hidden_width):
    width = coded.shape[-1] - lanes
    value = coded.astype(jnp.int32).astype(f32)
    down_scale = jnp.exp2(value[..., width : width + 1] - 15.0)
    up_scale = jnp.exp2(value[..., width + counts_lane // 2 : width + counts_lane // 2 + 1] - 15.0)
    return value[..., :hidden_width] * down_scale, value[..., hidden_width:width] * up_scale


def prepare_kernel(experts, *refs):
    (piece_ref, small_ref), sem, refs = refs[7:9], refs[-1], refs[:7] + refs[9:-1]
    copies = [pltpu.make_async_copy(refs[i], refs[7 + i], sem.at[i]) for i in range(7)]
    for copy in copies:
        copy.start()
    for copy in copies:
        copy.wait()
    expert, gate, curvature, down_direction, adapter_down, adapter_up, up_direction = [ref[...] for ref in refs[7:]]
    top = expert.shape[0]
    small_ref[...] = jnp.zeros_like(small_ref)
    small_ref[:top] = expert.astype(f32)
    small_ref[top : 2 * top] = gate.astype(f32)
    small_ref[2 * top : 2 * top + 1] = curvature
    lane = lax.broadcasted_iota(jnp.int32, (1, lanes), 1)
    counts = jnp.zeros((1, lanes), f32)
    for number in range(experts):
        named = jnp.where(expert == number, 1.0, 0.0)
        total = jnp.sum(jnp.sum(named, axis=0, keepdims=True), axis=1, keepdims=True)
        counts = jnp.where(lane == counts_lane + number, total, counts)
    piece_ref[0] = encode(down_direction, adapter_up, counts)
    piece_ref[1] = encode(adapter_down, up_direction, counts)


def token_columns(small_ref, top):
    experts = [small_ref[:, k : k + 1] for k in range(top)]
    gates = [small_ref[:, top + k : top + k + 1] for k in range(top)]
    return experts, gates, small_ref[:, 2 * top : 2 * top + 1]


def members(place_ref, wide, first=0, count=None):
    piece_of = lax.broadcasted_iota(jnp.int32, (1, wide), 1) // (wide // count)
    found = jnp.zeros((1, wide), jnp.int32)
    for number in range(count):
        found = jnp.where(piece_of == number, place_ref[1 + first + number], found)
    return found.astype(f32)


def prior_kernel(place_ref, *rest):
    piece_refs, prior_ref = rest[:-1], rest[-1]
    me = place_ref[0]
    prior_ref[...] = jnp.zeros_like(prior_ref)
    for block, number in enumerate((me, me ^ 1)):
        total = jnp.zeros((1, lanes), f32)
        for arrival, piece_ref in enumerate(piece_refs):
            tail = piece_ref[0, :, piece_ref.shape[2] - lanes :]
            counts = tail.astype(jnp.int32).astype(f32)[0:1]
            total = total + jnp.where(place_ref[1 + arrival] < number, counts, 0.0)
        prior_ref[block : block + 1] = total


def piece_part(refs, arrival, kind, halved):
    if halved and arrival == len(refs) - 2:
        return refs[arrival + kind][0]
    return refs[arrival][kind]


def tokens_kernel(top, slots, place_ref, own_ref, other_ref, hidden_other_ref, gradient_other_ref, *outs):
    small_ref, rank_ref, gate_ref, same_ref, mask_ref, hidden_ref, gradient_ref, sem = outs
    copies = [
        pltpu.make_async_copy(hidden_other_ref, hidden_ref, sem.at[0]),
        pltpu.make_async_copy(gradient_other_ref, gradient_ref, sem.at[1]),
    ]
    for copy in copies:
        copy.start()
    small_ref[...] = jnp.concatenate([own_ref[...], other_ref[...]], axis=1).T
    experts, gates, _ = token_columns(small_ref, top)
    _, tokens, wide = rank_ref.shape
    column = members(place_ref, wide, 0, slots)
    below = (
        lax.broadcasted_iota(jnp.int32, (tokens, tokens), 0)
        > lax.broadcasted_iota(jnp.int32, (tokens, tokens), 1)
    )
    below = jnp.where(below, 1.0, 0.0).astype(bf16)
    rows = same_ref.shape[0]
    row = lax.broadcasted_iota(jnp.int32, (rows, tokens), 0)
    same = jnp.where(row // top == lax.broadcasted_iota(jnp.int32, (rows, tokens), 1), 1.0, 0.0).astype(bf16)
    same_ref[...] = same
    for core in range(2):
        tokens_of = slice(core * tokens, (core + 1) * tokens)
        gate = jnp.zeros((tokens, wide), f32)
        member = jnp.zeros((tokens, wide), f32)
        for k in range(top):
            named = experts[k][tokens_of] == column
            gate = jnp.where(named, gates[k][tokens_of], gate)
            member = jnp.where(named, 1.0, member)
        gate_ref[core] = gate
        rank_ref[core] = dot(below, member.astype(bf16), 1, 0)
        named = dot(same, small_ref[tokens_of].astype(bf16), 1, 0)
        position = lax.broadcasted_iota(jnp.int32, named.shape, 0) % top
        own = lax.broadcasted_iota(jnp.int32, named.shape, 1) == position
        expert = jnp.sum(jnp.where(own, named, 0.0), axis=1, keepdims=True)
        mask_ref[core] = jnp.where(expert == column, 1.0, 0.0).astype(bf16)
    for copy in copies:
        copy.wait()


def pass_kernel(behind_ref, ahead_ref, behind_out_ref, ahead_out_ref):
    behind_out_ref[...] = behind_ref[...]
    ahead_out_ref[...] = ahead_ref[...]


def reduce_kernel(top, first, count, halved, place_ref, small_ref, own_ref, other_ref, *rest):
    piece_refs, (reduced_ref, full_ref) = rest[:-2], rest[-2:]
    hidden_width = own_ref.shape[1]
    downs = [
        decode(piece_part(piece_refs, arrival, kind, halved), hidden_width)[0]
        for kind in range(2)
        for arrival in range(count)
    ]
    factor = jnp.concatenate(halves(jnp.concatenate(downs, axis=0)), axis=0)
    experts, _, _ = token_columns(small_ref, top)
    wide = reduced_ref.shape[1]
    column = members(place_ref, wide // 2, first, count)
    column = jnp.concatenate([column, column], axis=1)
    tokens = own_ref.shape[0] // top
    for core, hidden_ref in enumerate((own_ref, other_ref)):
        full = dot(hidden_ref[...], factor, 1, 1)
        full_ref[...] = full[:, :wide] + full[:, wide:]
        tokens_of = slice(core * tokens, (core + 1) * tokens)
        total = jnp.zeros((tokens, wide), f32)
        for k in range(top):
            here = full_ref[pl.ds(k, tokens, stride=top), :]
            total = jnp.where(experts[k][tokens_of] == column, here, total)
        reduced_ref[tokens_of] = total


def rank_limits(place_ref, wide, slots, capacity_ref, prior_ref, arrived_ref):
    lane = lax.broadcasted_iota(jnp.int32, (1, lanes), 1)
    piece_of = lax.broadcasted_iota(jnp.int32, (1, wide), 1) // (wide // slots)
    limits = []
    for block in range(2):
        total = capacity_ref[...] - prior_ref[block : block + 1] - arrived_ref[1 - block : 2 - block]
        limit = jnp.zeros((1, wide), f32)
        for arrival in range(slots):
            picked = jnp.where(lane == counts_lane + place_ref[1 + arrival], total, 0.0)
            limit = jnp.where(piece_of == arrival, jnp.sum(picked, axis=1, keepdims=True), limit)
        limits.append(limit)
    return limits


def tangent_kernel(
    slots, place_ref, rank_ref, gate_ref, capacity_ref, prior_ref, arrived_ref, early_ref, late_ref, *rest
):
    piece_refs = rest[: slots + 1]
    weight_ref, weighted_ref, tangent_ref, coded_ref, high_ref, low_ref = rest[slots + 1 :]
    _, wide = weight_ref.shape
    model_width = tangent_ref.shape[1]
    hidden_width = piece_refs[0].shape[2] - model_width - lanes
    limits = rank_limits(place_ref, wide, slots, capacity_ref, prior_ref, arrived_ref)
    weights = [
        jnp.where(rank_ref[core] < limits[core], adapter_scale * gate_ref[core], 0.0) for core in range(2)
    ]
    weight = jnp.concatenate(weights, axis=0)
    weight_ref[...] = weight
    half = wide // 2
    reduced = [
        jnp.concatenate([ref[:, kind * half : (kind + 1) * half] for ref in (early_ref, late_ref)], axis=1)
        for kind in range(2)
    ]
    weighted = jnp.concatenate([weight * part for part in reduced], axis=1)
    weighted_ref[...] = weighted
    for arrival in range(slots):
        for kind in range(2):
            _, up = decode(piece_part(piece_refs, arrival, kind, True), hidden_width)
            high_ref[kind, arrival], low_ref[kind, arrival] = halves(up)
    factor = high_ref[...].reshape(2 * wide, model_width), low_ref[...].reshape(2 * wide, model_width)
    tangent = dot_pairs(halves(weighted), factor, 1, 0)
    tangent_ref[...] = tangent
    coded_ref[...] = tangent.astype(bf16)


def put_left(left_ref, same_ref, mask_ref, terms):
    both = jnp.concatenate(halves(terms), axis=1)
    tokens = terms.shape[0] // 2
    for core in range(2):
        repeated = dot(same_ref[...], both[core * tokens : (core + 1) * tokens], 1, 0).astype(bf16)
        mask = mask_ref[core]
        left_ref[core] = repeated * jnp.concatenate([mask, mask], axis=1)


def add_halves(both):
    middle = both.shape[0] // 2
    return both[:middle] + both[middle:]


def put_chunks(place_ref, down_ref, up_ref, keep_ref, near_ref, chunk_ref, far_ref, down, up):
    rank = keep_ref.shape[1]
    slots = down.shape[0] // rank
    down_ref[...] = down
    up_ref[...] = up

    def slot(number):
        start = pl.multiple_of(place_ref[1 + slots + number] * rank, rank)
        return down_ref[pl.ds(start, rank), :], up_ref[pl.ds(start, rank), :]

    for place in range(2):
        keep_ref[place] = jnp.concatenate(slot(place), axis=1)
        near_ref[place] = encode(*slot(slots // 2 + place))
        chunk_ref[place] = jnp.concatenate(slot(place * slots // 2 + 2), axis=1)
        far_ref[place] = encode(*slot(place * slots // 2 + 3))


def gradient_kernel(
    place_ref,
    same_ref,
    mask_ref,
    own_ref,
    other_ref,
    own_gradient_ref,
    other_gradient_ref,
    weight_ref,
    weighted_ref,
    high_ref,
    low_ref,
    keep_ref,
    near_ref,
    chunk_ref,
    far_ref,
    up_ref,
    to_ref,
    left_ref,
    down_sum_ref,
    up_sum_ref,
):
    wide = weight_ref.shape[1]
    model_width = up_ref.shape[1]
    gradient = jnp.concatenate([own_gradient_ref[...], other_gradient_ref[...]], axis=0)
    high = high_ref[...].reshape(2 * wide, model_width)
    low = low_ref[...].reshape(2 * wide, model_width)
    to_both = dot(gradient, high, 1, 1) + dot(gradient, low, 1, 1)
    to_ref[...] = to_both[:, wide:]
    put_left(left_ref, same_ref, mask_ref, weight_ref[...] * to_both[:, :wide])
    down = dot(left_ref[0], own_ref[...], 0, 0) + dot(left_ref[1], other_ref[...], 0, 0)
    up = add_halves(dot(jnp.concatenate(halves(weighted_ref[...]), axis=1), gradient, 0, 0))
    up_ref[...] = up[:wide]
    out_refs = keep_ref, near_ref, chunk_ref, far_ref
    put_chunks(place_ref, down_sum_ref, up_sum_ref, *out_refs, add_halves(down), up[wide:])


def curvature_kernel(
    top,
    place_ref,
    small_ref,
    same_ref,
    mask_ref,
    own_ref,
    other_ref,
    weight_ref,
    weighted_ref,
    high_ref,
    low_ref,
    up_ref,
    to_ref,
    tangent_ref,
    arrived_ref,
    keep_ref,
    near_ref,
    chunk_ref,
    far_ref,
    left_ref,
    down_sum_ref,
    up_sum_ref,
):
    _, _, curvature = token_columns(small_ref, top)
    tokens, wide = weight_ref.shape
    block = tokens // 2
    model_width = up_ref.shape[1]
    arrived = jnp.concatenate([arrived_ref[block:], arrived_ref[:block]], axis=0).astype(f32)
    resid = halves(curvature * (tangent_ref[...] + arrived))
    adapter_up = high_ref[0].reshape(wide, model_width), low_ref[0].reshape(wide, model_width)
    terms = weight_ref[...] * (dot_pairs(resid, adapter_up, 1, 1) + to_ref[...])
    put_left(left_ref, same_ref, mask_ref, terms)
    down = dot(left_ref[0], own_ref[...], 0, 0) + dot(left_ref[1], other_ref[...], 0, 0)
    weighted_u = halves(weighted_ref[:, wide:])
    up = add_halves(dot(jnp.concatenate(weighted_u, axis=1), resid[0], 0, 0)) + dot(weighted_u[0], resid[1], 0, 0)
    out_refs = keep_ref, near_ref, chunk_ref, far_ref
    put_chunks(place_ref, down_sum_ref, up_sum_ref, *out_refs, add_halves(down), up_ref[...] + up)


def pair_kernel(hidden_width, arrived_ref, chunk_ref, near_ref, across_ref, keep_ref, onward_ref):
    onward_ref[...] = near_ref[...]
    for x in range(2):
        down, up = decode(arrived_ref[x], hidden_width)
        down, up = chunk_ref[x, :, :hidden_width] + down, chunk_ref[x, :, hidden_width:] + up
        if x == 0:
            keep_ref[...] = jnp.concatenate([down, up], axis=1)
        else:
            across_ref[...] = encode(down, up)


def far_kernel(hidden_width, arrived_ref, keep_ref, out_ref):
    down, up = decode(arrived_ref[...], hidden_width)
    out_ref[...] = encode(keep_ref[:, :hidden_width] + down, keep_ref[:, hidden_width:] + up)


def near_kernel(
    hidden_width, gradient_ref, curvature_ref, gradient_keep_ref, curvature_keep_ref, onward_ref, total_ref
):
    pairs = ((gradient_ref, gradient_keep_ref), (curvature_ref, curvature_keep_ref))
    for kind, (arrived_ref, keep_ref) in enumerate(pairs):
        for z in range(2):
            down, up = decode(arrived_ref[z], hidden_width)
            down, up = keep_ref[z, :, :hidden_width] + down, keep_ref[z, :, hidden_width:] + up
            if z == 0:
                total_ref[kind] = jnp.concatenate([down, up], axis=1)
            else:
                onward_ref[kind] = encode(down, up)


def add_kernel(hidden_width, total_ref, arrived_ref, out_ref):
    down, up = decode(arrived_ref[...], hidden_width)
    out_ref[:, :hidden_width] = total_ref[0, :, :hidden_width] + down
    out_ref[:, hidden_width:] = total_ref[0, :, hidden_width:] + up


def total_kernel(hidden_width, gradient_ref, total_ref, far_ref, pair_ref, *out_refs):
    far = decode(far_ref[...], hidden_width)
    totals = [
        (gradient_ref[:, :hidden_width], gradient_ref[:, hidden_width:]),
        (total_ref[1, :, :hidden_width] + far[0], total_ref[1, :, hidden_width:] + far[1]),
    ]
    for kind in range(2):
        down, up = decode(pair_ref[kind], hidden_width)
        out_refs[2 * kind][...] = totals[kind][0] + down
        out_refs[2 * kind + 1][...] = totals[kind][1] + up


class Ring:
    def __init__(self, size):
        self.length = size // 2
        rows = self.length // 2
        self.order = [4 * z for z in range(rows)] + [4 * z + 2 for z in reversed(range(rows))]

    def shift(self, value, step):
        pairs = [
            (chip + core, self.order[(place + step) % self.length] + core)
            for place, chip in enumerate(self.order)
            for core in range(2)
        ]
        return lax.ppermute(value, "expert", pairs)

    def members(self, me):
        rows = self.length // 2
        place = jnp.where(me // 2 % 2 == 0, me // 4, self.length - 1 - me // 4)
        half = self.length // 2
        offsets = [0] + [offset for step in range(1, half) for offset in (self.length - step, step)] + [half]
        there = (place + jnp.array(offsets, jnp.int32)) % self.length
        return jnp.where(there < rows, 4 * there, 4 * (self.length - 1 - there) + 2) + me % 2

    def gather(self, own, passing):
        half = self.length // 2
        pieces = [own]
        ahead, behind = own, own
        for step in range(1, half):
            behind = self.shift(behind, 1)
            ahead = self.shift(ahead, -1)
            if step == 2:
                behind, ahead = passing(behind, ahead)
            pieces += [behind, ahead]
        pieces += [self.shift(behind[:1], 1), self.shift(ahead[1:], -1)]
        return pieces


def exchange(value, mask):
    size = lax.axis_size("expert")
    return lax.ppermute(value, "expert", [(device, device ^ mask) for device in range(size)])


def gathered_plan(
    hidden_of_route,
    expert_of_route,
    gate_of_route,
    capacity,
    output_gradient,
    curvature,
    adapter_down,
    adapter_up,
    down_direction,
    up_direction,
):
    ring = Ring(lax.axis_size("expert"))
    slots = ring.length
    rows = slots // 2
    masks = [4 * z for z in range(rows)] + [4 * z + 2 for z in range(rows)]
    me = lax.axis_index("expert")
    tokens, top = expert_of_route.shape
    both = 2 * tokens
    hidden_width = hidden_of_route.shape[2]
    rank = adapter_down.shape[2]
    model_width = output_gradient.shape[1]
    experts = capacity.shape[0]
    wide = slots * rank
    coded_width = hidden_width + model_width + lanes


    place = []

    def call(kernel, multiplies, outs, *operands, scratch=(), after=(), grant=kernel_vmem):
        space = pltpu.VMEM if grant == kernel_vmem else pltpu.HBM
        places = [pl.BlockSpec(memory_space=pl.ANY) for _ in after] + [
            pl.BlockSpec(memory_space=pltpu.SMEM if any(operand is it for it in place) else space) for operand in operands
        ]
        return pl.pallas_call(
            lambda *refs: kernel(*refs[len(after) :]),
            out_shape=[jax.ShapeDtypeStruct(shape, dtype) for shape, dtype in outs],
            in_specs=places,
            scratch_shapes=scratch,
            compiler_params=pltpu.CompilerParams(vmem_limit_bytes=grant),
            cost_estimate=pl.CostEstimate(flops=2 * multiplies, bytes_accessed=2**20, transcendentals=0),
        )(*after, *operands)

    down_multiplies = 2 * top * both * hidden_width * wide
    up_multiplies = both * model_width * wide

    first = (
        expert_of_route.T,
        gate_of_route.T,
        curvature[None],
        down_direction[0].T,
        adapter_down[0].T,
        adapter_up[0],
        up_direction[0],
    )
    piece, small = call(
        functools.partial(prepare_kernel, experts),
        10**8,
        [((2, rank, coded_width), i16), (((2 * top + 8) // 8 * 8, tokens), f32)],
        *first,
        scratch=[pltpu.VMEM(operand.shape, operand.dtype) for operand in first]
        + [pltpu.SemaphoreType.DMA((len(first),))],
        grant=whole_vmem,
    )
    arrivals = ring.members(me)
    number = jnp.arange(slots, dtype=jnp.int32)
    slot_of_arrival = (arrivals ^ me) // 4 + rows * ((arrivals ^ me) // 2 % 2)
    arrival_of_slot = jnp.sum(jnp.where(slot_of_arrival == number[:, None], number, 0), axis=1)
    place.append(jnp.concatenate([me[None], arrivals, arrival_of_slot]).astype(jnp.int32))
    small_other = exchange(small, 1)
    hidden = hidden_of_route.reshape(tokens * top, hidden_width)
    small_columns, local_rank, gate, same, mask, hidden_other, gradient_other = call(
        functools.partial(tokens_kernel, top, slots),
        10**9,
        [
            ((both, small.shape[0]), f32),
            ((2, tokens, wide), f32),
            ((2, tokens, wide), f32),
            ((top * tokens, tokens), bf16),
            ((2, top * tokens, wide), bf16),
            (hidden.shape, bf16),
            (output_gradient.shape, bf16),
        ],
        *place,
        small,
        small_other,
        exchange(hidden, 1),
        exchange(output_gradient, 1),
        scratch=[pltpu.SemaphoreType.DMA((2,))],
    )
    def passing(behind, ahead):
        return call(pass_kernel, 10**8, [(piece.shape, i16)] * 2, behind, ahead, after=[same])

    pieces = ring.gather(piece, passing)
    capacity_row = jnp.pad(capacity.astype(f32), (counts_lane, lanes - counts_lane - experts))[None, :]

    def reduced(first, count, halved, *parts, after=()):
        return call(
            functools.partial(reduce_kernel, top, first, count, halved),
            2 * down_multiplies * count // slots,
            [((both, 2 * count * rank), f32)],
            *place,
            small_columns,
            hidden,
            hidden_other,
            *parts,
            scratch=[pltpu.VMEM((tokens * top, 2 * count * rank), f32)],
            after=after,
        )[0]

    early = slots // 2
    reduced_early = reduced(0, early, False, *pieces[:early])
    (prior,) = call(prior_kernel, 10**8, [((8, lanes), f32)], *place, *pieces[:-1], after=[reduced_early])
    prior_arrived = exchange(prior, 1)
    reduced_late = reduced(early, slots - early, True, *pieces[early:], after=[prior])
    weight, weighted, tangent, coded, high, low = call(
        functools.partial(tangent_kernel, slots),
        6 * up_multiplies,
        [
            ((both, wide), f32),
            ((both, 2 * wide), f32),
            ((both, model_width), f32),
            ((both, model_width), bf16),
            ((2, slots, rank, model_width), bf16),
            ((2, slots, rank, model_width), bf16),
        ],
        *place,
        local_rank,
        gate,
        capacity_row,
        prior,
        prior_arrived,
        reduced_early,
        reduced_late,
        *pieces,
    )
    arrived = exchange(coded, 1)
    left = [
        pltpu.VMEM((2, top * tokens, 2 * wide), bf16),
        pltpu.VMEM((wide, hidden_width), f32),
        pltpu.VMEM((wide, model_width), f32),
    ]
    chunks = [((2, rank, hidden_width + model_width), f32), ((2, rank, coded_width), i16)] * 2
    gradient_keep, gradient_near, gradient_chunk, gradient_far, up, to = call(
        gradient_kernel,
        down_multiplies + 8 * up_multiplies,
        chunks + [((wide, model_width), f32), ((both, wide), f32)],
        *place,
        same,
        mask,
        hidden,
        hidden_other,
        output_gradient,
        gradient_other,
        weight,
        weighted,
        high,
        low,
        scratch=left,
    )
    gradient_far = exchange(gradient_far, 4)
    gradient_near = exchange(gradient_near, 2)
    curvature_keep, curvature_near, curvature_chunk, curvature_far = call(
        functools.partial(curvature_kernel, top),
        down_multiplies + 6 * up_multiplies,
        chunks,
        *place,
        small_columns,
        same,
        mask,
        hidden,
        hidden_other,
        weight,
        weighted,
        high,
        low,
        up,
        to,
        tangent,
        arrived,
        scratch=left,
    )

    hop = 2 * 10**9

    one = (rank, hidden_width + model_width)
    one_coded = (rank, coded_width)

    def hop_call(kernel, outs, *operands, after=()):
        return call(functools.partial(kernel, hidden_width), hop, outs, *operands, after=after)

    curvature_far = exchange(curvature_far, 4)
    pair = [(one_coded, i16), (one, f32), ((2,) + one_coded, i16)]
    gradient_across, gradient_pair, curvature_near = hop_call(
        pair_kernel, pair, gradient_far, gradient_chunk, curvature_near, after=[curvature_keep]
    )
    curvature_near = exchange(curvature_near, 2)
    curvature_across, curvature_pair, gradient_near = hop_call(
        pair_kernel, pair, curvature_far, curvature_chunk, gradient_near, after=[gradient_across]
    )
    (gradient_beyond,) = hop_call(
        far_kernel,
        [(one_coded, i16)],
        exchange(gradient_across, 2),
        gradient_pair,
        after=[curvature_across],
    )
    onward, total = hop_call(
        near_kernel,
        [((2,) + one_coded, i16), ((2,) + one, f32)],
        gradient_near,
        curvature_near,
        gradient_keep,
        curvature_keep,
        after=[gradient_beyond],
    )
    (curvature_beyond,) = hop_call(
        far_kernel, [(one_coded, i16)], exchange(curvature_across, 2), curvature_pair, after=[onward]
    )
    (gradient_total,) = hop_call(
        add_kernel, [(one, f32)], total, exchange(gradient_beyond, 8), after=[curvature_beyond]
    )
    down_gradient, up_gradient, curvature_down, curvature_up = hop_call(
        total_kernel,
        [((rank, hidden_width), f32), ((rank, model_width), f32)] * 2,
        gradient_total,
        total,
        exchange(curvature_beyond, 8),
        exchange(onward, 4),
    )
    return down_gradient.T[None], up_gradient[None], curvature_down.T[None], curvature_up[None]


def carried_in(value, axis, join, neutral):
    count, mine = (lax.axis_size(axis), lax.axis_index(axis))
    pieces = lax.all_gather(value, axis)
    so_far = jnp.full_like(value, 0) + jnp.asarray(neutral, value.dtype)

    def lap(position, so_far):
        longer = join(so_far, pieces[position])
        return jnp.where(position < mine, longer, so_far)

    return lax.fori_loop(0, count - 1, lap, so_far)


def add_counts(earlier, later):
    return earlier + later


def routed_plan(
    hidden_of_route,
    expert_of_route,
    gate_of_route,
    capacity,
    output_gradient,
    curvature,
    adapter_down,
    adapter_up,
    down_direction,
    up_direction,
):
    finest_precision = lax.Precision.HIGHEST
    group_size = lax.axis_size("expert")
    tok_rows, top_count = expert_of_route.shape
    hidden_width = hidden_of_route.shape[2]
    resident_experts = adapter_down.shape[0]
    adapter_rank = adapter_down.shape[2]
    model_width = output_gradient.shape[1]
    experts = resident_experts * group_size
    slot_most = 2 * tok_rows * top_count // experts
    routes = expert_of_route.reshape(-1)
    onehot = (routes[:, None] == jnp.arange(experts, dtype=jnp.int32)[None, :]).astype(jnp.int32)
    earlier = jnp.cumsum(onehot, axis=0) - onehot
    local_rank = jnp.sum(earlier * onehot, axis=1)
    counts = jnp.sum(onehot, axis=0)
    prior_count = carried_in(counts, "expert", add_counts, jnp.zeros_like(counts))
    global_rank = local_rank + jnp.sum(onehot * prior_count[None, :], axis=1)
    route_limit = jnp.sum(onehot * capacity[None, :], axis=1)
    retained_mask = (global_rank < route_limit).astype(jnp.float32)
    weight_of_route = (
        adapter_scale * gate_of_route.reshape(-1).astype(jnp.float32) * retained_mask
    ).astype(jnp.bfloat16)
    slot_index = routes * slot_most + local_rank
    layout = (group_size, resident_experts, slot_most)
    send_hidden = (
        jnp.zeros((experts * slot_most, hidden_width), jnp.bfloat16)
        .at[slot_index]
        .set(hidden_of_route.reshape(-1, hidden_width))
        .reshape(layout + (hidden_width,))
    )
    send_weight = (
        jnp.zeros((experts * slot_most,), jnp.bfloat16)
        .at[slot_index]
        .set(weight_of_route)
        .reshape(layout)
    )
    down_stacked = jnp.concatenate([adapter_down, down_direction], axis=2)
    up_stacked = jnp.concatenate([adapter_up, up_direction], axis=1)

    def spread(token_rows):
        per_route = jnp.repeat(token_rows, top_count, axis=0)
        placed = (
            jnp.zeros((experts * slot_most, model_width), jnp.bfloat16)
            .at[slot_index]
            .set(per_route)
        )
        return placed.reshape(layout + (model_width,))

    send_residual = spread(output_gradient)
    pieces = (
        lax.all_to_all(send_hidden, "expert", split_axis=0, concat_axis=0, tiled=True),
        lax.all_to_all(send_weight, "expert", split_axis=0, concat_axis=0, tiled=True),
    )
    hidden_rows = pieces[0].astype(jnp.float32)
    weight_rows = pieces[1].astype(jnp.float32)[..., None]
    reduced_hidden = jnp.einsum(
        "cjif,jfk->cjik", hidden_rows, down_stacked, precision=finest_precision
    )
    exchanged_rows = jnp.concatenate(
        [reduced_hidden[..., adapter_rank:], reduced_hidden[..., :adapter_rank]], axis=3
    )
    tangent_out = weight_rows * jnp.einsum(
        "cjik,jkd->cjid", exchanged_rows, up_stacked, precision=finest_precision
    )
    returned = lax.all_to_all(
        tangent_out.astype(jnp.bfloat16), "expert", split_axis=0, concat_axis=0, tiled=True
    )
    results = (returned, reduced_hidden) + tuple(pieces)
    returned = results[0]
    reduced_hidden = results[1]
    hidden_rows = results[2]
    weight_rows = results[3]
    route_tangent = returned.reshape(experts * slot_most, model_width)[slot_index]
    out_tangent = jnp.sum(
        route_tangent.reshape(tok_rows, top_count, model_width).astype(jnp.float32), axis=1
    )
    resid_tangent = (curvature[:, None] * out_tangent).astype(jnp.bfloat16)
    send_tangent = spread(resid_tangent)
    residual_rows, tangent_rows = (
        lax.all_to_all(send_residual, "expert", split_axis=0, concat_axis=0, tiled=True),
        lax.all_to_all(send_tangent, "expert", split_axis=0, concat_axis=0, tiled=True),
    )
    residual_full = residual_rows.astype(jnp.float32)
    complete_tangent = tangent_rows.astype(jnp.float32)
    weight_column = weight_rows.astype(jnp.float32)[..., None]
    residual_reduced = jnp.einsum(
        "wyov,yqv->wyoq", residual_full, up_stacked, precision=finest_precision
    )
    reduced_tangent = jnp.einsum(
        "wyov,yqv->wyoq", complete_tangent, adapter_up, precision=finest_precision
    )
    left_terms = jnp.concatenate(
        [
            weight_column * residual_reduced[..., :adapter_rank],
            weight_column * (reduced_tangent + residual_reduced[..., adapter_rank:]),
        ],
        axis=3,
    )
    down_terms = jnp.einsum(
        "cjif,cjik->jfk", hidden_rows.astype(jnp.float32), left_terms, precision=finest_precision
    )
    raised_update = weight_column * reduced_hidden[..., :adapter_rank]
    raised_tangent_update = weight_column * reduced_hidden[..., adapter_rank:]
    up_terms = jnp.einsum(
        "cjik,cjid->jkd",
        jnp.concatenate([raised_update, raised_tangent_update], axis=3),
        residual_full,
        precision=finest_precision,
    )
    curvature_piece = up_terms[:, adapter_rank:] + jnp.einsum(
        "cjik,cjid->jkd", raised_update, complete_tangent, precision=finest_precision
    )
    return (
        down_terms[..., :adapter_rank],
        up_terms[:, :adapter_rank],
        down_terms[..., adapter_rank:],
        curvature_piece,
    )


def local(*arguments):
    factor_bytes = 2 * 4 * (arguments[6].size + arguments[7].size) * lax.axis_size("expert")
    fits = lax.axis_size("expert") == 16 and 4 * factor_bytes <= kernel_vmem
    plan = gathered_plan if fits else routed_plan
    return plan(*arguments)


def solution(mesh):
    return jax.shard_map(
        local,
        mesh=mesh,
        in_specs=(
            P(("groups", "expert"), None, None),
            P(("groups", "expert"), None),
            P(("groups", "expert"), None),
            P("groups"),
            P(("groups", "expert"), None),
            P(("groups", "expert")),
            P("expert", None, None),
            P("expert", None, None),
            P(("groups", "expert"), None, None),
            P(("groups", "expert"), None, None),
        ),
        out_specs=(
            P(("groups", "expert"), None, None),
            P(("groups", "expert"), None, None),
            P(("groups", "expert"), None, None),
            P(("groups", "expert"), None, None),
        ),
        check_vma=False,
    )
```

```python
import functools

import jax
import jax.numpy as jnp
from jax import lax
from jax.experimental import pallas as pl
from jax.experimental.pallas import tpu as pltpu
from jax.sharding import PartitionSpec as P

adapter_scale = 2.0
f32 = jnp.float32
bf16 = jnp.bfloat16
i16 = jnp.int16
lanes = 128
counts_lane = 64
kernel_vmem = 32 * 2**20
whole_vmem = 60 * 2**20


def halves(value):
    high = value.astype(bf16)
    return high, (value - high.astype(f32)).astype(bf16)


def dot(a, b, a_dim, b_dim):
    return lax.dot_general(a, b, (((a_dim,), (b_dim,)), ((), ())), preferred_element_type=f32)


def dot_pairs(a, b, a_dim, b_dim):
    return dot(a[0], b[0], a_dim, b_dim) + (dot(a[1], b[0], a_dim, b_dim) + dot(a[0], b[1], a_dim, b_dim))


def encode(down, up, counts=0.0):
    def scaled(value):
        largest = jnp.max(jnp.abs(value), axis=-1, keepdims=True)
        exponent = jnp.ceil(jnp.log2(jnp.maximum(largest, 1e-30)))
        coded = jnp.round(value * jnp.exp2(15.0 - exponent))
        return jnp.clip(coded, -32767.0, 32767.0), exponent

    down, down_exponent = scaled(down)
    up, up_exponent = scaled(up)
    lane = lax.broadcasted_iota(jnp.int32, down.shape[:-1] + (lanes,), down.ndim - 1)
    tail = jnp.where(lane < counts_lane // 2, down_exponent, up_exponent)
    tail = jnp.where(lane < counts_lane, tail, counts)
    return jnp.concatenate([down, up, tail], axis=-1).astype(jnp.int32).astype(i16)


def decode(coded, hidden_width):
    width = coded.shape[-1] - lanes
    value = coded.astype(jnp.int32).astype(f32)
    down_scale = jnp.exp2(value[..., width : width + 1] - 15.0)
    up_scale = jnp.exp2(value[..., width + counts_lane // 2 : width + counts_lane // 2 + 1] - 15.0)
    return value[..., :hidden_width] * down_scale, value[..., hidden_width:width] * up_scale


def prepare_kernel(experts, *refs):
    (piece_ref, small_ref), sem, refs = refs[7:9], refs[-1], refs[:7] + refs[9:-1]
    copies = [pltpu.make_async_copy(refs[i], refs[7 + i], sem.at[i]) for i in range(7)]
    for copy in copies:
        copy.start()
    for copy in copies:
        copy.wait()
    expert, gate, curvature, down_direction, adapter_down, adapter_up, up_direction = [ref[...] for ref in refs[7:]]
    top = expert.shape[0]
    small_ref[...] = jnp.zeros_like(small_ref)
    small_ref[:top] = expert.astype(f32)
    small_ref[top : 2 * top] = gate.astype(f32)
    small_ref[2 * top : 2 * top + 1] = curvature
    lane = lax.broadcasted_iota(jnp.int32, (1, lanes), 1)
    counts = jnp.zeros((1, lanes), f32)
    for number in range(experts):
        named = jnp.where(expert == number, 1.0, 0.0)
        total = jnp.sum(jnp.sum(named, axis=0, keepdims=True), axis=1, keepdims=True)
        counts = jnp.where(lane == counts_lane + number, total, counts)
    piece_ref[0] = encode(down_direction, adapter_up, counts)
    piece_ref[1] = encode(adapter_down, up_direction, counts)


def token_columns(small_ref, top):
    experts = [small_ref[:, k : k + 1] for k in range(top)]
    gates = [small_ref[:, top + k : top + k + 1] for k in range(top)]
    return experts, gates, small_ref[:, 2 * top : 2 * top + 1]


def members(place_ref, wide, first, count, dim=1):
    shape = (1, wide) if dim == 1 else (wide, 1)
    piece_of = lax.broadcasted_iota(jnp.int32, shape, dim) // (wide // count)
    found = jnp.zeros(shape, jnp.int32)
    for number in range(count):
        found = jnp.where(piece_of == number, place_ref[1 + first + number], found)
    return found.astype(f32)


def prior_kernel(place_ref, *rest):
    piece_refs, prior_ref = rest[:-1], rest[-1]
    me = place_ref[0]
    prior_ref[...] = jnp.zeros_like(prior_ref)
    for block, number in enumerate((me, me ^ 1)):
        total = jnp.zeros((1, lanes), f32)
        for arrival, piece_ref in enumerate(piece_refs):
            tail = piece_ref[0, :, piece_ref.shape[2] - lanes :]
            counts = tail.astype(jnp.int32).astype(f32)[0:1]
            total = total + jnp.where(place_ref[1 + arrival] < number, counts, 0.0)
        prior_ref[block : block + 1] = total


def piece_part(refs, arrival, kind, halved):
    if halved and arrival == len(refs) - 2:
        return refs[arrival + kind][0]
    return refs[arrival][kind]


def tokens_kernel(top, slots, place_ref, own_ref, other_ref, hidden_other_ref, gradient_other_ref, *outs):
    small_ref, rank_ref, gate_ref, same_ref, mask_ref, hidden_ref, gradient_ref, sem = outs
    copies = [
        pltpu.make_async_copy(hidden_other_ref, hidden_ref, sem.at[0]),
        pltpu.make_async_copy(gradient_other_ref, gradient_ref, sem.at[1]),
    ]
    for copy in copies:
        copy.start()
    small_ref[...] = jnp.concatenate([own_ref[...], other_ref[...]], axis=1).T
    experts, gates, _ = token_columns(small_ref, top)
    _, tokens, wide = rank_ref.shape
    column = members(place_ref, wide, slots, slots)
    below = (
        lax.broadcasted_iota(jnp.int32, (tokens, tokens), 0)
        > lax.broadcasted_iota(jnp.int32, (tokens, tokens), 1)
    )
    below = jnp.where(below, 1.0, 0.0).astype(bf16)
    rows = same_ref.shape[0]
    row = lax.broadcasted_iota(jnp.int32, (rows, tokens), 0)
    same = jnp.where(row // top == lax.broadcasted_iota(jnp.int32, (rows, tokens), 1), 1.0, 0.0).astype(bf16)
    same_ref[...] = same
    for core in range(2):
        tokens_of = slice(core * tokens, (core + 1) * tokens)
        gate = jnp.zeros((tokens, wide), f32)
        member = jnp.zeros((tokens, wide), f32)
        for k in range(top):
            named = experts[k][tokens_of] == column
            gate = jnp.where(named, gates[k][tokens_of], gate)
            member = jnp.where(named, 1.0, member)
        gate_ref[core] = gate
        rank_ref[core] = dot(below, member.astype(bf16), 1, 0)
        named = dot(same, small_ref[tokens_of].astype(bf16), 1, 0)
        position = lax.broadcasted_iota(jnp.int32, named.shape, 0) % top
        own = lax.broadcasted_iota(jnp.int32, named.shape, 1) == position
        expert = jnp.sum(jnp.where(own, named, 0.0), axis=1, keepdims=True)
        mask_ref[core] = jnp.where(expert == column, 1.0, 0.0).astype(bf16)
    for copy in copies:
        copy.wait()


def pass_kernel(behind_ref, ahead_ref, behind_out_ref, ahead_out_ref):
    behind_out_ref[...] = behind_ref[...]
    ahead_out_ref[...] = ahead_ref[...]


def reduce_kernel(top, first, count, halved, place_ref, small_ref, own_ref, other_ref, *rest):
    piece_refs, (reduced_ref, full_ref) = rest[:-2], rest[-2:]
    hidden_width = own_ref.shape[1]
    downs = [
        decode(piece_part(piece_refs, arrival, kind, halved), hidden_width)[0]
        for kind in range(2)
        for arrival in range(count)
    ]
    factor = jnp.concatenate(halves(jnp.concatenate(downs, axis=0)), axis=0)
    experts, _, _ = token_columns(small_ref, top)
    wide = reduced_ref.shape[1]
    column = members(place_ref, wide // 2, first, count)
    column = jnp.concatenate([column, column], axis=1)
    tokens = own_ref.shape[0] // top
    for core, hidden_ref in enumerate((own_ref, other_ref)):
        full = dot(hidden_ref[...], factor, 1, 1)
        full_ref[...] = full[:, :wide] + full[:, wide:]
        tokens_of = slice(core * tokens, (core + 1) * tokens)
        total = jnp.zeros((tokens, wide), f32)
        for k in range(top):
            here = full_ref[pl.ds(k, tokens, stride=top), :]
            total = jnp.where(experts[k][tokens_of] == column, here, total)
        reduced_ref[tokens_of] = total


def rank_limits(place_ref, wide, slots, capacity_ref, prior_ref, arrived_ref):
    lane = lax.broadcasted_iota(jnp.int32, (1, lanes), 1)
    piece_of = lax.broadcasted_iota(jnp.int32, (1, wide), 1) // (wide // slots)
    limits = []
    for block in range(2):
        total = capacity_ref[...] - prior_ref[block : block + 1] - arrived_ref[1 - block : 2 - block]
        limit = jnp.zeros((1, wide), f32)
        for slot in range(slots):
            picked = jnp.where(lane == counts_lane + place_ref[1 + slots + slot], total, 0.0)
            limit = jnp.where(piece_of == slot, jnp.sum(picked, axis=1, keepdims=True), limit)
        limits.append(limit)
    return limits


def tangent_kernel(
    slots, place_ref, rank_ref, gate_ref, capacity_ref, prior_ref, arrived_ref, early_ref, late_ref, *rest
):
    piece_refs = rest[: slots + 1]
    weight_ref, weighted_ref, tangent_ref, coded_ref, high_ref, low_ref = rest[slots + 1 :]
    _, wide = weight_ref.shape
    model_width = tangent_ref.shape[1]
    hidden_width = piece_refs[0].shape[2] - model_width - lanes
    limits = rank_limits(place_ref, wide, slots, capacity_ref, prior_ref, arrived_ref)
    weights = [
        jnp.where(rank_ref[core] < limits[core], adapter_scale * gate_ref[core], 0.0) for core in range(2)
    ]
    weight = jnp.concatenate(weights, axis=0)
    weight_ref[...] = weight
    half = wide // 2
    reduced = [
        jnp.concatenate([ref[:, kind * half : (kind + 1) * half] for ref in (early_ref, late_ref)], axis=1)
        for kind in range(2)
    ]
    rank = wide // slots
    by_arrival = members(place_ref, wide, 0, slots, 0) == members(place_ref, wide, slots, slots)
    row = lax.broadcasted_iota(jnp.int32, (wide, wide), 0)
    same_index = row % rank == lax.broadcasted_iota(jnp.int32, (wide, wide), 1) % rank
    order = jnp.where(by_arrival & same_index, 1.0, 0.0).astype(bf16)
    reduced = [sum(dot(part, order, 1, 0) for part in halves(both)) for both in reduced]
    weighted = jnp.concatenate([weight * part for part in reduced], axis=1)
    weighted_ref[...] = weighted
    for arrival in range(slots):
        for kind in range(2):
            _, up = decode(piece_part(piece_refs, arrival, kind, True), hidden_width)
            slot = place_ref[1 + 2 * slots + arrival]
            high_ref[kind, slot], low_ref[kind, slot] = halves(up)
    factor = high_ref[...].reshape(2 * wide, model_width), low_ref[...].reshape(2 * wide, model_width)
    tangent = dot_pairs(halves(weighted), factor, 1, 0)
    tangent_ref[...] = tangent
    coded_ref[...] = tangent.astype(bf16)


def put_left(left_ref, same_ref, mask_ref, terms):
    both = jnp.concatenate(halves(terms), axis=1)
    tokens = terms.shape[0] // 2
    for core in range(2):
        repeated = dot(same_ref[...], both[core * tokens : (core + 1) * tokens], 1, 0).astype(bf16)
        mask = mask_ref[core]
        left_ref[core] = repeated * jnp.concatenate([mask, mask], axis=1)


def add_halves(both):
    middle = both.shape[0] // 2
    return both[:middle] + both[middle:]


def put_chunks(keep_ref, near_ref, chunk_ref, far_ref, down, up):
    rank = keep_ref.shape[1]
    rows = down.shape[0] // rank // 2

    def slot(number):
        start = number * rank
        return down[start : start + rank], up[start : start + rank]

    for place in range(2):
        keep_ref[place] = jnp.concatenate(slot(place), axis=1)
        near_ref[place] = encode(*slot(rows + place))
        chunk_ref[place] = jnp.concatenate(slot(place * rows + 2), axis=1)
        far_ref[place] = encode(*slot(place * rows + 3))


def gradient_kernel(
    same_ref,
    mask_ref,
    own_ref,
    other_ref,
    own_gradient_ref,
    other_gradient_ref,
    weight_ref,
    weighted_ref,
    high_ref,
    low_ref,
    keep_ref,
    near_ref,
    chunk_ref,
    far_ref,
    up_ref,
    to_ref,
    left_ref,
):
    wide = weight_ref.shape[1]
    model_width = up_ref.shape[1]
    gradient = jnp.concatenate([own_gradient_ref[...], other_gradient_ref[...]], axis=0)
    high = high_ref[...].reshape(2 * wide, model_width)
    low = low_ref[...].reshape(2 * wide, model_width)
    to_both = dot(gradient, high, 1, 1) + dot(gradient, low, 1, 1)
    to_ref[...] = to_both[:, wide:]
    put_left(left_ref, same_ref, mask_ref, weight_ref[...] * to_both[:, :wide])
    down = dot(left_ref[0], own_ref[...], 0, 0) + dot(left_ref[1], other_ref[...], 0, 0)
    up = add_halves(dot(jnp.concatenate(halves(weighted_ref[...]), axis=1), gradient, 0, 0))
    up_ref[...] = up[:wide]
    put_chunks(keep_ref, near_ref, chunk_ref, far_ref, add_halves(down), up[wide:])


def curvature_kernel(
    top,
    small_ref,
    same_ref,
    mask_ref,
    own_ref,
    other_ref,
    weight_ref,
    weighted_ref,
    high_ref,
    low_ref,
    up_ref,
    to_ref,
    tangent_ref,
    arrived_ref,
    gradient_near_ref,
    keep_ref,
    near_ref,
    chunk_ref,
    far_ref,
    onward_ref,
    left_ref,
):
    onward_ref[...] = gradient_near_ref[...]
    _, _, curvature = token_columns(small_ref, top)
    tokens, wide = weight_ref.shape
    block = tokens // 2
    model_width = up_ref.shape[1]
    arrived = jnp.concatenate([arrived_ref[block:], arrived_ref[:block]], axis=0).astype(f32)
    resid = halves(curvature * (tangent_ref[...] + arrived))
    adapter_up = high_ref[0].reshape(wide, model_width), low_ref[0].reshape(wide, model_width)
    terms = weight_ref[...] * (dot_pairs(resid, adapter_up, 1, 1) + to_ref[...])
    put_left(left_ref, same_ref, mask_ref, terms)
    down = dot(left_ref[0], own_ref[...], 0, 0) + dot(left_ref[1], other_ref[...], 0, 0)
    weighted_u = halves(weighted_ref[:, wide:])
    up = add_halves(dot(jnp.concatenate(weighted_u, axis=1), resid[0], 0, 0)) + dot(weighted_u[0], resid[1], 0, 0)
    put_chunks(keep_ref, near_ref, chunk_ref, far_ref, add_halves(down), up_ref[...] + up)


def pair_kernel(hidden_width, arrived_ref, chunk_ref, *refs):
    passing, (across_ref, keep_ref) = (refs[:1], refs[1:3]) if len(refs) == 4 else ((), refs)
    for near_ref in passing:
        refs[3][...] = near_ref[...]
    for x in range(2):
        down, up = decode(arrived_ref[x], hidden_width)
        down, up = chunk_ref[x, :, :hidden_width] + down, chunk_ref[x, :, hidden_width:] + up
        if x == 0:
            keep_ref[...] = jnp.concatenate([down, up], axis=1)
        else:
            across_ref[...] = encode(down, up)


def far_kernel(hidden_width, arrived_ref, keep_ref, out_ref):
    down, up = decode(arrived_ref[...], hidden_width)
    out_ref[...] = encode(keep_ref[:, :hidden_width] + down, keep_ref[:, hidden_width:] + up)


def near_kernel(hidden_width, arrived_ref, keep_ref, onward_ref, total_ref):
    for z in range(2):
        down, up = decode(arrived_ref[z], hidden_width)
        down, up = keep_ref[z, :, :hidden_width] + down, keep_ref[z, :, hidden_width:] + up
        if z == 0:
            total_ref[...] = jnp.concatenate([down, up], axis=1)
        else:
            onward_ref[...] = encode(down, up)


def add_kernel(hidden_width, total_ref, near_ref, far_ref, out_ref):
    near, far = decode(near_ref[...], hidden_width), decode(far_ref[...], hidden_width)
    out_ref[:, :hidden_width] = total_ref[:, :hidden_width] + near[0] + far[0]
    out_ref[:, hidden_width:] = total_ref[:, hidden_width:] + near[1] + far[1]


def total_kernel(hidden_width, gradient_ref, total_ref, near_ref, far_ref, *out_refs):
    near, far = decode(near_ref[...], hidden_width), decode(far_ref[...], hidden_width)
    out_refs[0][...] = gradient_ref[:, :hidden_width]
    out_refs[1][...] = gradient_ref[:, hidden_width:]
    out_refs[2][...] = total_ref[:, :hidden_width] + near[0] + far[0]
    out_refs[3][...] = total_ref[:, hidden_width:] + near[1] + far[1]


class Ring:
    def __init__(self, size):
        self.length = size // 2
        rows = self.length // 2
        self.order = [4 * z for z in range(rows)] + [4 * z + 2 for z in reversed(range(rows))]

    def shift(self, value, step):
        pairs = [
            (chip + core, self.order[(place + step) % self.length] + core)
            for place, chip in enumerate(self.order)
            for core in range(2)
        ]
        return lax.ppermute(value, "expert", pairs)

    def members(self, me):
        rows = self.length // 2
        place = jnp.where(me // 2 % 2 == 0, me // 4, self.length - 1 - me // 4)
        half = self.length // 2
        offsets = [0] + [offset for step in range(1, half) for offset in (self.length - step, step)] + [half]
        there = (place + jnp.array(offsets, jnp.int32)) % self.length
        return jnp.where(there < rows, 4 * there, 4 * (self.length - 1 - there) + 2) + me % 2

    def gather(self, own, passing):
        half = self.length // 2
        pieces = [own]
        ahead, behind = own, own
        for step in range(1, half):
            behind = self.shift(behind, 1)
            ahead = self.shift(ahead, -1)
            if step == 2:
                behind, ahead = passing(behind, ahead)
            pieces += [behind, ahead]
        pieces += [self.shift(behind[:1], 1), self.shift(ahead[1:], -1)]
        return pieces


def exchange(value, mask):
    size = lax.axis_size("expert")
    return lax.ppermute(value, "expert", [(device, device ^ mask) for device in range(size)])


def gathered_plan(
    hidden_of_route,
    expert_of_route,
    gate_of_route,
    capacity,
    output_gradient,
    curvature,
    adapter_down,
    adapter_up,
    down_direction,
    up_direction,
):
    ring = Ring(lax.axis_size("expert"))
    slots = ring.length
    rows = slots // 2
    masks = [4 * z for z in range(rows)] + [4 * z + 2 for z in range(rows)]
    me = lax.axis_index("expert")
    tokens, top = expert_of_route.shape
    both = 2 * tokens
    hidden_width = hidden_of_route.shape[2]
    rank = adapter_down.shape[2]
    model_width = output_gradient.shape[1]
    experts = capacity.shape[0]
    wide = slots * rank
    coded_width = hidden_width + model_width + lanes


    place = []

    def call(kernel, multiplies, outs, *operands, scratch=(), after=(), grant=kernel_vmem):
        space = pltpu.VMEM if grant == kernel_vmem else pltpu.HBM
        places = [pl.BlockSpec(memory_space=pl.ANY) for _ in after] + [
            pl.BlockSpec(memory_space=pltpu.SMEM if any(operand is it for it in place) else space) for operand in operands
        ]
        return pl.pallas_call(
            lambda *refs: kernel(*refs[len(after) :]),
            out_shape=[jax.ShapeDtypeStruct(shape, dtype) for shape, dtype in outs],
            in_specs=places,
            scratch_shapes=scratch,
            compiler_params=pltpu.CompilerParams(vmem_limit_bytes=grant),
            cost_estimate=pl.CostEstimate(flops=2 * multiplies, bytes_accessed=2**20, transcendentals=0),
        )(*after, *operands)

    down_multiplies = 2 * top * both * hidden_width * wide
    up_multiplies = both * model_width * wide

    first = (
        expert_of_route.T,
        gate_of_route.T,
        curvature[None],
        down_direction[0].T,
        adapter_down[0].T,
        adapter_up[0],
        up_direction[0],
    )
    piece, small = call(
        functools.partial(prepare_kernel, experts),
        10**8,
        [((2, rank, coded_width), i16), (((2 * top + 8) // 8 * 8, tokens), f32)],
        *first,
        scratch=[pltpu.VMEM(operand.shape, operand.dtype) for operand in first]
        + [pltpu.SemaphoreType.DMA((len(first),))],
        grant=whole_vmem,
    )
    arrivals = ring.members(me)
    slot_of_arrival = (arrivals ^ me) // 4 + rows * ((arrivals ^ me) // 2 % 2)
    place.append(jnp.concatenate([me[None], arrivals, me ^ jnp.array(masks, jnp.int32), slot_of_arrival]).astype(jnp.int32))
    small_other = exchange(small, 1)
    hidden = hidden_of_route.reshape(tokens * top, hidden_width)
    small_columns, local_rank, gate, same, mask, hidden_other, gradient_other = call(
        functools.partial(tokens_kernel, top, slots),
        10**9,
        [
            ((both, small.shape[0]), f32),
            ((2, tokens, wide), f32),
            ((2, tokens, wide), f32),
            ((top * tokens, tokens), bf16),
            ((2, top * tokens, wide), bf16),
            (hidden.shape, bf16),
            (output_gradient.shape, bf16),
        ],
        *place,
        small,
        small_other,
        exchange(hidden, 1),
        exchange(output_gradient, 1),
        scratch=[pltpu.SemaphoreType.DMA((2,))],
    )
    def passing(behind, ahead):
        return call(pass_kernel, 10**8, [(piece.shape, i16)] * 2, behind, ahead, after=[same])

    pieces = ring.gather(piece, passing)
    capacity_row = jnp.pad(capacity.astype(f32), (counts_lane, lanes - counts_lane - experts))[None, :]

    def reduced(first, count, halved, *parts, after=()):
        return call(
            functools.partial(reduce_kernel, top, first, count, halved),
            2 * down_multiplies * count // slots,
            [((both, 2 * count * rank), f32)],
            *place,
            small_columns,
            hidden,
            hidden_other,
            *parts,
            scratch=[pltpu.VMEM((tokens * top, 2 * count * rank), f32)],
            after=after,
        )[0]

    early = slots // 2
    reduced_early = reduced(0, early, False, *pieces[:early])
    (prior,) = call(prior_kernel, 10**8, [((8, lanes), f32)], *place, *pieces[:-1], after=[reduced_early])
    prior_arrived = exchange(prior, 1)
    reduced_late = reduced(early, slots - early, True, *pieces[early:], after=[prior])
    weight, weighted, tangent, coded, high, low = call(
        functools.partial(tangent_kernel, slots),
        6 * up_multiplies,
        [
            ((both, wide), f32),
            ((both, 2 * wide), f32),
            ((both, model_width), f32),
            ((both, model_width), bf16),
            ((2, slots, rank, model_width), bf16),
            ((2, slots, rank, model_width), bf16),
        ],
        *place,
        local_rank,
        gate,
        capacity_row,
        prior,
        prior_arrived,
        reduced_early,
        reduced_late,
        *pieces,
    )
    arrived = exchange(coded, 1)
    left = [pltpu.VMEM((2, top * tokens, 2 * wide), bf16)]
    chunks = [((2, rank, hidden_width + model_width), f32), ((2, rank, coded_width), i16)] * 2
    gradient_keep, gradient_near, gradient_chunk, gradient_far, up, to = call(
        gradient_kernel,
        down_multiplies + 8 * up_multiplies,
        chunks + [((wide, model_width), f32), ((both, wide), f32)],
        same,
        mask,
        hidden,
        hidden_other,
        output_gradient,
        gradient_other,
        weight,
        weighted,
        high,
        low,
        scratch=left,
    )
    gradient_far = exchange(gradient_far, 4)
    curvature_keep, curvature_near, curvature_chunk, curvature_far, gradient_near = call(
        functools.partial(curvature_kernel, top),
        down_multiplies + 6 * up_multiplies,
        chunks + [(gradient_near.shape, i16)],
        small_columns,
        same,
        mask,
        hidden,
        hidden_other,
        weight,
        weighted,
        high,
        low,
        up,
        to,
        tangent,
        arrived,
        gradient_near,
        scratch=left,
    )

    hop = 2 * 10**9

    one = (rank, hidden_width + model_width)
    one_coded = (rank, coded_width)

    def hop_call(kernel, outs, *operands, after=()):
        return call(functools.partial(kernel, hidden_width), hop, outs, *operands, after=after)

    curvature_far = exchange(curvature_far, 4)
    gradient_near = exchange(gradient_near, 2)
    pair = [(one_coded, i16), (one, f32)]
    gradient_across, gradient_pair, curvature_near = hop_call(
        pair_kernel,
        pair + [(curvature_near.shape, i16)],
        gradient_far,
        gradient_chunk,
        curvature_near,
        after=[curvature_keep],
    )
    curvature_near = exchange(curvature_near, 2)
    curvature_across, curvature_pair = hop_call(
        pair_kernel, pair, curvature_far, curvature_chunk, after=[gradient_across]
    )
    near = [(one_coded, i16), (one, f32)]
    gradient_onward, gradient_total = hop_call(
        near_kernel, near, gradient_near, gradient_keep, after=[curvature_across]
    )
    gradient_onward = exchange(gradient_onward, 4)
    (gradient_beyond,) = hop_call(
        far_kernel, [(one_coded, i16)], exchange(gradient_across, 2), gradient_pair, after=[gradient_total]
    )
    (curvature_beyond,) = hop_call(
        far_kernel, [(one_coded, i16)], exchange(curvature_across, 2), curvature_pair, after=[gradient_beyond]
    )
    curvature_onward, curvature_total = hop_call(
        near_kernel, near, curvature_near, curvature_keep, after=[curvature_beyond, gradient_onward]
    )
    (gradient_total,) = hop_call(
        add_kernel,
        [(one, f32)],
        gradient_total,
        gradient_onward,
        exchange(gradient_beyond, 8),
        after=[curvature_total],
    )
    down_gradient, up_gradient, curvature_down, curvature_up = hop_call(
        total_kernel,
        [((rank, hidden_width), f32), ((rank, model_width), f32)] * 2,
        gradient_total,
        curvature_total,
        exchange(curvature_onward, 4),
        exchange(curvature_beyond, 8),
    )
    return down_gradient.T[None], up_gradient[None], curvature_down.T[None], curvature_up[None]


def carried_in(value, axis, join, neutral):
    count, mine = (lax.axis_size(axis), lax.axis_index(axis))
    pieces = lax.all_gather(value, axis)
    so_far = jnp.full_like(value, 0) + jnp.asarray(neutral, value.dtype)

    def lap(position, so_far):
        longer = join(so_far, pieces[position])
        return jnp.where(position < mine, longer, so_far)

    return lax.fori_loop(0, count - 1, lap, so_far)


def add_counts(earlier, later):
    return earlier + later


def routed_plan(
    hidden_of_route,
    expert_of_route,
    gate_of_route,
    capacity,
    output_gradient,
    curvature,
    adapter_down,
    adapter_up,
    down_direction,
    up_direction,
):
    finest_precision = lax.Precision.HIGHEST
    group_size = lax.axis_size("expert")
    tok_rows, top_count = expert_of_route.shape
    hidden_width = hidden_of_route.shape[2]
    resident_experts = adapter_down.shape[0]
    adapter_rank = adapter_down.shape[2]
    model_width = output_gradient.shape[1]
    experts = resident_experts * group_size
    slot_most = 2 * tok_rows * top_count // experts
    routes = expert_of_route.reshape(-1)
    onehot = (routes[:, None] == jnp.arange(experts, dtype=jnp.int32)[None, :]).astype(jnp.int32)
    earlier = jnp.cumsum(onehot, axis=0) - onehot
    local_rank = jnp.sum(earlier * onehot, axis=1)
    counts = jnp.sum(onehot, axis=0)
    prior_count = carried_in(counts, "expert", add_counts, jnp.zeros_like(counts))
    global_rank = local_rank + jnp.sum(onehot * prior_count[None, :], axis=1)
    route_limit = jnp.sum(onehot * capacity[None, :], axis=1)
    retained_mask = (global_rank < route_limit).astype(jnp.float32)
    weight_of_route = (
        adapter_scale * gate_of_route.reshape(-1).astype(jnp.float32) * retained_mask
    ).astype(jnp.bfloat16)
    slot_index = routes * slot_most + local_rank
    layout = (group_size, resident_experts, slot_most)
    send_hidden = (
        jnp.zeros((experts * slot_most, hidden_width), jnp.bfloat16)
        .at[slot_index]
        .set(hidden_of_route.reshape(-1, hidden_width))
        .reshape(layout + (hidden_width,))
    )
    send_weight = (
        jnp.zeros((experts * slot_most,), jnp.bfloat16)
        .at[slot_index]
        .set(weight_of_route)
        .reshape(layout)
    )
    down_stacked = jnp.concatenate([adapter_down, down_direction], axis=2)
    up_stacked = jnp.concatenate([adapter_up, up_direction], axis=1)

    def spread(token_rows):
        per_route = jnp.repeat(token_rows, top_count, axis=0)
        placed = (
            jnp.zeros((experts * slot_most, model_width), jnp.bfloat16)
            .at[slot_index]
            .set(per_route)
        )
        return placed.reshape(layout + (model_width,))

    send_residual = spread(output_gradient)
    pieces = (
        lax.all_to_all(send_hidden, "expert", split_axis=0, concat_axis=0, tiled=True),
        lax.all_to_all(send_weight, "expert", split_axis=0, concat_axis=0, tiled=True),
    )
    hidden_rows = pieces[0].astype(jnp.float32)
    weight_rows = pieces[1].astype(jnp.float32)[..., None]
    reduced_hidden = jnp.einsum(
        "cjif,jfk->cjik", hidden_rows, down_stacked, precision=finest_precision
    )
    exchanged_rows = jnp.concatenate(
        [reduced_hidden[..., adapter_rank:], reduced_hidden[..., :adapter_rank]], axis=3
    )
    tangent_out = weight_rows * jnp.einsum(
        "cjik,jkd->cjid", exchanged_rows, up_stacked, precision=finest_precision
    )
    returned = lax.all_to_all(
        tangent_out.astype(jnp.bfloat16), "expert", split_axis=0, concat_axis=0, tiled=True
    )
    results = (returned, reduced_hidden) + tuple(pieces)
    returned = results[0]
    reduced_hidden = results[1]
    hidden_rows = results[2]
    weight_rows = results[3]
    route_tangent = returned.reshape(experts * slot_most, model_width)[slot_index]
    out_tangent = jnp.sum(
        route_tangent.reshape(tok_rows, top_count, model_width).astype(jnp.float32), axis=1
    )
    resid_tangent = (curvature[:, None] * out_tangent).astype(jnp.bfloat16)
    send_tangent = spread(resid_tangent)
    residual_rows, tangent_rows = (
        lax.all_to_all(send_residual, "expert", split_axis=0, concat_axis=0, tiled=True),
        lax.all_to_all(send_tangent, "expert", split_axis=0, concat_axis=0, tiled=True),
    )
    residual_full = residual_rows.astype(jnp.float32)
    complete_tangent = tangent_rows.astype(jnp.float32)
    weight_column = weight_rows.astype(jnp.float32)[..., None]
    residual_reduced = jnp.einsum(
        "wyov,yqv->wyoq", residual_full, up_stacked, precision=finest_precision
    )
    reduced_tangent = jnp.einsum(
        "wyov,yqv->wyoq", complete_tangent, adapter_up, precision=finest_precision
    )
    left_terms = jnp.concatenate(
        [
            weight_column * residual_reduced[..., :adapter_rank],
            weight_column * (reduced_tangent + residual_reduced[..., adapter_rank:]),
        ],
        axis=3,
    )
    down_terms = jnp.einsum(
        "cjif,cjik->jfk", hidden_rows.astype(jnp.float32), left_terms, precision=finest_precision
    )
    raised_update = weight_column * reduced_hidden[..., :adapter_rank]
    raised_tangent_update = weight_column * reduced_hidden[..., adapter_rank:]
    up_terms = jnp.einsum(
        "cjik,cjid->jkd",
        jnp.concatenate([raised_update, raised_tangent_update], axis=3),
        residual_full,
        precision=finest_precision,
    )
    curvature_piece = up_terms[:, adapter_rank:] + jnp.einsum(
        "cjik,cjid->jkd", raised_update, complete_tangent, precision=finest_precision
    )
    return (
        down_terms[..., :adapter_rank],
        up_terms[:, :adapter_rank],
        down_terms[..., adapter_rank:],
        curvature_piece,
    )


def local(*arguments):
    factor_bytes = 2 * 4 * (arguments[6].size + arguments[7].size) * lax.axis_size("expert")
    fits = lax.axis_size("expert") == 16 and 4 * factor_bytes <= kernel_vmem
    plan = gathered_plan if fits else routed_plan
    return plan(*arguments)


def solution(mesh):
    return jax.shard_map(
        local,
        mesh=mesh,
        in_specs=(
            P(("groups", "expert"), None, None),
            P(("groups", "expert"), None),
            P(("groups", "expert"), None),
            P("groups"),
            P(("groups", "expert"), None),
            P(("groups", "expert")),
            P("expert", None, None),
            P("expert", None, None),
            P(("groups", "expert"), None, None),
            P(("groups", "expert"), None, None),
        ),
        out_specs=(
            P(("groups", "expert"), None, None),
            P(("groups", "expert"), None, None),
            P(("groups", "expert"), None, None),
            P(("groups", "expert"), None, None),
        ),
        check_vma=False,
    )
```

```python
import functools

import jax
import jax.numpy as jnp
from jax import lax
from jax.experimental import pallas as pl
from jax.experimental.pallas import tpu as pltpu
from jax.sharding import PartitionSpec as P

adapter_scale = 2.0
f32 = jnp.float32
bf16 = jnp.bfloat16
i16 = jnp.int16
lanes = 128
counts_lane = 64
kernel_vmem = 32 * 2**20
whole_vmem = 60 * 2**20


def halves(value):
    high = value.astype(bf16)
    return high, (value - high.astype(f32)).astype(bf16)


def dot(a, b, a_dim, b_dim):
    return lax.dot_general(a, b, (((a_dim,), (b_dim,)), ((), ())), preferred_element_type=f32)


def dot_pairs(a, b, a_dim, b_dim):
    return dot(a[0], b[0], a_dim, b_dim) + (dot(a[1], b[0], a_dim, b_dim) + dot(a[0], b[1], a_dim, b_dim))


def encode(down, up, counts=0.0):
    def scaled(value):
        largest = jnp.max(jnp.abs(value), axis=-1, keepdims=True)
        exponent = jnp.ceil(jnp.log2(jnp.maximum(largest, 1e-30)))
        coded = jnp.round(value * jnp.exp2(15.0 - exponent))
        return jnp.clip(coded, -32767.0, 32767.0), exponent

    down, down_exponent = scaled(down)
    up, up_exponent = scaled(up)
    lane = lax.broadcasted_iota(jnp.int32, down.shape[:-1] + (lanes,), down.ndim - 1)
    tail = jnp.where(lane < counts_lane // 2, down_exponent, up_exponent)
    tail = jnp.where(lane < counts_lane, tail, counts)
    return jnp.concatenate([down, up, tail], axis=-1).astype(jnp.int32).astype(i16)


def decode(coded, hidden_width):
    width = coded.shape[-1] - lanes
    value = coded.astype(jnp.int32).astype(f32)
    down_scale = jnp.exp2(value[..., width : width + 1] - 15.0)
    up_scale = jnp.exp2(value[..., width + counts_lane // 2 : width + counts_lane // 2 + 1] - 15.0)
    return value[..., :hidden_width] * down_scale, value[..., hidden_width:width] * up_scale


def prepare_kernel(experts, *refs):
    (piece_ref, small_ref), sem, refs = refs[7:9], refs[-1], refs[:7] + refs[9:-1]
    copies = [pltpu.make_async_copy(refs[i], refs[7 + i], sem.at[i]) for i in range(7)]
    for copy in copies:
        copy.start()
    for copy in copies:
        copy.wait()
    expert, gate, curvature, down_direction, adapter_down, adapter_up, up_direction = [ref[...] for ref in refs[7:]]
    top = expert.shape[0]
    small_ref[...] = jnp.zeros_like(small_ref)
    small_ref[:top] = expert.astype(f32)
    small_ref[top : 2 * top] = gate.astype(f32)
    small_ref[2 * top : 2 * top + 1] = curvature
    lane = lax.broadcasted_iota(jnp.int32, (1, lanes), 1)
    counts = jnp.zeros((1, lanes), f32)
    for number in range(experts):
        named = jnp.where(expert == number, 1.0, 0.0)
        total = jnp.sum(jnp.sum(named, axis=0, keepdims=True), axis=1, keepdims=True)
        counts = jnp.where(lane == counts_lane + number, total, counts)
    piece_ref[0] = encode(down_direction, adapter_up, counts)
    piece_ref[1] = encode(adapter_down, up_direction, counts)


def token_columns(small_ref, top):
    experts = [small_ref[:, k : k + 1] for k in range(top)]
    gates = [small_ref[:, top + k : top + k + 1] for k in range(top)]
    return experts, gates, small_ref[:, 2 * top : 2 * top + 1]


def members(place_ref, wide, first, count, dim=1):
    shape = (1, wide) if dim == 1 else (wide, 1)
    piece_of = lax.broadcasted_iota(jnp.int32, shape, dim) // (wide // count)
    found = jnp.zeros(shape, jnp.int32)
    for number in range(count):
        found = jnp.where(piece_of == number, place_ref[1 + first + number], found)
    return found.astype(f32)


def prior_kernel(place_ref, *rest):
    piece_refs, prior_ref = rest[:-1], rest[-1]
    me = place_ref[0]
    prior_ref[...] = jnp.zeros_like(prior_ref)
    for block, number in enumerate((me, me ^ 1)):
        total = jnp.zeros((1, lanes), f32)
        for arrival, piece_ref in enumerate(piece_refs):
            tail = piece_ref[0, :, piece_ref.shape[2] - lanes :]
            counts = tail.astype(jnp.int32).astype(f32)[0:1]
            total = total + jnp.where(place_ref[1 + arrival] < number, counts, 0.0)
        prior_ref[block : block + 1] = total


def piece_part(refs, arrival, kind, halved):
    if halved and arrival == len(refs) - 2:
        return refs[arrival + kind][0]
    return refs[arrival][kind]


def tokens_kernel(top, slots, place_ref, own_ref, other_ref, hidden_other_ref, gradient_other_ref, *outs):
    small_ref, rank_ref, gate_ref, same_ref, mask_ref, hidden_ref, gradient_ref, sem = outs
    copies = [
        pltpu.make_async_copy(hidden_other_ref, hidden_ref, sem.at[0]),
        pltpu.make_async_copy(gradient_other_ref, gradient_ref, sem.at[1]),
    ]
    for copy in copies:
        copy.start()
    small_ref[...] = jnp.concatenate([own_ref[...], other_ref[...]], axis=1).T
    experts, gates, _ = token_columns(small_ref, top)
    _, tokens, wide = rank_ref.shape
    column = members(place_ref, wide, slots, slots)
    below = (
        lax.broadcasted_iota(jnp.int32, (tokens, tokens), 0)
        > lax.broadcasted_iota(jnp.int32, (tokens, tokens), 1)
    )
    below = jnp.where(below, 1.0, 0.0).astype(bf16)
    rows = same_ref.shape[0]
    row = lax.broadcasted_iota(jnp.int32, (rows, tokens), 0)
    same = jnp.where(row // top == lax.broadcasted_iota(jnp.int32, (rows, tokens), 1), 1.0, 0.0).astype(bf16)
    same_ref[...] = same
    for core in range(2):
        tokens_of = slice(core * tokens, (core + 1) * tokens)
        gate = jnp.zeros((tokens, wide), f32)
        member = jnp.zeros((tokens, wide), f32)
        for k in range(top):
            named = experts[k][tokens_of] == column
            gate = jnp.where(named, gates[k][tokens_of], gate)
            member = jnp.where(named, 1.0, member)
        gate_ref[core] = gate
        rank_ref[core] = dot(below, member.astype(bf16), 1, 0)
        named = dot(same, small_ref[tokens_of].astype(bf16), 1, 0)
        position = lax.broadcasted_iota(jnp.int32, named.shape, 0) % top
        own = lax.broadcasted_iota(jnp.int32, named.shape, 1) == position
        expert = jnp.sum(jnp.where(own, named, 0.0), axis=1, keepdims=True)
        mask_ref[core] = jnp.where(expert == column, 1.0, 0.0).astype(bf16)
    for copy in copies:
        copy.wait()


def pass_kernel(behind_ref, ahead_ref, behind_out_ref, ahead_out_ref):
    behind_out_ref[...] = behind_ref[...]
    ahead_out_ref[...] = ahead_ref[...]


def reduce_kernel(top, first, count, halved, place_ref, small_ref, own_ref, other_ref, *rest):
    piece_refs, (reduced_ref, full_ref) = rest[:-2], rest[-2:]
    hidden_width = own_ref.shape[1]
    downs = [
        decode(piece_part(piece_refs, arrival, kind, halved), hidden_width)[0]
        for kind in range(2)
        for arrival in range(count)
    ]
    factor = jnp.concatenate(halves(jnp.concatenate(downs, axis=0)), axis=0)
    experts, _, _ = token_columns(small_ref, top)
    wide = reduced_ref.shape[1]
    column = members(place_ref, wide // 2, first, count)
    column = jnp.concatenate([column, column], axis=1)
    tokens = own_ref.shape[0] // top
    for core, hidden_ref in enumerate((own_ref, other_ref)):
        full = dot(hidden_ref[...], factor, 1, 1)
        full_ref[...] = full[:, :wide] + full[:, wide:]
        tokens_of = slice(core * tokens, (core + 1) * tokens)
        total = jnp.zeros((tokens, wide), f32)
        for k in range(top):
            here = full_ref[pl.ds(k, tokens, stride=top), :]
            total = jnp.where(experts[k][tokens_of] == column, here, total)
        reduced_ref[tokens_of] = total


def rank_limits(place_ref, wide, slots, capacity_ref, prior_ref, arrived_ref):
    lane = lax.broadcasted_iota(jnp.int32, (1, lanes), 1)
    piece_of = lax.broadcasted_iota(jnp.int32, (1, wide), 1) // (wide // slots)
    limits = []
    for block in range(2):
        total = capacity_ref[...] - prior_ref[block : block + 1] - arrived_ref[1 - block : 2 - block]
        limit = jnp.zeros((1, wide), f32)
        for slot in range(slots):
            picked = jnp.where(lane == counts_lane + place_ref[1 + slots + slot], total, 0.0)
            limit = jnp.where(piece_of == slot, jnp.sum(picked, axis=1, keepdims=True), limit)
        limits.append(limit)
    return limits


def tangent_kernel(
    slots, place_ref, rank_ref, gate_ref, capacity_ref, prior_ref, arrived_ref, early_ref, late_ref, *rest
):
    piece_refs = rest[: slots + 1]
    weight_ref, weighted_ref, tangent_ref, coded_ref, high_ref, low_ref = rest[slots + 1 :]
    _, wide = weight_ref.shape
    model_width = tangent_ref.shape[1]
    hidden_width = piece_refs[0].shape[2] - model_width - lanes
    limits = rank_limits(place_ref, wide, slots, capacity_ref, prior_ref, arrived_ref)
    weights = [
        jnp.where(rank_ref[core] < limits[core], adapter_scale * gate_ref[core], 0.0) for core in range(2)
    ]
    weight = jnp.concatenate(weights, axis=0)
    weight_ref[...] = weight
    half = wide // 2
    reduced = [
        jnp.concatenate([ref[:, kind * half : (kind + 1) * half] for ref in (early_ref, late_ref)], axis=1)
        for kind in range(2)
    ]
    rank = wide // slots
    by_arrival = members(place_ref, wide, 0, slots, 0) == members(place_ref, wide, slots, slots)
    row = lax.broadcasted_iota(jnp.int32, (wide, wide), 0)
    same_index = row % rank == lax.broadcasted_iota(jnp.int32, (wide, wide), 1) % rank
    order = jnp.where(by_arrival & same_index, 1.0, 0.0).astype(bf16)
    reduced = [sum(dot(part, order, 1, 0) for part in halves(both)) for both in reduced]
    weighted = jnp.concatenate([weight * part for part in reduced], axis=1)
    weighted_ref[...] = weighted
    for arrival in range(slots):
        for kind in range(2):
            _, up = decode(piece_part(piece_refs, arrival, kind, True), hidden_width)
            slot = place_ref[1 + 2 * slots + arrival]
            high_ref[kind, slot], low_ref[kind, slot] = halves(up)
    factor = high_ref[...].reshape(2 * wide, model_width), low_ref[...].reshape(2 * wide, model_width)
    tangent = dot_pairs(halves(weighted), factor, 1, 0)
    tangent_ref[...] = tangent
    coded_ref[...] = tangent.astype(bf16)


def put_left(left_ref, same_ref, mask_ref, terms):
    both = jnp.concatenate(halves(terms), axis=1)
    tokens = terms.shape[0] // 2
    for core in range(2):
        repeated = dot(same_ref[...], both[core * tokens : (core + 1) * tokens], 1, 0).astype(bf16)
        mask = mask_ref[core]
        left_ref[core] = repeated * jnp.concatenate([mask, mask], axis=1)


def add_halves(both):
    middle = both.shape[0] // 2
    return both[:middle] + both[middle:]


def put_chunks(keep_ref, near_ref, chunk_ref, far_ref, step, down, up):
    rank = keep_ref.shape[1]
    rows = down.shape[0] // rank // 2

    def slot(number):
        start = number * rank
        return down[start : start + rank], up[start : start + rank]

    for place in range(2):
        keep_ref[place] = jnp.concatenate(slot(place * step), axis=1)
        near_ref[place] = encode(*slot(rows + 1 - step + place * step))
        chunk_ref[place] = jnp.concatenate(slot(place * rows + 2), axis=1)
        far_ref[place] = encode(*slot(place * rows + 3))


def gradient_kernel(
    same_ref,
    mask_ref,
    own_ref,
    other_ref,
    own_gradient_ref,
    other_gradient_ref,
    weight_ref,
    weighted_ref,
    high_ref,
    low_ref,
    keep_ref,
    near_ref,
    chunk_ref,
    far_ref,
    up_ref,
    to_ref,
    left_ref,
):
    wide = weight_ref.shape[1]
    model_width = up_ref.shape[1]
    gradient = jnp.concatenate([own_gradient_ref[...], other_gradient_ref[...]], axis=0)
    high = high_ref[...].reshape(2 * wide, model_width)
    low = low_ref[...].reshape(2 * wide, model_width)
    to_both = dot(gradient, high, 1, 1) + dot(gradient, low, 1, 1)
    to_ref[...] = to_both[:, wide:]
    put_left(left_ref, same_ref, mask_ref, weight_ref[...] * to_both[:, :wide])
    down = dot(left_ref[0], own_ref[...], 0, 0) + dot(left_ref[1], other_ref[...], 0, 0)
    up = add_halves(dot(jnp.concatenate(halves(weighted_ref[...]), axis=1), gradient, 0, 0))
    up_ref[...] = up[:wide]
    put_chunks(keep_ref, near_ref, chunk_ref, far_ref, 1, add_halves(down), up[wide:])


def curvature_kernel(
    top,
    slots,
    small_ref,
    same_ref,
    mask_ref,
    own_ref,
    other_ref,
    weight_ref,
    weighted_ref,
    high_ref,
    low_ref,
    up_ref,
    to_ref,
    tangent_ref,
    arrived_ref,
    gradient_near_ref,
    keep_ref,
    near_ref,
    chunk_ref,
    far_ref,
    onward_ref,
    left_ref,
):
    onward_ref[...] = gradient_near_ref[...]
    _, _, curvature = token_columns(small_ref, top)
    tokens, wide = weight_ref.shape
    block = tokens // 2
    model_width = up_ref.shape[1]
    arrived = jnp.concatenate([arrived_ref[block:], arrived_ref[:block]], axis=0).astype(f32)
    resid = halves(curvature * (tangent_ref[...] + arrived))
    adapter_up = high_ref[0].reshape(wide, model_width), low_ref[0].reshape(wide, model_width)
    terms = weight_ref[...] * (dot_pairs(resid, adapter_up, 1, 1) + to_ref[...])
    put_left(left_ref, same_ref, mask_ref, terms)
    down = dot(left_ref[0], own_ref[...], 0, 0) + dot(left_ref[1], other_ref[...], 0, 0)
    weighted_u = halves(weighted_ref[:, wide:])
    up = add_halves(dot(jnp.concatenate(weighted_u, axis=1), resid[0], 0, 0)) + dot(weighted_u[0], resid[1], 0, 0)
    put_chunks(keep_ref, near_ref, chunk_ref, far_ref, slots // 2, add_halves(down), up_ref[...] + up)


def pair_kernel(hidden_width, arrived_ref, chunk_ref, across_ref, keep_ref):
    for x in range(2):
        down, up = decode(arrived_ref[x], hidden_width)
        down, up = chunk_ref[x, :, :hidden_width] + down, chunk_ref[x, :, hidden_width:] + up
        if x == 0:
            keep_ref[...] = jnp.concatenate([down, up], axis=1)
        else:
            across_ref[...] = encode(down, up)


def far_kernel(hidden_width, arrived_ref, keep_ref, out_ref):
    down, up = decode(arrived_ref[...], hidden_width)
    out_ref[...] = encode(keep_ref[:, :hidden_width] + down, keep_ref[:, hidden_width:] + up)


def near_kernel(hidden_width, arrived_ref, keep_ref, onward_ref, total_ref):
    for place in range(2):
        down, up = decode(arrived_ref[place], hidden_width)
        down, up = keep_ref[place, :, :hidden_width] + down, keep_ref[place, :, hidden_width:] + up
        if place == 0:
            total_ref[...] = jnp.concatenate([down, up], axis=1)
        else:
            onward_ref[...] = encode(down, up)


def add_kernel(hidden_width, total_ref, near_ref, far_ref, out_ref):
    near, far = decode(near_ref[...], hidden_width), decode(far_ref[...], hidden_width)
    out_ref[:, :hidden_width] = total_ref[:, :hidden_width] + near[0] + far[0]
    out_ref[:, hidden_width:] = total_ref[:, hidden_width:] + near[1] + far[1]


def total_kernel(hidden_width, gradient_ref, total_ref, near_ref, far_ref, *out_refs):
    near, far = decode(near_ref[...], hidden_width), decode(far_ref[...], hidden_width)
    out_refs[0][...] = gradient_ref[:, :hidden_width]
    out_refs[1][...] = gradient_ref[:, hidden_width:]
    out_refs[2][...] = total_ref[:, :hidden_width] + near[0] + far[0]
    out_refs[3][...] = total_ref[:, hidden_width:] + near[1] + far[1]


class Ring:
    def __init__(self, size):
        self.length = size // 2
        rows = self.length // 2
        self.order = [4 * z for z in range(rows)] + [4 * z + 2 for z in reversed(range(rows))]

    def shift(self, value, step):
        pairs = [
            (chip + core, self.order[(place + step) % self.length] + core)
            for place, chip in enumerate(self.order)
            for core in range(2)
        ]
        return lax.ppermute(value, "expert", pairs)

    def members(self, me):
        rows = self.length // 2
        place = jnp.where(me // 2 % 2 == 0, me // 4, self.length - 1 - me // 4)
        half = self.length // 2
        offsets = [0] + [offset for step in range(1, half) for offset in (self.length - step, step)] + [half]
        there = (place + jnp.array(offsets, jnp.int32)) % self.length
        return jnp.where(there < rows, 4 * there, 4 * (self.length - 1 - there) + 2) + me % 2

    def gather(self, own, passing):
        half = self.length // 2
        pieces = [own]
        ahead, behind = own, own
        for step in range(1, half):
            behind = self.shift(behind, 1)
            ahead = self.shift(ahead, -1)
            if step == 2:
                behind, ahead = passing(behind, ahead)
            pieces += [behind, ahead]
        pieces += [self.shift(behind[:1], 1), self.shift(ahead[1:], -1)]
        return pieces


def exchange(value, mask):
    size = lax.axis_size("expert")
    return lax.ppermute(value, "expert", [(device, device ^ mask) for device in range(size)])


def gathered_plan(
    hidden_of_route,
    expert_of_route,
    gate_of_route,
    capacity,
    output_gradient,
    curvature,
    adapter_down,
    adapter_up,
    down_direction,
    up_direction,
):
    ring = Ring(lax.axis_size("expert"))
    slots = ring.length
    rows = slots // 2
    masks = [4 * z for z in range(rows)] + [4 * z + 2 for z in range(rows)]
    me = lax.axis_index("expert")
    tokens, top = expert_of_route.shape
    both = 2 * tokens
    hidden_width = hidden_of_route.shape[2]
    rank = adapter_down.shape[2]
    model_width = output_gradient.shape[1]
    experts = capacity.shape[0]
    wide = slots * rank
    coded_width = hidden_width + model_width + lanes


    place = []

    def call(kernel, multiplies, outs, *operands, scratch=(), after=(), grant=kernel_vmem):
        space = pltpu.VMEM if grant == kernel_vmem else pltpu.HBM
        places = [pl.BlockSpec(memory_space=pl.ANY) for _ in after] + [
            pl.BlockSpec(memory_space=pltpu.SMEM if any(operand is it for it in place) else space) for operand in operands
        ]
        return pl.pallas_call(
            lambda *refs: kernel(*refs[len(after) :]),
            out_shape=[jax.ShapeDtypeStruct(shape, dtype) for shape, dtype in outs],
            in_specs=places,
            scratch_shapes=scratch,
            compiler_params=pltpu.CompilerParams(vmem_limit_bytes=grant),
            cost_estimate=pl.CostEstimate(flops=2 * multiplies, bytes_accessed=2**20, transcendentals=0),
        )(*after, *operands)

    down_multiplies = 2 * top * both * hidden_width * wide
    up_multiplies = both * model_width * wide

    first = (
        expert_of_route.T,
        gate_of_route.T,
        curvature[None],
        down_direction[0].T,
        adapter_down[0].T,
        adapter_up[0],
        up_direction[0],
    )
    piece, small = call(
        functools.partial(prepare_kernel, experts),
        10**8,
        [((2, rank, coded_width), i16), (((2 * top + 8) // 8 * 8, tokens), f32)],
        *first,
        scratch=[pltpu.VMEM(operand.shape, operand.dtype) for operand in first]
        + [pltpu.SemaphoreType.DMA((len(first),))],
        grant=whole_vmem,
    )
    arrivals = ring.members(me)
    slot_of_arrival = (arrivals ^ me) // 4 + rows * ((arrivals ^ me) // 2 % 2)
    place.append(jnp.concatenate([me[None], arrivals, me ^ jnp.array(masks, jnp.int32), slot_of_arrival]).astype(jnp.int32))
    small_other = exchange(small, 1)
    hidden = hidden_of_route.reshape(tokens * top, hidden_width)
    small_columns, local_rank, gate, same, mask, hidden_other, gradient_other = call(
        functools.partial(tokens_kernel, top, slots),
        10**9,
        [
            ((both, small.shape[0]), f32),
            ((2, tokens, wide), f32),
            ((2, tokens, wide), f32),
            ((top * tokens, tokens), bf16),
            ((2, top * tokens, wide), bf16),
            (hidden.shape, bf16),
            (output_gradient.shape, bf16),
        ],
        *place,
        small,
        small_other,
        exchange(hidden, 1),
        exchange(output_gradient, 1),
        scratch=[pltpu.SemaphoreType.DMA((2,))],
    )
    def passing(behind, ahead):
        return call(pass_kernel, 10**8, [(piece.shape, i16)] * 2, behind, ahead, after=[same])

    pieces = ring.gather(piece, passing)
    capacity_row = jnp.pad(capacity.astype(f32), (counts_lane, lanes - counts_lane - experts))[None, :]

    def reduced(first, count, halved, *parts, after=()):
        return call(
            functools.partial(reduce_kernel, top, first, count, halved),
            2 * down_multiplies * count // slots,
            [((both, 2 * count * rank), f32)],
            *place,
            small_columns,
            hidden,
            hidden_other,
            *parts,
            scratch=[pltpu.VMEM((tokens * top, 2 * count * rank), f32)],
            after=after,
        )[0]

    early = slots // 2
    reduced_early = reduced(0, early, False, *pieces[:early])
    (prior,) = call(prior_kernel, 10**8, [((8, lanes), f32)], *place, *pieces[:-1], after=[reduced_early])
    prior_arrived = exchange(prior, 1)
    reduced_late = reduced(early, slots - early, True, *pieces[early:], after=[prior])
    weight, weighted, tangent, coded, high, low = call(
        functools.partial(tangent_kernel, slots),
        6 * up_multiplies,
        [
            ((both, wide), f32),
            ((both, 2 * wide), f32),
            ((both, model_width), f32),
            ((both, model_width), bf16),
            ((2, slots, rank, model_width), bf16),
            ((2, slots, rank, model_width), bf16),
        ],
        *place,
        local_rank,
        gate,
        capacity_row,
        prior,
        prior_arrived,
        reduced_early,
        reduced_late,
        *pieces,
    )
    arrived = exchange(coded, 1)
    left = [pltpu.VMEM((2, top * tokens, 2 * wide), bf16)]
    chunks = [((2, rank, hidden_width + model_width), f32), ((2, rank, coded_width), i16)] * 2
    gradient_keep, gradient_near, gradient_chunk, gradient_far, up, to = call(
        gradient_kernel,
        down_multiplies + 8 * up_multiplies,
        chunks + [((wide, model_width), f32), ((both, wide), f32)],
        same,
        mask,
        hidden,
        hidden_other,
        output_gradient,
        gradient_other,
        weight,
        weighted,
        high,
        low,
        scratch=left,
    )
    gradient_far = exchange(gradient_far, 4)
    curvature_keep, curvature_near, curvature_chunk, curvature_far, gradient_near = call(
        functools.partial(curvature_kernel, top, slots),
        down_multiplies + 6 * up_multiplies,
        chunks + [(gradient_near.shape, i16)],
        small_columns,
        same,
        mask,
        hidden,
        hidden_other,
        weight,
        weighted,
        high,
        low,
        up,
        to,
        tangent,
        arrived,
        gradient_near,
        scratch=left,
    )

    hop = 2 * 10**9

    one = (rank, hidden_width + model_width)
    one_coded = (rank, coded_width)

    def hop_call(kernel, outs, *operands, after=()):
        return call(functools.partial(kernel, hidden_width), hop, outs, *operands, after=after)

    curvature_far = exchange(curvature_far, 4)
    gradient_near = exchange(gradient_near, 2)
    pair = [(one_coded, i16), (one, f32)]
    gradient_across, gradient_pair = hop_call(
        pair_kernel, pair, gradient_far, gradient_chunk, after=[curvature_keep]
    )
    curvature_across, curvature_pair = hop_call(
        pair_kernel, pair, curvature_far, curvature_chunk, after=[gradient_across]
    )
    curvature_near = exchange(curvature_near, 4)
    near = [(one_coded, i16), (one, f32)]
    gradient_onward, gradient_total = hop_call(
        near_kernel, near, gradient_near, gradient_keep, after=[curvature_across]
    )
    gradient_onward = exchange(gradient_onward, 4)
    (gradient_beyond,) = hop_call(
        far_kernel, [(one_coded, i16)], exchange(gradient_across, 2), gradient_pair, after=[gradient_total, curvature_near]
    )
    (curvature_beyond,) = hop_call(
        far_kernel, [(one_coded, i16)], exchange(curvature_across, 2), curvature_pair, after=[gradient_beyond]
    )
    curvature_onward, curvature_total = hop_call(
        near_kernel, near, curvature_near, curvature_keep, after=[curvature_beyond, gradient_onward]
    )
    (gradient_total,) = hop_call(
        add_kernel,
        [(one, f32)],
        gradient_total,
        gradient_onward,
        exchange(gradient_beyond, 8),
        after=[curvature_total],
    )
    down_gradient, up_gradient, curvature_down, curvature_up = hop_call(
        total_kernel,
        [((rank, hidden_width), f32), ((rank, model_width), f32)] * 2,
        gradient_total,
        curvature_total,
        exchange(curvature_onward, 2),
        exchange(curvature_beyond, 8),
    )
    return down_gradient.T[None], up_gradient[None], curvature_down.T[None], curvature_up[None]


def carried_in(value, axis, join, neutral):
    count, mine = (lax.axis_size(axis), lax.axis_index(axis))
    pieces = lax.all_gather(value, axis)
    so_far = jnp.full_like(value, 0) + jnp.asarray(neutral, value.dtype)

    def lap(position, so_far):
        longer = join(so_far, pieces[position])
        return jnp.where(position < mine, longer, so_far)

    return lax.fori_loop(0, count - 1, lap, so_far)


def add_counts(earlier, later):
    return earlier + later


def routed_plan(
    hidden_of_route,
    expert_of_route,
    gate_of_route,
    capacity,
    output_gradient,
    curvature,
    adapter_down,
    adapter_up,
    down_direction,
    up_direction,
):
    finest_precision = lax.Precision.HIGHEST
    group_size = lax.axis_size("expert")
    tok_rows, top_count = expert_of_route.shape
    hidden_width = hidden_of_route.shape[2]
    resident_experts = adapter_down.shape[0]
    adapter_rank = adapter_down.shape[2]
    model_width = output_gradient.shape[1]
    experts = resident_experts * group_size
    slot_most = 2 * tok_rows * top_count // experts
    routes = expert_of_route.reshape(-1)
    onehot = (routes[:, None] == jnp.arange(experts, dtype=jnp.int32)[None, :]).astype(jnp.int32)
    earlier = jnp.cumsum(onehot, axis=0) - onehot
    local_rank = jnp.sum(earlier * onehot, axis=1)
    counts = jnp.sum(onehot, axis=0)
    prior_count = carried_in(counts, "expert", add_counts, jnp.zeros_like(counts))
    global_rank = local_rank + jnp.sum(onehot * prior_count[None, :], axis=1)
    route_limit = jnp.sum(onehot * capacity[None, :], axis=1)
    retained_mask = (global_rank < route_limit).astype(jnp.float32)
    weight_of_route = (
        adapter_scale * gate_of_route.reshape(-1).astype(jnp.float32) * retained_mask
    ).astype(jnp.bfloat16)
    slot_index = routes * slot_most + local_rank
    layout = (group_size, resident_experts, slot_most)
    send_hidden = (
        jnp.zeros((experts * slot_most, hidden_width), jnp.bfloat16)
        .at[slot_index]
        .set(hidden_of_route.reshape(-1, hidden_width))
        .reshape(layout + (hidden_width,))
    )
    send_weight = (
        jnp.zeros((experts * slot_most,), jnp.bfloat16)
        .at[slot_index]
        .set(weight_of_route)
        .reshape(layout)
    )
    down_stacked = jnp.concatenate([adapter_down, down_direction], axis=2)
    up_stacked = jnp.concatenate([adapter_up, up_direction], axis=1)

    def spread(token_rows):
        per_route = jnp.repeat(token_rows, top_count, axis=0)
        placed = (
            jnp.zeros((experts * slot_most, model_width), jnp.bfloat16)
            .at[slot_index]
            .set(per_route)
        )
        return placed.reshape(layout + (model_width,))

    send_residual = spread(output_gradient)
    pieces = (
        lax.all_to_all(send_hidden, "expert", split_axis=0, concat_axis=0, tiled=True),
        lax.all_to_all(send_weight, "expert", split_axis=0, concat_axis=0, tiled=True),
    )
    hidden_rows = pieces[0].astype(jnp.float32)
    weight_rows = pieces[1].astype(jnp.float32)[..., None]
    reduced_hidden = jnp.einsum(
        "cjif,jfk->cjik", hidden_rows, down_stacked, precision=finest_precision
    )
    exchanged_rows = jnp.concatenate(
        [reduced_hidden[..., adapter_rank:], reduced_hidden[..., :adapter_rank]], axis=3
    )
    tangent_out = weight_rows * jnp.einsum(
        "cjik,jkd->cjid", exchanged_rows, up_stacked, precision=finest_precision
    )
    returned = lax.all_to_all(
        tangent_out.astype(jnp.bfloat16), "expert", split_axis=0, concat_axis=0, tiled=True
    )
    results = (returned, reduced_hidden) + tuple(pieces)
    returned = results[0]
    reduced_hidden = results[1]
    hidden_rows = results[2]
    weight_rows = results[3]
    route_tangent = returned.reshape(experts * slot_most, model_width)[slot_index]
    out_tangent = jnp.sum(
        route_tangent.reshape(tok_rows, top_count, model_width).astype(jnp.float32), axis=1
    )
    resid_tangent = (curvature[:, None] * out_tangent).astype(jnp.bfloat16)
    send_tangent = spread(resid_tangent)
    residual_rows, tangent_rows = (
        lax.all_to_all(send_residual, "expert", split_axis=0, concat_axis=0, tiled=True),
        lax.all_to_all(send_tangent, "expert", split_axis=0, concat_axis=0, tiled=True),
    )
    residual_full = residual_rows.astype(jnp.float32)
    complete_tangent = tangent_rows.astype(jnp.float32)
    weight_column = weight_rows.astype(jnp.float32)[..., None]
    residual_reduced = jnp.einsum(
        "wyov,yqv->wyoq", residual_full, up_stacked, precision=finest_precision
    )
    reduced_tangent = jnp.einsum(
        "wyov,yqv->wyoq", complete_tangent, adapter_up, precision=finest_precision
    )
    left_terms = jnp.concatenate(
        [
            weight_column * residual_reduced[..., :adapter_rank],
            weight_column * (reduced_tangent + residual_reduced[..., adapter_rank:]),
        ],
        axis=3,
    )
    down_terms = jnp.einsum(
        "cjif,cjik->jfk", hidden_rows.astype(jnp.float32), left_terms, precision=finest_precision
    )
    raised_update = weight_column * reduced_hidden[..., :adapter_rank]
    raised_tangent_update = weight_column * reduced_hidden[..., adapter_rank:]
    up_terms = jnp.einsum(
        "cjik,cjid->jkd",
        jnp.concatenate([raised_update, raised_tangent_update], axis=3),
        residual_full,
        precision=finest_precision,
    )
    curvature_piece = up_terms[:, adapter_rank:] + jnp.einsum(
        "cjik,cjid->jkd", raised_update, complete_tangent, precision=finest_precision
    )
    return (
        down_terms[..., :adapter_rank],
        up_terms[:, :adapter_rank],
        down_terms[..., adapter_rank:],
        curvature_piece,
    )


def local(*arguments):
    factor_bytes = 2 * 4 * (arguments[6].size + arguments[7].size) * lax.axis_size("expert")
    fits = lax.axis_size("expert") == 16 and 4 * factor_bytes <= kernel_vmem
    plan = gathered_plan if fits else routed_plan
    return plan(*arguments)


def solution(mesh):
    return jax.shard_map(
        local,
        mesh=mesh,
        in_specs=(
            P(("groups", "expert"), None, None),
            P(("groups", "expert"), None),
            P(("groups", "expert"), None),
            P("groups"),
            P(("groups", "expert"), None),
            P(("groups", "expert")),
            P("expert", None, None),
            P("expert", None, None),
            P(("groups", "expert"), None, None),
            P(("groups", "expert"), None, None),
        ),
        out_specs=(
            P(("groups", "expert"), None, None),
            P(("groups", "expert"), None, None),
            P(("groups", "expert"), None, None),
            P(("groups", "expert"), None, None),
        ),
        check_vma=False,
    )
```

```python
import functools

import jax
import jax.numpy as jnp
from jax import lax
from jax.experimental import pallas as pl
from jax.experimental.pallas import tpu as pltpu
from jax.sharding import PartitionSpec as P

adapter_scale = 2.0
f32 = jnp.float32
bf16 = jnp.bfloat16
i16 = jnp.int16
lanes = 128
counts_lane = 64
kernel_vmem = 32 * 2**20
whole_vmem = 60 * 2**20


def halves(value):
    high = value.astype(bf16)
    return high, (value - high.astype(f32)).astype(bf16)


def dot(a, b, a_dim, b_dim):
    return lax.dot_general(a, b, (((a_dim,), (b_dim,)), ((), ())), preferred_element_type=f32)


def dot_pairs(a, b, a_dim, b_dim):
    return dot(a[0], b[0], a_dim, b_dim) + (dot(a[1], b[0], a_dim, b_dim) + dot(a[0], b[1], a_dim, b_dim))


def encode(down, up, counts=0.0):
    def scaled(value):
        largest = jnp.max(jnp.abs(value), axis=-1, keepdims=True)
        exponent = jnp.ceil(jnp.log2(jnp.maximum(largest, 1e-30)))
        coded = jnp.round(value * jnp.exp2(15.0 - exponent))
        return jnp.clip(coded, -32767.0, 32767.0), exponent

    down, down_exponent = scaled(down)
    up, up_exponent = scaled(up)
    lane = lax.broadcasted_iota(jnp.int32, down.shape[:-1] + (lanes,), down.ndim - 1)
    tail = jnp.where(lane < counts_lane // 2, down_exponent, up_exponent)
    tail = jnp.where(lane < counts_lane, tail, counts)
    return jnp.concatenate([down, up, tail], axis=-1).astype(jnp.int32).astype(i16)


def decode(coded, hidden_width):
    width = coded.shape[-1] - lanes
    value = coded.astype(jnp.int32).astype(f32)
    down_scale = jnp.exp2(value[..., width : width + 1] - 15.0)
    up_scale = jnp.exp2(value[..., width + counts_lane // 2 : width + counts_lane // 2 + 1] - 15.0)
    return value[..., :hidden_width] * down_scale, value[..., hidden_width:width] * up_scale


def prepare_kernel(experts, *refs):
    (piece_ref, small_ref), sem, refs = refs[7:9], refs[-1], refs[:7] + refs[9:-1]
    copies = [pltpu.make_async_copy(refs[i], refs[7 + i], sem.at[i]) for i in range(7)]
    for copy in copies:
        copy.start()
    for copy in copies:
        copy.wait()
    expert, gate, curvature, down_direction, adapter_down, adapter_up, up_direction = [ref[...] for ref in refs[7:]]
    top = expert.shape[0]
    small_ref[...] = jnp.zeros_like(small_ref)
    small_ref[:top] = expert.astype(f32)
    small_ref[top : 2 * top] = gate.astype(f32)
    small_ref[2 * top : 2 * top + 1] = curvature
    lane = lax.broadcasted_iota(jnp.int32, (1, lanes), 1)
    counts = jnp.zeros((1, lanes), f32)
    for number in range(experts):
        named = jnp.where(expert == number, 1.0, 0.0)
        total = jnp.sum(jnp.sum(named, axis=0, keepdims=True), axis=1, keepdims=True)
        counts = jnp.where(lane == counts_lane + number, total, counts)
    piece_ref[0] = encode(down_direction, adapter_up, counts)
    piece_ref[1] = encode(adapter_down, up_direction, counts)


def token_columns(small_ref, top):
    experts = [small_ref[:, k : k + 1] for k in range(top)]
    gates = [small_ref[:, top + k : top + k + 1] for k in range(top)]
    return experts, gates, small_ref[:, 2 * top : 2 * top + 1]


def members(place_ref, wide, first, count, dim=1):
    shape = (1, wide) if dim == 1 else (wide, 1)
    piece_of = lax.broadcasted_iota(jnp.int32, shape, dim) // (wide // count)
    found = jnp.zeros(shape, jnp.int32)
    for number in range(count):
        found = jnp.where(piece_of == number, place_ref[1 + first + number], found)
    return found.astype(f32)


def prior_kernel(place_ref, *rest):
    piece_refs, prior_ref = rest[:-1], rest[-1]
    me = place_ref[0]
    prior_ref[...] = jnp.zeros_like(prior_ref)
    for block, number in enumerate((me, me ^ 1)):
        total = jnp.zeros((1, lanes), f32)
        for arrival, piece_ref in enumerate(piece_refs):
            tail = piece_ref[0, :, piece_ref.shape[2] - lanes :]
            counts = tail.astype(jnp.int32).astype(f32)[0:1]
            total = total + jnp.where(place_ref[1 + arrival] < number, counts, 0.0)
        prior_ref[block : block + 1] = total


def piece_part(refs, arrival, kind, halved):
    if halved and arrival == len(refs) - 2:
        return refs[arrival + kind][0]
    return refs[arrival][kind]


def tokens_kernel(top, slots, place_ref, own_ref, other_ref, hidden_other_ref, gradient_other_ref, *outs):
    small_ref, rank_ref, gate_ref, same_ref, mask_ref, hidden_ref, gradient_ref, sem = outs
    copies = [
        pltpu.make_async_copy(hidden_other_ref, hidden_ref, sem.at[0]),
        pltpu.make_async_copy(gradient_other_ref, gradient_ref, sem.at[1]),
    ]
    for copy in copies:
        copy.start()
    small_ref[...] = jnp.concatenate([own_ref[...], other_ref[...]], axis=1).T
    experts, gates, _ = token_columns(small_ref, top)
    _, tokens, wide = rank_ref.shape
    column = members(place_ref, wide, slots, slots)
    below = (
        lax.broadcasted_iota(jnp.int32, (tokens, tokens), 0)
        > lax.broadcasted_iota(jnp.int32, (tokens, tokens), 1)
    )
    below = jnp.where(below, 1.0, 0.0).astype(bf16)
    rows = same_ref.shape[0]
    row = lax.broadcasted_iota(jnp.int32, (rows, tokens), 0)
    same = jnp.where(row // top == lax.broadcasted_iota(jnp.int32, (rows, tokens), 1), 1.0, 0.0).astype(bf16)
    same_ref[...] = same
    for core in range(2):
        tokens_of = slice(core * tokens, (core + 1) * tokens)
        gate = jnp.zeros((tokens, wide), f32)
        member = jnp.zeros((tokens, wide), f32)
        for k in range(top):
            named = experts[k][tokens_of] == column
            gate = jnp.where(named, gates[k][tokens_of], gate)
            member = jnp.where(named, 1.0, member)
        gate_ref[core] = gate
        rank_ref[core] = dot(below, member.astype(bf16), 1, 0)
        named = dot(same, small_ref[tokens_of].astype(bf16), 1, 0)
        position = lax.broadcasted_iota(jnp.int32, named.shape, 0) % top
        own = lax.broadcasted_iota(jnp.int32, named.shape, 1) == position
        expert = jnp.sum(jnp.where(own, named, 0.0), axis=1, keepdims=True)
        mask_ref[core] = jnp.where(expert == column, 1.0, 0.0).astype(bf16)
    for copy in copies:
        copy.wait()


def pass_kernel(behind_ref, ahead_ref, behind_out_ref, ahead_out_ref):
    behind_out_ref[...] = behind_ref[...]
    ahead_out_ref[...] = ahead_ref[...]


def reduce_kernel(top, first, count, halved, place_ref, small_ref, own_ref, other_ref, *rest):
    piece_refs, (reduced_ref, full_ref) = rest[:-2], rest[-2:]
    hidden_width = own_ref.shape[1]
    downs = [
        decode(piece_part(piece_refs, arrival, kind, halved), hidden_width)[0]
        for kind in range(2)
        for arrival in range(count)
    ]
    factor = jnp.concatenate(halves(jnp.concatenate(downs, axis=0)), axis=0)
    experts, _, _ = token_columns(small_ref, top)
    wide = reduced_ref.shape[1]
    column = members(place_ref, wide // 2, first, count)
    column = jnp.concatenate([column, column], axis=1)
    tokens = own_ref.shape[0] // top
    for core, hidden_ref in enumerate((own_ref, other_ref)):
        full = dot(hidden_ref[...], factor, 1, 1)
        full_ref[...] = full[:, :wide] + full[:, wide:]
        tokens_of = slice(core * tokens, (core + 1) * tokens)
        total = jnp.zeros((tokens, wide), f32)
        for k in range(top):
            here = full_ref[pl.ds(k, tokens, stride=top), :]
            total = jnp.where(experts[k][tokens_of] == column, here, total)
        reduced_ref[tokens_of] = total


def rank_limits(place_ref, wide, slots, capacity_ref, prior_ref, arrived_ref):
    lane = lax.broadcasted_iota(jnp.int32, (1, lanes), 1)
    piece_of = lax.broadcasted_iota(jnp.int32, (1, wide), 1) // (wide // slots)
    limits = []
    for block in range(2):
        total = capacity_ref[...] - prior_ref[block : block + 1] - arrived_ref[1 - block : 2 - block]
        limit = jnp.zeros((1, wide), f32)
        for slot in range(slots):
            picked = jnp.where(lane == counts_lane + place_ref[1 + slots + slot], total, 0.0)
            limit = jnp.where(piece_of == slot, jnp.sum(picked, axis=1, keepdims=True), limit)
        limits.append(limit)
    return limits


def tangent_kernel(
    slots, place_ref, rank_ref, gate_ref, capacity_ref, prior_ref, arrived_ref, early_ref, late_ref, *rest
):
    piece_refs = rest[: slots + 1]
    weight_ref, weighted_ref, tangent_ref, coded_ref, high_ref, low_ref = rest[slots + 1 :]
    _, wide = weight_ref.shape
    model_width = tangent_ref.shape[1]
    hidden_width = piece_refs[0].shape[2] - model_width - lanes
    limits = rank_limits(place_ref, wide, slots, capacity_ref, prior_ref, arrived_ref)
    weights = [
        jnp.where(rank_ref[core] < limits[core], adapter_scale * gate_ref[core], 0.0) for core in range(2)
    ]
    weight = jnp.concatenate(weights, axis=0)
    weight_ref[...] = weight
    half = wide // 2
    reduced = [
        jnp.concatenate([ref[:, kind * half : (kind + 1) * half] for ref in (early_ref, late_ref)], axis=1)
        for kind in range(2)
    ]
    rank = wide // slots
    by_arrival = members(place_ref, wide, 0, slots, 0) == members(place_ref, wide, slots, slots)
    row = lax.broadcasted_iota(jnp.int32, (wide, wide), 0)
    same_index = row % rank == lax.broadcasted_iota(jnp.int32, (wide, wide), 1) % rank
    order = jnp.where(by_arrival & same_index, 1.0, 0.0).astype(bf16)
    reduced = [sum(dot(part, order, 1, 0) for part in halves(both)) for both in reduced]
    weighted = jnp.concatenate([weight * part for part in reduced], axis=1)
    weighted_ref[...] = weighted
    for arrival in range(slots):
        for kind in range(2):
            _, up = decode(piece_part(piece_refs, arrival, kind, True), hidden_width)
            slot = place_ref[1 + 2 * slots + arrival]
            high_ref[kind, slot], low_ref[kind, slot] = halves(up)
    factor = high_ref[...].reshape(2 * wide, model_width), low_ref[...].reshape(2 * wide, model_width)
    tangent = dot_pairs(halves(weighted), factor, 1, 0)
    tangent_ref[...] = tangent
    coded_ref[...] = tangent.astype(bf16)


def put_left(left_ref, same_ref, mask_ref, terms):
    both = jnp.concatenate(halves(terms), axis=1)
    tokens = terms.shape[0] // 2
    for core in range(2):
        repeated = dot(same_ref[...], both[core * tokens : (core + 1) * tokens], 1, 0).astype(bf16)
        mask = mask_ref[core]
        left_ref[core] = repeated * jnp.concatenate([mask, mask], axis=1)


def add_halves(both):
    middle = both.shape[0] // 2
    return both[:middle] + both[middle:]


def put_chunks(keep_ref, near_ref, chunk_ref, far_ref, down, up):
    rank = keep_ref.shape[1]
    rows = down.shape[0] // rank // 2

    def slot(number):
        start = number * rank
        return down[start : start + rank], up[start : start + rank]

    for place in range(2):
        keep_ref[place] = jnp.concatenate(slot(place), axis=1)
        near_ref[place] = encode(*slot(rows + place))
        chunk_ref[place] = jnp.concatenate(slot(place * rows + 2), axis=1)
        far_ref[place] = encode(*slot(place * rows + 3))


def gradient_kernel(
    same_ref,
    mask_ref,
    own_ref,
    other_ref,
    own_gradient_ref,
    other_gradient_ref,
    weight_ref,
    weighted_ref,
    high_ref,
    low_ref,
    keep_ref,
    near_ref,
    chunk_ref,
    far_ref,
    up_ref,
    to_ref,
    left_ref,
):
    wide = weight_ref.shape[1]
    model_width = up_ref.shape[1]
    gradient = jnp.concatenate([own_gradient_ref[...], other_gradient_ref[...]], axis=0)
    high = high_ref[...].reshape(2 * wide, model_width)
    low = low_ref[...].reshape(2 * wide, model_width)
    to_both = dot(gradient, high, 1, 1) + dot(gradient, low, 1, 1)
    to_ref[...] = to_both[:, wide:]
    put_left(left_ref, same_ref, mask_ref, weight_ref[...] * to_both[:, :wide])
    down = dot(left_ref[0], own_ref[...], 0, 0) + dot(left_ref[1], other_ref[...], 0, 0)
    up = add_halves(dot(jnp.concatenate(halves(weighted_ref[...]), axis=1), gradient, 0, 0))
    up_ref[...] = up[:wide]
    put_chunks(keep_ref, near_ref, chunk_ref, far_ref, add_halves(down), up[wide:])


def curvature_kernel(
    top,
    small_ref,
    same_ref,
    mask_ref,
    own_ref,
    other_ref,
    weight_ref,
    weighted_ref,
    high_ref,
    low_ref,
    up_ref,
    to_ref,
    tangent_ref,
    arrived_ref,
    keep_ref,
    near_ref,
    chunk_ref,
    far_ref,
    left_ref,
):
    _, _, curvature = token_columns(small_ref, top)
    tokens, wide = weight_ref.shape
    block = tokens // 2
    model_width = up_ref.shape[1]
    arrived = jnp.concatenate([arrived_ref[block:], arrived_ref[:block]], axis=0).astype(f32)
    resid = halves(curvature * (tangent_ref[...] + arrived))
    adapter_up = high_ref[0].reshape(wide, model_width), low_ref[0].reshape(wide, model_width)
    terms = weight_ref[...] * (dot_pairs(resid, adapter_up, 1, 1) + to_ref[...])
    put_left(left_ref, same_ref, mask_ref, terms)
    down = dot(left_ref[0], own_ref[...], 0, 0) + dot(left_ref[1], other_ref[...], 0, 0)
    weighted_u = halves(weighted_ref[:, wide:])
    up = add_halves(dot(jnp.concatenate(weighted_u, axis=1), resid[0], 0, 0)) + dot(weighted_u[0], resid[1], 0, 0)
    put_chunks(keep_ref, near_ref, chunk_ref, far_ref, add_halves(down), up_ref[...] + up)


def pair_kernel(hidden_width, arrived_ref, chunk_ref, *refs):
    passing, (across_ref, keep_ref) = (refs[:1], refs[1:3]) if len(refs) == 4 else ((), refs)
    for near_ref in passing:
        refs[3][...] = near_ref[...]
    for x in range(2):
        down, up = decode(arrived_ref[x], hidden_width)
        down, up = chunk_ref[x, :, :hidden_width] + down, chunk_ref[x, :, hidden_width:] + up
        if x == 0:
            keep_ref[...] = jnp.concatenate([down, up], axis=1)
        else:
            across_ref[...] = encode(down, up)


def far_kernel(hidden_width, arrived_ref, keep_ref, out_ref):
    down, up = decode(arrived_ref[...], hidden_width)
    out_ref[...] = encode(keep_ref[:, :hidden_width] + down, keep_ref[:, hidden_width:] + up)


def near_kernel(hidden_width, arrived_ref, keep_ref, onward_ref, total_ref):
    for place in range(2):
        down, up = decode(arrived_ref[place], hidden_width)
        down, up = keep_ref[place, :, :hidden_width] + down, keep_ref[place, :, hidden_width:] + up
        if place == 0:
            total_ref[...] = jnp.concatenate([down, up], axis=1)
        else:
            onward_ref[...] = encode(down, up)


def add_kernel(hidden_width, total_ref, near_ref, far_ref, out_ref):
    near, far = decode(near_ref[...], hidden_width), decode(far_ref[...], hidden_width)
    out_ref[:, :hidden_width] = total_ref[:, :hidden_width] + near[0] + far[0]
    out_ref[:, hidden_width:] = total_ref[:, hidden_width:] + near[1] + far[1]


def total_kernel(hidden_width, gradient_ref, total_ref, near_ref, far_ref, *out_refs):
    near, far = decode(near_ref[...], hidden_width), decode(far_ref[...], hidden_width)
    out_refs[0][...] = gradient_ref[:, :hidden_width]
    out_refs[1][...] = gradient_ref[:, hidden_width:]
    out_refs[2][...] = total_ref[:, :hidden_width] + near[0] + far[0]
    out_refs[3][...] = total_ref[:, hidden_width:] + near[1] + far[1]


class Ring:
    def __init__(self, size):
        self.length = size // 2
        rows = self.length // 2
        self.order = [4 * z for z in range(rows)] + [4 * z + 2 for z in reversed(range(rows))]

    def shift(self, value, step):
        pairs = [
            (chip + core, self.order[(place + step) % self.length] + core)
            for place, chip in enumerate(self.order)
            for core in range(2)
        ]
        return lax.ppermute(value, "expert", pairs)

    def members(self, me):
        rows = self.length // 2
        place = jnp.where(me // 2 % 2 == 0, me // 4, self.length - 1 - me // 4)
        half = self.length // 2
        offsets = [0] + [offset for step in range(1, half) for offset in (self.length - step, step)] + [half]
        there = (place + jnp.array(offsets, jnp.int32)) % self.length
        return jnp.where(there < rows, 4 * there, 4 * (self.length - 1 - there) + 2) + me % 2

    def gather(self, own, passing):
        half = self.length // 2
        pieces = [own]
        ahead, behind = own, own
        for step in range(1, half):
            behind = self.shift(behind, 1)
            ahead = self.shift(ahead, -1)
            if step == 2:
                behind, ahead = passing(behind, ahead)
            pieces += [behind, ahead]
        pieces += [self.shift(behind[:1], 1), self.shift(ahead[1:], -1)]
        return pieces


def exchange(value, mask):
    size = lax.axis_size("expert")
    return lax.ppermute(value, "expert", [(device, device ^ mask) for device in range(size)])


def gathered_plan(
    hidden_of_route,
    expert_of_route,
    gate_of_route,
    capacity,
    output_gradient,
    curvature,
    adapter_down,
    adapter_up,
    down_direction,
    up_direction,
):
    ring = Ring(lax.axis_size("expert"))
    slots = ring.length
    rows = slots // 2
    masks = [4 * z for z in range(rows)] + [4 * z + 2 for z in range(rows)]
    me = lax.axis_index("expert")
    tokens, top = expert_of_route.shape
    both = 2 * tokens
    hidden_width = hidden_of_route.shape[2]
    rank = adapter_down.shape[2]
    model_width = output_gradient.shape[1]
    experts = capacity.shape[0]
    wide = slots * rank
    coded_width = hidden_width + model_width + lanes


    place = []

    def call(kernel, multiplies, outs, *operands, scratch=(), after=(), grant=kernel_vmem):
        space = pltpu.VMEM if grant == kernel_vmem else pltpu.HBM
        places = [pl.BlockSpec(memory_space=pl.ANY) for _ in after] + [
            pl.BlockSpec(memory_space=pltpu.SMEM if any(operand is it for it in place) else space) for operand in operands
        ]
        return pl.pallas_call(
            lambda *refs: kernel(*refs[len(after) :]),
            out_shape=[jax.ShapeDtypeStruct(shape, dtype) for shape, dtype in outs],
            in_specs=places,
            scratch_shapes=scratch,
            compiler_params=pltpu.CompilerParams(vmem_limit_bytes=grant),
            cost_estimate=pl.CostEstimate(flops=2 * multiplies, bytes_accessed=2**20, transcendentals=0),
        )(*after, *operands)

    down_multiplies = 2 * top * both * hidden_width * wide
    up_multiplies = both * model_width * wide

    first = (
        expert_of_route.T,
        gate_of_route.T,
        curvature[None],
        down_direction[0].T,
        adapter_down[0].T,
        adapter_up[0],
        up_direction[0],
    )
    piece, small = call(
        functools.partial(prepare_kernel, experts),
        10**8,
        [((2, rank, coded_width), i16), (((2 * top + 8) // 8 * 8, tokens), f32)],
        *first,
        scratch=[pltpu.VMEM(operand.shape, operand.dtype) for operand in first]
        + [pltpu.SemaphoreType.DMA((len(first),))],
        grant=whole_vmem,
    )
    arrivals = ring.members(me)
    slot_of_arrival = (arrivals ^ me) // 4 + rows * ((arrivals ^ me) // 2 % 2)
    place.append(jnp.concatenate([me[None], arrivals, me ^ jnp.array(masks, jnp.int32), slot_of_arrival]).astype(jnp.int32))
    small_other = exchange(small, 1)
    hidden = hidden_of_route.reshape(tokens * top, hidden_width)
    small_columns, local_rank, gate, same, mask, hidden_other, gradient_other = call(
        functools.partial(tokens_kernel, top, slots),
        10**9,
        [
            ((both, small.shape[0]), f32),
            ((2, tokens, wide), f32),
            ((2, tokens, wide), f32),
            ((top * tokens, tokens), bf16),
            ((2, top * tokens, wide), bf16),
            (hidden.shape, bf16),
            (output_gradient.shape, bf16),
        ],
        *place,
        small,
        small_other,
        exchange(hidden, 1),
        exchange(output_gradient, 1),
        scratch=[pltpu.SemaphoreType.DMA((2,))],
    )
    def passing(behind, ahead):
        return call(pass_kernel, 10**8, [(piece.shape, i16)] * 2, behind, ahead, after=[same])

    pieces = ring.gather(piece, passing)
    capacity_row = jnp.pad(capacity.astype(f32), (counts_lane, lanes - counts_lane - experts))[None, :]

    def reduced(first, count, halved, *parts, after=()):
        return call(
            functools.partial(reduce_kernel, top, first, count, halved),
            2 * down_multiplies * count // slots,
            [((both, 2 * count * rank), f32)],
            *place,
            small_columns,
            hidden,
            hidden_other,
            *parts,
            scratch=[pltpu.VMEM((tokens * top, 2 * count * rank), f32)],
            after=after,
        )[0]

    early = slots // 2
    reduced_early = reduced(0, early, False, *pieces[:early])
    (prior,) = call(prior_kernel, 10**8, [((8, lanes), f32)], *place, *pieces[:-1], after=[reduced_early])
    prior_arrived = exchange(prior, 1)
    reduced_late = reduced(early, slots - early, True, *pieces[early:], after=[prior])
    weight, weighted, tangent, coded, high, low = call(
        functools.partial(tangent_kernel, slots),
        6 * up_multiplies,
        [
            ((both, wide), f32),
            ((both, 2 * wide), f32),
            ((both, model_width), f32),
            ((both, model_width), bf16),
            ((2, slots, rank, model_width), bf16),
            ((2, slots, rank, model_width), bf16),
        ],
        *place,
        local_rank,
        gate,
        capacity_row,
        prior,
        prior_arrived,
        reduced_early,
        reduced_late,
        *pieces,
    )
    arrived = exchange(coded, 1)
    left = [pltpu.VMEM((2, top * tokens, 2 * wide), bf16)]
    chunks = [((2, rank, hidden_width + model_width), f32), ((2, rank, coded_width), i16)] * 2
    gradient_keep, gradient_near, gradient_chunk, gradient_far, up, to = call(
        gradient_kernel,
        down_multiplies + 8 * up_multiplies,
        chunks + [((wide, model_width), f32), ((both, wide), f32)],
        same,
        mask,
        hidden,
        hidden_other,
        output_gradient,
        gradient_other,
        weight,
        weighted,
        high,
        low,
        scratch=left,
    )
    gradient_far = exchange(gradient_far, 4)
    gradient_near = exchange(gradient_near, 2)
    curvature_keep, curvature_near, curvature_chunk, curvature_far = call(
        functools.partial(curvature_kernel, top),
        down_multiplies + 6 * up_multiplies,
        chunks,
        small_columns,
        same,
        mask,
        hidden,
        hidden_other,
        weight,
        weighted,
        high,
        low,
        up,
        to,
        tangent,
        arrived,
        scratch=left,
    )

    hop = 2 * 10**9

    one = (rank, hidden_width + model_width)
    one_coded = (rank, coded_width)

    def hop_call(kernel, outs, *operands, after=()):
        return call(functools.partial(kernel, hidden_width), hop, outs, *operands, after=after)

    curvature_far = exchange(curvature_far, 4)
    pair = [(one_coded, i16), (one, f32)]
    gradient_across, gradient_pair, curvature_near = hop_call(
        pair_kernel,
        pair + [(curvature_near.shape, i16)],
        gradient_far,
        gradient_chunk,
        curvature_near,
        after=[curvature_keep],
    )
    curvature_near = exchange(curvature_near, 2)
    near = [(one_coded, i16), (one, f32)]
    gradient_onward, gradient_total = hop_call(
        near_kernel, near, gradient_near, gradient_keep, after=[gradient_across]
    )
    gradient_onward = exchange(gradient_onward, 4)
    curvature_across, curvature_pair = hop_call(
        pair_kernel, pair, curvature_far, curvature_chunk, after=[gradient_total]
    )
    (gradient_beyond,) = hop_call(
        far_kernel, [(one_coded, i16)], exchange(gradient_across, 2), gradient_pair, after=[curvature_across, gradient_onward]
    )
    (curvature_beyond,) = hop_call(
        far_kernel, [(one_coded, i16)], exchange(curvature_across, 2), curvature_pair, after=[gradient_beyond]
    )
    curvature_onward, curvature_total = hop_call(
        near_kernel, near, curvature_near, curvature_keep, after=[curvature_beyond]
    )
    (gradient_total,) = hop_call(
        add_kernel,
        [(one, f32)],
        gradient_total,
        gradient_onward,
        exchange(gradient_beyond, 8),
        after=[curvature_total],
    )
    down_gradient, up_gradient, curvature_down, curvature_up = hop_call(
        total_kernel,
        [((rank, hidden_width), f32), ((rank, model_width), f32)] * 2,
        gradient_total,
        curvature_total,
        exchange(curvature_onward, 4),
        exchange(curvature_beyond, 8),
    )
    return down_gradient.T[None], up_gradient[None], curvature_down.T[None], curvature_up[None]


def carried_in(value, axis, join, neutral):
    count, mine = (lax.axis_size(axis), lax.axis_index(axis))
    pieces = lax.all_gather(value, axis)
    so_far = jnp.full_like(value, 0) + jnp.asarray(neutral, value.dtype)

    def lap(position, so_far):
        longer = join(so_far, pieces[position])
        return jnp.where(position < mine, longer, so_far)

    return lax.fori_loop(0, count - 1, lap, so_far)


def add_counts(earlier, later):
    return earlier + later


def routed_plan(
    hidden_of_route,
    expert_of_route,
    gate_of_route,
    capacity,
    output_gradient,
    curvature,
    adapter_down,
    adapter_up,
    down_direction,
    up_direction,
):
    finest_precision = lax.Precision.HIGHEST
    group_size = lax.axis_size("expert")
    tok_rows, top_count = expert_of_route.shape
    hidden_width = hidden_of_route.shape[2]
    resident_experts = adapter_down.shape[0]
    adapter_rank = adapter_down.shape[2]
    model_width = output_gradient.shape[1]
    experts = resident_experts * group_size
    slot_most = 2 * tok_rows * top_count // experts
    routes = expert_of_route.reshape(-1)
    onehot = (routes[:, None] == jnp.arange(experts, dtype=jnp.int32)[None, :]).astype(jnp.int32)
    earlier = jnp.cumsum(onehot, axis=0) - onehot
    local_rank = jnp.sum(earlier * onehot, axis=1)
    counts = jnp.sum(onehot, axis=0)
    prior_count = carried_in(counts, "expert", add_counts, jnp.zeros_like(counts))
    global_rank = local_rank + jnp.sum(onehot * prior_count[None, :], axis=1)
    route_limit = jnp.sum(onehot * capacity[None, :], axis=1)
    retained_mask = (global_rank < route_limit).astype(jnp.float32)
    weight_of_route = (
        adapter_scale * gate_of_route.reshape(-1).astype(jnp.float32) * retained_mask
    ).astype(jnp.bfloat16)
    slot_index = routes * slot_most + local_rank
    layout = (group_size, resident_experts, slot_most)
    send_hidden = (
        jnp.zeros((experts * slot_most, hidden_width), jnp.bfloat16)
        .at[slot_index]
        .set(hidden_of_route.reshape(-1, hidden_width))
        .reshape(layout + (hidden_width,))
    )
    send_weight = (
        jnp.zeros((experts * slot_most,), jnp.bfloat16)
        .at[slot_index]
        .set(weight_of_route)
        .reshape(layout)
    )
    down_stacked = jnp.concatenate([adapter_down, down_direction], axis=2)
    up_stacked = jnp.concatenate([adapter_up, up_direction], axis=1)

    def spread(token_rows):
        per_route = jnp.repeat(token_rows, top_count, axis=0)
        placed = (
            jnp.zeros((experts * slot_most, model_width), jnp.bfloat16)
            .at[slot_index]
            .set(per_route)
        )
        return placed.reshape(layout + (model_width,))

    send_residual = spread(output_gradient)
    pieces = (
        lax.all_to_all(send_hidden, "expert", split_axis=0, concat_axis=0, tiled=True),
        lax.all_to_all(send_weight, "expert", split_axis=0, concat_axis=0, tiled=True),
    )
    hidden_rows = pieces[0].astype(jnp.float32)
    weight_rows = pieces[1].astype(jnp.float32)[..., None]
    reduced_hidden = jnp.einsum(
        "cjif,jfk->cjik", hidden_rows, down_stacked, precision=finest_precision
    )
    exchanged_rows = jnp.concatenate(
        [reduced_hidden[..., adapter_rank:], reduced_hidden[..., :adapter_rank]], axis=3
    )
    tangent_out = weight_rows * jnp.einsum(
        "cjik,jkd->cjid", exchanged_rows, up_stacked, precision=finest_precision
    )
    returned = lax.all_to_all(
        tangent_out.astype(jnp.bfloat16), "expert", split_axis=0, concat_axis=0, tiled=True
    )
    results = (returned, reduced_hidden) + tuple(pieces)
    returned = results[0]
    reduced_hidden = results[1]
    hidden_rows = results[2]
    weight_rows = results[3]
    route_tangent = returned.reshape(experts * slot_most, model_width)[slot_index]
    out_tangent = jnp.sum(
        route_tangent.reshape(tok_rows, top_count, model_width).astype(jnp.float32), axis=1
    )
    resid_tangent = (curvature[:, None] * out_tangent).astype(jnp.bfloat16)
    send_tangent = spread(resid_tangent)
    residual_rows, tangent_rows = (
        lax.all_to_all(send_residual, "expert", split_axis=0, concat_axis=0, tiled=True),
        lax.all_to_all(send_tangent, "expert", split_axis=0, concat_axis=0, tiled=True),
    )
    residual_full = residual_rows.astype(jnp.float32)
    complete_tangent = tangent_rows.astype(jnp.float32)
    weight_column = weight_rows.astype(jnp.float32)[..., None]
    residual_reduced = jnp.einsum(
        "wyov,yqv->wyoq", residual_full, up_stacked, precision=finest_precision
    )
    reduced_tangent = jnp.einsum(
        "wyov,yqv->wyoq", complete_tangent, adapter_up, precision=finest_precision
    )
    left_terms = jnp.concatenate(
        [
            weight_column * residual_reduced[..., :adapter_rank],
            weight_column * (reduced_tangent + residual_reduced[..., adapter_rank:]),
        ],
        axis=3,
    )
    down_terms = jnp.einsum(
        "cjif,cjik->jfk", hidden_rows.astype(jnp.float32), left_terms, precision=finest_precision
    )
    raised_update = weight_column * reduced_hidden[..., :adapter_rank]
    raised_tangent_update = weight_column * reduced_hidden[..., adapter_rank:]
    up_terms = jnp.einsum(
        "cjik,cjid->jkd",
        jnp.concatenate([raised_update, raised_tangent_update], axis=3),
        residual_full,
        precision=finest_precision,
    )
    curvature_piece = up_terms[:, adapter_rank:] + jnp.einsum(
        "cjik,cjid->jkd", raised_update, complete_tangent, precision=finest_precision
    )
    return (
        down_terms[..., :adapter_rank],
        up_terms[:, :adapter_rank],
        down_terms[..., adapter_rank:],
        curvature_piece,
    )


def local(*arguments):
    factor_bytes = 2 * 4 * (arguments[6].size + arguments[7].size) * lax.axis_size("expert")
    fits = lax.axis_size("expert") == 16 and 4 * factor_bytes <= kernel_vmem
    plan = gathered_plan if fits else routed_plan
    return plan(*arguments)


def solution(mesh):
    return jax.shard_map(
        local,
        mesh=mesh,
        in_specs=(
            P(("groups", "expert"), None, None),
            P(("groups", "expert"), None),
            P(("groups", "expert"), None),
            P("groups"),
            P(("groups", "expert"), None),
            P(("groups", "expert")),
            P("expert", None, None),
            P("expert", None, None),
            P(("groups", "expert"), None, None),
            P(("groups", "expert"), None, None),
        ),
        out_specs=(
            P(("groups", "expert"), None, None),
            P(("groups", "expert"), None, None),
            P(("groups", "expert"), None, None),
            P(("groups", "expert"), None, None),
        ),
        check_vma=False,
    )
```

```python
import functools

import jax
import jax.numpy as jnp
from jax import lax
from jax.experimental import pallas as pl
from jax.experimental.pallas import tpu as pltpu
from jax.sharding import PartitionSpec as P

adapter_scale = 2.0
f32 = jnp.float32
bf16 = jnp.bfloat16
i16 = jnp.int16
lanes = 128
counts_lane = 64
kernel_vmem = 32 * 2**20
whole_vmem = 60 * 2**20


def halves(value):
    high = value.astype(bf16)
    return high, (value - high.astype(f32)).astype(bf16)


def dot(a, b, a_dim, b_dim):
    return lax.dot_general(a, b, (((a_dim,), (b_dim,)), ((), ())), preferred_element_type=f32)


def dot_pairs(a, b, a_dim, b_dim):
    return dot(a[0], b[0], a_dim, b_dim) + (dot(a[1], b[0], a_dim, b_dim) + dot(a[0], b[1], a_dim, b_dim))


def encode(down, up, counts=0.0):
    def scaled(value):
        largest = jnp.max(jnp.abs(value), axis=-1, keepdims=True)
        exponent = jnp.ceil(jnp.log2(jnp.maximum(largest, 1e-30)))
        coded = jnp.round(value * jnp.exp2(15.0 - exponent))
        return jnp.clip(coded, -32767.0, 32767.0), exponent

    down, down_exponent = scaled(down)
    up, up_exponent = scaled(up)
    lane = lax.broadcasted_iota(jnp.int32, down.shape[:-1] + (lanes,), down.ndim - 1)
    tail = jnp.where(lane < counts_lane // 2, down_exponent, up_exponent)
    tail = jnp.where(lane < counts_lane, tail, counts)
    return jnp.concatenate([down, up, tail], axis=-1).astype(jnp.int32).astype(i16)


def decode(coded, hidden_width):
    width = coded.shape[-1] - lanes
    value = coded.astype(jnp.int32).astype(f32)
    down_scale = jnp.exp2(value[..., width : width + 1] - 15.0)
    up_scale = jnp.exp2(value[..., width + counts_lane // 2 : width + counts_lane // 2 + 1] - 15.0)
    return value[..., :hidden_width] * down_scale, value[..., hidden_width:width] * up_scale


def prepare_kernel(experts, *refs):
    (piece_ref, small_ref), sem, refs = refs[7:9], refs[-1], refs[:7] + refs[9:-1]
    copies = [pltpu.make_async_copy(refs[i], refs[7 + i], sem.at[i]) for i in range(7)]
    for copy in copies:
        copy.start()
    for copy in copies:
        copy.wait()
    expert, gate, curvature, down_direction, adapter_down, adapter_up, up_direction = [ref[...] for ref in refs[7:]]
    top = expert.shape[0]
    small_ref[...] = jnp.zeros_like(small_ref)
    small_ref[:top] = expert.astype(f32)
    small_ref[top : 2 * top] = gate.astype(f32)
    small_ref[2 * top : 2 * top + 1] = curvature
    lane = lax.broadcasted_iota(jnp.int32, (1, lanes), 1)
    counts = jnp.zeros((1, lanes), f32)
    for number in range(experts):
        named = jnp.where(expert == number, 1.0, 0.0)
        total = jnp.sum(jnp.sum(named, axis=0, keepdims=True), axis=1, keepdims=True)
        counts = jnp.where(lane == counts_lane + number, total, counts)
    piece_ref[0] = encode(down_direction, adapter_up, counts)
    piece_ref[1] = encode(adapter_down, up_direction, counts)


def token_columns(small_ref, top):
    experts = [small_ref[:, k : k + 1] for k in range(top)]
    gates = [small_ref[:, top + k : top + k + 1] for k in range(top)]
    return experts, gates, small_ref[:, 2 * top : 2 * top + 1]


def members(place_ref, wide, first, count, dim=1):
    shape = (1, wide) if dim == 1 else (wide, 1)
    piece_of = lax.broadcasted_iota(jnp.int32, shape, dim) // (wide // count)
    found = jnp.zeros(shape, jnp.int32)
    for number in range(count):
        found = jnp.where(piece_of == number, place_ref[1 + first + number], found)
    return found.astype(f32)


def prior_kernel(place_ref, *rest):
    piece_refs, prior_ref = rest[:-1], rest[-1]
    me = place_ref[0]
    prior_ref[...] = jnp.zeros_like(prior_ref)
    for block, number in enumerate((me, me ^ 1)):
        total = jnp.zeros((1, lanes), f32)
        for arrival, piece_ref in enumerate(piece_refs):
            tail = piece_ref[0, :, piece_ref.shape[2] - lanes :]
            counts = tail.astype(jnp.int32).astype(f32)[0:1]
            total = total + jnp.where(place_ref[1 + arrival] < number, counts, 0.0)
        prior_ref[block : block + 1] = total


def piece_part(refs, arrival, kind, halved):
    if halved and arrival == len(refs) - 2:
        return refs[arrival + kind][0]
    return refs[arrival][kind]


def tokens_kernel(top, slots, place_ref, own_ref, other_ref, hidden_other_ref, gradient_other_ref, *outs):
    small_ref, rank_ref, gate_ref, same_ref, mask_ref, hidden_ref, gradient_ref, sem = outs
    copies = [
        pltpu.make_async_copy(hidden_other_ref, hidden_ref, sem.at[0]),
        pltpu.make_async_copy(gradient_other_ref, gradient_ref, sem.at[1]),
    ]
    for copy in copies:
        copy.start()
    small_ref[...] = jnp.concatenate([own_ref[...], other_ref[...]], axis=1).T
    experts, gates, _ = token_columns(small_ref, top)
    _, tokens, wide = rank_ref.shape
    column = members(place_ref, wide, slots, slots)
    below = (
        lax.broadcasted_iota(jnp.int32, (tokens, tokens), 0)
        > lax.broadcasted_iota(jnp.int32, (tokens, tokens), 1)
    )
    below = jnp.where(below, 1.0, 0.0).astype(bf16)
    rows = same_ref.shape[0]
    row = lax.broadcasted_iota(jnp.int32, (rows, tokens), 0)
    same = jnp.where(row // top == lax.broadcasted_iota(jnp.int32, (rows, tokens), 1), 1.0, 0.0).astype(bf16)
    same_ref[...] = same
    for core in range(2):
        tokens_of = slice(core * tokens, (core + 1) * tokens)
        gate = jnp.zeros((tokens, wide), f32)
        member = jnp.zeros((tokens, wide), f32)
        for k in range(top):
            named = experts[k][tokens_of] == column
            gate = jnp.where(named, gates[k][tokens_of], gate)
            member = jnp.where(named, 1.0, member)
        gate_ref[core] = gate
        rank_ref[core] = dot(below, member.astype(bf16), 1, 0)
        named = dot(same, small_ref[tokens_of].astype(bf16), 1, 0)
        position = lax.broadcasted_iota(jnp.int32, named.shape, 0) % top
        own = lax.broadcasted_iota(jnp.int32, named.shape, 1) == position
        expert = jnp.sum(jnp.where(own, named, 0.0), axis=1, keepdims=True)
        mask_ref[core] = jnp.where(expert == column, 1.0, 0.0).astype(bf16)
    for copy in copies:
        copy.wait()


def pass_kernel(behind_ref, ahead_ref, behind_out_ref, ahead_out_ref):
    behind_out_ref[...] = behind_ref[...]
    ahead_out_ref[...] = ahead_ref[...]


def reduce_kernel(top, first, count, halved, place_ref, small_ref, own_ref, other_ref, *rest):
    piece_refs, (reduced_ref, full_ref) = rest[:-2], rest[-2:]
    hidden_width = own_ref.shape[1]
    downs = [
        decode(piece_part(piece_refs, arrival, kind, halved), hidden_width)[0]
        for kind in range(2)
        for arrival in range(count)
    ]
    factor = jnp.concatenate(halves(jnp.concatenate(downs, axis=0)), axis=0)
    experts, _, _ = token_columns(small_ref, top)
    wide = reduced_ref.shape[1]
    column = members(place_ref, wide // 2, first, count)
    column = jnp.concatenate([column, column], axis=1)
    tokens = own_ref.shape[0] // top
    for core, hidden_ref in enumerate((own_ref, other_ref)):
        full = dot(hidden_ref[...], factor, 1, 1)
        full_ref[...] = full[:, :wide] + full[:, wide:]
        tokens_of = slice(core * tokens, (core + 1) * tokens)
        total = jnp.zeros((tokens, wide), f32)
        for k in range(top):
            here = full_ref[pl.ds(k, tokens, stride=top), :]
            total = jnp.where(experts[k][tokens_of] == column, here, total)
        reduced_ref[tokens_of] = total


def rank_limits(place_ref, wide, slots, capacity_ref, prior_ref, arrived_ref):
    lane = lax.broadcasted_iota(jnp.int32, (1, lanes), 1)
    piece_of = lax.broadcasted_iota(jnp.int32, (1, wide), 1) // (wide // slots)
    limits = []
    for block in range(2):
        total = capacity_ref[...] - prior_ref[block : block + 1] - arrived_ref[1 - block : 2 - block]
        limit = jnp.zeros((1, wide), f32)
        for slot in range(slots):
            picked = jnp.where(lane == counts_lane + place_ref[1 + slots + slot], total, 0.0)
            limit = jnp.where(piece_of == slot, jnp.sum(picked, axis=1, keepdims=True), limit)
        limits.append(limit)
    return limits


def tangent_kernel(
    slots, place_ref, rank_ref, gate_ref, capacity_ref, prior_ref, arrived_ref, early_ref, late_ref, *rest
):
    piece_refs = rest[: slots + 1]
    weight_ref, weighted_ref, tangent_ref, coded_ref, high_ref, low_ref = rest[slots + 1 :]
    _, wide = weight_ref.shape
    model_width = tangent_ref.shape[1]
    hidden_width = piece_refs[0].shape[2] - model_width - lanes
    limits = rank_limits(place_ref, wide, slots, capacity_ref, prior_ref, arrived_ref)
    weights = [
        jnp.where(rank_ref[core] < limits[core], adapter_scale * gate_ref[core], 0.0) for core in range(2)
    ]
    weight = jnp.concatenate(weights, axis=0)
    weight_ref[...] = weight
    half = wide // 2
    reduced = [
        jnp.concatenate([ref[:, kind * half : (kind + 1) * half] for ref in (early_ref, late_ref)], axis=1)
        for kind in range(2)
    ]
    rank = wide // slots
    by_arrival = members(place_ref, wide, 0, slots, 0) == members(place_ref, wide, slots, slots)
    row = lax.broadcasted_iota(jnp.int32, (wide, wide), 0)
    same_index = row % rank == lax.broadcasted_iota(jnp.int32, (wide, wide), 1) % rank
    order = jnp.where(by_arrival & same_index, 1.0, 0.0).astype(bf16)
    reduced = [sum(dot(part, order, 1, 0) for part in halves(both)) for both in reduced]
    weighted = jnp.concatenate([weight * part for part in reduced], axis=1)
    weighted_ref[...] = weighted
    for arrival in range(slots):
        for kind in range(2):
            _, up = decode(piece_part(piece_refs, arrival, kind, True), hidden_width)
            slot = place_ref[1 + 2 * slots + arrival]
            high_ref[kind, slot], low_ref[kind, slot] = halves(up)
    factor = high_ref[...].reshape(2 * wide, model_width), low_ref[...].reshape(2 * wide, model_width)
    tangent = dot_pairs(halves(weighted), factor, 1, 0)
    tangent_ref[...] = tangent
    coded_ref[...] = tangent.astype(bf16)


def put_left(left_ref, same_ref, mask_ref, terms):
    both = jnp.concatenate(halves(terms), axis=1)
    tokens = terms.shape[0] // 2
    for core in range(2):
        repeated = dot(same_ref[...], both[core * tokens : (core + 1) * tokens], 1, 0).astype(bf16)
        mask = mask_ref[core]
        left_ref[core] = repeated * jnp.concatenate([mask, mask], axis=1)


def add_halves(both):
    middle = both.shape[0] // 2
    return both[:middle] + both[middle:]


def put_chunks(keep_ref, near_ref, chunk_ref, far_ref, down, up):
    rank = keep_ref.shape[1]
    rows = down.shape[0] // rank // 2

    def slot(number):
        start = number * rank
        return down[start : start + rank], up[start : start + rank]

    for place in range(2):
        keep_ref[place] = jnp.concatenate(slot(place), axis=1)
        near_ref[place] = encode(*slot(rows + place))
        chunk_ref[place] = jnp.concatenate(slot(place * rows + 2), axis=1)
        far_ref[place] = encode(*slot(place * rows + 3))


def gradient_kernel(
    same_ref,
    mask_ref,
    own_ref,
    other_ref,
    own_gradient_ref,
    other_gradient_ref,
    weight_ref,
    weighted_ref,
    high_ref,
    low_ref,
    keep_ref,
    near_ref,
    chunk_ref,
    far_ref,
    up_ref,
    to_ref,
    left_ref,
):
    wide = weight_ref.shape[1]
    model_width = up_ref.shape[1]
    gradient = jnp.concatenate([own_gradient_ref[...], other_gradient_ref[...]], axis=0)
    high = high_ref[...].reshape(2 * wide, model_width)
    low = low_ref[...].reshape(2 * wide, model_width)
    to_both = dot(gradient, high, 1, 1) + dot(gradient, low, 1, 1)
    to_ref[...] = to_both[:, wide:]
    put_left(left_ref, same_ref, mask_ref, weight_ref[...] * to_both[:, :wide])
    down = dot(left_ref[0], own_ref[...], 0, 0) + dot(left_ref[1], other_ref[...], 0, 0)
    up = add_halves(dot(jnp.concatenate(halves(weighted_ref[...]), axis=1), gradient, 0, 0))
    up_ref[...] = up[:wide]
    put_chunks(keep_ref, near_ref, chunk_ref, far_ref, add_halves(down), up[wide:])


def curvature_kernel(
    top,
    small_ref,
    same_ref,
    mask_ref,
    own_ref,
    other_ref,
    weight_ref,
    weighted_ref,
    high_ref,
    low_ref,
    up_ref,
    to_ref,
    tangent_ref,
    arrived_ref,
    keep_ref,
    near_ref,
    chunk_ref,
    far_ref,
    left_ref,
):
    _, _, curvature = token_columns(small_ref, top)
    tokens, wide = weight_ref.shape
    block = tokens // 2
    model_width = up_ref.shape[1]
    arrived = jnp.concatenate([arrived_ref[block:], arrived_ref[:block]], axis=0).astype(f32)
    resid = halves(curvature * (tangent_ref[...] + arrived))
    adapter_up = high_ref[0].reshape(wide, model_width), low_ref[0].reshape(wide, model_width)
    terms = weight_ref[...] * (dot_pairs(resid, adapter_up, 1, 1) + to_ref[...])
    put_left(left_ref, same_ref, mask_ref, terms)
    down = dot(left_ref[0], own_ref[...], 0, 0) + dot(left_ref[1], other_ref[...], 0, 0)
    weighted_u = halves(weighted_ref[:, wide:])
    up = add_halves(dot(jnp.concatenate(weighted_u, axis=1), resid[0], 0, 0)) + dot(weighted_u[0], resid[1], 0, 0)
    put_chunks(keep_ref, near_ref, chunk_ref, far_ref, add_halves(down), up_ref[...] + up)


def pair_kernel(hidden_width, arrived_ref, chunk_ref, near_ref, across_ref, keep_ref, onward_ref):
    onward_ref[...] = near_ref[...]
    for x in range(2):
        down, up = decode(arrived_ref[x], hidden_width)
        down, up = chunk_ref[x, :, :hidden_width] + down, chunk_ref[x, :, hidden_width:] + up
        if x == 0:
            keep_ref[...] = jnp.concatenate([down, up], axis=1)
        else:
            across_ref[...] = encode(down, up)


def far_kernel(hidden_width, arrived_ref, keep_ref, out_ref):
    down, up = decode(arrived_ref[...], hidden_width)
    out_ref[...] = encode(keep_ref[:, :hidden_width] + down, keep_ref[:, hidden_width:] + up)


def near_kernel(
    hidden_width, gradient_ref, curvature_ref, gradient_keep_ref, curvature_keep_ref, onward_ref, total_ref
):
    pairs = ((gradient_ref, gradient_keep_ref), (curvature_ref, curvature_keep_ref))
    for kind, (arrived_ref, keep_ref) in enumerate(pairs):
        for z in range(2):
            down, up = decode(arrived_ref[z], hidden_width)
            down, up = keep_ref[z, :, :hidden_width] + down, keep_ref[z, :, hidden_width:] + up
            if z == 0:
                total_ref[kind] = jnp.concatenate([down, up], axis=1)
            else:
                onward_ref[kind] = encode(down, up)


def add_kernel(hidden_width, total_ref, arrived_ref, out_ref):
    down, up = decode(arrived_ref[...], hidden_width)
    out_ref[:, :hidden_width] = total_ref[0, :, :hidden_width] + down
    out_ref[:, hidden_width:] = total_ref[0, :, hidden_width:] + up


def total_kernel(hidden_width, gradient_ref, total_ref, far_ref, pair_ref, *out_refs):
    far = decode(far_ref[...], hidden_width)
    totals = [
        (gradient_ref[:, :hidden_width], gradient_ref[:, hidden_width:]),
        (total_ref[1, :, :hidden_width] + far[0], total_ref[1, :, hidden_width:] + far[1]),
    ]
    for kind in range(2):
        down, up = decode(pair_ref[kind], hidden_width)
        out_refs[2 * kind][...] = totals[kind][0] + down
        out_refs[2 * kind + 1][...] = totals[kind][1] + up


class Ring:
    def __init__(self, size):
        self.length = size // 2
        rows = self.length // 2
        self.order = [4 * z for z in range(rows)] + [4 * z + 2 for z in reversed(range(rows))]

    def shift(self, value, step):
        pairs = [
            (chip + core, self.order[(place + step) % self.length] + core)
            for place, chip in enumerate(self.order)
            for core in range(2)
        ]
        return lax.ppermute(value, "expert", pairs)

    def members(self, me):
        rows = self.length // 2
        place = jnp.where(me // 2 % 2 == 0, me // 4, self.length - 1 - me // 4)
        half = self.length // 2
        offsets = [0] + [offset for step in range(1, half) for offset in (self.length - step, step)] + [half]
        there = (place + jnp.array(offsets, jnp.int32)) % self.length
        return jnp.where(there < rows, 4 * there, 4 * (self.length - 1 - there) + 2) + me % 2

    def gather(self, own, passing):
        half = self.length // 2
        pieces = [own]
        ahead, behind = own, own
        for step in range(1, half):
            behind = self.shift(behind, 1)
            ahead = self.shift(ahead, -1)
            if step == 2:
                behind, ahead = passing(behind, ahead)
            pieces += [behind, ahead]
        pieces += [self.shift(behind[:1], 1), self.shift(ahead[1:], -1)]
        return pieces


def exchange(value, mask):
    size = lax.axis_size("expert")
    return lax.ppermute(value, "expert", [(device, device ^ mask) for device in range(size)])


def gathered_plan(
    hidden_of_route,
    expert_of_route,
    gate_of_route,
    capacity,
    output_gradient,
    curvature,
    adapter_down,
    adapter_up,
    down_direction,
    up_direction,
):
    ring = Ring(lax.axis_size("expert"))
    slots = ring.length
    rows = slots // 2
    masks = [4 * z for z in range(rows)] + [4 * z + 2 for z in range(rows)]
    me = lax.axis_index("expert")
    tokens, top = expert_of_route.shape
    both = 2 * tokens
    hidden_width = hidden_of_route.shape[2]
    rank = adapter_down.shape[2]
    model_width = output_gradient.shape[1]
    experts = capacity.shape[0]
    wide = slots * rank
    coded_width = hidden_width + model_width + lanes


    place = []

    def call(kernel, multiplies, outs, *operands, scratch=(), after=(), grant=kernel_vmem):
        space = pltpu.VMEM if grant == kernel_vmem else pltpu.HBM
        places = [pl.BlockSpec(memory_space=pl.ANY) for _ in after] + [
            pl.BlockSpec(memory_space=pltpu.SMEM if any(operand is it for it in place) else space) for operand in operands
        ]
        return pl.pallas_call(
            lambda *refs: kernel(*refs[len(after) :]),
            out_shape=[jax.ShapeDtypeStruct(shape, dtype) for shape, dtype in outs],
            in_specs=places,
            scratch_shapes=scratch,
            compiler_params=pltpu.CompilerParams(vmem_limit_bytes=grant),
            cost_estimate=pl.CostEstimate(flops=2 * multiplies, bytes_accessed=2**20, transcendentals=0),
        )(*after, *operands)

    down_multiplies = 2 * top * both * hidden_width * wide
    up_multiplies = both * model_width * wide

    first = (
        expert_of_route.T,
        gate_of_route.T,
        curvature[None],
        down_direction[0].T,
        adapter_down[0].T,
        adapter_up[0],
        up_direction[0],
    )
    piece, small = call(
        functools.partial(prepare_kernel, experts),
        10**8,
        [((2, rank, coded_width), i16), (((2 * top + 8) // 8 * 8, tokens), f32)],
        *first,
        scratch=[pltpu.VMEM(operand.shape, operand.dtype) for operand in first]
        + [pltpu.SemaphoreType.DMA((len(first),))],
        grant=whole_vmem,
    )
    arrivals = ring.members(me)
    slot_of_arrival = (arrivals ^ me) // 4 + rows * ((arrivals ^ me) // 2 % 2)
    place.append(jnp.concatenate([me[None], arrivals, me ^ jnp.array(masks, jnp.int32), slot_of_arrival]).astype(jnp.int32))
    small_other = exchange(small, 1)
    hidden = hidden_of_route.reshape(tokens * top, hidden_width)
    small_columns, local_rank, gate, same, mask, hidden_other, gradient_other = call(
        functools.partial(tokens_kernel, top, slots),
        10**9,
        [
            ((both, small.shape[0]), f32),
            ((2, tokens, wide), f32),
            ((2, tokens, wide), f32),
            ((top * tokens, tokens), bf16),
            ((2, top * tokens, wide), bf16),
            (hidden.shape, bf16),
            (output_gradient.shape, bf16),
        ],
        *place,
        small,
        small_other,
        exchange(hidden, 1),
        exchange(output_gradient, 1),
        scratch=[pltpu.SemaphoreType.DMA((2,))],
    )
    def passing(behind, ahead):
        return call(pass_kernel, 10**8, [(piece.shape, i16)] * 2, behind, ahead, after=[same])

    pieces = ring.gather(piece, passing)
    capacity_row = jnp.pad(capacity.astype(f32), (counts_lane, lanes - counts_lane - experts))[None, :]

    def reduced(first, count, halved, *parts, after=()):
        return call(
            functools.partial(reduce_kernel, top, first, count, halved),
            2 * down_multiplies * count // slots,
            [((both, 2 * count * rank), f32)],
            *place,
            small_columns,
            hidden,
            hidden_other,
            *parts,
            scratch=[pltpu.VMEM((tokens * top, 2 * count * rank), f32)],
            after=after,
        )[0]

    early = slots // 2
    reduced_early = reduced(0, early, False, *pieces[:early])
    (prior,) = call(prior_kernel, 10**8, [((8, lanes), f32)], *place, *pieces[:-1], after=[reduced_early])
    prior_arrived = exchange(prior, 1)
    reduced_late = reduced(early, slots - early, True, *pieces[early:], after=[prior])
    weight, weighted, tangent, coded, high, low = call(
        functools.partial(tangent_kernel, slots),
        6 * up_multiplies,
        [
            ((both, wide), f32),
            ((both, 2 * wide), f32),
            ((both, model_width), f32),
            ((both, model_width), bf16),
            ((2, slots, rank, model_width), bf16),
            ((2, slots, rank, model_width), bf16),
        ],
        *place,
        local_rank,
        gate,
        capacity_row,
        prior,
        prior_arrived,
        reduced_early,
        reduced_late,
        *pieces,
    )
    arrived = exchange(coded, 1)
    left = [pltpu.VMEM((2, top * tokens, 2 * wide), bf16)]
    chunks = [((2, rank, hidden_width + model_width), f32), ((2, rank, coded_width), i16)] * 2
    gradient_keep, gradient_near, gradient_chunk, gradient_far, up, to = call(
        gradient_kernel,
        down_multiplies + 8 * up_multiplies,
        chunks + [((wide, model_width), f32), ((both, wide), f32)],
        same,
        mask,
        hidden,
        hidden_other,
        output_gradient,
        gradient_other,
        weight,
        weighted,
        high,
        low,
        scratch=left,
    )
    gradient_far = exchange(gradient_far, 4)
    gradient_near = exchange(gradient_near, 2)
    curvature_keep, curvature_near, curvature_chunk, curvature_far = call(
        functools.partial(curvature_kernel, top),
        down_multiplies + 6 * up_multiplies,
        chunks,
        small_columns,
        same,
        mask,
        hidden,
        hidden_other,
        weight,
        weighted,
        high,
        low,
        up,
        to,
        tangent,
        arrived,
        scratch=left,
    )

    hop = 2 * 10**9

    one = (rank, hidden_width + model_width)
    one_coded = (rank, coded_width)

    def hop_call(kernel, outs, *operands, after=()):
        return call(functools.partial(kernel, hidden_width), hop, outs, *operands, after=after)

    curvature_far = exchange(curvature_far, 4)
    pair = [(one_coded, i16), (one, f32), ((2,) + one_coded, i16)]
    gradient_across, gradient_pair, curvature_near = hop_call(
        pair_kernel, pair, gradient_far, gradient_chunk, curvature_near, after=[curvature_keep]
    )
    curvature_near = exchange(curvature_near, 2)
    curvature_across, curvature_pair, gradient_near = hop_call(
        pair_kernel, pair, curvature_far, curvature_chunk, gradient_near, after=[gradient_across]
    )
    (gradient_beyond,) = hop_call(
        far_kernel,
        [(one_coded, i16)],
        exchange(gradient_across, 2),
        gradient_pair,
        after=[curvature_across],
    )
    onward, total = hop_call(
        near_kernel,
        [((2,) + one_coded, i16), ((2,) + one, f32)],
        gradient_near,
        curvature_near,
        gradient_keep,
        curvature_keep,
        after=[gradient_beyond],
    )
    (curvature_beyond,) = hop_call(
        far_kernel, [(one_coded, i16)], exchange(curvature_across, 2), curvature_pair, after=[onward]
    )
    (gradient_total,) = hop_call(
        add_kernel, [(one, f32)], total, exchange(gradient_beyond, 8), after=[curvature_beyond]
    )
    down_gradient, up_gradient, curvature_down, curvature_up = hop_call(
        total_kernel,
        [((rank, hidden_width), f32), ((rank, model_width), f32)] * 2,
        gradient_total,
        total,
        exchange(curvature_beyond, 8),
        exchange(onward, 4),
    )
    return down_gradient.T[None], up_gradient[None], curvature_down.T[None], curvature_up[None]


def carried_in(value, axis, join, neutral):
    count, mine = (lax.axis_size(axis), lax.axis_index(axis))
    pieces = lax.all_gather(value, axis)
    so_far = jnp.full_like(value, 0) + jnp.asarray(neutral, value.dtype)

    def lap(position, so_far):
        longer = join(so_far, pieces[position])
        return jnp.where(position < mine, longer, so_far)

    return lax.fori_loop(0, count - 1, lap, so_far)


def add_counts(earlier, later):
    return earlier + later


def routed_plan(
    hidden_of_route,
    expert_of_route,
    gate_of_route,
    capacity,
    output_gradient,
    curvature,
    adapter_down,
    adapter_up,
    down_direction,
    up_direction,
):
    finest_precision = lax.Precision.HIGHEST
    group_size = lax.axis_size("expert")
    tok_rows, top_count = expert_of_route.shape
    hidden_width = hidden_of_route.shape[2]
    resident_experts = adapter_down.shape[0]
    adapter_rank = adapter_down.shape[2]
    model_width = output_gradient.shape[1]
    experts = resident_experts * group_size
    slot_most = 2 * tok_rows * top_count // experts
    routes = expert_of_route.reshape(-1)
    onehot = (routes[:, None] == jnp.arange(experts, dtype=jnp.int32)[None, :]).astype(jnp.int32)
    earlier = jnp.cumsum(onehot, axis=0) - onehot
    local_rank = jnp.sum(earlier * onehot, axis=1)
    counts = jnp.sum(onehot, axis=0)
    prior_count = carried_in(counts, "expert", add_counts, jnp.zeros_like(counts))
    global_rank = local_rank + jnp.sum(onehot * prior_count[None, :], axis=1)
    route_limit = jnp.sum(onehot * capacity[None, :], axis=1)
    retained_mask = (global_rank < route_limit).astype(jnp.float32)
    weight_of_route = (
        adapter_scale * gate_of_route.reshape(-1).astype(jnp.float32) * retained_mask
    ).astype(jnp.bfloat16)
    slot_index = routes * slot_most + local_rank
    layout = (group_size, resident_experts, slot_most)
    send_hidden = (
        jnp.zeros((experts * slot_most, hidden_width), jnp.bfloat16)
        .at[slot_index]
        .set(hidden_of_route.reshape(-1, hidden_width))
        .reshape(layout + (hidden_width,))
    )
    send_weight = (
        jnp.zeros((experts * slot_most,), jnp.bfloat16)
        .at[slot_index]
        .set(weight_of_route)
        .reshape(layout)
    )
    down_stacked = jnp.concatenate([adapter_down, down_direction], axis=2)
    up_stacked = jnp.concatenate([adapter_up, up_direction], axis=1)

    def spread(token_rows):
        per_route = jnp.repeat(token_rows, top_count, axis=0)
        placed = (
            jnp.zeros((experts * slot_most, model_width), jnp.bfloat16)
            .at[slot_index]
            .set(per_route)
        )
        return placed.reshape(layout + (model_width,))

    send_residual = spread(output_gradient)
    pieces = (
        lax.all_to_all(send_hidden, "expert", split_axis=0, concat_axis=0, tiled=True),
        lax.all_to_all(send_weight, "expert", split_axis=0, concat_axis=0, tiled=True),
    )
    hidden_rows = pieces[0].astype(jnp.float32)
    weight_rows = pieces[1].astype(jnp.float32)[..., None]
    reduced_hidden = jnp.einsum(
        "cjif,jfk->cjik", hidden_rows, down_stacked, precision=finest_precision
    )
    exchanged_rows = jnp.concatenate(
        [reduced_hidden[..., adapter_rank:], reduced_hidden[..., :adapter_rank]], axis=3
    )
    tangent_out = weight_rows * jnp.einsum(
        "cjik,jkd->cjid", exchanged_rows, up_stacked, precision=finest_precision
    )
    returned = lax.all_to_all(
        tangent_out.astype(jnp.bfloat16), "expert", split_axis=0, concat_axis=0, tiled=True
    )
    results = (returned, reduced_hidden) + tuple(pieces)
    returned = results[0]
    reduced_hidden = results[1]
    hidden_rows = results[2]
    weight_rows = results[3]
    route_tangent = returned.reshape(experts * slot_most, model_width)[slot_index]
    out_tangent = jnp.sum(
        route_tangent.reshape(tok_rows, top_count, model_width).astype(jnp.float32), axis=1
    )
    resid_tangent = (curvature[:, None] * out_tangent).astype(jnp.bfloat16)
    send_tangent = spread(resid_tangent)
    residual_rows, tangent_rows = (
        lax.all_to_all(send_residual, "expert", split_axis=0, concat_axis=0, tiled=True),
        lax.all_to_all(send_tangent, "expert", split_axis=0, concat_axis=0, tiled=True),
    )
    residual_full = residual_rows.astype(jnp.float32)
    complete_tangent = tangent_rows.astype(jnp.float32)
    weight_column = weight_rows.astype(jnp.float32)[..., None]
    residual_reduced = jnp.einsum(
        "wyov,yqv->wyoq", residual_full, up_stacked, precision=finest_precision
    )
    reduced_tangent = jnp.einsum(
        "wyov,yqv->wyoq", complete_tangent, adapter_up, precision=finest_precision
    )
    left_terms = jnp.concatenate(
        [
            weight_column * residual_reduced[..., :adapter_rank],
            weight_column * (reduced_tangent + residual_reduced[..., adapter_rank:]),
        ],
        axis=3,
    )
    down_terms = jnp.einsum(
        "cjif,cjik->jfk", hidden_rows.astype(jnp.float32), left_terms, precision=finest_precision
    )
    raised_update = weight_column * reduced_hidden[..., :adapter_rank]
    raised_tangent_update = weight_column * reduced_hidden[..., adapter_rank:]
    up_terms = jnp.einsum(
        "cjik,cjid->jkd",
        jnp.concatenate([raised_update, raised_tangent_update], axis=3),
        residual_full,
        precision=finest_precision,
    )
    curvature_piece = up_terms[:, adapter_rank:] + jnp.einsum(
        "cjik,cjid->jkd", raised_update, complete_tangent, precision=finest_precision
    )
    return (
        down_terms[..., :adapter_rank],
        up_terms[:, :adapter_rank],
        down_terms[..., adapter_rank:],
        curvature_piece,
    )


def local(*arguments):
    factor_bytes = 2 * 4 * (arguments[6].size + arguments[7].size) * lax.axis_size("expert")
    fits = lax.axis_size("expert") == 16 and 4 * factor_bytes <= kernel_vmem
    plan = gathered_plan if fits else routed_plan
    return plan(*arguments)


def solution(mesh):
    return jax.shard_map(
        local,
        mesh=mesh,
        in_specs=(
            P(("groups", "expert"), None, None),
            P(("groups", "expert"), None),
            P(("groups", "expert"), None),
            P("groups"),
            P(("groups", "expert"), None),
            P(("groups", "expert")),
            P("expert", None, None),
            P("expert", None, None),
            P(("groups", "expert"), None, None),
            P(("groups", "expert"), None, None),
        ),
        out_specs=(
            P(("groups", "expert"), None, None),
            P(("groups", "expert"), None, None),
            P(("groups", "expert"), None, None),
            P(("groups", "expert"), None, None),
        ),
        check_vma=False,
    )
```

```python
import functools

import jax
import jax.numpy as jnp
from jax import lax
from jax.experimental import pallas as pl
from jax.experimental.pallas import tpu as pltpu
from jax.sharding import PartitionSpec as P

adapter_scale = 2.0
f32 = jnp.float32
bf16 = jnp.bfloat16
i16 = jnp.int16
lanes = 128
counts_lane = 64
kernel_vmem = 32 * 2**20
whole_vmem = 60 * 2**20


def halves(value):
    high = value.astype(bf16)
    return high, (value - high.astype(f32)).astype(bf16)


def dot(a, b, a_dim, b_dim):
    return lax.dot_general(a, b, (((a_dim,), (b_dim,)), ((), ())), preferred_element_type=f32)


def dot_pairs(a, b, a_dim, b_dim):
    return dot(a[0], b[0], a_dim, b_dim) + (dot(a[1], b[0], a_dim, b_dim) + dot(a[0], b[1], a_dim, b_dim))


def encode(down, up, counts=0.0):
    def scaled(value):
        largest = jnp.max(jnp.abs(value), axis=-1, keepdims=True)
        exponent = jnp.ceil(jnp.log2(jnp.maximum(largest, 1e-30)))
        coded = jnp.round(value * jnp.exp2(15.0 - exponent))
        return jnp.clip(coded, -32767.0, 32767.0), exponent

    down, down_exponent = scaled(down)
    up, up_exponent = scaled(up)
    lane = lax.broadcasted_iota(jnp.int32, down.shape[:-1] + (lanes,), down.ndim - 1)
    tail = jnp.where(lane < counts_lane // 2, down_exponent, up_exponent)
    tail = jnp.where(lane < counts_lane, tail, counts)
    return jnp.concatenate([down, up, tail], axis=-1).astype(jnp.int32).astype(i16)


def decode(coded, hidden_width):
    width = coded.shape[-1] - lanes
    value = coded.astype(jnp.int32).astype(f32)
    down_scale = jnp.exp2(value[..., width : width + 1] - 15.0)
    up_scale = jnp.exp2(value[..., width + counts_lane // 2 : width + counts_lane // 2 + 1] - 15.0)
    return value[..., :hidden_width] * down_scale, value[..., hidden_width:width] * up_scale


def prepare_kernel(experts, *refs):
    (piece_ref, small_ref), sem, refs = refs[7:9], refs[-1], refs[:7] + refs[9:-1]
    copies = [pltpu.make_async_copy(refs[i], refs[7 + i], sem.at[i]) for i in range(7)]
    for copy in copies:
        copy.start()
    for copy in copies:
        copy.wait()
    expert, gate, curvature, down_direction, adapter_down, adapter_up, up_direction = [ref[...] for ref in refs[7:]]
    top = expert.shape[0]
    small_ref[...] = jnp.zeros_like(small_ref)
    small_ref[:top] = expert.astype(f32)
    small_ref[top : 2 * top] = gate.astype(f32)
    small_ref[2 * top : 2 * top + 1] = curvature
    lane = lax.broadcasted_iota(jnp.int32, (1, lanes), 1)
    counts = jnp.zeros((1, lanes), f32)
    for number in range(experts):
        named = jnp.where(expert == number, 1.0, 0.0)
        total = jnp.sum(jnp.sum(named, axis=0, keepdims=True), axis=1, keepdims=True)
        counts = jnp.where(lane == counts_lane + number, total, counts)
    piece_ref[0] = encode(down_direction, adapter_up, counts)
    piece_ref[1] = encode(adapter_down, up_direction, counts)


def token_columns(small_ref, top):
    experts = [small_ref[:, k : k + 1] for k in range(top)]
    gates = [small_ref[:, top + k : top + k + 1] for k in range(top)]
    return experts, gates, small_ref[:, 2 * top : 2 * top + 1]


def members(place_ref, wide, first, count, dim=1):
    shape = (1, wide) if dim == 1 else (wide, 1)
    piece_of = lax.broadcasted_iota(jnp.int32, shape, dim) // (wide // count)
    found = jnp.zeros(shape, jnp.int32)
    for number in range(count):
        found = jnp.where(piece_of == number, place_ref[1 + first + number], found)
    return found.astype(f32)


def prior_kernel(place_ref, *rest):
    piece_refs, prior_ref = rest[:-1], rest[-1]
    me = place_ref[0]
    prior_ref[...] = jnp.zeros_like(prior_ref)
    for block, number in enumerate((me, me ^ 1)):
        total = jnp.zeros((1, lanes), f32)
        for arrival, piece_ref in enumerate(piece_refs):
            tail = piece_ref[0, :, piece_ref.shape[2] - lanes :]
            counts = tail.astype(jnp.int32).astype(f32)[0:1]
            total = total + jnp.where(place_ref[1 + arrival] < number, counts, 0.0)
        prior_ref[block : block + 1] = total


def piece_part(refs, arrival, kind, halved):
    if halved and arrival == len(refs) - 2:
        return refs[arrival + kind][0]
    return refs[arrival][kind]


def tokens_kernel(top, slots, place_ref, own_ref, other_ref, hidden_other_ref, gradient_other_ref, *outs):
    small_ref, rank_ref, gate_ref, same_ref, mask_ref, hidden_ref, gradient_ref, sem = outs
    copies = [
        pltpu.make_async_copy(hidden_other_ref, hidden_ref, sem.at[0]),
        pltpu.make_async_copy(gradient_other_ref, gradient_ref, sem.at[1]),
    ]
    for copy in copies:
        copy.start()
    small_ref[...] = jnp.concatenate([own_ref[...], other_ref[...]], axis=1).T
    experts, gates, _ = token_columns(small_ref, top)
    _, tokens, wide = rank_ref.shape
    column = members(place_ref, wide, slots, slots)
    below = (
        lax.broadcasted_iota(jnp.int32, (tokens, tokens), 0)
        > lax.broadcasted_iota(jnp.int32, (tokens, tokens), 1)
    )
    below = jnp.where(below, 1.0, 0.0).astype(bf16)
    rows = same_ref.shape[0]
    row = lax.broadcasted_iota(jnp.int32, (rows, tokens), 0)
    same = jnp.where(row // top == lax.broadcasted_iota(jnp.int32, (rows, tokens), 1), 1.0, 0.0).astype(bf16)
    same_ref[...] = same
    for core in range(2):
        tokens_of = slice(core * tokens, (core + 1) * tokens)
        gate = jnp.zeros((tokens, wide), f32)
        member = jnp.zeros((tokens, wide), f32)
        for k in range(top):
            named = experts[k][tokens_of] == column
            gate = jnp.where(named, gates[k][tokens_of], gate)
            member = jnp.where(named, 1.0, member)
        gate_ref[core] = gate
        rank_ref[core] = dot(below, member.astype(bf16), 1, 0)
        named = dot(same, small_ref[tokens_of].astype(bf16), 1, 0)
        position = lax.broadcasted_iota(jnp.int32, named.shape, 0) % top
        own = lax.broadcasted_iota(jnp.int32, named.shape, 1) == position
        expert = jnp.sum(jnp.where(own, named, 0.0), axis=1, keepdims=True)
        mask_ref[core] = jnp.where(expert == column, 1.0, 0.0).astype(bf16)
    for copy in copies:
        copy.wait()


def pass_kernel(behind_ref, ahead_ref, behind_out_ref, ahead_out_ref):
    behind_out_ref[...] = behind_ref[...]
    ahead_out_ref[...] = ahead_ref[...]


def reduce_kernel(top, first, count, halved, place_ref, small_ref, own_ref, other_ref, *rest):
    piece_refs, (reduced_ref, full_ref) = rest[:-2], rest[-2:]
    hidden_width = own_ref.shape[1]
    downs = [
        decode(piece_part(piece_refs, arrival, kind, halved), hidden_width)[0]
        for kind in range(2)
        for arrival in range(count)
    ]
    factor = jnp.concatenate(halves(jnp.concatenate(downs, axis=0)), axis=0)
    experts, _, _ = token_columns(small_ref, top)
    wide = reduced_ref.shape[1]
    column = members(place_ref, wide // 2, first, count)
    column = jnp.concatenate([column, column], axis=1)
    tokens = own_ref.shape[0] // top
    for core, hidden_ref in enumerate((own_ref, other_ref)):
        full = dot(hidden_ref[...], factor, 1, 1)
        full_ref[...] = full[:, :wide] + full[:, wide:]
        tokens_of = slice(core * tokens, (core + 1) * tokens)
        total = jnp.zeros((tokens, wide), f32)
        for k in range(top):
            here = full_ref[pl.ds(k, tokens, stride=top), :]
            total = jnp.where(experts[k][tokens_of] == column, here, total)
        reduced_ref[tokens_of] = total


def rank_limits(place_ref, wide, slots, capacity_ref, prior_ref, arrived_ref):
    lane = lax.broadcasted_iota(jnp.int32, (1, lanes), 1)
    piece_of = lax.broadcasted_iota(jnp.int32, (1, wide), 1) // (wide // slots)
    limits = []
    for block in range(2):
        total = capacity_ref[...] - prior_ref[block : block + 1] - arrived_ref[1 - block : 2 - block]
        limit = jnp.zeros((1, wide), f32)
        for slot in range(slots):
            picked = jnp.where(lane == counts_lane + place_ref[1 + slots + slot], total, 0.0)
            limit = jnp.where(piece_of == slot, jnp.sum(picked, axis=1, keepdims=True), limit)
        limits.append(limit)
    return limits


def unpack_kernel(slots, hidden_width, place_ref, *refs):
    piece_refs, (high_ref, low_ref) = refs[:-2], refs[-2:]
    for arrival in range(slots):
        slot = place_ref[1 + 2 * slots + arrival]
        for kind in range(2):
            if arrival < len(piece_refs):
                _, up = decode(piece_refs[arrival][kind], hidden_width)
                high_ref[kind, slot], low_ref[kind, slot] = halves(up)
            else:
                high_ref[kind, slot] = low_ref[kind, slot] = jnp.zeros(high_ref.shape[2:], bf16)


def tangent_kernel(
    slots,
    place_ref,
    rank_ref,
    gate_ref,
    capacity_ref,
    prior_ref,
    arrived_ref,
    early_ref,
    late_ref,
    most_high_ref,
    most_low_ref,
    *rest,
):
    piece_refs = rest[:2]
    weight_ref, weighted_ref, tangent_ref, coded_ref, high_ref, low_ref = rest[2:]
    _, wide = weight_ref.shape
    model_width = tangent_ref.shape[1]
    hidden_width = piece_refs[0].shape[2] - model_width - lanes
    limits = rank_limits(place_ref, wide, slots, capacity_ref, prior_ref, arrived_ref)
    weights = [
        jnp.where(rank_ref[core] < limits[core], adapter_scale * gate_ref[core], 0.0) for core in range(2)
    ]
    weight = jnp.concatenate(weights, axis=0)
    weight_ref[...] = weight
    half = wide // 2
    reduced = [
        jnp.concatenate([ref[:, kind * half : (kind + 1) * half] for ref in (early_ref, late_ref)], axis=1)
        for kind in range(2)
    ]
    rank = wide // slots
    by_arrival = members(place_ref, wide, 0, slots, 0) == members(place_ref, wide, slots, slots)
    row = lax.broadcasted_iota(jnp.int32, (wide, wide), 0)
    same_index = row % rank == lax.broadcasted_iota(jnp.int32, (wide, wide), 1) % rank
    order = jnp.where(by_arrival & same_index, 1.0, 0.0).astype(bf16)
    reduced = [sum(dot(part, order, 1, 0) for part in halves(both)) for both in reduced]
    weighted = jnp.concatenate([weight * part for part in reduced], axis=1)
    weighted_ref[...] = weighted
    high_ref[...], low_ref[...] = most_high_ref[...], most_low_ref[...]
    slot = place_ref[3 * slots]
    for kind, piece_ref in enumerate(piece_refs):
        _, up = decode(piece_ref[0], hidden_width)
        high_ref[kind, slot], low_ref[kind, slot] = halves(up)
    factor = high_ref[...].reshape(2 * wide, model_width), low_ref[...].reshape(2 * wide, model_width)
    tangent = dot_pairs(halves(weighted), factor, 1, 0)
    tangent_ref[...] = tangent
    coded_ref[...] = tangent.astype(bf16)


def put_left(left_ref, same_ref, mask_ref, terms):
    both = jnp.concatenate(halves(terms), axis=1)
    tokens = terms.shape[0] // 2
    for core in range(2):
        repeated = dot(same_ref[...], both[core * tokens : (core + 1) * tokens], 1, 0).astype(bf16)
        mask = mask_ref[core]
        left_ref[core] = repeated * jnp.concatenate([mask, mask], axis=1)


def add_halves(both):
    middle = both.shape[0] // 2
    return both[:middle] + both[middle:]


def put_chunks(keep_ref, near_ref, chunk_ref, far_ref, down, up):
    rank = keep_ref.shape[1]
    rows = down.shape[0] // rank // 2

    def slot(number):
        start = number * rank
        return down[start : start + rank], up[start : start + rank]

    for place in range(2):
        keep_ref[place] = jnp.concatenate(slot(place), axis=1)
        near_ref[place] = encode(*slot(rows + place))
        chunk_ref[place] = jnp.concatenate(slot(place * rows + 2), axis=1)
        far_ref[place] = encode(*slot(place * rows + 3))


def gradient_kernel(
    same_ref,
    mask_ref,
    own_ref,
    other_ref,
    own_gradient_ref,
    other_gradient_ref,
    weight_ref,
    weighted_ref,
    high_ref,
    low_ref,
    keep_ref,
    near_ref,
    chunk_ref,
    far_ref,
    up_ref,
    to_ref,
    left_ref,
):
    wide = weight_ref.shape[1]
    model_width = up_ref.shape[1]
    gradient = jnp.concatenate([own_gradient_ref[...], other_gradient_ref[...]], axis=0)
    high = high_ref[...].reshape(2 * wide, model_width)
    low = low_ref[...].reshape(2 * wide, model_width)
    to_both = dot(gradient, high, 1, 1) + dot(gradient, low, 1, 1)
    to_ref[...] = to_both[:, wide:]
    put_left(left_ref, same_ref, mask_ref, weight_ref[...] * to_both[:, :wide])
    down = dot(left_ref[0], own_ref[...], 0, 0) + dot(left_ref[1], other_ref[...], 0, 0)
    up = add_halves(dot(jnp.concatenate(halves(weighted_ref[...]), axis=1), gradient, 0, 0))
    up_ref[...] = up[:wide]
    put_chunks(keep_ref, near_ref, chunk_ref, far_ref, add_halves(down), up[wide:])


def curvature_kernel(
    top,
    small_ref,
    same_ref,
    mask_ref,
    own_ref,
    other_ref,
    weight_ref,
    weighted_ref,
    high_ref,
    low_ref,
    up_ref,
    to_ref,
    tangent_ref,
    arrived_ref,
    keep_ref,
    near_ref,
    chunk_ref,
    far_ref,
    left_ref,
):
    _, _, curvature = token_columns(small_ref, top)
    tokens, wide = weight_ref.shape
    block = tokens // 2
    model_width = up_ref.shape[1]
    arrived = jnp.concatenate([arrived_ref[block:], arrived_ref[:block]], axis=0).astype(f32)
    resid = halves(curvature * (tangent_ref[...] + arrived))
    adapter_up = high_ref[0].reshape(wide, model_width), low_ref[0].reshape(wide, model_width)
    terms = weight_ref[...] * (dot_pairs(resid, adapter_up, 1, 1) + to_ref[...])
    put_left(left_ref, same_ref, mask_ref, terms)
    down = dot(left_ref[0], own_ref[...], 0, 0) + dot(left_ref[1], other_ref[...], 0, 0)
    weighted_u = halves(weighted_ref[:, wide:])
    up = add_halves(dot(jnp.concatenate(weighted_u, axis=1), resid[0], 0, 0)) + dot(weighted_u[0], resid[1], 0, 0)
    put_chunks(keep_ref, near_ref, chunk_ref, far_ref, add_halves(down), up_ref[...] + up)


def pair_kernel(hidden_width, arrived_ref, chunk_ref, near_ref, across_ref, keep_ref, onward_ref):
    onward_ref[...] = near_ref[...]
    for x in range(2):
        down, up = decode(arrived_ref[x], hidden_width)
        down, up = chunk_ref[x, :, :hidden_width] + down, chunk_ref[x, :, hidden_width:] + up
        if x == 0:
            keep_ref[...] = jnp.concatenate([down, up], axis=1)
        else:
            across_ref[...] = encode(down, up)


def far_kernel(hidden_width, arrived_ref, keep_ref, out_ref):
    down, up = decode(arrived_ref[...], hidden_width)
    out_ref[...] = encode(keep_ref[:, :hidden_width] + down, keep_ref[:, hidden_width:] + up)


def near_kernel(
    hidden_width, gradient_ref, curvature_ref, gradient_keep_ref, curvature_keep_ref, onward_ref, total_ref
):
    pairs = ((gradient_ref, gradient_keep_ref), (curvature_ref, curvature_keep_ref))
    for kind, (arrived_ref, keep_ref) in enumerate(pairs):
        for z in range(2):
            down, up = decode(arrived_ref[z], hidden_width)
            down, up = keep_ref[z, :, :hidden_width] + down, keep_ref[z, :, hidden_width:] + up
            if z == 0:
                total_ref[kind] = jnp.concatenate([down, up], axis=1)
            else:
                onward_ref[kind] = encode(down, up)


def add_kernel(hidden_width, total_ref, arrived_ref, out_ref):
    down, up = decode(arrived_ref[...], hidden_width)
    out_ref[:, :hidden_width] = total_ref[0, :, :hidden_width] + down
    out_ref[:, hidden_width:] = total_ref[0, :, hidden_width:] + up


def total_kernel(hidden_width, gradient_ref, total_ref, far_ref, pair_ref, *out_refs):
    far = decode(far_ref[...], hidden_width)
    totals = [
        (gradient_ref[:, :hidden_width], gradient_ref[:, hidden_width:]),
        (total_ref[1, :, :hidden_width] + far[0], total_ref[1, :, hidden_width:] + far[1]),
    ]
    for kind in range(2):
        down, up = decode(pair_ref[kind], hidden_width)
        out_refs[2 * kind][...] = totals[kind][0] + down
        out_refs[2 * kind + 1][...] = totals[kind][1] + up


class Ring:
    def __init__(self, size):
        self.length = size // 2
        rows = self.length // 2
        self.order = [4 * z for z in range(rows)] + [4 * z + 2 for z in reversed(range(rows))]

    def shift(self, value, step):
        pairs = [
            (chip + core, self.order[(place + step) % self.length] + core)
            for place, chip in enumerate(self.order)
            for core in range(2)
        ]
        return lax.ppermute(value, "expert", pairs)

    def members(self, me):
        rows = self.length // 2
        place = jnp.where(me // 2 % 2 == 0, me // 4, self.length - 1 - me // 4)
        half = self.length // 2
        offsets = [0] + [offset for step in range(1, half) for offset in (self.length - step, step)] + [half]
        there = (place + jnp.array(offsets, jnp.int32)) % self.length
        return jnp.where(there < rows, 4 * there, 4 * (self.length - 1 - there) + 2) + me % 2

    def gather(self, own, passing):
        half = self.length // 2
        pieces = [own]
        ahead, behind = own, own
        for step in range(1, half):
            behind = self.shift(behind, 1)
            ahead = self.shift(ahead, -1)
            if step > 1:
                behind, ahead = passing(behind, ahead, pieces)
            pieces += [behind, ahead]
        pieces += [self.shift(behind[:1], 1), self.shift(ahead[1:], -1)]
        return pieces


def exchange(value, mask):
    size = lax.axis_size("expert")
    return lax.ppermute(value, "expert", [(device, device ^ mask) for device in range(size)])


def gathered_plan(
    hidden_of_route,
    expert_of_route,
    gate_of_route,
    capacity,
    output_gradient,
    curvature,
    adapter_down,
    adapter_up,
    down_direction,
    up_direction,
):
    ring = Ring(lax.axis_size("expert"))
    slots = ring.length
    rows = slots // 2
    masks = [4 * z for z in range(rows)] + [4 * z + 2 for z in range(rows)]
    me = lax.axis_index("expert")
    tokens, top = expert_of_route.shape
    both = 2 * tokens
    hidden_width = hidden_of_route.shape[2]
    rank = adapter_down.shape[2]
    model_width = output_gradient.shape[1]
    experts = capacity.shape[0]
    wide = slots * rank
    coded_width = hidden_width + model_width + lanes


    place = []

    def call(kernel, multiplies, outs, *operands, scratch=(), after=(), grant=kernel_vmem):
        space = pltpu.VMEM if grant == kernel_vmem else pltpu.HBM
        places = [pl.BlockSpec(memory_space=pl.ANY) for _ in after] + [
            pl.BlockSpec(memory_space=pltpu.SMEM if any(operand is it for it in place) else space) for operand in operands
        ]
        return pl.pallas_call(
            lambda *refs: kernel(*refs[len(after) :]),
            out_shape=[jax.ShapeDtypeStruct(shape, dtype) for shape, dtype in outs],
            in_specs=places,
            scratch_shapes=scratch,
            compiler_params=pltpu.CompilerParams(vmem_limit_bytes=grant),
            cost_estimate=pl.CostEstimate(flops=2 * multiplies, bytes_accessed=2**20, transcendentals=0),
        )(*after, *operands)

    down_multiplies = 2 * top * both * hidden_width * wide
    up_multiplies = both * model_width * wide

    first = (
        expert_of_route.T,
        gate_of_route.T,
        curvature[None],
        down_direction[0].T,
        adapter_down[0].T,
        adapter_up[0],
        up_direction[0],
    )
    piece, small = call(
        functools.partial(prepare_kernel, experts),
        10**8,
        [((2, rank, coded_width), i16), (((2 * top + 8) // 8 * 8, tokens), f32)],
        *first,
        scratch=[pltpu.VMEM(operand.shape, operand.dtype) for operand in first]
        + [pltpu.SemaphoreType.DMA((len(first),))],
        grant=whole_vmem,
    )
    arrivals = ring.members(me)
    slot_of_arrival = (arrivals ^ me) // 4 + rows * ((arrivals ^ me) // 2 % 2)
    place.append(jnp.concatenate([me[None], arrivals, me ^ jnp.array(masks, jnp.int32), slot_of_arrival]).astype(jnp.int32))
    small_other = exchange(small, 1)
    hidden = hidden_of_route.reshape(tokens * top, hidden_width)
    small_columns, local_rank, gate, same, mask, hidden_other, gradient_other = call(
        functools.partial(tokens_kernel, top, slots),
        10**9,
        [
            ((both, small.shape[0]), f32),
            ((2, tokens, wide), f32),
            ((2, tokens, wide), f32),
            ((top * tokens, tokens), bf16),
            ((2, top * tokens, wide), bf16),
            (hidden.shape, bf16),
            (output_gradient.shape, bf16),
        ],
        *place,
        small,
        small_other,
        exchange(hidden, 1),
        exchange(output_gradient, 1),
        scratch=[pltpu.SemaphoreType.DMA((2,))],
    )
    def reduced(first, count, halved, *parts, after=()):
        return call(
            functools.partial(reduce_kernel, top, first, count, halved),
            2 * down_multiplies * count // slots,
            [((both, 2 * count * rank), f32)],
            *place,
            small_columns,
            hidden,
            hidden_other,
            *parts,
            scratch=[pltpu.VMEM((tokens * top, 2 * count * rank), f32)],
            after=after,
        )[0]

    early = slots // 2
    first_half = []

    def passing(behind, ahead, pieces):
        beside = same
        if len(pieces) > early:
            beside = reduced(0, early, False, *pieces[:early])
            first_half.append(beside)
        return call(pass_kernel, 10**8, [(piece.shape, i16)] * 2, behind, ahead, after=[beside])

    pieces = ring.gather(piece, passing)
    capacity_row = jnp.pad(capacity.astype(f32), (counts_lane, lanes - counts_lane - experts))[None, :]

    (reduced_early,) = first_half
    up_halves = [((2, slots, rank, model_width), bf16)] * 2
    high, low = call(
        functools.partial(unpack_kernel, slots, hidden_width), 10**8, up_halves, *place, *pieces[:-2]
    )
    (prior,) = call(prior_kernel, 10**8, [((8, lanes), f32)], *place, *pieces[:-1], after=[high])
    prior_arrived = exchange(prior, 1)
    reduced_late = reduced(early, slots - early, True, *pieces[early:], after=[prior])
    weight, weighted, tangent, coded, high, low = call(
        functools.partial(tangent_kernel, slots),
        6 * up_multiplies,
        [
            ((both, wide), f32),
            ((both, 2 * wide), f32),
            ((both, model_width), f32),
            ((both, model_width), bf16),
        ]
        + up_halves,
        *place,
        local_rank,
        gate,
        capacity_row,
        prior,
        prior_arrived,
        reduced_early,
        reduced_late,
        high,
        low,
        *pieces[-2:],
    )
    arrived = exchange(coded, 1)
    left = [pltpu.VMEM((2, top * tokens, 2 * wide), bf16)]
    chunks = [((2, rank, hidden_width + model_width), f32), ((2, rank, coded_width), i16)] * 2
    gradient_keep, gradient_near, gradient_chunk, gradient_far, up, to = call(
        gradient_kernel,
        down_multiplies + 8 * up_multiplies,
        chunks + [((wide, model_width), f32), ((both, wide), f32)],
        same,
        mask,
        hidden,
        hidden_other,
        output_gradient,
        gradient_other,
        weight,
        weighted,
        high,
        low,
        scratch=left,
    )
    gradient_far = exchange(gradient_far, 4)
    gradient_near = exchange(gradient_near, 2)
    curvature_keep, curvature_near, curvature_chunk, curvature_far = call(
        functools.partial(curvature_kernel, top),
        down_multiplies + 6 * up_multiplies,
        chunks,
        small_columns,
        same,
        mask,
        hidden,
        hidden_other,
        weight,
        weighted,
        high,
        low,
        up,
        to,
        tangent,
        arrived,
        scratch=left,
    )

    hop = 2 * 10**9

    one = (rank, hidden_width + model_width)
    one_coded = (rank, coded_width)

    def hop_call(kernel, outs, *operands, after=()):
        return call(functools.partial(kernel, hidden_width), hop, outs, *operands, after=after)

    curvature_far = exchange(curvature_far, 4)
    pair = [(one_coded, i16), (one, f32), ((2,) + one_coded, i16)]
    gradient_across, gradient_pair, curvature_near = hop_call(
        pair_kernel, pair, gradient_far, gradient_chunk, curvature_near, after=[curvature_keep]
    )
    curvature_near = exchange(curvature_near, 2)
    curvature_across, curvature_pair, gradient_near = hop_call(
        pair_kernel, pair, curvature_far, curvature_chunk, gradient_near, after=[gradient_across]
    )
    (gradient_beyond,) = hop_call(
        far_kernel,
        [(one_coded, i16)],
        exchange(gradient_across, 2),
        gradient_pair,
        after=[curvature_across],
    )
    onward, total = hop_call(
        near_kernel,
        [((2,) + one_coded, i16), ((2,) + one, f32)],
        gradient_near,
        curvature_near,
        gradient_keep,
        curvature_keep,
        after=[gradient_beyond],
    )
    (curvature_beyond,) = hop_call(
        far_kernel, [(one_coded, i16)], exchange(curvature_across, 2), curvature_pair, after=[onward]
    )
    (gradient_total,) = hop_call(
        add_kernel, [(one, f32)], total, exchange(gradient_beyond, 8), after=[curvature_beyond]
    )
    down_gradient, up_gradient, curvature_down, curvature_up = hop_call(
        total_kernel,
        [((rank, hidden_width), f32), ((rank, model_width), f32)] * 2,
        gradient_total,
        total,
        exchange(curvature_beyond, 8),
        exchange(onward, 4),
    )
    return down_gradient.T[None], up_gradient[None], curvature_down.T[None], curvature_up[None]


def carried_in(value, axis, join, neutral):
    count, mine = (lax.axis_size(axis), lax.axis_index(axis))
    pieces = lax.all_gather(value, axis)
    so_far = jnp.full_like(value, 0) + jnp.asarray(neutral, value.dtype)

    def lap(position, so_far):
        longer = join(so_far, pieces[position])
        return jnp.where(position < mine, longer, so_far)

    return lax.fori_loop(0, count - 1, lap, so_far)


def add_counts(earlier, later):
    return earlier + later


def routed_plan(
    hidden_of_route,
    expert_of_route,
    gate_of_route,
    capacity,
    output_gradient,
    curvature,
    adapter_down,
    adapter_up,
    down_direction,
    up_direction,
):
    finest_precision = lax.Precision.HIGHEST
    group_size = lax.axis_size("expert")
    tok_rows, top_count = expert_of_route.shape
    hidden_width = hidden_of_route.shape[2]
    resident_experts = adapter_down.shape[0]
    adapter_rank = adapter_down.shape[2]
    model_width = output_gradient.shape[1]
    experts = resident_experts * group_size
    slot_most = 2 * tok_rows * top_count // experts
    routes = expert_of_route.reshape(-1)
    onehot = (routes[:, None] == jnp.arange(experts, dtype=jnp.int32)[None, :]).astype(jnp.int32)
    earlier = jnp.cumsum(onehot, axis=0) - onehot
    local_rank = jnp.sum(earlier * onehot, axis=1)
    counts = jnp.sum(onehot, axis=0)
    prior_count = carried_in(counts, "expert", add_counts, jnp.zeros_like(counts))
    global_rank = local_rank + jnp.sum(onehot * prior_count[None, :], axis=1)
    route_limit = jnp.sum(onehot * capacity[None, :], axis=1)
    retained_mask = (global_rank < route_limit).astype(jnp.float32)
    weight_of_route = (
        adapter_scale * gate_of_route.reshape(-1).astype(jnp.float32) * retained_mask
    ).astype(jnp.bfloat16)
    slot_index = routes * slot_most + local_rank
    layout = (group_size, resident_experts, slot_most)
    send_hidden = (
        jnp.zeros((experts * slot_most, hidden_width), jnp.bfloat16)
        .at[slot_index]
        .set(hidden_of_route.reshape(-1, hidden_width))
        .reshape(layout + (hidden_width,))
    )
    send_weight = (
        jnp.zeros((experts * slot_most,), jnp.bfloat16)
        .at[slot_index]
        .set(weight_of_route)
        .reshape(layout)
    )
    down_stacked = jnp.concatenate([adapter_down, down_direction], axis=2)
    up_stacked = jnp.concatenate([adapter_up, up_direction], axis=1)

    def spread(token_rows):
        per_route = jnp.repeat(token_rows, top_count, axis=0)
        placed = (
            jnp.zeros((experts * slot_most, model_width), jnp.bfloat16)
            .at[slot_index]
            .set(per_route)
        )
        return placed.reshape(layout + (model_width,))

    send_residual = spread(output_gradient)
    pieces = (
        lax.all_to_all(send_hidden, "expert", split_axis=0, concat_axis=0, tiled=True),
        lax.all_to_all(send_weight, "expert", split_axis=0, concat_axis=0, tiled=True),
    )
    hidden_rows = pieces[0].astype(jnp.float32)
    weight_rows = pieces[1].astype(jnp.float32)[..., None]
    reduced_hidden = jnp.einsum(
        "cjif,jfk->cjik", hidden_rows, down_stacked, precision=finest_precision
    )
    exchanged_rows = jnp.concatenate(
        [reduced_hidden[..., adapter_rank:], reduced_hidden[..., :adapter_rank]], axis=3
    )
    tangent_out = weight_rows * jnp.einsum(
        "cjik,jkd->cjid", exchanged_rows, up_stacked, precision=finest_precision
    )
    returned = lax.all_to_all(
        tangent_out.astype(jnp.bfloat16), "expert", split_axis=0, concat_axis=0, tiled=True
    )
    results = (returned, reduced_hidden) + tuple(pieces)
    returned = results[0]
    reduced_hidden = results[1]
    hidden_rows = results[2]
    weight_rows = results[3]
    route_tangent = returned.reshape(experts * slot_most, model_width)[slot_index]
    out_tangent = jnp.sum(
        route_tangent.reshape(tok_rows, top_count, model_width).astype(jnp.float32), axis=1
    )
    resid_tangent = (curvature[:, None] * out_tangent).astype(jnp.bfloat16)
    send_tangent = spread(resid_tangent)
    residual_rows, tangent_rows = (
        lax.all_to_all(send_residual, "expert", split_axis=0, concat_axis=0, tiled=True),
        lax.all_to_all(send_tangent, "expert", split_axis=0, concat_axis=0, tiled=True),
    )
    residual_full = residual_rows.astype(jnp.float32)
    complete_tangent = tangent_rows.astype(jnp.float32)
    weight_column = weight_rows.astype(jnp.float32)[..., None]
    residual_reduced = jnp.einsum(
        "wyov,yqv->wyoq", residual_full, up_stacked, precision=finest_precision
    )
    reduced_tangent = jnp.einsum(
        "wyov,yqv->wyoq", complete_tangent, adapter_up, precision=finest_precision
    )
    left_terms = jnp.concatenate(
        [
            weight_column * residual_reduced[..., :adapter_rank],
            weight_column * (reduced_tangent + residual_reduced[..., adapter_rank:]),
        ],
        axis=3,
    )
    down_terms = jnp.einsum(
        "cjif,cjik->jfk", hidden_rows.astype(jnp.float32), left_terms, precision=finest_precision
    )
    raised_update = weight_column * reduced_hidden[..., :adapter_rank]
    raised_tangent_update = weight_column * reduced_hidden[..., adapter_rank:]
    up_terms = jnp.einsum(
        "cjik,cjid->jkd",
        jnp.concatenate([raised_update, raised_tangent_update], axis=3),
        residual_full,
        precision=finest_precision,
    )
    curvature_piece = up_terms[:, adapter_rank:] + jnp.einsum(
        "cjik,cjid->jkd", raised_update, complete_tangent, precision=finest_precision
    )
    return (
        down_terms[..., :adapter_rank],
        up_terms[:, :adapter_rank],
        down_terms[..., adapter_rank:],
        curvature_piece,
    )


def local(*arguments):
    factor_bytes = 2 * 4 * (arguments[6].size + arguments[7].size) * lax.axis_size("expert")
    fits = lax.axis_size("expert") == 16 and 4 * factor_bytes <= kernel_vmem
    plan = gathered_plan if fits else routed_plan
    return plan(*arguments)


def solution(mesh):
    return jax.shard_map(
        local,
        mesh=mesh,
        in_specs=(
            P(("groups", "expert"), None, None),
            P(("groups", "expert"), None),
            P(("groups", "expert"), None),
            P("groups"),
            P(("groups", "expert"), None),
            P(("groups", "expert")),
            P("expert", None, None),
            P("expert", None, None),
            P(("groups", "expert"), None, None),
            P(("groups", "expert"), None, None),
        ),
        out_specs=(
            P(("groups", "expert"), None, None),
            P(("groups", "expert"), None, None),
            P(("groups", "expert"), None, None),
            P(("groups", "expert"), None, None),
        ),
        check_vma=False,
    )
```

```python
import functools

import jax
import jax.numpy as jnp
from jax import lax
from jax.experimental import pallas as pl
from jax.experimental.pallas import tpu as pltpu
from jax.sharding import PartitionSpec as P

adapter_scale = 2.0
f32 = jnp.float32
bf16 = jnp.bfloat16
i16 = jnp.int16
lanes = 128
counts_lane = 64
kernel_vmem = 32 * 2**20
whole_vmem = 60 * 2**20


def halves(value):
    high = value.astype(bf16)
    return high, (value - high.astype(f32)).astype(bf16)


def dot(a, b, a_dim, b_dim):
    return lax.dot_general(a, b, (((a_dim,), (b_dim,)), ((), ())), preferred_element_type=f32)


def dot_pairs(a, b, a_dim, b_dim):
    return dot(a[0], b[0], a_dim, b_dim) + (dot(a[1], b[0], a_dim, b_dim) + dot(a[0], b[1], a_dim, b_dim))


def encode(down, up, counts=0.0):
    def scaled(value):
        largest = jnp.max(jnp.abs(value), axis=-1, keepdims=True)
        exponent = jnp.ceil(jnp.log2(jnp.maximum(largest, 1e-30)))
        coded = jnp.round(value * jnp.exp2(15.0 - exponent))
        return jnp.clip(coded, -32767.0, 32767.0), exponent

    down, down_exponent = scaled(down)
    up, up_exponent = scaled(up)
    lane = lax.broadcasted_iota(jnp.int32, down.shape[:-1] + (lanes,), down.ndim - 1)
    tail = jnp.where(lane < counts_lane // 2, down_exponent, up_exponent)
    tail = jnp.where(lane < counts_lane, tail, counts)
    return jnp.concatenate([down, up, tail], axis=-1).astype(jnp.int32).astype(i16)


def decode(coded, hidden_width):
    width = coded.shape[-1] - lanes
    value = coded.astype(jnp.int32).astype(f32)
    down_scale = jnp.exp2(value[..., width : width + 1] - 15.0)
    up_scale = jnp.exp2(value[..., width + counts_lane // 2 : width + counts_lane // 2 + 1] - 15.0)
    return value[..., :hidden_width] * down_scale, value[..., hidden_width:width] * up_scale


def prepare_kernel(experts, *refs):
    (piece_ref, small_ref), sem, refs = refs[7:9], refs[-1], refs[:7] + refs[9:-1]
    copies = [pltpu.make_async_copy(refs[i], refs[7 + i], sem.at[i]) for i in range(7)]
    for copy in copies:
        copy.start()
    for copy in copies:
        copy.wait()
    expert, gate, curvature, down_direction, adapter_down, adapter_up, up_direction = [ref[...] for ref in refs[7:]]
    top = expert.shape[0]
    small_ref[...] = jnp.zeros_like(small_ref)
    small_ref[:top] = expert.astype(f32)
    small_ref[top : 2 * top] = gate.astype(f32)
    small_ref[2 * top : 2 * top + 1] = curvature
    lane = lax.broadcasted_iota(jnp.int32, (1, lanes), 1)
    counts = jnp.zeros((1, lanes), f32)
    for number in range(experts):
        named = jnp.where(expert == number, 1.0, 0.0)
        total = jnp.sum(jnp.sum(named, axis=0, keepdims=True), axis=1, keepdims=True)
        counts = jnp.where(lane == counts_lane + number, total, counts)
    piece_ref[0] = encode(down_direction, adapter_up, counts)
    piece_ref[1] = encode(adapter_down, up_direction, counts)


def token_columns(small_ref, top):
    experts = [small_ref[:, k : k + 1] for k in range(top)]
    gates = [small_ref[:, top + k : top + k + 1] for k in range(top)]
    return experts, gates, small_ref[:, 2 * top : 2 * top + 1]


def members(place_ref, wide, first, count, dim=1):
    shape = (1, wide) if dim == 1 else (wide, 1)
    piece_of = lax.broadcasted_iota(jnp.int32, shape, dim) // (wide // count)
    found = jnp.zeros(shape, jnp.int32)
    for number in range(count):
        found = jnp.where(piece_of == number, place_ref[1 + first + number], found)
    return found.astype(f32)


def prior_kernel(place_ref, *rest):
    piece_refs, prior_ref = rest[:-1], rest[-1]
    me = place_ref[0]
    prior_ref[...] = jnp.zeros_like(prior_ref)
    for block, number in enumerate((me, me ^ 1)):
        total = jnp.zeros((1, lanes), f32)
        for arrival, piece_ref in enumerate(piece_refs):
            tail = piece_ref[0, :, piece_ref.shape[2] - lanes :]
            counts = tail.astype(jnp.int32).astype(f32)[0:1]
            total = total + jnp.where(place_ref[1 + arrival] < number, counts, 0.0)
        prior_ref[block : block + 1] = total


def piece_part(refs, arrival, kind, halved):
    if halved and arrival == len(refs) - 2:
        return refs[arrival + kind][0]
    return refs[arrival][kind]


def tokens_kernel(top, slots, place_ref, own_ref, other_ref, hidden_other_ref, gradient_other_ref, *outs):
    small_ref, rank_ref, gate_ref, same_ref, mask_ref, hidden_ref, gradient_ref, sem = outs
    copies = [
        pltpu.make_async_copy(hidden_other_ref, hidden_ref, sem.at[0]),
        pltpu.make_async_copy(gradient_other_ref, gradient_ref, sem.at[1]),
    ]
    for copy in copies:
        copy.start()
    small_ref[...] = jnp.concatenate([own_ref[...], other_ref[...]], axis=1).T
    experts, gates, _ = token_columns(small_ref, top)
    _, tokens, wide = rank_ref.shape
    column = members(place_ref, wide, slots, slots)
    below = (
        lax.broadcasted_iota(jnp.int32, (tokens, tokens), 0)
        > lax.broadcasted_iota(jnp.int32, (tokens, tokens), 1)
    )
    below = jnp.where(below, 1.0, 0.0).astype(bf16)
    rows = same_ref.shape[0]
    row = lax.broadcasted_iota(jnp.int32, (rows, tokens), 0)
    same = jnp.where(row // top == lax.broadcasted_iota(jnp.int32, (rows, tokens), 1), 1.0, 0.0).astype(bf16)
    same_ref[...] = same
    for core in range(2):
        tokens_of = slice(core * tokens, (core + 1) * tokens)
        gate = jnp.zeros((tokens, wide), f32)
        member = jnp.zeros((tokens, wide), f32)
        for k in range(top):
            named = experts[k][tokens_of] == column
            gate = jnp.where(named, gates[k][tokens_of], gate)
            member = jnp.where(named, 1.0, member)
        gate_ref[core] = gate
        rank_ref[core] = dot(below, member.astype(bf16), 1, 0)
        named = dot(same, small_ref[tokens_of].astype(bf16), 1, 0)
        position = lax.broadcasted_iota(jnp.int32, named.shape, 0) % top
        own = lax.broadcasted_iota(jnp.int32, named.shape, 1) == position
        expert = jnp.sum(jnp.where(own, named, 0.0), axis=1, keepdims=True)
        mask_ref[core] = jnp.where(expert == column, 1.0, 0.0).astype(bf16)
    for copy in copies:
        copy.wait()


def pass_kernel(behind_ref, ahead_ref, behind_out_ref, ahead_out_ref):
    behind_out_ref[...] = behind_ref[...]
    ahead_out_ref[...] = ahead_ref[...]


def reduce_kernel(top, first, count, halved, place_ref, small_ref, own_ref, other_ref, *rest):
    piece_refs, (reduced_ref, full_ref) = rest[:-2], rest[-2:]
    hidden_width = own_ref.shape[1]
    downs = [
        decode(piece_part(piece_refs, arrival, kind, halved), hidden_width)[0]
        for kind in range(2)
        for arrival in range(count)
    ]
    factor = jnp.concatenate(halves(jnp.concatenate(downs, axis=0)), axis=0)
    experts, _, _ = token_columns(small_ref, top)
    wide = reduced_ref.shape[1]
    column = members(place_ref, wide // 2, first, count)
    column = jnp.concatenate([column, column], axis=1)
    tokens = own_ref.shape[0] // top
    for core, hidden_ref in enumerate((own_ref, other_ref)):
        full = dot(hidden_ref[...], factor, 1, 1)
        full_ref[...] = full[:, :wide] + full[:, wide:]
        tokens_of = slice(core * tokens, (core + 1) * tokens)
        total = jnp.zeros((tokens, wide), f32)
        for k in range(top):
            here = full_ref[pl.ds(k, tokens, stride=top), :]
            total = jnp.where(experts[k][tokens_of] == column, here, total)
        reduced_ref[tokens_of] = total


def rank_limits(place_ref, wide, slots, capacity_ref, prior_ref, arrived_ref):
    lane = lax.broadcasted_iota(jnp.int32, (1, lanes), 1)
    piece_of = lax.broadcasted_iota(jnp.int32, (1, wide), 1) // (wide // slots)
    limits = []
    for block in range(2):
        total = capacity_ref[...] - prior_ref[block : block + 1] - arrived_ref[1 - block : 2 - block]
        limit = jnp.zeros((1, wide), f32)
        for slot in range(slots):
            picked = jnp.where(lane == counts_lane + place_ref[1 + slots + slot], total, 0.0)
            limit = jnp.where(piece_of == slot, jnp.sum(picked, axis=1, keepdims=True), limit)
        limits.append(limit)
    return limits


def tangent_kernel(
    slots, place_ref, rank_ref, gate_ref, capacity_ref, prior_ref, arrived_ref, early_ref, late_ref, *rest
):
    piece_refs = rest[: slots + 1]
    weight_ref, weighted_ref, tangent_ref, coded_ref, high_ref, low_ref = rest[slots + 1 :]
    _, wide = weight_ref.shape
    model_width = tangent_ref.shape[1]
    hidden_width = piece_refs[0].shape[2] - model_width - lanes
    limits = rank_limits(place_ref, wide, slots, capacity_ref, prior_ref, arrived_ref)
    weights = [
        jnp.where(rank_ref[core] < limits[core], adapter_scale * gate_ref[core], 0.0) for core in range(2)
    ]
    weight = jnp.concatenate(weights, axis=0)
    weight_ref[...] = weight
    half = wide // 2
    reduced = [
        jnp.concatenate([ref[:, kind * half : (kind + 1) * half] for ref in (early_ref, late_ref)], axis=1)
        for kind in range(2)
    ]
    rank = wide // slots
    by_arrival = members(place_ref, wide, 0, slots, 0) == members(place_ref, wide, slots, slots)
    row = lax.broadcasted_iota(jnp.int32, (wide, wide), 0)
    same_index = row % rank == lax.broadcasted_iota(jnp.int32, (wide, wide), 1) % rank
    order = jnp.where(by_arrival & same_index, 1.0, 0.0).astype(bf16)
    reduced = [sum(dot(part, order, 1, 0) for part in halves(both)) for both in reduced]
    weighted = jnp.concatenate([weight * part for part in reduced], axis=1)
    weighted_ref[...] = weighted
    for arrival in range(slots):
        for kind in range(2):
            _, up = decode(piece_part(piece_refs, arrival, kind, True), hidden_width)
            slot = place_ref[1 + 2 * slots + arrival]
            high_ref[kind, slot], low_ref[kind, slot] = halves(up)
    factor = high_ref[...].reshape(2 * wide, model_width), low_ref[...].reshape(2 * wide, model_width)
    tangent = dot_pairs(halves(weighted), factor, 1, 0)
    tangent_ref[...] = tangent
    coded_ref[...] = tangent.astype(bf16)


def put_left(left_ref, same_ref, mask_ref, terms):
    both = jnp.concatenate(halves(terms), axis=1)
    tokens = terms.shape[0] // 2
    for core in range(2):
        repeated = dot(same_ref[...], both[core * tokens : (core + 1) * tokens], 1, 0).astype(bf16)
        mask = mask_ref[core]
        left_ref[core] = repeated * jnp.concatenate([mask, mask], axis=1)


def add_halves(both):
    middle = both.shape[0] // 2
    return both[:middle] + both[middle:]


def put_chunks(keep_ref, near_ref, chunk_ref, far_ref, step, down, up):
    rank = keep_ref.shape[1]
    rows = down.shape[0] // rank // 2

    def slot(number):
        start = number * rank
        return down[start : start + rank], up[start : start + rank]

    for place in range(2):
        keep_ref[place] = jnp.concatenate(slot(place * step), axis=1)
        near_ref[place] = encode(*slot(rows + 1 - step + place * step))
        chunk_ref[place] = jnp.concatenate(slot(place * rows + 2), axis=1)
        far_ref[place] = encode(*slot(place * rows + 3))


def gradient_kernel(
    same_ref,
    mask_ref,
    own_ref,
    other_ref,
    own_gradient_ref,
    other_gradient_ref,
    weight_ref,
    weighted_ref,
    high_ref,
    low_ref,
    keep_ref,
    near_ref,
    chunk_ref,
    far_ref,
    up_ref,
    to_ref,
    left_ref,
):
    wide = weight_ref.shape[1]
    model_width = up_ref.shape[1]
    gradient = jnp.concatenate([own_gradient_ref[...], other_gradient_ref[...]], axis=0)
    high = high_ref[...].reshape(2 * wide, model_width)
    low = low_ref[...].reshape(2 * wide, model_width)
    to_both = dot(gradient, high, 1, 1) + dot(gradient, low, 1, 1)
    to_ref[...] = to_both[:, wide:]
    put_left(left_ref, same_ref, mask_ref, weight_ref[...] * to_both[:, :wide])
    down = dot(left_ref[0], own_ref[...], 0, 0) + dot(left_ref[1], other_ref[...], 0, 0)
    up = add_halves(dot(jnp.concatenate(halves(weighted_ref[...]), axis=1), gradient, 0, 0))
    up_ref[...] = up[:wide]
    put_chunks(keep_ref, near_ref, chunk_ref, far_ref, 1, add_halves(down), up[wide:])


def curvature_kernel(
    top,
    slots,
    small_ref,
    same_ref,
    mask_ref,
    own_ref,
    other_ref,
    weight_ref,
    weighted_ref,
    high_ref,
    low_ref,
    up_ref,
    to_ref,
    tangent_ref,
    arrived_ref,
    gradient_near_ref,
    keep_ref,
    near_ref,
    chunk_ref,
    far_ref,
    onward_ref,
    left_ref,
):
    onward_ref[...] = gradient_near_ref[...]
    _, _, curvature = token_columns(small_ref, top)
    tokens, wide = weight_ref.shape
    block = tokens // 2
    model_width = up_ref.shape[1]
    arrived = jnp.concatenate([arrived_ref[block:], arrived_ref[:block]], axis=0).astype(f32)
    resid = halves(curvature * (tangent_ref[...] + arrived))
    adapter_up = high_ref[0].reshape(wide, model_width), low_ref[0].reshape(wide, model_width)
    terms = weight_ref[...] * (dot_pairs(resid, adapter_up, 1, 1) + to_ref[...])
    put_left(left_ref, same_ref, mask_ref, terms)
    down = dot(left_ref[0], own_ref[...], 0, 0) + dot(left_ref[1], other_ref[...], 0, 0)
    weighted_u = halves(weighted_ref[:, wide:])
    up = add_halves(dot(jnp.concatenate(weighted_u, axis=1), resid[0], 0, 0)) + dot(weighted_u[0], resid[1], 0, 0)
    put_chunks(keep_ref, near_ref, chunk_ref, far_ref, slots // 2, add_halves(down), up_ref[...] + up)


def pair_kernel(hidden_width, arrived_ref, chunk_ref, *refs):
    passing, (across_ref, keep_ref) = (refs[:1], refs[1:3]) if len(refs) == 4 else ((), refs)
    for near_ref in passing:
        refs[3][...] = near_ref[...]
    for x in range(2):
        down, up = decode(arrived_ref[x], hidden_width)
        down, up = chunk_ref[x, :, :hidden_width] + down, chunk_ref[x, :, hidden_width:] + up
        if x == 0:
            keep_ref[...] = jnp.concatenate([down, up], axis=1)
        else:
            across_ref[...] = encode(down, up)


def far_kernel(hidden_width, arrived_ref, keep_ref, out_ref):
    down, up = decode(arrived_ref[...], hidden_width)
    out_ref[...] = encode(keep_ref[:, :hidden_width] + down, keep_ref[:, hidden_width:] + up)


def near_kernel(hidden_width, arrived_ref, keep_ref, onward_ref, total_ref):
    for place in range(2):
        down, up = decode(arrived_ref[place], hidden_width)
        down, up = keep_ref[place, :, :hidden_width] + down, keep_ref[place, :, hidden_width:] + up
        if place == 0:
            total_ref[...] = jnp.concatenate([down, up], axis=1)
        else:
            onward_ref[...] = encode(down, up)


def add_kernel(hidden_width, total_ref, near_ref, far_ref, out_ref):
    near, far = decode(near_ref[...], hidden_width), decode(far_ref[...], hidden_width)
    out_ref[:, :hidden_width] = total_ref[:, :hidden_width] + near[0] + far[0]
    out_ref[:, hidden_width:] = total_ref[:, hidden_width:] + near[1] + far[1]


def total_kernel(hidden_width, gradient_ref, total_ref, near_ref, far_ref, *out_refs):
    near, far = decode(near_ref[...], hidden_width), decode(far_ref[...], hidden_width)
    out_refs[0][...] = gradient_ref[:, :hidden_width]
    out_refs[1][...] = gradient_ref[:, hidden_width:]
    out_refs[2][...] = total_ref[:, :hidden_width] + near[0] + far[0]
    out_refs[3][...] = total_ref[:, hidden_width:] + near[1] + far[1]


class Ring:
    def __init__(self, size):
        self.length = size // 2
        rows = self.length // 2
        self.order = [4 * z for z in range(rows)] + [4 * z + 2 for z in reversed(range(rows))]

    def shift(self, value, step):
        pairs = [
            (chip + core, self.order[(place + step) % self.length] + core)
            for place, chip in enumerate(self.order)
            for core in range(2)
        ]
        return lax.ppermute(value, "expert", pairs)

    def members(self, me):
        rows = self.length // 2
        place = jnp.where(me // 2 % 2 == 0, me // 4, self.length - 1 - me // 4)
        half = self.length // 2
        offsets = [0] + [offset for step in range(1, half) for offset in (self.length - step, step)] + [half]
        there = (place + jnp.array(offsets, jnp.int32)) % self.length
        return jnp.where(there < rows, 4 * there, 4 * (self.length - 1 - there) + 2) + me % 2

    def gather(self, own, passing):
        half = self.length // 2
        pieces = [own]
        ahead, behind = own, own
        for step in range(1, half):
            behind = self.shift(behind, 1)
            ahead = self.shift(ahead, -1)
            if step == 2:
                behind, ahead = passing(behind, ahead)
            pieces += [behind, ahead]
        pieces += [self.shift(behind[:1], 1), self.shift(ahead[1:], -1)]
        return pieces


def exchange(value, mask):
    size = lax.axis_size("expert")
    return lax.ppermute(value, "expert", [(device, device ^ mask) for device in range(size)])


def gathered_plan(
    hidden_of_route,
    expert_of_route,
    gate_of_route,
    capacity,
    output_gradient,
    curvature,
    adapter_down,
    adapter_up,
    down_direction,
    up_direction,
):
    ring = Ring(lax.axis_size("expert"))
    slots = ring.length
    rows = slots // 2
    masks = [4 * z for z in range(rows)] + [4 * z + 2 for z in range(rows)]
    me = lax.axis_index("expert")
    tokens, top = expert_of_route.shape
    both = 2 * tokens
    hidden_width = hidden_of_route.shape[2]
    rank = adapter_down.shape[2]
    model_width = output_gradient.shape[1]
    experts = capacity.shape[0]
    wide = slots * rank
    coded_width = hidden_width + model_width + lanes


    place = []

    def call(kernel, multiplies, outs, *operands, scratch=(), after=(), grant=kernel_vmem):
        space = pltpu.VMEM if grant == kernel_vmem else pltpu.HBM
        places = [pl.BlockSpec(memory_space=pl.ANY) for _ in after] + [
            pl.BlockSpec(memory_space=pltpu.SMEM if any(operand is it for it in place) else space) for operand in operands
        ]
        return pl.pallas_call(
            lambda *refs: kernel(*refs[len(after) :]),
            out_shape=[jax.ShapeDtypeStruct(shape, dtype) for shape, dtype in outs],
            in_specs=places,
            scratch_shapes=scratch,
            compiler_params=pltpu.CompilerParams(vmem_limit_bytes=grant),
            cost_estimate=pl.CostEstimate(flops=2 * multiplies, bytes_accessed=2**20, transcendentals=0),
        )(*after, *operands)

    down_multiplies = 2 * top * both * hidden_width * wide
    up_multiplies = both * model_width * wide

    first = (
        expert_of_route.T,
        gate_of_route.T,
        curvature[None],
        down_direction[0].T,
        adapter_down[0].T,
        adapter_up[0],
        up_direction[0],
    )
    piece, small = call(
        functools.partial(prepare_kernel, experts),
        10**8,
        [((2, rank, coded_width), i16), (((2 * top + 8) // 8 * 8, tokens), f32)],
        *first,
        scratch=[pltpu.VMEM(operand.shape, operand.dtype) for operand in first]
        + [pltpu.SemaphoreType.DMA((len(first),))],
        grant=whole_vmem,
    )
    arrivals = ring.members(me)
    slot_of_arrival = (arrivals ^ me) // 4 + rows * ((arrivals ^ me) // 2 % 2)
    place.append(jnp.concatenate([me[None], arrivals, me ^ jnp.array(masks, jnp.int32), slot_of_arrival]).astype(jnp.int32))
    small_other = exchange(small, 1)
    hidden = hidden_of_route.reshape(tokens * top, hidden_width)
    small_columns, local_rank, gate, same, mask, hidden_other, gradient_other = call(
        functools.partial(tokens_kernel, top, slots),
        10**9,
        [
            ((both, small.shape[0]), f32),
            ((2, tokens, wide), f32),
            ((2, tokens, wide), f32),
            ((top * tokens, tokens), bf16),
            ((2, top * tokens, wide), bf16),
            (hidden.shape, bf16),
            (output_gradient.shape, bf16),
        ],
        *place,
        small,
        small_other,
        exchange(hidden, 1),
        exchange(output_gradient, 1),
        scratch=[pltpu.SemaphoreType.DMA((2,))],
    )
    def passing(behind, ahead):
        return call(pass_kernel, 10**8, [(piece.shape, i16)] * 2, behind, ahead, after=[same])

    pieces = ring.gather(piece, passing)
    capacity_row = jnp.pad(capacity.astype(f32), (counts_lane, lanes - counts_lane - experts))[None, :]

    def reduced(first, count, halved, *parts, after=()):
        return call(
            functools.partial(reduce_kernel, top, first, count, halved),
            2 * down_multiplies * count // slots,
            [((both, 2 * count * rank), f32)],
            *place,
            small_columns,
            hidden,
            hidden_other,
            *parts,
            scratch=[pltpu.VMEM((tokens * top, 2 * count * rank), f32)],
            after=after,
        )[0]

    early = slots // 2
    reduced_early = reduced(0, early, False, *pieces[:early])
    (prior,) = call(prior_kernel, 10**8, [((8, lanes), f32)], *place, *pieces[:-1], after=[reduced_early])
    prior_arrived = exchange(prior, 1)
    reduced_late = reduced(early, slots - early, True, *pieces[early:], after=[prior])
    weight, weighted, tangent, coded, high, low = call(
        functools.partial(tangent_kernel, slots),
        6 * up_multiplies,
        [
            ((both, wide), f32),
            ((both, 2 * wide), f32),
            ((both, model_width), f32),
            ((both, model_width), bf16),
            ((2, slots, rank, model_width), bf16),
            ((2, slots, rank, model_width), bf16),
        ],
        *place,
        local_rank,
        gate,
        capacity_row,
        prior,
        prior_arrived,
        reduced_early,
        reduced_late,
        *pieces,
    )
    arrived = exchange(coded, 1)
    left = [pltpu.VMEM((2, top * tokens, 2 * wide), bf16)]
    chunks = [((2, rank, hidden_width + model_width), f32), ((2, rank, coded_width), i16)] * 2
    gradient_keep, gradient_near, gradient_chunk, gradient_far, up, to = call(
        gradient_kernel,
        down_multiplies + 8 * up_multiplies,
        chunks + [((wide, model_width), f32), ((both, wide), f32)],
        same,
        mask,
        hidden,
        hidden_other,
        output_gradient,
        gradient_other,
        weight,
        weighted,
        high,
        low,
        scratch=left,
    )
    gradient_far = exchange(gradient_far, 4)
    curvature_keep, curvature_near, curvature_chunk, curvature_far, gradient_near = call(
        functools.partial(curvature_kernel, top, slots),
        down_multiplies + 6 * up_multiplies,
        chunks + [(gradient_near.shape, i16)],
        small_columns,
        same,
        mask,
        hidden,
        hidden_other,
        weight,
        weighted,
        high,
        low,
        up,
        to,
        tangent,
        arrived,
        gradient_near,
        scratch=left,
    )

    hop = 2 * 10**9

    one = (rank, hidden_width + model_width)
    one_coded = (rank, coded_width)

    def hop_call(kernel, outs, *operands, after=()):
        return call(functools.partial(kernel, hidden_width), hop, outs, *operands, after=after)

    curvature_far = exchange(curvature_far, 4)
    gradient_near = exchange(gradient_near, 2)
    pair = [(one_coded, i16), (one, f32)]
    gradient_across, gradient_pair, curvature_near = hop_call(
        pair_kernel,
        pair + [(curvature_near.shape, i16)],
        gradient_far,
        gradient_chunk,
        curvature_near,
        after=[curvature_keep],
    )
    curvature_near = exchange(curvature_near, 4)
    curvature_across, curvature_pair = hop_call(
        pair_kernel, pair, curvature_far, curvature_chunk, after=[gradient_across]
    )
    near = [(one_coded, i16), (one, f32)]
    gradient_onward, gradient_total = hop_call(
        near_kernel, near, gradient_near, gradient_keep, after=[curvature_across]
    )
    gradient_onward = exchange(gradient_onward, 4)
    (gradient_beyond,) = hop_call(
        far_kernel, [(one_coded, i16)], exchange(gradient_across, 2), gradient_pair, after=[gradient_total]
    )
    curvature_onward, curvature_total = hop_call(
        near_kernel, near, curvature_near, curvature_keep, after=[gradient_beyond]
    )
    (curvature_beyond,) = hop_call(
        far_kernel,
        [(one_coded, i16)],
        exchange(curvature_across, 2),
        curvature_pair,
        after=[curvature_total, gradient_onward],
    )
    (gradient_total,) = hop_call(
        add_kernel,
        [(one, f32)],
        gradient_total,
        gradient_onward,
        exchange(gradient_beyond, 8),
        after=[curvature_beyond],
    )
    down_gradient, up_gradient, curvature_down, curvature_up = hop_call(
        total_kernel,
        [((rank, hidden_width), f32), ((rank, model_width), f32)] * 2,
        gradient_total,
        curvature_total,
        exchange(curvature_onward, 2),
        exchange(curvature_beyond, 8),
    )
    return down_gradient.T[None], up_gradient[None], curvature_down.T[None], curvature_up[None]


def carried_in(value, axis, join, neutral):
    count, mine = (lax.axis_size(axis), lax.axis_index(axis))
    pieces = lax.all_gather(value, axis)
    so_far = jnp.full_like(value, 0) + jnp.asarray(neutral, value.dtype)

    def lap(position, so_far):
        longer = join(so_far, pieces[position])
        return jnp.where(position < mine, longer, so_far)

    return lax.fori_loop(0, count - 1, lap, so_far)


def add_counts(earlier, later):
    return earlier + later


def routed_plan(
    hidden_of_route,
    expert_of_route,
    gate_of_route,
    capacity,
    output_gradient,
    curvature,
    adapter_down,
    adapter_up,
    down_direction,
    up_direction,
):
    finest_precision = lax.Precision.HIGHEST
    group_size = lax.axis_size("expert")
    tok_rows, top_count = expert_of_route.shape
    hidden_width = hidden_of_route.shape[2]
    resident_experts = adapter_down.shape[0]
    adapter_rank = adapter_down.shape[2]
    model_width = output_gradient.shape[1]
    experts = resident_experts * group_size
    slot_most = 2 * tok_rows * top_count // experts
    routes = expert_of_route.reshape(-1)
    onehot = (routes[:, None] == jnp.arange(experts, dtype=jnp.int32)[None, :]).astype(jnp.int32)
    earlier = jnp.cumsum(onehot, axis=0) - onehot
    local_rank = jnp.sum(earlier * onehot, axis=1)
    counts = jnp.sum(onehot, axis=0)
    prior_count = carried_in(counts, "expert", add_counts, jnp.zeros_like(counts))
    global_rank = local_rank + jnp.sum(onehot * prior_count[None, :], axis=1)
    route_limit = jnp.sum(onehot * capacity[None, :], axis=1)
    retained_mask = (global_rank < route_limit).astype(jnp.float32)
    weight_of_route = (
        adapter_scale * gate_of_route.reshape(-1).astype(jnp.float32) * retained_mask
    ).astype(jnp.bfloat16)
    slot_index = routes * slot_most + local_rank
    layout = (group_size, resident_experts, slot_most)
    send_hidden = (
        jnp.zeros((experts * slot_most, hidden_width), jnp.bfloat16)
        .at[slot_index]
        .set(hidden_of_route.reshape(-1, hidden_width))
        .reshape(layout + (hidden_width,))
    )
    send_weight = (
        jnp.zeros((experts * slot_most,), jnp.bfloat16)
        .at[slot_index]
        .set(weight_of_route)
        .reshape(layout)
    )
    down_stacked = jnp.concatenate([adapter_down, down_direction], axis=2)
    up_stacked = jnp.concatenate([adapter_up, up_direction], axis=1)

    def spread(token_rows):
        per_route = jnp.repeat(token_rows, top_count, axis=0)
        placed = (
            jnp.zeros((experts * slot_most, model_width), jnp.bfloat16)
            .at[slot_index]
            .set(per_route)
        )
        return placed.reshape(layout + (model_width,))

    send_residual = spread(output_gradient)
    pieces = (
        lax.all_to_all(send_hidden, "expert", split_axis=0, concat_axis=0, tiled=True),
        lax.all_to_all(send_weight, "expert", split_axis=0, concat_axis=0, tiled=True),
    )
    hidden_rows = pieces[0].astype(jnp.float32)
    weight_rows = pieces[1].astype(jnp.float32)[..., None]
    reduced_hidden = jnp.einsum(
        "cjif,jfk->cjik", hidden_rows, down_stacked, precision=finest_precision
    )
    exchanged_rows = jnp.concatenate(
        [reduced_hidden[..., adapter_rank:], reduced_hidden[..., :adapter_rank]], axis=3
    )
    tangent_out = weight_rows * jnp.einsum(
        "cjik,jkd->cjid", exchanged_rows, up_stacked, precision=finest_precision
    )
    returned = lax.all_to_all(
        tangent_out.astype(jnp.bfloat16), "expert", split_axis=0, concat_axis=0, tiled=True
    )
    results = (returned, reduced_hidden) + tuple(pieces)
    returned = results[0]
    reduced_hidden = results[1]
    hidden_rows = results[2]
    weight_rows = results[3]
    route_tangent = returned.reshape(experts * slot_most, model_width)[slot_index]
    out_tangent = jnp.sum(
        route_tangent.reshape(tok_rows, top_count, model_width).astype(jnp.float32), axis=1
    )
    resid_tangent = (curvature[:, None] * out_tangent).astype(jnp.bfloat16)
    send_tangent = spread(resid_tangent)
    residual_rows, tangent_rows = (
        lax.all_to_all(send_residual, "expert", split_axis=0, concat_axis=0, tiled=True),
        lax.all_to_all(send_tangent, "expert", split_axis=0, concat_axis=0, tiled=True),
    )
    residual_full = residual_rows.astype(jnp.float32)
    complete_tangent = tangent_rows.astype(jnp.float32)
    weight_column = weight_rows.astype(jnp.float32)[..., None]
    residual_reduced = jnp.einsum(
        "wyov,yqv->wyoq", residual_full, up_stacked, precision=finest_precision
    )
    reduced_tangent = jnp.einsum(
        "wyov,yqv->wyoq", complete_tangent, adapter_up, precision=finest_precision
    )
    left_terms = jnp.concatenate(
        [
            weight_column * residual_reduced[..., :adapter_rank],
            weight_column * (reduced_tangent + residual_reduced[..., adapter_rank:]),
        ],
        axis=3,
    )
    down_terms = jnp.einsum(
        "cjif,cjik->jfk", hidden_rows.astype(jnp.float32), left_terms, precision=finest_precision
    )
    raised_update = weight_column * reduced_hidden[..., :adapter_rank]
    raised_tangent_update = weight_column * reduced_hidden[..., adapter_rank:]
    up_terms = jnp.einsum(
        "cjik,cjid->jkd",
        jnp.concatenate([raised_update, raised_tangent_update], axis=3),
        residual_full,
        precision=finest_precision,
    )
    curvature_piece = up_terms[:, adapter_rank:] + jnp.einsum(
        "cjik,cjid->jkd", raised_update, complete_tangent, precision=finest_precision
    )
    return (
        down_terms[..., :adapter_rank],
        up_terms[:, :adapter_rank],
        down_terms[..., adapter_rank:],
        curvature_piece,
    )


def local(*arguments):
    factor_bytes = 2 * 4 * (arguments[6].size + arguments[7].size) * lax.axis_size("expert")
    fits = lax.axis_size("expert") == 16 and 4 * factor_bytes <= kernel_vmem
    plan = gathered_plan if fits else routed_plan
    return plan(*arguments)


def solution(mesh):
    return jax.shard_map(
        local,
        mesh=mesh,
        in_specs=(
            P(("groups", "expert"), None, None),
            P(("groups", "expert"), None),
            P(("groups", "expert"), None),
            P("groups"),
            P(("groups", "expert"), None),
            P(("groups", "expert")),
            P("expert", None, None),
            P("expert", None, None),
            P(("groups", "expert"), None, None),
            P(("groups", "expert"), None, None),
        ),
        out_specs=(
            P(("groups", "expert"), None, None),
            P(("groups", "expert"), None, None),
            P(("groups", "expert"), None, None),
            P(("groups", "expert"), None, None),
        ),
        check_vma=False,
    )
```

```python
import functools

import jax
import jax.numpy as jnp
from jax import lax
from jax.experimental import pallas as pl
from jax.experimental.pallas import tpu as pltpu
from jax.sharding import PartitionSpec as P

adapter_scale = 2.0
f32 = jnp.float32
bf16 = jnp.bfloat16
i16 = jnp.int16
lanes = 128
counts_lane = 64
kernel_vmem = 32 * 2**20
whole_vmem = 60 * 2**20


def halves(value):
    high = value.astype(bf16)
    return high, (value - high.astype(f32)).astype(bf16)


def dot(a, b, a_dim, b_dim):
    return lax.dot_general(a, b, (((a_dim,), (b_dim,)), ((), ())), preferred_element_type=f32)


def dot_pairs(a, b, a_dim, b_dim):
    return dot(a[0], b[0], a_dim, b_dim) + (dot(a[1], b[0], a_dim, b_dim) + dot(a[0], b[1], a_dim, b_dim))


def encode(down, up, counts=0.0):
    def scaled(value):
        largest = jnp.max(jnp.abs(value), axis=-1, keepdims=True)
        exponent = jnp.ceil(jnp.log2(jnp.maximum(largest, 1e-30)))
        coded = jnp.round(value * jnp.exp2(15.0 - exponent))
        return jnp.clip(coded, -32767.0, 32767.0), exponent

    down, down_exponent = scaled(down)
    up, up_exponent = scaled(up)
    lane = lax.broadcasted_iota(jnp.int32, down.shape[:-1] + (lanes,), down.ndim - 1)
    tail = jnp.where(lane < counts_lane // 2, down_exponent, up_exponent)
    tail = jnp.where(lane < counts_lane, tail, counts)
    return jnp.concatenate([down, up, tail], axis=-1).astype(jnp.int32).astype(i16)


def decode(coded, hidden_width):
    width = coded.shape[-1] - lanes
    value = coded.astype(jnp.int32).astype(f32)
    down_scale = jnp.exp2(value[..., width : width + 1] - 15.0)
    up_scale = jnp.exp2(value[..., width + counts_lane // 2 : width + counts_lane // 2 + 1] - 15.0)
    return value[..., :hidden_width] * down_scale, value[..., hidden_width:width] * up_scale


def prepare_kernel(experts, *refs):
    (piece_ref, small_ref), sem, refs = refs[7:9], refs[-1], refs[:7] + refs[9:-1]
    copies = [pltpu.make_async_copy(refs[i], refs[7 + i], sem.at[i]) for i in range(7)]
    for copy in copies:
        copy.start()
    for copy in copies[:3]:
        copy.wait()
    expert, gate, curvature = [ref[...] for ref in refs[7:10]]
    top = expert.shape[0]
    small_ref[...] = jnp.zeros_like(small_ref)
    small_ref[:top] = expert.astype(f32)
    small_ref[top : 2 * top] = gate.astype(f32)
    small_ref[2 * top : 2 * top + 1] = curvature
    lane = lax.broadcasted_iota(jnp.int32, (1, lanes), 1)
    counts = jnp.zeros((1, lanes), f32)
    for number in range(experts):
        named = jnp.where(expert == number, 1.0, 0.0)
        total = jnp.sum(jnp.sum(named, axis=0, keepdims=True), axis=1, keepdims=True)
        counts = jnp.where(lane == counts_lane + number, total, counts)
    for copy in copies[3:]:
        copy.wait()
    down_direction, adapter_down, adapter_up, up_direction = [ref[...] for ref in refs[10:]]
    piece_ref[0] = encode(down_direction, adapter_up, counts)
    piece_ref[1] = encode(adapter_down, up_direction, counts)


def token_columns(small_ref, top):
    experts = [small_ref[:, k : k + 1] for k in range(top)]
    gates = [small_ref[:, top + k : top + k + 1] for k in range(top)]
    return experts, gates, small_ref[:, 2 * top : 2 * top + 1]


def members(place_ref, wide, first, count, dim=1):
    shape = (1, wide) if dim == 1 else (wide, 1)
    piece_of = lax.broadcasted_iota(jnp.int32, shape, dim) // (wide // count)
    found = jnp.zeros(shape, jnp.int32)
    for number in range(count):
        found = jnp.where(piece_of == number, place_ref[1 + first + number], found)
    return found.astype(f32)


def prior_kernel(place_ref, *rest):
    piece_refs, prior_ref = rest[:-1], rest[-1]
    me = place_ref[0]
    prior_ref[...] = jnp.zeros_like(prior_ref)
    for block, number in enumerate((me, me ^ 1)):
        total = jnp.zeros((1, lanes), f32)
        for arrival, piece_ref in enumerate(piece_refs):
            tail = piece_ref[0, :, piece_ref.shape[2] - lanes :]
            counts = tail.astype(jnp.int32).astype(f32)[0:1]
            total = total + jnp.where(place_ref[1 + arrival] < number, counts, 0.0)
        prior_ref[block : block + 1] = total


def piece_part(refs, arrival, kind, halved):
    if halved and arrival == len(refs) - 2:
        return refs[arrival + kind][0]
    return refs[arrival][kind]


def tokens_kernel(top, slots, place_ref, own_ref, other_ref, hidden_other_ref, gradient_other_ref, *outs):
    small_ref, rank_ref, gate_ref, same_ref, mask_ref, hidden_ref, gradient_ref, sem = outs
    copies = [
        pltpu.make_async_copy(hidden_other_ref, hidden_ref, sem.at[0]),
        pltpu.make_async_copy(gradient_other_ref, gradient_ref, sem.at[1]),
    ]
    for copy in copies:
        copy.start()
    small_ref[...] = jnp.concatenate([own_ref[...], other_ref[...]], axis=1).T
    experts, gates, _ = token_columns(small_ref, top)
    _, tokens, wide = rank_ref.shape
    column = members(place_ref, wide, slots, slots)
    below = (
        lax.broadcasted_iota(jnp.int32, (tokens, tokens), 0)
        > lax.broadcasted_iota(jnp.int32, (tokens, tokens), 1)
    )
    below = jnp.where(below, 1.0, 0.0).astype(bf16)
    rows = same_ref.shape[0]
    row = lax.broadcasted_iota(jnp.int32, (rows, tokens), 0)
    same = jnp.where(row // top == lax.broadcasted_iota(jnp.int32, (rows, tokens), 1), 1.0, 0.0).astype(bf16)
    same_ref[...] = same
    for core in range(2):
        tokens_of = slice(core * tokens, (core + 1) * tokens)
        gate = jnp.zeros((tokens, wide), f32)
        member = jnp.zeros((tokens, wide), f32)
        for k in range(top):
            named = experts[k][tokens_of] == column
            gate = jnp.where(named, gates[k][tokens_of], gate)
            member = jnp.where(named, 1.0, member)
        gate_ref[core] = gate
        rank_ref[core] = dot(below, member.astype(bf16), 1, 0)
        named = dot(same, small_ref[tokens_of].astype(bf16), 1, 0)
        position = lax.broadcasted_iota(jnp.int32, named.shape, 0) % top
        own = lax.broadcasted_iota(jnp.int32, named.shape, 1) == position
        expert = jnp.sum(jnp.where(own, named, 0.0), axis=1, keepdims=True)
        mask_ref[core] = jnp.where(expert == column, 1.0, 0.0).astype(bf16)
    for copy in copies:
        copy.wait()


def pass_kernel(behind_ref, ahead_ref, behind_out_ref, ahead_out_ref):
    behind_out_ref[...] = behind_ref[...]
    ahead_out_ref[...] = ahead_ref[...]


def reduce_kernel(top, first, count, halved, place_ref, small_ref, own_ref, other_ref, *rest):
    piece_refs, (reduced_ref, full_ref) = rest[:-2], rest[-2:]
    hidden_width = own_ref.shape[1]
    downs = [
        decode(piece_part(piece_refs, arrival, kind, halved), hidden_width)[0]
        for kind in range(2)
        for arrival in range(count)
    ]
    factor = jnp.concatenate(halves(jnp.concatenate(downs, axis=0)), axis=0)
    experts, _, _ = token_columns(small_ref, top)
    wide = reduced_ref.shape[1]
    column = members(place_ref, wide // 2, first, count)
    column = jnp.concatenate([column, column], axis=1)
    tokens = own_ref.shape[0] // top
    for core, hidden_ref in enumerate((own_ref, other_ref)):
        full = dot(hidden_ref[...], factor, 1, 1)
        full_ref[: tokens * top] = full[:, :wide] + full[:, wide:]
        tokens_of = slice(core * tokens, (core + 1) * tokens)
        total = jnp.zeros((tokens, wide), f32)
        for k in range(top):
            here = full_ref[pl.ds(k, tokens, stride=top), :]
            total = jnp.where(experts[k][tokens_of] == column, here, total)
        reduced_ref[tokens_of] = total


def rank_limits(place_ref, wide, slots, capacity_ref, prior_ref, arrived_ref):
    lane = lax.broadcasted_iota(jnp.int32, (1, lanes), 1)
    piece_of = lax.broadcasted_iota(jnp.int32, (1, wide), 1) // (wide // slots)
    limits = []
    for block in range(2):
        total = capacity_ref[...] - prior_ref[block : block + 1] - arrived_ref[1 - block : 2 - block]
        limit = jnp.zeros((1, wide), f32)
        for slot in range(slots):
            picked = jnp.where(lane == counts_lane + place_ref[1 + slots + slot], total, 0.0)
            limit = jnp.where(piece_of == slot, jnp.sum(picked, axis=1, keepdims=True), limit)
        limits.append(limit)
    return limits


def tangent_kernel(
    slots, place_ref, rank_ref, gate_ref, capacity_ref, prior_ref, arrived_ref, early_ref, late_ref, *rest
):
    piece_refs = rest[: slots + 1]
    weight_ref, weighted_ref, tangent_ref, coded_ref, high_ref, low_ref = rest[slots + 1 :]
    _, wide = weight_ref.shape
    model_width = tangent_ref.shape[1]
    hidden_width = piece_refs[0].shape[2] - model_width - lanes
    limits = rank_limits(place_ref, wide, slots, capacity_ref, prior_ref, arrived_ref)
    weights = [
        jnp.where(rank_ref[core] < limits[core], adapter_scale * gate_ref[core], 0.0) for core in range(2)
    ]
    weight = jnp.concatenate(weights, axis=0)
    weight_ref[...] = weight
    half = wide // 2
    reduced = [
        jnp.concatenate([ref[:, kind * half : (kind + 1) * half] for ref in (early_ref, late_ref)], axis=1)
        for kind in range(2)
    ]
    rank = wide // slots
    by_arrival = members(place_ref, wide, 0, slots, 0) == members(place_ref, wide, slots, slots)
    row = lax.broadcasted_iota(jnp.int32, (wide, wide), 0)
    same_index = row % rank == lax.broadcasted_iota(jnp.int32, (wide, wide), 1) % rank
    order = jnp.where(by_arrival & same_index, 1.0, 0.0).astype(bf16)
    reduced = [sum(dot(part, order, 1, 0) for part in halves(both)) for both in reduced]
    weighted = jnp.concatenate([weight * part for part in reduced], axis=1)
    weighted_ref[...] = weighted
    for arrival in range(slots):
        for kind in range(2):
            _, up = decode(piece_part(piece_refs, arrival, kind, True), hidden_width)
            slot = place_ref[1 + 2 * slots + arrival]
            high_ref[kind, slot], low_ref[kind, slot] = halves(up)
    factor = high_ref[...].reshape(2 * wide, model_width), low_ref[...].reshape(2 * wide, model_width)
    tangent = dot_pairs(halves(weighted), factor, 1, 0)
    tangent_ref[...] = tangent
    coded_ref[...] = tangent.astype(bf16)


def put_left(left_ref, same_ref, mask_ref, terms):
    both = jnp.concatenate(halves(terms), axis=1)
    tokens = terms.shape[0] // 2
    for core in range(2):
        repeated = dot(same_ref[...], both[core * tokens : (core + 1) * tokens], 1, 0).astype(bf16)
        mask = mask_ref[core]
        left_ref[core] = repeated * jnp.concatenate([mask, mask], axis=1)


def add_halves(both):
    middle = both.shape[0] // 2
    return both[:middle] + both[middle:]


def put_chunks(keep_ref, near_ref, chunk_ref, far_ref, down, up):
    rank = keep_ref.shape[1]
    rows = down.shape[0] // rank // 2

    def slot(number):
        start = number * rank
        return down[start : start + rank], up[start : start + rank]

    for place in range(2):
        keep_ref[place] = jnp.concatenate(slot(place), axis=1)
        near_ref[place] = encode(*slot(rows + place))
        chunk_ref[place] = jnp.concatenate(slot(place * rows + 2), axis=1)
        far_ref[place] = encode(*slot(place * rows + 3))


def gradient_kernel(
    same_ref,
    mask_ref,
    own_ref,
    other_ref,
    own_gradient_ref,
    other_gradient_ref,
    weight_ref,
    weighted_ref,
    high_ref,
    low_ref,
    keep_ref,
    near_ref,
    chunk_ref,
    far_ref,
    up_ref,
    to_ref,
    left_ref,
):
    wide = weight_ref.shape[1]
    model_width = up_ref.shape[1]
    gradient = jnp.concatenate([own_gradient_ref[...], other_gradient_ref[...]], axis=0)
    high = high_ref[...].reshape(2 * wide, model_width)
    low = low_ref[...].reshape(2 * wide, model_width)
    to_both = dot(gradient, high, 1, 1) + dot(gradient, low, 1, 1)
    to_ref[...] = to_both[:, wide:]
    put_left(left_ref, same_ref, mask_ref, weight_ref[...] * to_both[:, :wide])
    down = dot(left_ref[0], own_ref[...], 0, 0) + dot(left_ref[1], other_ref[...], 0, 0)
    up = add_halves(dot(jnp.concatenate(halves(weighted_ref[...]), axis=1), gradient, 0, 0))
    up_ref[...] = up[:wide]
    put_chunks(keep_ref, near_ref, chunk_ref, far_ref, add_halves(down), up[wide:])


def curvature_kernel(
    top,
    small_ref,
    same_ref,
    mask_ref,
    own_ref,
    other_ref,
    weight_ref,
    weighted_ref,
    high_ref,
    low_ref,
    up_ref,
    to_ref,
    tangent_ref,
    arrived_ref,
    keep_ref,
    near_ref,
    chunk_ref,
    far_ref,
    left_ref,
):
    _, _, curvature = token_columns(small_ref, top)
    tokens, wide = weight_ref.shape
    block = tokens // 2
    model_width = up_ref.shape[1]
    arrived = jnp.concatenate([arrived_ref[block:], arrived_ref[:block]], axis=0).astype(f32)
    resid = halves(curvature * (tangent_ref[...] + arrived))
    adapter_up = high_ref[0].reshape(wide, model_width), low_ref[0].reshape(wide, model_width)
    terms = weight_ref[...] * (dot_pairs(resid, adapter_up, 1, 1) + to_ref[...])
    put_left(left_ref, same_ref, mask_ref, terms)
    down = dot(left_ref[0], own_ref[...], 0, 0) + dot(left_ref[1], other_ref[...], 0, 0)
    weighted_u = halves(weighted_ref[:, wide:])
    up = add_halves(dot(jnp.concatenate(weighted_u, axis=1), resid[0], 0, 0)) + dot(weighted_u[0], resid[1], 0, 0)
    put_chunks(keep_ref, near_ref, chunk_ref, far_ref, add_halves(down), up_ref[...] + up)


def pair_kernel(hidden_width, arrived_ref, chunk_ref, near_ref, across_ref, keep_ref, onward_ref):
    onward_ref[...] = near_ref[...]
    for x in range(2):
        down, up = decode(arrived_ref[x], hidden_width)
        down, up = chunk_ref[x, :, :hidden_width] + down, chunk_ref[x, :, hidden_width:] + up
        if x == 0:
            keep_ref[...] = jnp.concatenate([down, up], axis=1)
        else:
            across_ref[...] = encode(down, up)


def far_kernel(hidden_width, arrived_ref, keep_ref, out_ref):
    down, up = decode(arrived_ref[...], hidden_width)
    out_ref[...] = encode(keep_ref[:, :hidden_width] + down, keep_ref[:, hidden_width:] + up)


def near_kernel(
    hidden_width, gradient_ref, curvature_ref, gradient_keep_ref, curvature_keep_ref, onward_ref, total_ref
):
    pairs = ((gradient_ref, gradient_keep_ref), (curvature_ref, curvature_keep_ref))
    for kind, (arrived_ref, keep_ref) in enumerate(pairs):
        for z in range(2):
            down, up = decode(arrived_ref[z], hidden_width)
            down, up = keep_ref[z, :, :hidden_width] + down, keep_ref[z, :, hidden_width:] + up
            if z == 0:
                total_ref[kind] = jnp.concatenate([down, up], axis=1)
            else:
                onward_ref[kind] = encode(down, up)


def add_kernel(hidden_width, total_ref, arrived_ref, out_ref):
    down, up = decode(arrived_ref[...], hidden_width)
    out_ref[:, :hidden_width] = total_ref[0, :, :hidden_width] + down
    out_ref[:, hidden_width:] = total_ref[0, :, hidden_width:] + up


def total_kernel(hidden_width, gradient_ref, total_ref, far_ref, pair_ref, *out_refs):
    far = decode(far_ref[...], hidden_width)
    totals = [
        (gradient_ref[:, :hidden_width], gradient_ref[:, hidden_width:]),
        (total_ref[1, :, :hidden_width] + far[0], total_ref[1, :, hidden_width:] + far[1]),
    ]
    for kind in range(2):
        down, up = decode(pair_ref[kind], hidden_width)
        out_refs[2 * kind][...] = totals[kind][0] + down
        out_refs[2 * kind + 1][...] = totals[kind][1] + up


class Ring:
    def __init__(self, size):
        self.length = size // 2
        rows = self.length // 2
        self.order = [4 * z for z in range(rows)] + [4 * z + 2 for z in reversed(range(rows))]

    def shift(self, value, step):
        pairs = [
            (chip + core, self.order[(place + step) % self.length] + core)
            for place, chip in enumerate(self.order)
            for core in range(2)
        ]
        return lax.ppermute(value, "expert", pairs)

    def members(self, me):
        rows = self.length // 2
        place = jnp.where(me // 2 % 2 == 0, me // 4, self.length - 1 - me // 4)
        half = self.length // 2
        offsets = [0] + [offset for step in range(1, half) for offset in (self.length - step, step)] + [half]
        there = (place + jnp.array(offsets, jnp.int32)) % self.length
        return jnp.where(there < rows, 4 * there, 4 * (self.length - 1 - there) + 2) + me % 2

    def gather(self, own, passing):
        half = self.length // 2
        pieces = [own]
        ahead, behind = own, own
        for step in range(1, half):
            behind = self.shift(behind, 1)
            ahead = self.shift(ahead, -1)
            if step == 2:
                behind, ahead = passing(behind, ahead)
            pieces += [behind, ahead]
        pieces += [self.shift(behind[:1], 1), self.shift(ahead[1:], -1)]
        return pieces


def exchange(value, mask):
    size = lax.axis_size("expert")
    return lax.ppermute(value, "expert", [(device, device ^ mask) for device in range(size)])


def gathered_plan(
    hidden_of_route,
    expert_of_route,
    gate_of_route,
    capacity,
    output_gradient,
    curvature,
    adapter_down,
    adapter_up,
    down_direction,
    up_direction,
):
    ring = Ring(lax.axis_size("expert"))
    slots = ring.length
    rows = slots // 2
    masks = [4 * z for z in range(rows)] + [4 * z + 2 for z in range(rows)]
    me = lax.axis_index("expert")
    tokens, top = expert_of_route.shape
    both = 2 * tokens
    hidden_width = hidden_of_route.shape[2]
    rank = adapter_down.shape[2]
    model_width = output_gradient.shape[1]
    experts = capacity.shape[0]
    wide = slots * rank
    coded_width = hidden_width + model_width + lanes


    place = []

    def call(kernel, multiplies, outs, *operands, scratch=(), after=(), grant=kernel_vmem):
        space = pltpu.VMEM if grant == kernel_vmem else pltpu.HBM
        places = [pl.BlockSpec(memory_space=pl.ANY) for _ in after] + [
            pl.BlockSpec(memory_space=pltpu.SMEM if any(operand is it for it in place) else space) for operand in operands
        ]
        return pl.pallas_call(
            lambda *refs: kernel(*refs[len(after) :]),
            out_shape=[jax.ShapeDtypeStruct(shape, dtype) for shape, dtype in outs],
            in_specs=places,
            scratch_shapes=scratch,
            compiler_params=pltpu.CompilerParams(vmem_limit_bytes=grant),
            cost_estimate=pl.CostEstimate(flops=2 * multiplies, bytes_accessed=2**20, transcendentals=0),
        )(*after, *operands)

    down_multiplies = 2 * top * both * hidden_width * wide
    up_multiplies = both * model_width * wide

    first = (
        expert_of_route.T,
        gate_of_route.T,
        curvature[None],
        down_direction[0].T,
        adapter_down[0].T,
        adapter_up[0],
        up_direction[0],
    )
    piece, small = call(
        functools.partial(prepare_kernel, experts),
        10**8,
        [((2, rank, coded_width), i16), (((2 * top + 8) // 8 * 8, tokens), f32)],
        *first,
        scratch=[pltpu.VMEM(operand.shape, operand.dtype) for operand in first]
        + [pltpu.SemaphoreType.DMA((len(first),))],
        grant=whole_vmem,
    )
    arrivals = ring.members(me)
    slot_of_arrival = (arrivals ^ me) // 4 + rows * ((arrivals ^ me) // 2 % 2)
    place.append(jnp.concatenate([me[None], arrivals, me ^ jnp.array(masks, jnp.int32), slot_of_arrival]).astype(jnp.int32))
    small_other = exchange(small, 1)
    hidden = hidden_of_route.reshape(tokens * top, hidden_width)
    small_columns, local_rank, gate, same, mask, hidden_other, gradient_other = call(
        functools.partial(tokens_kernel, top, slots),
        10**9,
        [
            ((both, small.shape[0]), f32),
            ((2, tokens, wide), f32),
            ((2, tokens, wide), f32),
            ((top * tokens, tokens), bf16),
            ((2, top * tokens, wide), bf16),
            (hidden.shape, bf16),
            (output_gradient.shape, bf16),
        ],
        *place,
        small,
        small_other,
        exchange(hidden, 1),
        exchange(output_gradient, 1),
        scratch=[pltpu.SemaphoreType.DMA((2,))],
    )
    def passing(behind, ahead):
        return call(pass_kernel, 10**8, [(piece.shape, i16)] * 2, behind, ahead, after=[same])

    pieces = ring.gather(piece, passing)
    capacity_row = jnp.pad(capacity.astype(f32), (counts_lane, lanes - counts_lane - experts))[None, :]

    def reduced(first, count, halved, *parts, after=()):
        return call(
            functools.partial(reduce_kernel, top, first, count, halved),
            2 * down_multiplies * count // slots,
            [((both, 2 * count * rank), f32)],
            *place,
            small_columns,
            hidden,
            hidden_other,
            *parts,
            scratch=[pltpu.VMEM((tokens * top + top, 2 * count * rank), f32)],
            after=after,
        )[0]

    early = slots // 2
    reduced_early = reduced(0, early, False, *pieces[:early])
    (prior,) = call(prior_kernel, 10**8, [((8, lanes), f32)], *place, *pieces[:-1], after=[reduced_early])
    prior_arrived = exchange(prior, 1)
    reduced_late = reduced(early, slots - early, True, *pieces[early:], after=[prior])
    weight, weighted, tangent, coded, high, low = call(
        functools.partial(tangent_kernel, slots),
        6 * up_multiplies,
        [
            ((both, wide), f32),
            ((both, 2 * wide), f32),
            ((both, model_width), f32),
            ((both, model_width), bf16),
            ((2, slots, rank, model_width), bf16),
            ((2, slots, rank, model_width), bf16),
        ],
        *place,
        local_rank,
        gate,
        capacity_row,
        prior,
        prior_arrived,
        reduced_early,
        reduced_late,
        *pieces,
    )
    arrived = exchange(coded, 1)
    left = [pltpu.VMEM((2, top * tokens, 2 * wide), bf16)]
    chunks = [((2, rank, hidden_width + model_width), f32), ((2, rank, coded_width), i16)] * 2
    gradient_keep, gradient_near, gradient_chunk, gradient_far, up, to = call(
        gradient_kernel,
        down_multiplies + 8 * up_multiplies,
        chunks + [((wide, model_width), f32), ((both, wide), f32)],
        same,
        mask,
        hidden,
        hidden_other,
        output_gradient,
        gradient_other,
        weight,
        weighted,
        high,
        low,
        scratch=left,
    )
    gradient_far = exchange(gradient_far, 4)
    gradient_near = exchange(gradient_near, 2)
    curvature_keep, curvature_near, curvature_chunk, curvature_far = call(
        functools.partial(curvature_kernel, top),
        down_multiplies + 6 * up_multiplies,
        chunks,
        small_columns,
        same,
        mask,
        hidden,
        hidden_other,
        weight,
        weighted,
        high,
        low,
        up,
        to,
        tangent,
        arrived,
        scratch=left,
    )

    hop = 2 * 10**9

    one = (rank, hidden_width + model_width)
    one_coded = (rank, coded_width)

    def hop_call(kernel, outs, *operands, after=()):
        return call(functools.partial(kernel, hidden_width), hop, outs, *operands, after=after)

    curvature_far = exchange(curvature_far, 4)
    pair = [(one_coded, i16), (one, f32), ((2,) + one_coded, i16)]
    gradient_across, gradient_pair, curvature_near = hop_call(
        pair_kernel, pair, gradient_far, gradient_chunk, curvature_near, after=[curvature_keep]
    )
    curvature_near = exchange(curvature_near, 2)
    curvature_across, curvature_pair, gradient_near = hop_call(
        pair_kernel, pair, curvature_far, curvature_chunk, gradient_near, after=[gradient_across]
    )
    (gradient_beyond,) = hop_call(
        far_kernel,
        [(one_coded, i16)],
        exchange(gradient_across, 2),
        gradient_pair,
        after=[curvature_across],
    )
    onward, total = hop_call(
        near_kernel,
        [((2,) + one_coded, i16), ((2,) + one, f32)],
        gradient_near,
        curvature_near,
        gradient_keep,
        curvature_keep,
        after=[gradient_beyond],
    )
    (curvature_beyond,) = hop_call(
        far_kernel, [(one_coded, i16)], exchange(curvature_across, 2), curvature_pair, after=[onward]
    )
    (gradient_total,) = hop_call(
        add_kernel, [(one, f32)], total, exchange(gradient_beyond, 8), after=[curvature_beyond]
    )
    down_gradient, up_gradient, curvature_down, curvature_up = hop_call(
        total_kernel,
        [((rank, hidden_width), f32), ((rank, model_width), f32)] * 2,
        gradient_total,
        total,
        exchange(curvature_beyond, 8),
        exchange(onward, 4),
    )
    return down_gradient.T[None], up_gradient[None], curvature_down.T[None], curvature_up[None]


def carried_in(value, axis, join, neutral):
    count, mine = (lax.axis_size(axis), lax.axis_index(axis))
    pieces = lax.all_gather(value, axis)
    so_far = jnp.full_like(value, 0) + jnp.asarray(neutral, value.dtype)

    def lap(position, so_far):
        longer = join(so_far, pieces[position])
        return jnp.where(position < mine, longer, so_far)

    return lax.fori_loop(0, count - 1, lap, so_far)


def add_counts(earlier, later):
    return earlier + later


def routed_plan(
    hidden_of_route,
    expert_of_route,
    gate_of_route,
    capacity,
    output_gradient,
    curvature,
    adapter_down,
    adapter_up,
    down_direction,
    up_direction,
):
    finest_precision = lax.Precision.HIGHEST
    group_size = lax.axis_size("expert")
    tok_rows, top_count = expert_of_route.shape
    hidden_width = hidden_of_route.shape[2]
    resident_experts = adapter_down.shape[0]
    adapter_rank = adapter_down.shape[2]
    model_width = output_gradient.shape[1]
    experts = resident_experts * group_size
    slot_most = 2 * tok_rows * top_count // experts
    routes = expert_of_route.reshape(-1)
    onehot = (routes[:, None] == jnp.arange(experts, dtype=jnp.int32)[None, :]).astype(jnp.int32)
    earlier = jnp.cumsum(onehot, axis=0) - onehot
    local_rank = jnp.sum(earlier * onehot, axis=1)
    counts = jnp.sum(onehot, axis=0)
    prior_count = carried_in(counts, "expert", add_counts, jnp.zeros_like(counts))
    global_rank = local_rank + jnp.sum(onehot * prior_count[None, :], axis=1)
    route_limit = jnp.sum(onehot * capacity[None, :], axis=1)
    retained_mask = (global_rank < route_limit).astype(jnp.float32)
    weight_of_route = (
        adapter_scale * gate_of_route.reshape(-1).astype(jnp.float32) * retained_mask
    ).astype(jnp.bfloat16)
    slot_index = routes * slot_most + local_rank
    layout = (group_size, resident_experts, slot_most)
    send_hidden = (
        jnp.zeros((experts * slot_most, hidden_width), jnp.bfloat16)
        .at[slot_index]
        .set(hidden_of_route.reshape(-1, hidden_width))
        .reshape(layout + (hidden_width,))
    )
    send_weight = (
        jnp.zeros((experts * slot_most,), jnp.bfloat16)
        .at[slot_index]
        .set(weight_of_route)
        .reshape(layout)
    )
    down_stacked = jnp.concatenate([adapter_down, down_direction], axis=2)
    up_stacked = jnp.concatenate([adapter_up, up_direction], axis=1)

    def spread(token_rows):
        per_route = jnp.repeat(token_rows, top_count, axis=0)
        placed = (
            jnp.zeros((experts * slot_most, model_width), jnp.bfloat16)
            .at[slot_index]
            .set(per_route)
        )
        return placed.reshape(layout + (model_width,))

    send_residual = spread(output_gradient)
    pieces = (
        lax.all_to_all(send_hidden, "expert", split_axis=0, concat_axis=0, tiled=True),
        lax.all_to_all(send_weight, "expert", split_axis=0, concat_axis=0, tiled=True),
    )
    hidden_rows = pieces[0].astype(jnp.float32)
    weight_rows = pieces[1].astype(jnp.float32)[..., None]
    reduced_hidden = jnp.einsum(
        "cjif,jfk->cjik", hidden_rows, down_stacked, precision=finest_precision
    )
    exchanged_rows = jnp.concatenate(
        [reduced_hidden[..., adapter_rank:], reduced_hidden[..., :adapter_rank]], axis=3
    )
    tangent_out = weight_rows * jnp.einsum(
        "cjik,jkd->cjid", exchanged_rows, up_stacked, precision=finest_precision
    )
    returned = lax.all_to_all(
        tangent_out.astype(jnp.bfloat16), "expert", split_axis=0, concat_axis=0, tiled=True
    )
    results = (returned, reduced_hidden) + tuple(pieces)
    returned = results[0]
    reduced_hidden = results[1]
    hidden_rows = results[2]
    weight_rows = results[3]
    route_tangent = returned.reshape(experts * slot_most, model_width)[slot_index]
    out_tangent = jnp.sum(
        route_tangent.reshape(tok_rows, top_count, model_width).astype(jnp.float32), axis=1
    )
    resid_tangent = (curvature[:, None] * out_tangent).astype(jnp.bfloat16)
    send_tangent = spread(resid_tangent)
    residual_rows, tangent_rows = (
        lax.all_to_all(send_residual, "expert", split_axis=0, concat_axis=0, tiled=True),
        lax.all_to_all(send_tangent, "expert", split_axis=0, concat_axis=0, tiled=True),
    )
    residual_full = residual_rows.astype(jnp.float32)
    complete_tangent = tangent_rows.astype(jnp.float32)
    weight_column = weight_rows.astype(jnp.float32)[..., None]
    residual_reduced = jnp.einsum(
        "wyov,yqv->wyoq", residual_full, up_stacked, precision=finest_precision
    )
    reduced_tangent = jnp.einsum(
        "wyov,yqv->wyoq", complete_tangent, adapter_up, precision=finest_precision
    )
    left_terms = jnp.concatenate(
        [
            weight_column * residual_reduced[..., :adapter_rank],
            weight_column * (reduced_tangent + residual_reduced[..., adapter_rank:]),
        ],
        axis=3,
    )
    down_terms = jnp.einsum(
        "cjif,cjik->jfk", hidden_rows.astype(jnp.float32), left_terms, precision=finest_precision
    )
    raised_update = weight_column * reduced_hidden[..., :adapter_rank]
    raised_tangent_update = weight_column * reduced_hidden[..., adapter_rank:]
    up_terms = jnp.einsum(
        "cjik,cjid->jkd",
        jnp.concatenate([raised_update, raised_tangent_update], axis=3),
        residual_full,
        precision=finest_precision,
    )
    curvature_piece = up_terms[:, adapter_rank:] + jnp.einsum(
        "cjik,cjid->jkd", raised_update, complete_tangent, precision=finest_precision
    )
    return (
        down_terms[..., :adapter_rank],
        up_terms[:, :adapter_rank],
        down_terms[..., adapter_rank:],
        curvature_piece,
    )


def local(*arguments):
    factor_bytes = 2 * 4 * (arguments[6].size + arguments[7].size) * lax.axis_size("expert")
    fits = lax.axis_size("expert") == 16 and 4 * factor_bytes <= kernel_vmem
    plan = gathered_plan if fits else routed_plan
    return plan(*arguments)


def solution(mesh):
    return jax.shard_map(
        local,
        mesh=mesh,
        in_specs=(
            P(("groups", "expert"), None, None),
            P(("groups", "expert"), None),
            P(("groups", "expert"), None),
            P("groups"),
            P(("groups", "expert"), None),
            P(("groups", "expert")),
            P("expert", None, None),
            P("expert", None, None),
            P(("groups", "expert"), None, None),
            P(("groups", "expert"), None, None),
        ),
        out_specs=(
            P(("groups", "expert"), None, None),
            P(("groups", "expert"), None, None),
            P(("groups", "expert"), None, None),
            P(("groups", "expert"), None, None),
        ),
        check_vma=False,
    )
```

```python
import functools

import jax
import jax.numpy as jnp
from jax import lax
from jax.experimental import pallas as pl
from jax.experimental.pallas import tpu as pltpu
from jax.sharding import PartitionSpec as P

adapter_scale = 2.0
f32 = jnp.float32
bf16 = jnp.bfloat16
i16 = jnp.int16
lanes = 128
counts_lane = 64
kernel_vmem = 32 * 2**20
whole_vmem = 60 * 2**20


def halves(value):
    high = value.astype(bf16)
    return high, (value - high.astype(f32)).astype(bf16)


def dot(a, b, a_dim, b_dim):
    return lax.dot_general(a, b, (((a_dim,), (b_dim,)), ((), ())), preferred_element_type=f32)


def dot_pairs(a, b, a_dim, b_dim):
    return dot(a[0], b[0], a_dim, b_dim) + (dot(a[1], b[0], a_dim, b_dim) + dot(a[0], b[1], a_dim, b_dim))


def encode(down, up, counts=0.0):
    def scaled(value):
        largest = jnp.max(jnp.abs(value), axis=-1, keepdims=True)
        exponent = jnp.ceil(jnp.log2(jnp.maximum(largest, 1e-30)))
        coded = jnp.round(value * jnp.exp2(15.0 - exponent))
        return jnp.clip(coded, -32767.0, 32767.0), exponent

    down, down_exponent = scaled(down)
    up, up_exponent = scaled(up)
    lane = lax.broadcasted_iota(jnp.int32, down.shape[:-1] + (lanes,), down.ndim - 1)
    tail = jnp.where(lane < counts_lane // 2, down_exponent, up_exponent)
    tail = jnp.where(lane < counts_lane, tail, counts)
    return jnp.concatenate([down, up, tail], axis=-1).astype(jnp.int32).astype(i16)


def decode(coded, hidden_width):
    width = coded.shape[-1] - lanes
    value = coded.astype(jnp.int32).astype(f32)
    down_scale = jnp.exp2(value[..., width : width + 1] - 15.0)
    up_scale = jnp.exp2(value[..., width + counts_lane // 2 : width + counts_lane // 2 + 1] - 15.0)
    return value[..., :hidden_width] * down_scale, value[..., hidden_width:width] * up_scale


def prepare_kernel(experts, *refs):
    (piece_ref, small_ref), sem, refs = refs[7:9], refs[-1], refs[:7] + refs[9:-1]
    copies = [pltpu.make_async_copy(refs[i], refs[7 + i], sem.at[i]) for i in range(7)]
    for copy in copies:
        copy.start()
    for copy in copies:
        copy.wait()
    expert, gate, curvature, down_direction, adapter_down, adapter_up, up_direction = [ref[...] for ref in refs[7:]]
    top = expert.shape[0]
    small_ref[...] = jnp.zeros_like(small_ref)
    small_ref[:top] = expert.astype(f32)
    small_ref[top : 2 * top] = gate.astype(f32)
    small_ref[2 * top : 2 * top + 1] = curvature
    lane = lax.broadcasted_iota(jnp.int32, (1, lanes), 1)
    counts = jnp.zeros((1, lanes), f32)
    for number in range(experts):
        named = jnp.where(expert == number, 1.0, 0.0)
        total = jnp.sum(jnp.sum(named, axis=0, keepdims=True), axis=1, keepdims=True)
        counts = jnp.where(lane == counts_lane + number, total, counts)
    piece_ref[0] = encode(down_direction, adapter_up, counts)
    piece_ref[1] = encode(adapter_down, up_direction, counts)


def token_columns(small_ref, top):
    experts = [small_ref[:, k : k + 1] for k in range(top)]
    gates = [small_ref[:, top + k : top + k + 1] for k in range(top)]
    return experts, gates, small_ref[:, 2 * top : 2 * top + 1]


def members(place_ref, wide, first, count, dim=1):
    shape = (1, wide) if dim == 1 else (wide, 1)
    piece_of = lax.broadcasted_iota(jnp.int32, shape, dim) // (wide // count)
    found = jnp.zeros(shape, jnp.int32)
    for number in range(count):
        found = jnp.where(piece_of == number, place_ref[1 + first + number], found)
    return found.astype(f32)


def prior_kernel(place_ref, *rest):
    piece_refs, prior_ref = rest[:-1], rest[-1]
    me = place_ref[0]
    prior_ref[...] = jnp.zeros_like(prior_ref)
    for block, number in enumerate((me, me ^ 1)):
        total = jnp.zeros((1, lanes), f32)
        for arrival, piece_ref in enumerate(piece_refs):
            tail = piece_ref[0, :, piece_ref.shape[2] - lanes :]
            counts = tail.astype(jnp.int32).astype(f32)[0:1]
            total = total + jnp.where(place_ref[1 + arrival] < number, counts, 0.0)
        prior_ref[block : block + 1] = total


def piece_part(refs, arrival, kind, halved):
    if halved and arrival == len(refs) - 2:
        return refs[arrival + kind][0]
    return refs[arrival][kind]


def tokens_kernel(top, slots, place_ref, own_ref, other_ref, hidden_other_ref, gradient_other_ref, *outs):
    small_ref, rank_ref, gate_ref, same_ref, mask_ref, hidden_ref, gradient_ref, sem = outs
    copies = [
        pltpu.make_async_copy(hidden_other_ref, hidden_ref, sem.at[0]),
        pltpu.make_async_copy(gradient_other_ref, gradient_ref, sem.at[1]),
    ]
    for copy in copies:
        copy.start()
    small_ref[...] = jnp.concatenate([own_ref[...], other_ref[...]], axis=1).T
    experts, gates, _ = token_columns(small_ref, top)
    _, tokens, wide = rank_ref.shape
    column = members(place_ref, wide, slots, slots)
    below = (
        lax.broadcasted_iota(jnp.int32, (tokens, tokens), 0)
        > lax.broadcasted_iota(jnp.int32, (tokens, tokens), 1)
    )
    below = jnp.where(below, 1.0, 0.0).astype(bf16)
    rows = same_ref.shape[0]
    row = lax.broadcasted_iota(jnp.int32, (rows, tokens), 0)
    same = jnp.where(row // top == lax.broadcasted_iota(jnp.int32, (rows, tokens), 1), 1.0, 0.0).astype(bf16)
    same_ref[...] = same
    for core in range(2):
        tokens_of = slice(core * tokens, (core + 1) * tokens)
        gate = jnp.zeros((tokens, wide), f32)
        member = jnp.zeros((tokens, wide), f32)
        for k in range(top):
            named = experts[k][tokens_of] == column
            gate = jnp.where(named, gates[k][tokens_of], gate)
            member = jnp.where(named, 1.0, member)
        gate_ref[core] = gate
        rank_ref[core] = dot(below, member.astype(bf16), 1, 0)
        named = dot(same, small_ref[tokens_of].astype(bf16), 1, 0)
        position = lax.broadcasted_iota(jnp.int32, named.shape, 0) % top
        own = lax.broadcasted_iota(jnp.int32, named.shape, 1) == position
        expert = jnp.sum(jnp.where(own, named, 0.0), axis=1, keepdims=True)
        mask_ref[core] = jnp.where(expert == column, 1.0, 0.0).astype(bf16)
    for copy in copies:
        copy.wait()


def pass_kernel(behind_ref, ahead_ref, behind_out_ref, ahead_out_ref):
    behind_out_ref[...] = behind_ref[...]
    ahead_out_ref[...] = ahead_ref[...]


def reduce_kernel(top, first, count, halved, place_ref, small_ref, own_ref, other_ref, *rest):
    piece_refs, (reduced_ref, full_ref) = rest[:-2], rest[-2:]
    hidden_width = own_ref.shape[1]
    downs = [
        decode(piece_part(piece_refs, arrival, kind, halved), hidden_width)[0]
        for kind in range(2)
        for arrival in range(count)
    ]
    factor = jnp.concatenate(halves(jnp.concatenate(downs, axis=0)), axis=0)
    experts, _, _ = token_columns(small_ref, top)
    wide = reduced_ref.shape[1]
    column = members(place_ref, wide // 2, first, count)
    column = jnp.concatenate([column, column], axis=1)
    tokens = own_ref.shape[0] // top
    for core, hidden_ref in enumerate((own_ref, other_ref)):
        full = dot(hidden_ref[...], factor, 1, 1)
        full_ref[...] = full[:, :wide] + full[:, wide:]
        tokens_of = slice(core * tokens, (core + 1) * tokens)
        total = jnp.zeros((tokens, wide), f32)
        for k in range(top):
            here = full_ref[pl.ds(k, tokens, stride=top), :]
            total = jnp.where(experts[k][tokens_of] == column, here, total)
        reduced_ref[tokens_of] = total


def rank_limits(place_ref, wide, slots, capacity_ref, prior_ref, arrived_ref):
    lane = lax.broadcasted_iota(jnp.int32, (1, lanes), 1)
    piece_of = lax.broadcasted_iota(jnp.int32, (1, wide), 1) // (wide // slots)
    limits = []
    for block in range(2):
        total = capacity_ref[...] - prior_ref[block : block + 1] - arrived_ref[1 - block : 2 - block]
        limit = jnp.zeros((1, wide), f32)
        for slot in range(slots):
            picked = jnp.where(lane == counts_lane + place_ref[1 + slots + slot], total, 0.0)
            limit = jnp.where(piece_of == slot, jnp.sum(picked, axis=1, keepdims=True), limit)
        limits.append(limit)
    return limits


def tangent_kernel(
    slots, place_ref, rank_ref, gate_ref, capacity_ref, prior_ref, arrived_ref, early_ref, late_ref, *rest
):
    piece_refs = rest[: slots + 1]
    weight_ref, weighted_ref, tangent_ref, coded_ref, high_ref, low_ref = rest[slots + 1 :]
    _, wide = weight_ref.shape
    model_width = tangent_ref.shape[1]
    hidden_width = piece_refs[0].shape[2] - model_width - lanes
    limits = rank_limits(place_ref, wide, slots, capacity_ref, prior_ref, arrived_ref)
    weights = [
        jnp.where(rank_ref[core] < limits[core], adapter_scale * gate_ref[core], 0.0) for core in range(2)
    ]
    weight = jnp.concatenate(weights, axis=0)
    weight_ref[...] = weight
    half = wide // 2
    reduced = [
        jnp.concatenate([ref[:, kind * half : (kind + 1) * half] for ref in (early_ref, late_ref)], axis=1)
        for kind in range(2)
    ]
    rank = wide // slots
    by_arrival = members(place_ref, wide, 0, slots, 0) == members(place_ref, wide, slots, slots)
    row = lax.broadcasted_iota(jnp.int32, (wide, wide), 0)
    same_index = row % rank == lax.broadcasted_iota(jnp.int32, (wide, wide), 1) % rank
    order = jnp.where(by_arrival & same_index, 1.0, 0.0).astype(bf16)
    reduced = [sum(dot(part, order, 1, 0) for part in halves(both)) for both in reduced]
    weighted = jnp.concatenate([weight * part for part in reduced], axis=1)
    weighted_ref[...] = weighted
    for arrival in range(slots):
        for kind in range(2):
            _, up = decode(piece_part(piece_refs, arrival, kind, True), hidden_width)
            slot = place_ref[1 + 2 * slots + arrival]
            high_ref[kind, slot], low_ref[kind, slot] = halves(up)
    factor = high_ref[...].reshape(2 * wide, model_width), low_ref[...].reshape(2 * wide, model_width)
    tangent = dot_pairs(halves(weighted), factor, 1, 0)
    tangent_ref[...] = tangent
    coded_ref[...] = tangent.astype(bf16)


def put_left(left_ref, same_ref, mask_ref, terms):
    both = jnp.concatenate(halves(terms), axis=1)
    tokens = terms.shape[0] // 2
    for core in range(2):
        repeated = dot(same_ref[...], both[core * tokens : (core + 1) * tokens], 1, 0).astype(bf16)
        mask = mask_ref[core]
        left_ref[core] = repeated * jnp.concatenate([mask, mask], axis=1)


def add_halves(both):
    middle = both.shape[0] // 2
    return both[:middle] + both[middle:]


def put_chunks(keep_ref, near_ref, chunk_ref, far_ref, down, up):
    rank = keep_ref.shape[1]
    rows = down.shape[0] // rank // 2

    def slot(number):
        start = number * rank
        return down[start : start + rank], up[start : start + rank]

    for place in range(2):
        keep_ref[place] = jnp.concatenate(slot(place), axis=1)
        near_ref[place] = encode(*slot(rows + place))
        chunk_ref[place] = jnp.concatenate(slot(place * rows + 2), axis=1)
        far_ref[place] = encode(*slot(place * rows + 3))


def gradient_kernel(
    same_ref,
    mask_ref,
    own_ref,
    other_ref,
    own_gradient_ref,
    other_gradient_ref,
    weight_ref,
    weighted_ref,
    high_ref,
    low_ref,
    keep_ref,
    near_ref,
    chunk_ref,
    far_ref,
    up_ref,
    to_ref,
    left_ref,
):
    wide = weight_ref.shape[1]
    model_width = up_ref.shape[1]
    gradient = jnp.concatenate([own_gradient_ref[...], other_gradient_ref[...]], axis=0)
    high = high_ref[...].reshape(2 * wide, model_width)
    low = low_ref[...].reshape(2 * wide, model_width)
    to_both = dot(gradient, high, 1, 1) + dot(gradient, low, 1, 1)
    to_ref[...] = to_both[:, wide:]
    put_left(left_ref, same_ref, mask_ref, weight_ref[...] * to_both[:, :wide])
    down = dot(left_ref[0], own_ref[...], 0, 0) + dot(left_ref[1], other_ref[...], 0, 0)
    up = add_halves(dot(jnp.concatenate(halves(weighted_ref[...]), axis=1), gradient, 0, 0))
    up_ref[...] = up[:wide]
    put_chunks(keep_ref, near_ref, chunk_ref, far_ref, add_halves(down), up[wide:])


def curvature_kernel(
    top,
    small_ref,
    same_ref,
    mask_ref,
    own_ref,
    other_ref,
    weight_ref,
    weighted_ref,
    high_ref,
    low_ref,
    up_ref,
    to_ref,
    tangent_ref,
    arrived_ref,
    keep_ref,
    near_ref,
    chunk_ref,
    far_ref,
    left_ref,
):
    _, _, curvature = token_columns(small_ref, top)
    tokens, wide = weight_ref.shape
    block = tokens // 2
    model_width = up_ref.shape[1]
    arrived = jnp.concatenate([arrived_ref[block:], arrived_ref[:block]], axis=0).astype(f32)
    resid = halves(curvature * (tangent_ref[...] + arrived))
    adapter_up = high_ref[0].reshape(wide, model_width), low_ref[0].reshape(wide, model_width)
    terms = weight_ref[...] * (dot_pairs(resid, adapter_up, 1, 1) + to_ref[...])
    put_left(left_ref, same_ref, mask_ref, terms)
    down = dot(left_ref[0], own_ref[...], 0, 0) + dot(left_ref[1], other_ref[...], 0, 0)
    weighted_u = halves(weighted_ref[:, wide:])
    up = add_halves(dot(jnp.concatenate(weighted_u, axis=1), resid[0], 0, 0)) + dot(weighted_u[0], resid[1], 0, 0)
    put_chunks(keep_ref, near_ref, chunk_ref, far_ref, add_halves(down), up_ref[...] + up)


def pair_kernel(hidden_width, arrived_ref, chunk_ref, near_ref, across_ref, keep_ref, onward_ref):
    onward_ref[...] = near_ref[...]
    for x in range(2):
        down, up = decode(arrived_ref[x], hidden_width)
        down, up = chunk_ref[x, :, :hidden_width] + down, chunk_ref[x, :, hidden_width:] + up
        if x == 0:
            keep_ref[...] = jnp.concatenate([down, up], axis=1)
        else:
            across_ref[...] = encode(down, up)


def far_kernel(hidden_width, arrived_ref, keep_ref, out_ref):
    down, up = decode(arrived_ref[...], hidden_width)
    out_ref[...] = encode(keep_ref[:, :hidden_width] + down, keep_ref[:, hidden_width:] + up)


def near_kernel(
    hidden_width, gradient_ref, curvature_ref, gradient_keep_ref, curvature_keep_ref, onward_ref, total_ref
):
    pairs = ((gradient_ref, gradient_keep_ref), (curvature_ref, curvature_keep_ref))
    for kind, (arrived_ref, keep_ref) in enumerate(pairs):
        for z in range(2):
            down, up = decode(arrived_ref[z], hidden_width)
            down, up = keep_ref[z, :, :hidden_width] + down, keep_ref[z, :, hidden_width:] + up
            if z == 0:
                total_ref[kind] = jnp.concatenate([down, up], axis=1)
            else:
                onward_ref[kind] = encode(down, up)


def add_kernel(hidden_width, total_ref, arrived_ref, out_ref):
    down, up = decode(arrived_ref[...], hidden_width)
    out_ref[:, :hidden_width] = total_ref[0, :, :hidden_width] + down
    out_ref[:, hidden_width:] = total_ref[0, :, hidden_width:] + up


def total_kernel(hidden_width, gradient_ref, total_ref, far_ref, pair_ref, *out_refs):
    far = decode(far_ref[...], hidden_width)
    totals = [
        (gradient_ref[:, :hidden_width], gradient_ref[:, hidden_width:]),
        (total_ref[1, :, :hidden_width] + far[0], total_ref[1, :, hidden_width:] + far[1]),
    ]
    for kind in range(2):
        down, up = decode(pair_ref[kind], hidden_width)
        out_refs[2 * kind][...] = totals[kind][0] + down
        out_refs[2 * kind + 1][...] = totals[kind][1] + up


class Ring:
    def __init__(self, size):
        self.length = size // 2
        rows = self.length // 2
        self.order = [4 * z for z in range(rows)] + [4 * z + 2 for z in reversed(range(rows))]

    def shift(self, value, step):
        pairs = [
            (chip + core, self.order[(place + step) % self.length] + core)
            for place, chip in enumerate(self.order)
            for core in range(2)
        ]
        return lax.ppermute(value, "expert", pairs)

    def members(self, me):
        rows = self.length // 2
        place = jnp.where(me // 2 % 2 == 0, me // 4, self.length - 1 - me // 4)
        half = self.length // 2
        offsets = [0] + [offset for step in range(1, half) for offset in (self.length - step, step)] + [half]
        there = (place + jnp.array(offsets, jnp.int32)) % self.length
        return jnp.where(there < rows, 4 * there, 4 * (self.length - 1 - there) + 2) + me % 2

    def gather(self, own, passing):
        half = self.length // 2
        pieces = [own]
        ahead, behind = own, own
        for step in range(1, half):
            behind = self.shift(behind, 1)
            ahead = self.shift(ahead, -1)
            if step == 1:
                behind, ahead = passing(behind, ahead)
            pieces += [behind, ahead]
        pieces += [self.shift(behind[:1], 1), self.shift(ahead[1:], -1)]
        return pieces


def exchange(value, mask):
    size = lax.axis_size("expert")
    return lax.ppermute(value, "expert", [(device, device ^ mask) for device in range(size)])


def gathered_plan(
    hidden_of_route,
    expert_of_route,
    gate_of_route,
    capacity,
    output_gradient,
    curvature,
    adapter_down,
    adapter_up,
    down_direction,
    up_direction,
):
    ring = Ring(lax.axis_size("expert"))
    slots = ring.length
    rows = slots // 2
    masks = [4 * z for z in range(rows)] + [4 * z + 2 for z in range(rows)]
    me = lax.axis_index("expert")
    tokens, top = expert_of_route.shape
    both = 2 * tokens
    hidden_width = hidden_of_route.shape[2]
    rank = adapter_down.shape[2]
    model_width = output_gradient.shape[1]
    experts = capacity.shape[0]
    wide = slots * rank
    coded_width = hidden_width + model_width + lanes


    place = []

    def call(kernel, multiplies, outs, *operands, scratch=(), after=(), grant=kernel_vmem):
        space = pltpu.VMEM if grant == kernel_vmem else pltpu.HBM
        places = [pl.BlockSpec(memory_space=pl.ANY) for _ in after] + [
            pl.BlockSpec(memory_space=pltpu.SMEM if any(operand is it for it in place) else space) for operand in operands
        ]
        return pl.pallas_call(
            lambda *refs: kernel(*refs[len(after) :]),
            out_shape=[jax.ShapeDtypeStruct(shape, dtype) for shape, dtype in outs],
            in_specs=places,
            scratch_shapes=scratch,
            compiler_params=pltpu.CompilerParams(vmem_limit_bytes=grant),
            cost_estimate=pl.CostEstimate(flops=2 * multiplies, bytes_accessed=2**20, transcendentals=0),
        )(*after, *operands)

    down_multiplies = 2 * top * both * hidden_width * wide
    up_multiplies = both * model_width * wide

    first = (
        expert_of_route.T,
        gate_of_route.T,
        curvature[None],
        down_direction[0].T,
        adapter_down[0].T,
        adapter_up[0],
        up_direction[0],
    )
    piece, small = call(
        functools.partial(prepare_kernel, experts),
        10**8,
        [((2, rank, coded_width), i16), (((2 * top + 8) // 8 * 8, tokens), f32)],
        *first,
        scratch=[pltpu.VMEM(operand.shape, operand.dtype) for operand in first]
        + [pltpu.SemaphoreType.DMA((len(first),))],
        grant=whole_vmem,
    )
    arrivals = ring.members(me)
    slot_of_arrival = (arrivals ^ me) // 4 + rows * ((arrivals ^ me) // 2 % 2)
    place.append(jnp.concatenate([me[None], arrivals, me ^ jnp.array(masks, jnp.int32), slot_of_arrival]).astype(jnp.int32))
    small_other = exchange(small, 1)
    hidden = hidden_of_route.reshape(tokens * top, hidden_width)
    small_columns, local_rank, gate, same, mask, hidden_other, gradient_other = call(
        functools.partial(tokens_kernel, top, slots),
        10**9,
        [
            ((both, small.shape[0]), f32),
            ((2, tokens, wide), f32),
            ((2, tokens, wide), f32),
            ((top * tokens, tokens), bf16),
            ((2, top * tokens, wide), bf16),
            (hidden.shape, bf16),
            (output_gradient.shape, bf16),
        ],
        *place,
        small,
        small_other,
        exchange(hidden, 1),
        exchange(output_gradient, 1),
        scratch=[pltpu.SemaphoreType.DMA((2,))],
    )
    def passing(behind, ahead):
        return call(pass_kernel, 10**8, [(piece.shape, i16)] * 2, behind, ahead, after=[same])

    pieces = ring.gather(piece, passing)
    capacity_row = jnp.pad(capacity.astype(f32), (counts_lane, lanes - counts_lane - experts))[None, :]

    def reduced(first, count, halved, *parts, after=()):
        return call(
            functools.partial(reduce_kernel, top, first, count, halved),
            2 * down_multiplies * count // slots,
            [((both, 2 * count * rank), f32)],
            *place,
            small_columns,
            hidden,
            hidden_other,
            *parts,
            scratch=[pltpu.VMEM((tokens * top, 2 * count * rank), f32)],
            after=after,
        )[0]

    early = slots // 2
    reduced_early = reduced(0, early, False, *pieces[:early])
    (prior,) = call(prior_kernel, 10**8, [((8, lanes), f32)], *place, *pieces[:-1], after=[reduced_early])
    prior_arrived = exchange(prior, 1)
    reduced_late = reduced(early, slots - early, True, *pieces[early:], after=[prior])
    weight, weighted, tangent, coded, high, low = call(
        functools.partial(tangent_kernel, slots),
        6 * up_multiplies,
        [
            ((both, wide), f32),
            ((both, 2 * wide), f32),
            ((both, model_width), f32),
            ((both, model_width), bf16),
            ((2, slots, rank, model_width), bf16),
            ((2, slots, rank, model_width), bf16),
        ],
        *place,
        local_rank,
        gate,
        capacity_row,
        prior,
        prior_arrived,
        reduced_early,
        reduced_late,
        *pieces,
    )
    arrived = exchange(coded, 1)
    left = [pltpu.VMEM((2, top * tokens, 2 * wide), bf16)]
    chunks = [((2, rank, hidden_width + model_width), f32), ((2, rank, coded_width), i16)] * 2
    gradient_keep, gradient_near, gradient_chunk, gradient_far, up, to = call(
        gradient_kernel,
        down_multiplies + 8 * up_multiplies,
        chunks + [((wide, model_width), f32), ((both, wide), f32)],
        same,
        mask,
        hidden,
        hidden_other,
        output_gradient,
        gradient_other,
        weight,
        weighted,
        high,
        low,
        scratch=left,
    )
    gradient_far = exchange(gradient_far, 4)
    gradient_near = exchange(gradient_near, 2)
    curvature_keep, curvature_near, curvature_chunk, curvature_far = call(
        functools.partial(curvature_kernel, top),
        down_multiplies + 6 * up_multiplies,
        chunks,
        small_columns,
        same,
        mask,
        hidden,
        hidden_other,
        weight,
        weighted,
        high,
        low,
        up,
        to,
        tangent,
        arrived,
        scratch=left,
    )

    hop = 2 * 10**9

    one = (rank, hidden_width + model_width)
    one_coded = (rank, coded_width)

    def hop_call(kernel, outs, *operands, after=()):
        return call(functools.partial(kernel, hidden_width), hop, outs, *operands, after=after)

    curvature_far = exchange(curvature_far, 4)
    pair = [(one_coded, i16), (one, f32), ((2,) + one_coded, i16)]
    gradient_across, gradient_pair, curvature_near = hop_call(
        pair_kernel, pair, gradient_far, gradient_chunk, curvature_near, after=[curvature_keep]
    )
    curvature_near = exchange(curvature_near, 2)
    curvature_across, curvature_pair, gradient_near = hop_call(
        pair_kernel, pair, curvature_far, curvature_chunk, gradient_near, after=[gradient_across]
    )
    (gradient_beyond,) = hop_call(
        far_kernel,
        [(one_coded, i16)],
        exchange(gradient_across, 2),
        gradient_pair,
        after=[curvature_across],
    )
    onward, total = hop_call(
        near_kernel,
        [((2,) + one_coded, i16), ((2,) + one, f32)],
        gradient_near,
        curvature_near,
        gradient_keep,
        curvature_keep,
        after=[gradient_beyond],
    )
    (curvature_beyond,) = hop_call(
        far_kernel, [(one_coded, i16)], exchange(curvature_across, 2), curvature_pair, after=[onward]
    )
    (gradient_total,) = hop_call(
        add_kernel, [(one, f32)], total, exchange(gradient_beyond, 8), after=[curvature_beyond]
    )
    down_gradient, up_gradient, curvature_down, curvature_up = hop_call(
        total_kernel,
        [((rank, hidden_width), f32), ((rank, model_width), f32)] * 2,
        gradient_total,
        total,
        exchange(curvature_beyond, 8),
        exchange(onward, 4),
    )
    return down_gradient.T[None], up_gradient[None], curvature_down.T[None], curvature_up[None]


def carried_in(value, axis, join, neutral):
    count, mine = (lax.axis_size(axis), lax.axis_index(axis))
    pieces = lax.all_gather(value, axis)
    so_far = jnp.full_like(value, 0) + jnp.asarray(neutral, value.dtype)

    def lap(position, so_far):
        longer = join(so_far, pieces[position])
        return jnp.where(position < mine, longer, so_far)

    return lax.fori_loop(0, count - 1, lap, so_far)


def add_counts(earlier, later):
    return earlier + later


def routed_plan(
    hidden_of_route,
    expert_of_route,
    gate_of_route,
    capacity,
    output_gradient,
    curvature,
    adapter_down,
    adapter_up,
    down_direction,
    up_direction,
):
    finest_precision = lax.Precision.HIGHEST
    group_size = lax.axis_size("expert")
    tok_rows, top_count = expert_of_route.shape
    hidden_width = hidden_of_route.shape[2]
    resident_experts = adapter_down.shape[0]
    adapter_rank = adapter_down.shape[2]
    model_width = output_gradient.shape[1]
    experts = resident_experts * group_size
    slot_most = 2 * tok_rows * top_count // experts
    routes = expert_of_route.reshape(-1)
    onehot = (routes[:, None] == jnp.arange(experts, dtype=jnp.int32)[None, :]).astype(jnp.int32)
    earlier = jnp.cumsum(onehot, axis=0) - onehot
    local_rank = jnp.sum(earlier * onehot, axis=1)
    counts = jnp.sum(onehot, axis=0)
    prior_count = carried_in(counts, "expert", add_counts, jnp.zeros_like(counts))
    global_rank = local_rank + jnp.sum(onehot * prior_count[None, :], axis=1)
    route_limit = jnp.sum(onehot * capacity[None, :], axis=1)
    retained_mask = (global_rank < route_limit).astype(jnp.float32)
    weight_of_route = (
        adapter_scale * gate_of_route.reshape(-1).astype(jnp.float32) * retained_mask
    ).astype(jnp.bfloat16)
    slot_index = routes * slot_most + local_rank
    layout = (group_size, resident_experts, slot_most)
    send_hidden = (
        jnp.zeros((experts * slot_most, hidden_width), jnp.bfloat16)
        .at[slot_index]
        .set(hidden_of_route.reshape(-1, hidden_width))
        .reshape(layout + (hidden_width,))
    )
    send_weight = (
        jnp.zeros((experts * slot_most,), jnp.bfloat16)
        .at[slot_index]
        .set(weight_of_route)
        .reshape(layout)
    )
    down_stacked = jnp.concatenate([adapter_down, down_direction], axis=2)
    up_stacked = jnp.concatenate([adapter_up, up_direction], axis=1)

    def spread(token_rows):
        per_route = jnp.repeat(token_rows, top_count, axis=0)
        placed = (
            jnp.zeros((experts * slot_most, model_width), jnp.bfloat16)
            .at[slot_index]
            .set(per_route)
        )
        return placed.reshape(layout + (model_width,))

    send_residual = spread(output_gradient)
    pieces = (
        lax.all_to_all(send_hidden, "expert", split_axis=0, concat_axis=0, tiled=True),
        lax.all_to_all(send_weight, "expert", split_axis=0, concat_axis=0, tiled=True),
    )
    hidden_rows = pieces[0].astype(jnp.float32)
    weight_rows = pieces[1].astype(jnp.float32)[..., None]
    reduced_hidden = jnp.einsum(
        "cjif,jfk->cjik", hidden_rows, down_stacked, precision=finest_precision
    )
    exchanged_rows = jnp.concatenate(
        [reduced_hidden[..., adapter_rank:], reduced_hidden[..., :adapter_rank]], axis=3
    )
    tangent_out = weight_rows * jnp.einsum(
        "cjik,jkd->cjid", exchanged_rows, up_stacked, precision=finest_precision
    )
    returned = lax.all_to_all(
        tangent_out.astype(jnp.bfloat16), "expert", split_axis=0, concat_axis=0, tiled=True
    )
    results = (returned, reduced_hidden) + tuple(pieces)
    returned = results[0]
    reduced_hidden = results[1]
    hidden_rows = results[2]
    weight_rows = results[3]
    route_tangent = returned.reshape(experts * slot_most, model_width)[slot_index]
    out_tangent = jnp.sum(
        route_tangent.reshape(tok_rows, top_count, model_width).astype(jnp.float32), axis=1
    )
    resid_tangent = (curvature[:, None] * out_tangent).astype(jnp.bfloat16)
    send_tangent = spread(resid_tangent)
    residual_rows, tangent_rows = (
        lax.all_to_all(send_residual, "expert", split_axis=0, concat_axis=0, tiled=True),
        lax.all_to_all(send_tangent, "expert", split_axis=0, concat_axis=0, tiled=True),
    )
    residual_full = residual_rows.astype(jnp.float32)
    complete_tangent = tangent_rows.astype(jnp.float32)
    weight_column = weight_rows.astype(jnp.float32)[..., None]
    residual_reduced = jnp.einsum(
        "wyov,yqv->wyoq", residual_full, up_stacked, precision=finest_precision
    )
    reduced_tangent = jnp.einsum(
        "wyov,yqv->wyoq", complete_tangent, adapter_up, precision=finest_precision
    )
    left_terms = jnp.concatenate(
        [
            weight_column * residual_reduced[..., :adapter_rank],
            weight_column * (reduced_tangent + residual_reduced[..., adapter_rank:]),
        ],
        axis=3,
    )
    down_terms = jnp.einsum(
        "cjif,cjik->jfk", hidden_rows.astype(jnp.float32), left_terms, precision=finest_precision
    )
    raised_update = weight_column * reduced_hidden[..., :adapter_rank]
    raised_tangent_update = weight_column * reduced_hidden[..., adapter_rank:]
    up_terms = jnp.einsum(
        "cjik,cjid->jkd",
        jnp.concatenate([raised_update, raised_tangent_update], axis=3),
        residual_full,
        precision=finest_precision,
    )
    curvature_piece = up_terms[:, adapter_rank:] + jnp.einsum(
        "cjik,cjid->jkd", raised_update, complete_tangent, precision=finest_precision
    )
    return (
        down_terms[..., :adapter_rank],
        up_terms[:, :adapter_rank],
        down_terms[..., adapter_rank:],
        curvature_piece,
    )


def local(*arguments):
    factor_bytes = 2 * 4 * (arguments[6].size + arguments[7].size) * lax.axis_size("expert")
    fits = lax.axis_size("expert") == 16 and 4 * factor_bytes <= kernel_vmem
    plan = gathered_plan if fits else routed_plan
    return plan(*arguments)


def solution(mesh):
    return jax.shard_map(
        local,
        mesh=mesh,
        in_specs=(
            P(("groups", "expert"), None, None),
            P(("groups", "expert"), None),
            P(("groups", "expert"), None),
            P("groups"),
            P(("groups", "expert"), None),
            P(("groups", "expert")),
            P("expert", None, None),
            P("expert", None, None),
            P(("groups", "expert"), None, None),
            P(("groups", "expert"), None, None),
        ),
        out_specs=(
            P(("groups", "expert"), None, None),
            P(("groups", "expert"), None, None),
            P(("groups", "expert"), None, None),
            P(("groups", "expert"), None, None),
        ),
        check_vma=False,
    )
```

```python
import functools

import jax
import jax.numpy as jnp
from jax import lax
from jax.experimental import pallas as pl
from jax.experimental.pallas import tpu as pltpu
from jax.sharding import PartitionSpec as P

adapter_scale = 2.0
f32 = jnp.float32
bf16 = jnp.bfloat16
i16 = jnp.int16
lanes = 128
counts_lane = 64
kernel_vmem = 32 * 2**20
whole_vmem = 60 * 2**20


def halves(value):
    high = value.astype(bf16)
    return high, (value - high.astype(f32)).astype(bf16)


def dot(a, b, a_dim, b_dim):
    return lax.dot_general(a, b, (((a_dim,), (b_dim,)), ((), ())), preferred_element_type=f32)


def dot_pairs(a, b, a_dim, b_dim):
    return dot(a[0], b[0], a_dim, b_dim) + (dot(a[1], b[0], a_dim, b_dim) + dot(a[0], b[1], a_dim, b_dim))


def encode(down, up, counts=0.0):
    def scaled(value):
        largest = jnp.max(jnp.abs(value), axis=-1, keepdims=True)
        exponent = jnp.ceil(jnp.log2(jnp.maximum(largest, 1e-30)))
        coded = jnp.round(value * jnp.exp2(15.0 - exponent))
        return jnp.clip(coded, -32767.0, 32767.0), exponent

    down, down_exponent = scaled(down)
    up, up_exponent = scaled(up)
    lane = lax.broadcasted_iota(jnp.int32, down.shape[:-1] + (lanes,), down.ndim - 1)
    tail = jnp.where(lane < counts_lane // 2, down_exponent, up_exponent)
    tail = jnp.where(lane < counts_lane, tail, counts)
    return jnp.concatenate([down, up, tail], axis=-1).astype(jnp.int32).astype(i16)


def decode(coded, hidden_width):
    width = coded.shape[-1] - lanes
    value = coded.astype(jnp.int32).astype(f32)
    down_scale = jnp.exp2(value[..., width : width + 1] - 15.0)
    up_scale = jnp.exp2(value[..., width + counts_lane // 2 : width + counts_lane // 2 + 1] - 15.0)
    return value[..., :hidden_width] * down_scale, value[..., hidden_width:width] * up_scale


def prepare_kernel(experts, *refs):
    (piece_ref, small_ref), sem, refs = refs[7:9], refs[-1], refs[:7] + refs[9:-1]
    copies = [pltpu.make_async_copy(refs[i], refs[7 + i], sem.at[i]) for i in range(7)]
    for copy in copies:
        copy.start()
    for copy in copies:
        copy.wait()
    expert, gate, curvature, down_direction, adapter_down, adapter_up, up_direction = [ref[...] for ref in refs[7:]]
    top = expert.shape[0]
    small_ref[...] = jnp.zeros_like(small_ref)
    small_ref[:top] = expert.astype(f32)
    small_ref[top : 2 * top] = gate.astype(f32)
    small_ref[2 * top : 2 * top + 1] = curvature
    lane = lax.broadcasted_iota(jnp.int32, (1, lanes), 1)
    counts = jnp.zeros((1, lanes), f32)
    for number in range(experts):
        named = jnp.where(expert == number, 1.0, 0.0)
        total = jnp.sum(jnp.sum(named, axis=0, keepdims=True), axis=1, keepdims=True)
        counts = jnp.where(lane == counts_lane + number, total, counts)
    piece_ref[0] = encode(down_direction, adapter_up, counts)
    piece_ref[1] = encode(adapter_down, up_direction, counts)


def token_columns(small_ref, top):
    experts = [small_ref[:, k : k + 1] for k in range(top)]
    gates = [small_ref[:, top + k : top + k + 1] for k in range(top)]
    return experts, gates, small_ref[:, 2 * top : 2 * top + 1]


def members(place_ref, wide, first, count, dim=1):
    shape = (1, wide) if dim == 1 else (wide, 1)
    piece_of = lax.broadcasted_iota(jnp.int32, shape, dim) // (wide // count)
    found = jnp.zeros(shape, jnp.int32)
    for number in range(count):
        found = jnp.where(piece_of == number, place_ref[1 + first + number], found)
    return found.astype(f32)


def prior_kernel(place_ref, *rest):
    piece_refs, prior_ref = rest[:-1], rest[-1]
    me = place_ref[0]
    prior_ref[...] = jnp.zeros_like(prior_ref)
    for block, number in enumerate((me, me ^ 1)):
        total = jnp.zeros((1, lanes), f32)
        for arrival, piece_ref in enumerate(piece_refs):
            tail = piece_ref[0, :, piece_ref.shape[2] - lanes :]
            counts = tail.astype(jnp.int32).astype(f32)[0:1]
            total = total + jnp.where(place_ref[1 + arrival] < number, counts, 0.0)
        prior_ref[block : block + 1] = total


def piece_part(refs, arrival, kind, halved):
    if halved and arrival == len(refs) - 2:
        return refs[arrival + kind][0]
    return refs[arrival][kind]


def tokens_kernel(top, slots, place_ref, own_ref, other_ref, hidden_other_ref, gradient_other_ref, *outs):
    small_ref, rank_ref, gate_ref, same_ref, mask_ref, hidden_ref, gradient_ref, sem = outs
    copies = [
        pltpu.make_async_copy(hidden_other_ref, hidden_ref, sem.at[0]),
        pltpu.make_async_copy(gradient_other_ref, gradient_ref, sem.at[1]),
    ]
    for copy in copies:
        copy.start()
    small_ref[...] = jnp.concatenate([own_ref[...], other_ref[...]], axis=1).T
    experts, gates, _ = token_columns(small_ref, top)
    _, tokens, wide = rank_ref.shape
    column = members(place_ref, wide, slots, slots)
    below = (
        lax.broadcasted_iota(jnp.int32, (tokens, tokens), 0)
        > lax.broadcasted_iota(jnp.int32, (tokens, tokens), 1)
    )
    below = jnp.where(below, 1.0, 0.0).astype(bf16)
    rows = same_ref.shape[0]
    row = lax.broadcasted_iota(jnp.int32, (rows, tokens), 0)
    same = jnp.where(row // top == lax.broadcasted_iota(jnp.int32, (rows, tokens), 1), 1.0, 0.0).astype(bf16)
    same_ref[...] = same
    for core in range(2):
        tokens_of = slice(core * tokens, (core + 1) * tokens)
        gate = jnp.zeros((tokens, wide), f32)
        member = jnp.zeros((tokens, wide), f32)
        for k in range(top):
            named = experts[k][tokens_of] == column
            gate = jnp.where(named, gates[k][tokens_of], gate)
            member = jnp.where(named, 1.0, member)
        gate_ref[core] = gate
        rank_ref[core] = dot(below, member.astype(bf16), 1, 0)
        named = dot(same, small_ref[tokens_of].astype(bf16), 1, 0)
        position = lax.broadcasted_iota(jnp.int32, named.shape, 0) % top
        own = lax.broadcasted_iota(jnp.int32, named.shape, 1) == position
        expert = jnp.sum(jnp.where(own, named, 0.0), axis=1, keepdims=True)
        mask_ref[core] = jnp.where(expert == column, 1.0, 0.0).astype(bf16)
    for copy in copies:
        copy.wait()


def pass_kernel(behind_ref, ahead_ref, behind_out_ref, ahead_out_ref):
    behind_out_ref[...] = behind_ref[...]
    ahead_out_ref[...] = ahead_ref[...]


def reduce_kernel(top, first, count, halved, place_ref, small_ref, own_ref, other_ref, *rest):
    piece_refs, (reduced_ref, full_ref) = rest[:-2], rest[-2:]
    hidden_width = own_ref.shape[1]
    downs = [
        decode(piece_part(piece_refs, arrival, kind, halved), hidden_width)[0]
        for kind in range(2)
        for arrival in range(count)
    ]
    factor = jnp.concatenate(halves(jnp.concatenate(downs, axis=0)), axis=0)
    experts, _, _ = token_columns(small_ref, top)
    wide = reduced_ref.shape[1]
    column = members(place_ref, wide // 2, first, count)
    column = jnp.concatenate([column, column], axis=1)
    tokens = own_ref.shape[0] // top
    for core, hidden_ref in enumerate((own_ref, other_ref)):
        full = dot(hidden_ref[...], factor, 1, 1)
        full_ref[...] = full[:, :wide] + full[:, wide:]
        tokens_of = slice(core * tokens, (core + 1) * tokens)
        total = jnp.zeros((tokens, wide), f32)
        for k in range(top):
            here = full_ref[pl.ds(k, tokens, stride=top), :]
            total = jnp.where(experts[k][tokens_of] == column, here, total)
        reduced_ref[tokens_of] = total


def rank_limits(place_ref, wide, slots, capacity_ref, prior_ref, arrived_ref):
    lane = lax.broadcasted_iota(jnp.int32, (1, lanes), 1)
    piece_of = lax.broadcasted_iota(jnp.int32, (1, wide), 1) // (wide // slots)
    limits = []
    for block in range(2):
        total = capacity_ref[...] - prior_ref[block : block + 1] - arrived_ref[1 - block : 2 - block]
        limit = jnp.zeros((1, wide), f32)
        for slot in range(slots):
            picked = jnp.where(lane == counts_lane + place_ref[1 + slots + slot], total, 0.0)
            limit = jnp.where(piece_of == slot, jnp.sum(picked, axis=1, keepdims=True), limit)
        limits.append(limit)
    return limits


def tangent_kernel(
    slots, place_ref, rank_ref, gate_ref, capacity_ref, prior_ref, arrived_ref, early_ref, late_ref, *rest
):
    piece_refs = rest[: slots + 1]
    weight_ref, weighted_ref, tangent_ref, coded_ref, high_ref, low_ref = rest[slots + 1 :]
    _, wide = weight_ref.shape
    model_width = tangent_ref.shape[1]
    hidden_width = piece_refs[0].shape[2] - model_width - lanes
    limits = rank_limits(place_ref, wide, slots, capacity_ref, prior_ref, arrived_ref)
    weights = [
        jnp.where(rank_ref[core] < limits[core], adapter_scale * gate_ref[core], 0.0) for core in range(2)
    ]
    weight = jnp.concatenate(weights, axis=0)
    weight_ref[...] = weight
    half = wide // 2
    reduced = [
        jnp.concatenate([ref[:, kind * half : (kind + 1) * half] for ref in (early_ref, late_ref)], axis=1)
        for kind in range(2)
    ]
    rank = wide // slots
    by_arrival = members(place_ref, wide, 0, slots, 0) == members(place_ref, wide, slots, slots)
    row = lax.broadcasted_iota(jnp.int32, (wide, wide), 0)
    same_index = row % rank == lax.broadcasted_iota(jnp.int32, (wide, wide), 1) % rank
    order = jnp.where(by_arrival & same_index, 1.0, 0.0).astype(bf16)
    reduced = [sum(dot(part, order, 1, 0) for part in halves(both)) for both in reduced]
    weighted = jnp.concatenate([weight * part for part in reduced], axis=1)
    weighted_ref[...] = weighted
    for arrival in range(slots):
        for kind in range(2):
            _, up = decode(piece_part(piece_refs, arrival, kind, True), hidden_width)
            slot = place_ref[1 + 2 * slots + arrival]
            high_ref[kind, slot], low_ref[kind, slot] = halves(up)
    factor = high_ref[...].reshape(2 * wide, model_width), low_ref[...].reshape(2 * wide, model_width)
    tangent = dot_pairs(halves(weighted), factor, 1, 0)
    tangent_ref[...] = tangent
    coded_ref[...] = tangent.astype(bf16)


def put_left(left_ref, same_ref, mask_ref, terms):
    both = jnp.concatenate(halves(terms), axis=1)
    tokens = terms.shape[0] // 2
    for core in range(2):
        repeated = dot(same_ref[...], both[core * tokens : (core + 1) * tokens], 1, 0).astype(bf16)
        mask = mask_ref[core]
        left_ref[core] = repeated * jnp.concatenate([mask, mask], axis=1)


def add_halves(both):
    middle = both.shape[0] // 2
    return both[:middle] + both[middle:]


def put_chunks(keep_ref, near_ref, chunk_ref, far_ref, down, up):
    rank = keep_ref.shape[1]
    rows = down.shape[0] // rank // 2

    def slot(number):
        start = number * rank
        return down[start : start + rank], up[start : start + rank]

    for place in range(2):
        keep_ref[place] = jnp.concatenate(slot(place), axis=1)
        near_ref[place] = encode(*slot(rows + place))
        chunk_ref[place] = jnp.concatenate(slot(place * rows + 2), axis=1)
        far_ref[place] = encode(*slot(place * rows + 3))


def gradient_kernel(
    same_ref,
    mask_ref,
    own_ref,
    other_ref,
    own_gradient_ref,
    other_gradient_ref,
    weight_ref,
    weighted_ref,
    high_ref,
    low_ref,
    keep_ref,
    near_ref,
    chunk_ref,
    far_ref,
    up_ref,
    to_ref,
    left_ref,
):
    wide = weight_ref.shape[1]
    model_width = up_ref.shape[1]
    gradient = jnp.concatenate([own_gradient_ref[...], other_gradient_ref[...]], axis=0)
    high = high_ref[...].reshape(2 * wide, model_width)
    low = low_ref[...].reshape(2 * wide, model_width)
    to_both = dot(gradient, high, 1, 1) + dot(gradient, low, 1, 1)
    to_ref[...] = to_both[:, wide:]
    put_left(left_ref, same_ref, mask_ref, weight_ref[...] * to_both[:, :wide])
    down = dot(left_ref[0], own_ref[...], 0, 0) + dot(left_ref[1], other_ref[...], 0, 0)
    up = add_halves(dot(jnp.concatenate(halves(weighted_ref[...]), axis=1), gradient, 0, 0))
    up_ref[...] = up[:wide]
    put_chunks(keep_ref, near_ref, chunk_ref, far_ref, add_halves(down), up[wide:])


def curvature_kernel(
    top,
    small_ref,
    same_ref,
    mask_ref,
    own_ref,
    other_ref,
    weight_ref,
    weighted_ref,
    high_ref,
    low_ref,
    up_ref,
    to_ref,
    tangent_ref,
    arrived_ref,
    keep_ref,
    near_ref,
    chunk_ref,
    far_ref,
    left_ref,
):
    _, _, curvature = token_columns(small_ref, top)
    tokens, wide = weight_ref.shape
    block = tokens // 2
    model_width = up_ref.shape[1]
    arrived = jnp.concatenate([arrived_ref[block:], arrived_ref[:block]], axis=0).astype(f32)
    resid = (curvature * (tangent_ref[...] + arrived)).astype(bf16)
    adapter_up = high_ref[0].reshape(wide, model_width), low_ref[0].reshape(wide, model_width)
    terms = weight_ref[...] * (dot(resid, adapter_up[0], 1, 1) + dot(resid, adapter_up[1], 1, 1) + to_ref[...])
    put_left(left_ref, same_ref, mask_ref, terms)
    down = dot(left_ref[0], own_ref[...], 0, 0) + dot(left_ref[1], other_ref[...], 0, 0)
    weighted_u = halves(weighted_ref[:, wide:])
    up = add_halves(dot(jnp.concatenate(weighted_u, axis=1), resid, 0, 0))
    put_chunks(keep_ref, near_ref, chunk_ref, far_ref, add_halves(down), up_ref[...] + up)


def pair_kernel(hidden_width, arrived_ref, chunk_ref, near_ref, across_ref, keep_ref, onward_ref):
    onward_ref[...] = near_ref[...]
    for x in range(2):
        down, up = decode(arrived_ref[x], hidden_width)
        down, up = chunk_ref[x, :, :hidden_width] + down, chunk_ref[x, :, hidden_width:] + up
        if x == 0:
            keep_ref[...] = jnp.concatenate([down, up], axis=1)
        else:
            across_ref[...] = encode(down, up)


def far_kernel(hidden_width, arrived_ref, keep_ref, out_ref):
    down, up = decode(arrived_ref[...], hidden_width)
    out_ref[...] = encode(keep_ref[:, :hidden_width] + down, keep_ref[:, hidden_width:] + up)


def near_kernel(
    hidden_width, gradient_ref, curvature_ref, gradient_keep_ref, curvature_keep_ref, onward_ref, total_ref
):
    pairs = ((gradient_ref, gradient_keep_ref), (curvature_ref, curvature_keep_ref))
    for kind, (arrived_ref, keep_ref) in enumerate(pairs):
        for z in range(2):
            down, up = decode(arrived_ref[z], hidden_width)
            down, up = keep_ref[z, :, :hidden_width] + down, keep_ref[z, :, hidden_width:] + up
            if z == 0:
                total_ref[kind] = jnp.concatenate([down, up], axis=1)
            else:
                onward_ref[kind] = encode(down, up)


def add_kernel(hidden_width, total_ref, arrived_ref, out_ref):
    down, up = decode(arrived_ref[...], hidden_width)
    out_ref[:, :hidden_width] = total_ref[0, :, :hidden_width] + down
    out_ref[:, hidden_width:] = total_ref[0, :, hidden_width:] + up


def total_kernel(hidden_width, gradient_ref, total_ref, far_ref, pair_ref, *out_refs):
    far = decode(far_ref[...], hidden_width)
    totals = [
        (gradient_ref[:, :hidden_width], gradient_ref[:, hidden_width:]),
        (total_ref[1, :, :hidden_width] + far[0], total_ref[1, :, hidden_width:] + far[1]),
    ]
    for kind in range(2):
        down, up = decode(pair_ref[kind], hidden_width)
        out_refs[2 * kind][...] = totals[kind][0] + down
        out_refs[2 * kind + 1][...] = totals[kind][1] + up


class Ring:
    def __init__(self, size):
        self.length = size // 2
        rows = self.length // 2
        self.order = [4 * z for z in range(rows)] + [4 * z + 2 for z in reversed(range(rows))]

    def shift(self, value, step):
        pairs = [
            (chip + core, self.order[(place + step) % self.length] + core)
            for place, chip in enumerate(self.order)
            for core in range(2)
        ]
        return lax.ppermute(value, "expert", pairs)

    def members(self, me):
        rows = self.length // 2
        place = jnp.where(me // 2 % 2 == 0, me // 4, self.length - 1 - me // 4)
        half = self.length // 2
        offsets = [0] + [offset for step in range(1, half) for offset in (self.length - step, step)] + [half]
        there = (place + jnp.array(offsets, jnp.int32)) % self.length
        return jnp.where(there < rows, 4 * there, 4 * (self.length - 1 - there) + 2) + me % 2

    def gather(self, own, passing):
        half = self.length // 2
        pieces = [own]
        ahead, behind = own, own
        for step in range(1, half):
            behind = self.shift(behind, 1)
            ahead = self.shift(ahead, -1)
            if step == 2:
                behind, ahead = passing(behind, ahead)
            pieces += [behind, ahead]
        pieces += [self.shift(behind[:1], 1), self.shift(ahead[1:], -1)]
        return pieces


def exchange(value, mask):
    size = lax.axis_size("expert")
    return lax.ppermute(value, "expert", [(device, device ^ mask) for device in range(size)])


def gathered_plan(
    hidden_of_route,
    expert_of_route,
    gate_of_route,
    capacity,
    output_gradient,
    curvature,
    adapter_down,
    adapter_up,
    down_direction,
    up_direction,
):
    ring = Ring(lax.axis_size("expert"))
    slots = ring.length
    rows = slots // 2
    masks = [4 * z for z in range(rows)] + [4 * z + 2 for z in range(rows)]
    me = lax.axis_index("expert")
    tokens, top = expert_of_route.shape
    both = 2 * tokens
    hidden_width = hidden_of_route.shape[2]
    rank = adapter_down.shape[2]
    model_width = output_gradient.shape[1]
    experts = capacity.shape[0]
    wide = slots * rank
    coded_width = hidden_width + model_width + lanes


    place = []

    def call(kernel, multiplies, outs, *operands, scratch=(), after=(), grant=kernel_vmem):
        space = pltpu.VMEM if grant == kernel_vmem else pltpu.HBM
        places = [pl.BlockSpec(memory_space=pl.ANY) for _ in after] + [
            pl.BlockSpec(memory_space=pltpu.SMEM if any(operand is it for it in place) else space) for operand in operands
        ]
        return pl.pallas_call(
            lambda *refs: kernel(*refs[len(after) :]),
            out_shape=[jax.ShapeDtypeStruct(shape, dtype) for shape, dtype in outs],
            in_specs=places,
            scratch_shapes=scratch,
            compiler_params=pltpu.CompilerParams(vmem_limit_bytes=grant),
            cost_estimate=pl.CostEstimate(flops=2 * multiplies, bytes_accessed=2**20, transcendentals=0),
        )(*after, *operands)

    down_multiplies = 2 * top * both * hidden_width * wide
    up_multiplies = both * model_width * wide

    first = (
        expert_of_route.T,
        gate_of_route.T,
        curvature[None],
        down_direction[0].T,
        adapter_down[0].T,
        adapter_up[0],
        up_direction[0],
    )
    piece, small = call(
        functools.partial(prepare_kernel, experts),
        10**8,
        [((2, rank, coded_width), i16), (((2 * top + 8) // 8 * 8, tokens), f32)],
        *first,
        scratch=[pltpu.VMEM(operand.shape, operand.dtype) for operand in first]
        + [pltpu.SemaphoreType.DMA((len(first),))],
        grant=whole_vmem,
    )
    arrivals = ring.members(me)
    slot_of_arrival = (arrivals ^ me) // 4 + rows * ((arrivals ^ me) // 2 % 2)
    place.append(jnp.concatenate([me[None], arrivals, me ^ jnp.array(masks, jnp.int32), slot_of_arrival]).astype(jnp.int32))
    small_other = exchange(small, 1)
    hidden = hidden_of_route.reshape(tokens * top, hidden_width)
    small_columns, local_rank, gate, same, mask, hidden_other, gradient_other = call(
        functools.partial(tokens_kernel, top, slots),
        10**9,
        [
            ((both, small.shape[0]), f32),
            ((2, tokens, wide), f32),
            ((2, tokens, wide), f32),
            ((top * tokens, tokens), bf16),
            ((2, top * tokens, wide), bf16),
            (hidden.shape, bf16),
            (output_gradient.shape, bf16),
        ],
        *place,
        small,
        small_other,
        exchange(hidden, 1),
        exchange(output_gradient, 1),
        scratch=[pltpu.SemaphoreType.DMA((2,))],
    )
    def passing(behind, ahead):
        return call(pass_kernel, 10**8, [(piece.shape, i16)] * 2, behind, ahead, after=[same])

    pieces = ring.gather(piece, passing)
    capacity_row = jnp.pad(capacity.astype(f32), (counts_lane, lanes - counts_lane - experts))[None, :]

    def reduced(first, count, halved, *parts, after=()):
        return call(
            functools.partial(reduce_kernel, top, first, count, halved),
            2 * down_multiplies * count // slots,
            [((both, 2 * count * rank), f32)],
            *place,
            small_columns,
            hidden,
            hidden_other,
            *parts,
            scratch=[pltpu.VMEM((tokens * top, 2 * count * rank), f32)],
            after=after,
        )[0]

    early = slots // 2
    reduced_early = reduced(0, early, False, *pieces[:early])
    (prior,) = call(prior_kernel, 10**8, [((8, lanes), f32)], *place, *pieces[:-1], after=[reduced_early])
    prior_arrived = exchange(prior, 1)
    reduced_late = reduced(early, slots - early, True, *pieces[early:], after=[prior])
    weight, weighted, tangent, coded, high, low = call(
        functools.partial(tangent_kernel, slots),
        6 * up_multiplies,
        [
            ((both, wide), f32),
            ((both, 2 * wide), f32),
            ((both, model_width), f32),
            ((both, model_width), bf16),
            ((2, slots, rank, model_width), bf16),
            ((2, slots, rank, model_width), bf16),
        ],
        *place,
        local_rank,
        gate,
        capacity_row,
        prior,
        prior_arrived,
        reduced_early,
        reduced_late,
        *pieces,
    )
    arrived = exchange(coded, 1)
    left = [pltpu.VMEM((2, top * tokens, 2 * wide), bf16)]
    chunks = [((2, rank, hidden_width + model_width), f32), ((2, rank, coded_width), i16)] * 2
    gradient_keep, gradient_near, gradient_chunk, gradient_far, up, to = call(
        gradient_kernel,
        down_multiplies + 8 * up_multiplies,
        chunks + [((wide, model_width), f32), ((both, wide), f32)],
        same,
        mask,
        hidden,
        hidden_other,
        output_gradient,
        gradient_other,
        weight,
        weighted,
        high,
        low,
        scratch=left,
    )
    gradient_far = exchange(gradient_far, 4)
    gradient_near = exchange(gradient_near, 2)
    curvature_keep, curvature_near, curvature_chunk, curvature_far = call(
        functools.partial(curvature_kernel, top),
        down_multiplies + 6 * up_multiplies,
        chunks,
        small_columns,
        same,
        mask,
        hidden,
        hidden_other,
        weight,
        weighted,
        high,
        low,
        up,
        to,
        tangent,
        arrived,
        scratch=left,
    )

    hop = 2 * 10**9

    one = (rank, hidden_width + model_width)
    one_coded = (rank, coded_width)

    def hop_call(kernel, outs, *operands, after=()):
        return call(functools.partial(kernel, hidden_width), hop, outs, *operands, after=after)

    curvature_far = exchange(curvature_far, 4)
    pair = [(one_coded, i16), (one, f32), ((2,) + one_coded, i16)]
    gradient_across, gradient_pair, curvature_near = hop_call(
        pair_kernel, pair, gradient_far, gradient_chunk, curvature_near, after=[curvature_keep]
    )
    curvature_near = exchange(curvature_near, 2)
    curvature_across, curvature_pair, gradient_near = hop_call(
        pair_kernel, pair, curvature_far, curvature_chunk, gradient_near, after=[gradient_across]
    )
    (gradient_beyond,) = hop_call(
        far_kernel,
        [(one_coded, i16)],
        exchange(gradient_across, 2),
        gradient_pair,
        after=[curvature_across],
    )
    onward, total = hop_call(
        near_kernel,
        [((2,) + one_coded, i16), ((2,) + one, f32)],
        gradient_near,
        curvature_near,
        gradient_keep,
        curvature_keep,
        after=[gradient_beyond],
    )
    (curvature_beyond,) = hop_call(
        far_kernel, [(one_coded, i16)], exchange(curvature_across, 2), curvature_pair, after=[onward]
    )
    (gradient_total,) = hop_call(
        add_kernel, [(one, f32)], total, exchange(gradient_beyond, 8), after=[curvature_beyond]
    )
    down_gradient, up_gradient, curvature_down, curvature_up = hop_call(
        total_kernel,
        [((rank, hidden_width), f32), ((rank, model_width), f32)] * 2,
        gradient_total,
        total,
        exchange(curvature_beyond, 8),
        exchange(onward, 4),
    )
    return down_gradient.T[None], up_gradient[None], curvature_down.T[None], curvature_up[None]


def carried_in(value, axis, join, neutral):
    count, mine = (lax.axis_size(axis), lax.axis_index(axis))
    pieces = lax.all_gather(value, axis)
    so_far = jnp.full_like(value, 0) + jnp.asarray(neutral, value.dtype)

    def lap(position, so_far):
        longer = join(so_far, pieces[position])
        return jnp.where(position < mine, longer, so_far)

    return lax.fori_loop(0, count - 1, lap, so_far)


def add_counts(earlier, later):
    return earlier + later


def routed_plan(
    hidden_of_route,
    expert_of_route,
    gate_of_route,
    capacity,
    output_gradient,
    curvature,
    adapter_down,
    adapter_up,
    down_direction,
    up_direction,
):
    finest_precision = lax.Precision.HIGHEST
    group_size = lax.axis_size("expert")
    tok_rows, top_count = expert_of_route.shape
    hidden_width = hidden_of_route.shape[2]
    resident_experts = adapter_down.shape[0]
    adapter_rank = adapter_down.shape[2]
    model_width = output_gradient.shape[1]
    experts = resident_experts * group_size
    slot_most = 2 * tok_rows * top_count // experts
    routes = expert_of_route.reshape(-1)
    onehot = (routes[:, None] == jnp.arange(experts, dtype=jnp.int32)[None, :]).astype(jnp.int32)
    earlier = jnp.cumsum(onehot, axis=0) - onehot
    local_rank = jnp.sum(earlier * onehot, axis=1)
    counts = jnp.sum(onehot, axis=0)
    prior_count = carried_in(counts, "expert", add_counts, jnp.zeros_like(counts))
    global_rank = local_rank + jnp.sum(onehot * prior_count[None, :], axis=1)
    route_limit = jnp.sum(onehot * capacity[None, :], axis=1)
    retained_mask = (global_rank < route_limit).astype(jnp.float32)
    weight_of_route = (
        adapter_scale * gate_of_route.reshape(-1).astype(jnp.float32) * retained_mask
    ).astype(jnp.bfloat16)
    slot_index = routes * slot_most + local_rank
    layout = (group_size, resident_experts, slot_most)
    send_hidden = (
        jnp.zeros((experts * slot_most, hidden_width), jnp.bfloat16)
        .at[slot_index]
        .set(hidden_of_route.reshape(-1, hidden_width))
        .reshape(layout + (hidden_width,))
    )
    send_weight = (
        jnp.zeros((experts * slot_most,), jnp.bfloat16)
        .at[slot_index]
        .set(weight_of_route)
        .reshape(layout)
    )
    down_stacked = jnp.concatenate([adapter_down, down_direction], axis=2)
    up_stacked = jnp.concatenate([adapter_up, up_direction], axis=1)

    def spread(token_rows):
        per_route = jnp.repeat(token_rows, top_count, axis=0)
        placed = (
            jnp.zeros((experts * slot_most, model_width), jnp.bfloat16)
            .at[slot_index]
            .set(per_route)
        )
        return placed.reshape(layout + (model_width,))

    send_residual = spread(output_gradient)
    pieces = (
        lax.all_to_all(send_hidden, "expert", split_axis=0, concat_axis=0, tiled=True),
        lax.all_to_all(send_weight, "expert", split_axis=0, concat_axis=0, tiled=True),
    )
    hidden_rows = pieces[0].astype(jnp.float32)
    weight_rows = pieces[1].astype(jnp.float32)[..., None]
    reduced_hidden = jnp.einsum(
        "cjif,jfk->cjik", hidden_rows, down_stacked, precision=finest_precision
    )
    exchanged_rows = jnp.concatenate(
        [reduced_hidden[..., adapter_rank:], reduced_hidden[..., :adapter_rank]], axis=3
    )
    tangent_out = weight_rows * jnp.einsum(
        "cjik,jkd->cjid", exchanged_rows, up_stacked, precision=finest_precision
    )
    returned = lax.all_to_all(
        tangent_out.astype(jnp.bfloat16), "expert", split_axis=0, concat_axis=0, tiled=True
    )
    results = (returned, reduced_hidden) + tuple(pieces)
    returned = results[0]
    reduced_hidden = results[1]
    hidden_rows = results[2]
    weight_rows = results[3]
    route_tangent = returned.reshape(experts * slot_most, model_width)[slot_index]
    out_tangent = jnp.sum(
        route_tangent.reshape(tok_rows, top_count, model_width).astype(jnp.float32), axis=1
    )
    resid_tangent = (curvature[:, None] * out_tangent).astype(jnp.bfloat16)
    send_tangent = spread(resid_tangent)
    residual_rows, tangent_rows = (
        lax.all_to_all(send_residual, "expert", split_axis=0, concat_axis=0, tiled=True),
        lax.all_to_all(send_tangent, "expert", split_axis=0, concat_axis=0, tiled=True),
    )
    residual_full = residual_rows.astype(jnp.float32)
    complete_tangent = tangent_rows.astype(jnp.float32)
    weight_column = weight_rows.astype(jnp.float32)[..., None]
    residual_reduced = jnp.einsum(
        "wyov,yqv->wyoq", residual_full, up_stacked, precision=finest_precision
    )
    reduced_tangent = jnp.einsum(
        "wyov,yqv->wyoq", complete_tangent, adapter_up, precision=finest_precision
    )
    left_terms = jnp.concatenate(
        [
            weight_column * residual_reduced[..., :adapter_rank],
            weight_column * (reduced_tangent + residual_reduced[..., adapter_rank:]),
        ],
        axis=3,
    )
    down_terms = jnp.einsum(
        "cjif,cjik->jfk", hidden_rows.astype(jnp.float32), left_terms, precision=finest_precision
    )
    raised_update = weight_column * reduced_hidden[..., :adapter_rank]
    raised_tangent_update = weight_column * reduced_hidden[..., adapter_rank:]
    up_terms = jnp.einsum(
        "cjik,cjid->jkd",
        jnp.concatenate([raised_update, raised_tangent_update], axis=3),
        residual_full,
        precision=finest_precision,
    )
    curvature_piece = up_terms[:, adapter_rank:] + jnp.einsum(
        "cjik,cjid->jkd", raised_update, complete_tangent, precision=finest_precision
    )
    return (
        down_terms[..., :adapter_rank],
        up_terms[:, :adapter_rank],
        down_terms[..., adapter_rank:],
        curvature_piece,
    )


def local(*arguments):
    factor_bytes = 2 * 4 * (arguments[6].size + arguments[7].size) * lax.axis_size("expert")
    fits = lax.axis_size("expert") == 16 and 4 * factor_bytes <= kernel_vmem
    plan = gathered_plan if fits else routed_plan
    return plan(*arguments)


def solution(mesh):
    return jax.shard_map(
        local,
        mesh=mesh,
        in_specs=(
            P(("groups", "expert"), None, None),
            P(("groups", "expert"), None),
            P(("groups", "expert"), None),
            P("groups"),
            P(("groups", "expert"), None),
            P(("groups", "expert")),
            P("expert", None, None),
            P("expert", None, None),
            P(("groups", "expert"), None, None),
            P(("groups", "expert"), None, None),
        ),
        out_specs=(
            P(("groups", "expert"), None, None),
            P(("groups", "expert"), None, None),
            P(("groups", "expert"), None, None),
            P(("groups", "expert"), None, None),
        ),
        check_vma=False,
    )
```
